32 devices in a mesh: grp: 16 (over z, y, x), tile: 2 (over core).
Axes of the slice: x: 2, y: 2, z: 4, core: 2. Of those that a mesh axis runs over, the one named last changes fastest.
Arguments:
- starting_realizations: float32 [1024, 2, 4, 16, 128], P('grp', None, None, 'tile'), may hold values from -6 to 6
- diffusivity: float32 [4, 128], replicated, may hold values from 0.1 to 0.24
- eastward_velocity: float32 [4], replicated, may hold values from -0.4 to 0.4
- northward_velocity: float32 [4], replicated, may hold values from -0.4 to 0.4
- obs_cell: int32 [2, 16, 256], P('tile'), may hold values from 0 to 2047
- obs_count: int32 [2, 16], P('tile', 'grp'), may hold values from 1 to 256
- obs_value: float32 [2, 16, 256], P('tile', 'grp'), may hold values from -15 to 15
- obs_weight: float32 [2, 16, 256], P('tile', 'grp'), may hold values from 0.05 to 0.5
Outputs:
- analysis: bfloat16 [1024, 2, 4, 16, 128], P('grp', None, None, 'tile')
The draws below stay inside these ranges and needn't reach their ends.
All inputs are finite; a program needn't handle non-finite values.
Results may differ from the reference program's by a relative error of at most 0.0062.
Values may be sent and summed in bfloat16 or wider, within the bound.
No kernel may reach another device: no remote copies, remote signals or barrier semaphores. Data moves between devices by JAX's collectives and lax.ppermute only.
A program may use at most 128 MiB of HBM per device.

```python
import math
import jax
import jax.numpy as jnp
from jax import lax

REALIZATIONS = 1024
LAYER_NUMBER = 4
TILE_SPAN = 8
STEPS = 2
OBS = 256
GRID_SPAN_FIRST = 16
GRID_SPAN_SECOND = 128
STATE = 512
REGION = 2048
N_GRP = 16
N_TILE = 2


def touch_ends(values, own_key, least, top_value):
    extent = values.shape
    place = [jax.random.randint(jax.random.fold_in(own_key, axis), (), 0, extent[axis]) for axis in range(len(extent))]
    values = values.at[tuple(place)].set(least)
    longest = extent.index(max(extent))
    place[longest] = (place[longest] + 1) % extent[longest]
    return values.at[tuple(place)].set(top_value)


def block_levels(own_key, dims, pieces, least, largest):
    def one(position, blocks):
        heights = jax.random.uniform(jax.random.fold_in(jax.random.fold_in(own_key, 6), position), (blocks,), jnp.float32, least / len(pieces), largest / len(pieces))
        return jnp.repeat(jnp.exp(heights), dims[position] // blocks).reshape((-1,) + (1,) * (len(dims) - position - 1))

    factor_of = one(*pieces[0])
    for cut in pieces[1:]:
        factor_of = factor_of * one(*cut)
    return factor_of


def gaussian(rng, dims, width, bound, shards=(), kind=jnp.bfloat16):
    entries = width * jax.random.normal(rng, dims, jnp.float32)
    if shards:
        entries = entries * block_levels(rng, dims, shards, -0.22, 0.18)
    return jnp.clip(entries, -bound, bound).astype(kind)


def setup_inputs(seed: int = 0) -> dict:
    arg_keys = jax.random.split(jax.random.key(seed), 9)
    starting_realizations = gaussian(arg_keys[0], (REALIZATIONS, 2, LAYER_NUMBER, GRID_SPAN_FIRST, GRID_SPAN_SECOND), 1.0, 6.0, ((0, 16), (3, 2)), jnp.float32)
    diffusivity = jnp.clip(jnp.exp(jax.random.uniform(arg_keys[1], (LAYER_NUMBER, GRID_SPAN_SECOND), jnp.float32, math.log(0.1), math.log(0.24))), 0.1, 0.24)
    eastward_velocity = jnp.clip(jax.random.uniform(arg_keys[2], (LAYER_NUMBER,), jnp.float32, -0.4, 0.4), -0.4, 0.4)
    northward_velocity = jnp.clip(jax.random.uniform(arg_keys[3], (LAYER_NUMBER,), jnp.float32, -0.4, 0.4), -0.4, 0.4)
    obs_cell = touch_ends(jax.random.randint(arg_keys[4], (N_TILE, N_GRP, OBS), 0, REGION), jax.random.fold_in(arg_keys[4], 1), 0, REGION - 1).astype(jnp.int32)
    obs_count = touch_ends(jax.random.randint(arg_keys[5], (N_TILE, N_GRP), 1, OBS + 1), jax.random.fold_in(arg_keys[5], 1), 1, OBS).astype(jnp.int32)
    obs_value = gaussian(arg_keys[6], (N_TILE, N_GRP, OBS), 3.0, 15.0, ((0, 2), (1, 16)), jnp.float32)
    obs_weight = jnp.clip(jnp.exp(math.log(0.5) - 2.3025851 * jax.random.uniform(arg_keys[7], (N_TILE, N_GRP, OBS), jnp.float32) ** block_levels(arg_keys[7], (N_TILE, N_GRP, OBS), ((0, 2), (1, 16)), -0.2, 0.2)), 0.05, 0.5)
    return {"starting_realizations": starting_realizations, "diffusivity": diffusivity, "eastward_velocity": eastward_velocity, "northward_velocity": northward_velocity, "obs_cell": obs_cell, "obs_count": obs_count, "obs_value": obs_value, "obs_weight": obs_weight}


HIGH = lax.Precision.HIGHEST

def tendency(center, east_cell, west_cell, north_cell, south_cell, diffusivity, eastward_velocity, northward_velocity):
    laplace = east_cell + west_cell + north_cell + south_cell - 4.0 * center
    transport = eastward_velocity[:, None, None] * (east_cell - west_cell) * 0.5 + northward_velocity[:, None, None] * (north_cell - south_cell) * 0.5
    return center + diffusivity[:, None, :] * laplace - transport

def analyze(packed):
    realization_fields, measured_realizations, obs_total, obs_value, obs_weight = packed
    members = realization_fields.shape[0]
    average = lax.optimization_barrier(jnp.mean(measured_realizations, 0))
    obs_dev = measured_realizations - average
    active = (jnp.arange(OBS) < obs_total).astype(jnp.float32)
    obs_scale = active * obs_weight
    weighted = obs_dev * obs_scale
    gram_sum = jnp.dot(weighted, obs_dev.T, precision=HIGH, preferred_element_type=jnp.float32)
    innovation = jnp.dot(weighted, obs_value - average, precision=HIGH, preferred_element_type=jnp.float32)
    identity = jnp.eye(members, dtype=jnp.float32)
    system = gram_sum + (members - 1.0) * identity
    trace_mean = jnp.trace(system) / members
    first_iter = system / trace_mean
    first_poly = 1.5 * identity - 0.5 * first_iter
    second_iter = jnp.dot(first_iter, first_poly, precision=HIGH, preferred_element_type=jnp.float32)
    second_poly = 1.5 * identity - 0.5 * jnp.dot(first_poly, second_iter, precision=HIGH, preferred_element_type=jnp.float32)
    root_iter = jnp.dot(second_poly, first_poly, precision=HIGH, preferred_element_type=jnp.float32)
    inv_root = root_iter / jnp.sqrt(trace_mean)
    mean_weights = jnp.dot(inv_root, jnp.dot(inv_root, innovation, precision=HIGH, preferred_element_type=jnp.float32), precision=HIGH, preferred_element_type=jnp.float32)
    weights = (jnp.sqrt(members - 1.0) * inv_root + mean_weights[:, None]).astype(jnp.bfloat16)
    flat_states = realization_fields.astype(jnp.float32)
    centre = lax.optimization_barrier(jnp.mean(flat_states, 0))
    deviation = (flat_states - centre).astype(jnp.bfloat16)
    updated = centre + lax.dot_general(weights, deviation, (((0,), (0,)), ((), ())), preferred_element_type=jnp.float32)
    return updated.astype(jnp.bfloat16)

def reference(starting_realizations, diffusivity, eastward_velocity, northward_velocity, obs_cell, obs_count, obs_value, obs_weight):

    def handle_bundle(member_batch):
        field_now = member_batch
        for repeat in range(STEPS):
            field_now = tendency(field_now, jnp.roll(field_now, -1, 3), jnp.roll(field_now, 1, 3), jnp.roll(field_now, -1, 4), jnp.roll(field_now, 1, 4), diffusivity, eastward_velocity, northward_velocity)
        return field_now
    bundled_subdomains = starting_realizations.reshape(N_GRP, REALIZATIONS // N_GRP, 2, LAYER_NUMBER, GRID_SPAN_FIRST, GRID_SPAN_SECOND)
    predicted_field = lax.map(handle_bundle, bundled_subdomains).reshape(REALIZATIONS, 2, LAYER_NUMBER, GRID_SPAN_FIRST, GRID_SPAN_SECOND)
    tile_index = jnp.arange(N_TILE, dtype=jnp.int32)[:, None, None]
    block_index = jnp.arange(N_GRP, dtype=jnp.int32)[None, :, None]
    layer_index = obs_cell // (4 * TILE_SPAN * TILE_SPAN)
    remainder = obs_cell % (4 * TILE_SPAN * TILE_SPAN)
    row_off = remainder // (2 * TILE_SPAN)
    col_off = remainder % (2 * TILE_SPAN)
    row_global = (tile_index * TILE_SPAN - TILE_SPAN // 2 + row_off) % GRID_SPAN_FIRST
    col_global = (block_index * TILE_SPAN - TILE_SPAN // 2 + col_off) % GRID_SPAN_SECOND
    flattened_position = ((layer_index * GRID_SPAN_FIRST + row_global) * GRID_SPAN_SECOND + col_global).astype(jnp.int32)
    measured_realizations = jnp.take(predicted_field.reshape(REALIZATIONS, -1), flattened_position.reshape(-1), axis=1)
    measured_realizations = measured_realizations.reshape(REALIZATIONS, N_TILE * N_GRP, OBS).transpose(1, 0, 2)
    realization_fields = predicted_field.astype(jnp.bfloat16).reshape(REALIZATIONS, 2, LAYER_NUMBER, N_TILE, TILE_SPAN, N_GRP, TILE_SPAN)
    realization_fields = realization_fields.transpose(3, 5, 0, 1, 2, 4, 6).reshape(N_TILE * N_GRP, REALIZATIONS, STATE)
    result = lax.map(analyze, (realization_fields, measured_realizations, obs_count.reshape(-1), obs_value.reshape(-1, OBS), obs_weight.reshape(-1, OBS)))
    result = result.reshape(N_TILE, N_GRP, REALIZATIONS, 2, LAYER_NUMBER, TILE_SPAN, TILE_SPAN).transpose(2, 3, 4, 0, 5, 1, 6)
    return result.reshape(REALIZATIONS, 2, LAYER_NUMBER, GRID_SPAN_FIRST, GRID_SPAN_SECOND)
```

```python
import functools

import jax
import jax.numpy as jnp
from jax import lax
from jax.experimental import pallas as pl
from jax.experimental.pallas import tpu as pltpu
from jax.sharding import PartitionSpec as P

SPAN = 8
STEPS = 2
EDGE = SPAN // 2
VMEM_LIMIT = 48 * 1024 * 1024

HIGH = lax.Precision.HIGHEST
ROWS = (((1,), (1,)), ((), ()))


def params():
    return pltpu.CompilerParams(vmem_limit_bytes=VMEM_LIMIT)


def vmem(count):
    return [pl.BlockSpec(memory_space=pltpu.VMEM)] * count


def smem(count):
    return [pl.BlockSpec(memory_space=pltpu.SMEM)] * count


def dot(a, b, **kw):
    return jnp.dot(a, b, preferred_element_type=jnp.float32, **kw)


def dot_rows(a, b):
    return lax.dot_general(a, b, ROWS, preferred_element_type=jnp.float32)


def permutation(size, shift):
    row = lax.broadcasted_iota(jnp.int32, (size, size), 0)
    column = lax.broadcasted_iota(jnp.int32, (size, size), 1)
    return (lax.rem(row + shift + size, size) == column).astype(jnp.bfloat16)


def eye(size):
    row = lax.broadcasted_iota(jnp.int32, (size, size), 0)
    column = lax.broadcasted_iota(jnp.int32, (size, size), 1)
    return row == column


def column_of(row):
    return jnp.sum(jnp.where(eye(row.shape[1]), row, 0.0), axis=1, keepdims=True)


def row_of(column):
    return jnp.sum(jnp.where(eye(column.shape[0]), column, 0.0), axis=0, keepdims=True)


def forecast_rows(read, first, last, coefficients, write):
    middle, east, west, north, south = coefficients

    def step(below, here, above):
        columns = here.shape[1]
        return (
            middle * here
            + east * above
            + west * below
            + north * pltpu.roll(here, columns - 1, 1)
            + south * pltpu.roll(here, 1, 1)
        )

    start = [read(first - 2), read(first - 1), read(first)]
    once = [None, None, None]
    for r in range(first - 1, last + 1):
        once = [once[1], once[2], step(*start)]
        if r >= first + 1:
            write(r - 1, step(*once))
        if r < last:
            start = [start[1], start[2], read(r + 2)]


def coefficients_of(level, diff_ref, east_ref, north_ref):
    spread = diff_ref[pl.ds(level, 1), :]
    u = 0.5 * east_ref[level]
    w = 0.5 * north_ref[level]
    return 1.0 - 4.0 * spread, spread - u, spread + u, spread - w, spread + w


def row_reader(level, var, dims, own, low, high):
    members, variables, levels, span = dims
    stride = variables * levels * span

    def read(r):
        ref, at = (low, r + span) if r < 0 else (own, r) if r < span else (high, r - span)
        return ref[pl.ds((var * levels + level) * span + at, members, stride=stride), :]

    return read


def forecast_kernel(dims, own, low, high, diff, east, north, fields, packed):
    members, variables, levels, span = dims
    columns = own.shape[1]
    identity = permutation(columns, 0)

    @pl.loop(0, levels)
    def _(level):
        coefficients = coefficients_of(level, diff, east, north)
        for var in range(variables):

            def write(r, value):
                fields[level * span + r, var * members : (var + 1) * members, :] = value.astype(
                    jnp.bfloat16
                )

            read = row_reader(level, var, dims, own, low, high)
            forecast_rows(read, 0, span, coefficients, write)
        for r in range(0, span, 2):
            pair = [
                dot_rows(identity, fields[level * span + r + i]).reshape(
                    columns // SPAN, SPAN, variables * members
                )
                for i in range(2)
            ]
            at = pl.multiple_of((level * span + r) * SPAN, 2 * SPAN)
            packed[:, pl.ds(at, 2 * SPAN), :] = jnp.concatenate(pair, axis=1).astype(jnp.bfloat16)


def forecast(dims, own, low, high, diff, east, north):
    members, variables, levels, span = dims
    columns = own.shape[1]
    lanes = variables * members
    return pl.pallas_call(
        functools.partial(forecast_kernel, dims),
        out_shape=(
            jax.ShapeDtypeStruct((levels * span, lanes, columns), jnp.bfloat16),
            jax.ShapeDtypeStruct((columns // SPAN, levels * span * SPAN, lanes), jnp.bfloat16),
        ),
        in_specs=vmem(4) + smem(2),
        out_specs=tuple(vmem(2)),
        compiler_params=params(),
        cost_estimate=pl.CostEstimate(flops=10**9, bytes_accessed=8 * 2**20, transcendentals=0),
    )(own, low, high, diff, east, north)


def observe_kernel(
    dims, own, low, high, fields, cells, diff, east, north, out, edges, region
):
    members, variables, levels, span = dims
    columns = own.shape[1]
    lanes = variables * members
    slots = cells.shape[1]
    width = 2 * EDGE + SPAN
    rows = 2 * EDGE + span
    even = permutation(columns, -EDGE)
    odd = permutation(columns, SPAN - EDGE)

    @pl.loop(0, levels)
    def _(level):
        coefficients = coefficients_of(level, diff, east, north)
        for var in range(variables):

            def write(r, value):
                slot = r + EDGE if r < 0 else r - span + EDGE
                edges[slot, var * members : (var + 1) * members, :] = value.astype(jnp.bfloat16)

            read = row_reader(level, var, dims, own, low, high)
            forecast_rows(read, -EDGE, 0, coefficients, write)
            forecast_rows(read, span, span + EDGE, coefficients, write)
        for r in range(rows):
            if r < EDGE:
                field = edges[r]
            elif r < EDGE + span:
                field = fields[level * span + r - EDGE]
            else:
                field = edges[r - span]
            at = pl.multiple_of((level * rows + r) * width, width)
            for first, order in ((0, even), (1, odd)):
                turned = dot_rows(order, field).astype(jnp.bfloat16)
                for j in range(columns // width):
                    region[2 * j + first, pl.ds(at, width), :] = turned[
                        j * width : (j + 1) * width, :
                    ]

    entries = levels * rows * width
    chunk = 256
    left = lax.broadcasted_iota(jnp.int32, (slots, lanes), 1) < members
    lane = lax.broadcasted_iota(jnp.int32, (slots, chunk), 1)

    @pl.loop(0, columns // SPAN)
    def _(block):
        cell = column_of(cells[pl.ds(block, 1), :].astype(jnp.float32)).astype(jnp.int32)
        second = cell >= entries
        offset = jnp.where(second, cell - entries, cell) - lane
        total = jnp.zeros((slots, lanes), jnp.float32)
        for at in range(0, entries, chunk):
            pick = jnp.where(offset == at, 1.0, 0.0).astype(jnp.bfloat16)
            total += dot(pick, region[block, at : at + chunk, :])
        other = pltpu.roll(total, members, 1)
        to_left = jnp.where(second, other, total)[: slots // 2]
        to_right = jnp.where(second, total, other)[slots // 2 :]
        out[block] = jnp.where(left[: slots // 2], to_left, to_right).astype(jnp.bfloat16)


def observe(dims, own, low, high, fields, cells, diff, east, north):
    members, variables, levels, span = dims
    columns = own.shape[1]
    lanes = variables * members
    blocks, slots = cells.shape
    rows = 2 * EDGE + span
    return pl.pallas_call(
        functools.partial(observe_kernel, dims),
        out_shape=jax.ShapeDtypeStruct((blocks, slots // 2, lanes), jnp.bfloat16),
        in_specs=vmem(6) + smem(2),
        out_specs=pl.BlockSpec(memory_space=pltpu.VMEM),
        scratch_shapes=[
            pltpu.VMEM((2 * EDGE, lanes, columns), jnp.bfloat16),
            pltpu.VMEM((blocks, levels * rows * (2 * EDGE + SPAN), lanes), jnp.bfloat16),
        ],
        compiler_params=params(),
        cost_estimate=pl.CostEstimate(flops=6 * 10**9, bytes_accessed=8 * 2**20, transcendentals=0),
    )(own, low, high, fields, cells, diff, east, north)


def analyse_kernel(states, seen, count, value, weight, out, raw, dev, obs, high, low):
    groups, half, lanes = states.shape
    members = lanes // 2
    total_members = groups * members
    slots = 2 * seen.shape[1]
    left_s = lax.broadcasted_iota(jnp.int32, (half, lanes), 1) < members
    left_o = lax.broadcasted_iota(jnp.int32, (slots // 2, lanes), 1) < members

    for j in range(groups // 2):
        a = seen[2 * j].astype(jnp.float32)
        b = seen[2 * j + 1].astype(jnp.float32)
        here = slice(j * lanes, (j + 1) * lanes)
        obs[: slots // 2, here] = jnp.where(left_o, a, pltpu.roll(b, members, 1))
        obs[slots // 2 :, here] = jnp.where(left_o, pltpu.roll(a, members, 1), b)

    used = lax.broadcasted_iota(jnp.int32, (1, slots), 1) < count[0, 0]
    root = column_of(jnp.where(used, jnp.sqrt(weight[...]), 0.0))
    observed = obs[...]
    mean = jnp.sum(observed, axis=1, keepdims=True) * (1.0 / total_members)
    scaled = (observed - mean) * root
    energy = jnp.sum(jnp.sum(scaled * scaled, axis=1, keepdims=True), axis=0, keepdims=True)
    top = scaled.astype(jnp.bfloat16)
    high[...] = top
    low[...] = (scaled - top.astype(jnp.float32)).astype(jnp.bfloat16)
    misfit = row_of(root * (column_of(value[...]) - mean))

    c = total_members - 1.0
    s = energy * (1.0 / total_members) + c
    inverse = 1.0 / s
    a = c * inverse
    p = 1.5 - 0.5 * a
    p2 = p * p
    p3 = p2 * p
    base = 1.5 * p - 0.5 * a * p3
    q0 = -0.75 - 0.5 * (p3 - 1.5 * a * p2)
    q1 = -0.5 * (0.75 * a * p - 1.5 * p2)
    q2 = -0.5 * (0.75 * p - 0.125 * a)
    small = (
        dot_rows(high[...], high[...])
        + dot_rows(high[...], low[...])
        + dot_rows(low[...], high[...])
    ) * inverse
    diagonal = eye(slots)
    square = dot(small, small, precision=HIGH)
    tail = dot(square, jnp.where(diagonal, q2, 0.0) + 0.0625 * small, precision=HIGH)
    poly = jnp.where(diagonal, q0, 0.0) + q1 * small + tail

    def apply_column(vector):
        inner = jnp.sum(poly * vector, axis=1, keepdims=True)
        return jnp.sum(small * inner, axis=0, keepdims=True) + base * vector

    gain = apply_column(apply_column(misfit)) * inverse

    sums = [jnp.zeros((half, lanes), jnp.float32)] * 2
    for j in range(groups // 2):
        x = states[2 * j].astype(jnp.float32)
        y = states[2 * j + 1].astype(jnp.float32)
        first = jnp.where(left_s, x, pltpu.roll(y, members, 1))
        second = jnp.where(left_s, pltpu.roll(x, members, 1), y)
        here = slice(j * lanes, (j + 1) * lanes)
        raw[:half, here] = first.astype(jnp.bfloat16)
        raw[half:, here] = second.astype(jnp.bfloat16)
        sums = [sums[0] + first, sums[1] + second]
    centre = jnp.concatenate([jnp.sum(x, axis=1, keepdims=True) for x in sums], axis=0) * (
        1.0 / total_members
    )
    dev[...] = (raw[...].astype(jnp.float32) - centre).astype(jnp.bfloat16)

    cross = dot_rows(dev[...], high[...]) + dot_rows(dev[...], low[...])
    shift = centre + jnp.sum(cross * gain, axis=1, keepdims=True)
    stretch = jnp.sqrt(a)
    mix = (dot(cross, poly, precision=HIGH) * (stretch * inverse)).astype(jnp.bfloat16)
    alpha = stretch * base
    for j in range(groups // 2):
        here = slice(j * lanes, (j + 1) * lanes)
        new = dot(mix, high[:, here]) + alpha * dev[:, here].astype(jnp.float32) + shift
        x, y = new[:half], new[half:]
        out[2 * j] = jnp.where(left_s, x, pltpu.roll(y, members, 1)).astype(jnp.bfloat16)
        out[2 * j + 1] = jnp.where(left_s, pltpu.roll(x, members, 1), y).astype(jnp.bfloat16)


def analyse(states, seen, count, value, weight):
    groups, half, lanes = states.shape
    total = groups * lanes // 2
    slots = value.shape[1]
    return pl.pallas_call(
        analyse_kernel,
        out_shape=jax.ShapeDtypeStruct(states.shape, jnp.bfloat16),
        in_specs=vmem(2) + smem(1) + vmem(2),
        out_specs=pl.BlockSpec(memory_space=pltpu.VMEM),
        scratch_shapes=[
            pltpu.VMEM((2 * half, total), jnp.bfloat16),
            pltpu.VMEM((2 * half, total), jnp.bfloat16),
            pltpu.VMEM((slots, total), jnp.float32),
            pltpu.VMEM((slots, total), jnp.bfloat16),
            pltpu.VMEM((slots, total), jnp.bfloat16),
        ],
        compiler_params=params(),
        cost_estimate=pl.CostEstimate(flops=5 * 10**9, bytes_accessed=8 * 2**20, transcendentals=0),
    )(states, seen, count, value, weight)


def restore_kernel(dims, blocks_ref, out, turned):
    members, variables, levels, span = dims
    blocks, _, lanes = blocks_ref.shape
    columns = blocks * SPAN
    identity = permutation(lanes, 0)

    @pl.loop(0, levels)
    def _(level):
        for r in range(0, span, 2):
            at = pl.multiple_of((level * span + r) * SPAN, 2 * SPAN)
            pair = blocks_ref[:, pl.ds(at, 2 * SPAN), :].astype(jnp.float32)
            for i in range(2):
                one = pair[:, i * SPAN : (i + 1) * SPAN, :].reshape(columns, lanes)
                rows = dot_rows(identity, one.astype(jnp.bfloat16))
                turned[pl.ds(r + i, lanes, stride=span), :] = rows
        for var in range(variables):
            half = turned[var * members * span : (var + 1) * members * span, :]
            out[:, var, level] = half.reshape(members, span, columns).astype(jnp.bfloat16)


def restore(dims, blocks):
    members, variables, levels, span = dims
    columns = blocks.shape[0] * SPAN
    return pl.pallas_call(
        functools.partial(restore_kernel, dims),
        out_shape=jax.ShapeDtypeStruct((members, variables, levels, span, columns), jnp.bfloat16),
        in_specs=vmem(1),
        out_specs=pl.BlockSpec(memory_space=pltpu.VMEM),
        scratch_shapes=[pltpu.VMEM((variables * members * span, columns), jnp.float32)],
        compiler_params=params(),
        cost_estimate=pl.CostEstimate(flops=10**9, bytes_accessed=2 * 2**20, transcendentals=0),
    )(blocks)


def neighbours(field, axis):
    count = lax.axis_size(axis)
    low = lax.ppermute(field, axis, [(i, (i + 1) % count) for i in range(count)])
    if count == 2:
        return low, low
    return low, lax.ppermute(field, axis, [((i + 1) % count, i) for i in range(count)])


def exchange(blocks):
    return lax.all_to_all(blocks, "grp", split_axis=0, concat_axis=0, tiled=True)


def on_device(start, diffusivity, eastward, northward, cells, count, value, weight):
    dims = start.shape[:4]
    own = start.reshape(-1, start.shape[4])
    low, high = neighbours(own, "tile")
    fields, packed = forecast(dims, own, low, high, diffusivity, eastward, northward)
    states = exchange(packed)
    seen = exchange(
        observe(dims, own, low, high, fields, cells[0], diffusivity, eastward, northward)
    )
    updated = analyse(states, seen, count, value[0], weight[0])
    return restore(dims, exchange(updated))


def solution(mesh):
    return jax.shard_map(
        on_device,
        mesh=mesh,
        in_specs=(
            P("grp", None, None, "tile", None),
            P(),
            P(),
            P(),
            P("tile", None, None),
            P("tile", "grp"),
            P("tile", "grp", None),
            P("tile", "grp", None),
        ),
        out_specs=P("grp", None, None, "tile", None),
        check_vma=False,
    )
```

```python
import functools

import jax
import jax.numpy as jnp
from jax import lax
from jax.experimental import pallas as pl
from jax.experimental.pallas import tpu as pltpu
from jax.sharding import PartitionSpec as P

SPAN = 8
STEPS = 2
EDGE = SPAN // 2

HIGH = lax.Precision.HIGHEST
ROWS = (((1,), (1,)), ((), ()))


def params(mebibytes):
    return pltpu.CompilerParams(vmem_limit_bytes=mebibytes * 2**20)


def cost(flops, size):
    return pl.CostEstimate(flops=flops, bytes_accessed=size, transcendentals=0)


def vmem(count):
    return [pl.BlockSpec(memory_space=pltpu.VMEM)] * count


def hbm(count):
    return [pl.BlockSpec(memory_space=pltpu.HBM)] * count


def smem(count):
    return [pl.BlockSpec(memory_space=pltpu.SMEM)] * count


def dot(a, b, **kw):
    return jnp.dot(a, b, preferred_element_type=jnp.float32, **kw)


def dot_rows(a, b):
    return lax.dot_general(a, b, ROWS, preferred_element_type=jnp.float32)


def permutation(size, shift):
    row = lax.broadcasted_iota(jnp.int32, (size, size), 0)
    column = lax.broadcasted_iota(jnp.int32, (size, size), 1)
    return (lax.rem(row + shift + size, size) == column).astype(jnp.bfloat16)


def eye(size):
    row = lax.broadcasted_iota(jnp.int32, (size, size), 0)
    column = lax.broadcasted_iota(jnp.int32, (size, size), 1)
    return row == column


def column_of(row):
    return jnp.sum(jnp.where(eye(row.shape[1]), row, 0.0), axis=1, keepdims=True)


def row_of(column):
    return jnp.sum(jnp.where(eye(column.shape[0]), column, 0.0), axis=0, keepdims=True)


def forecast_rows(read, first, last, coefficients, write):
    middle, east, west, north, south = coefficients

    def step(below, here, above):
        columns = here.shape[1]
        return (
            middle * here
            + east * above
            + west * below
            + north * pltpu.roll(here, columns - 1, 1)
            + south * pltpu.roll(here, 1, 1)
        )

    start = [read(first - 2), read(first - 1), read(first)]
    once = [None, None, None]
    for r in range(first - 1, last + 1):
        once = [once[1], once[2], step(*start)]
        if r >= first + 1:
            write(r - 1, step(*once))
        if r < last:
            start = [start[1], start[2], read(r + 2)]


def model_coefficients(diffusivity, eastward, northward):
    u = 0.5 * eastward[:, None]
    w = 0.5 * northward[:, None]
    d = diffusivity
    return jnp.stack([1.0 - 4.0 * d, d - u, d + u, d - w, d + w], axis=1)


def coefficients_of(ref, level):
    return [ref[level, i : i + 1, :] for i in range(5)]


def row_reader(level, var, variables, own, low, high):
    span = own.shape[2]
    rows = own.shape[1] * span
    members = own.shape[1] // variables

    def read(r):
        ref, at = (low, r + span) if r < 0 else (own, r) if r < span else (high, r - span)
        view = ref.at[level].reshape(rows, ref.shape[3])
        return view[pl.ds(var * span + at, members, stride=variables * span), :]

    return read


def fetch(sources, slabs, sems):
    copies = [
        [
            pltpu.make_async_copy(source.at[:, level], slab.at[level], sem.at[level])
            for source, slab, sem in zip(sources, slabs, sems)
        ]
        for level in range(slabs[0].shape[0])
    ]
    for level in copies:
        for copy in level:
            copy.start()
    return copies


def pack_rows(pair, identity, store, at):
    lanes = pair.shape[0] // 2
    turned = dot_rows(identity, pair)
    parts = [turned[:, i * lanes : (i + 1) * lanes].reshape(-1, SPAN, lanes) for i in range(2)]
    store[:, at : at + 2 * SPAN, :] = jnp.concatenate(parts, axis=1).astype(jnp.bfloat16)


def hand_out(me, packed, outs):
    for d, out in enumerate(outs):
        out[...] = packed[me ^ d]


def inner_kernel(variables, me, own, coef, fields, *rest):
    outs, (slab, packed, sem) = rest[:-3], rest[-3:]
    levels, rows, span, columns = slab.shape
    members = rows // variables
    copies = fetch([own], [slab], [sem])
    identity = permutation(columns, 0)
    count = span - 2 * STEPS
    for level in range(levels):
        copies[level][0].wait()
        coefficients = coefficients_of(coef, level)
        for var in range(variables):

            def write(r, value):
                pair, half = divmod(r - STEPS, 2)
                at = half * rows + var * members
                fields[level, pair, at : at + members, :] = value.astype(jnp.bfloat16)

            read = row_reader(level, var, variables, slab, None, None)
            forecast_rows(read, STEPS, span - STEPS, coefficients, write)
        for pair in range(count // 2):
            at = (level * count + 2 * pair) * SPAN
            pack_rows(fields[level, pair], identity, packed, at)
    hand_out(me[0], packed, outs)


def inner(dims, me, own, coef):
    members, variables, levels, span, columns = dims
    lanes = members * variables
    blocks = columns // SPAN
    count = span - 2 * STEPS
    share = (levels * count * SPAN, lanes)
    return pl.pallas_call(
        functools.partial(inner_kernel, variables),
        out_shape=[jax.ShapeDtypeStruct((levels, count // 2, 2 * lanes, columns), jnp.bfloat16)]
        + [jax.ShapeDtypeStruct(share, jnp.bfloat16)] * blocks,
        in_specs=smem(1) + hbm(1) + vmem(1),
        out_specs=vmem(1 + blocks),
        scratch_shapes=[
            pltpu.VMEM((levels, lanes, span, columns), jnp.float32),
            pltpu.VMEM((blocks,) + share, jnp.bfloat16),
            pltpu.SemaphoreType.DMA((levels,)),
        ],
        compiler_params=params(10),
        cost_estimate=cost(2 * 10**9, 4 * 2**20),
    )(me, own, coef)


def outer_kernel(me, fields, *rest):
    outs, packed = rest[:-1], rest[-1]
    levels, pairs, _, columns = fields.shape
    identity = permutation(columns, 0)
    for level in range(levels):
        for pair in range(pairs):
            pack_rows(fields[level, pair], identity, packed, (level * pairs + pair) * 2 * SPAN)
    hand_out(me[0], packed, outs)


def outer(me, fields):
    levels, pairs, twice, columns = fields.shape
    blocks = columns // SPAN
    share = (levels * pairs * 2 * SPAN, twice // 2)
    return pl.pallas_call(
        outer_kernel,
        out_shape=[jax.ShapeDtypeStruct(share, jnp.bfloat16)] * blocks,
        in_specs=smem(1) + vmem(1),
        out_specs=vmem(blocks),
        scratch_shapes=[pltpu.VMEM((blocks,) + share, jnp.bfloat16)],
        compiler_params=params(6),
        cost_estimate=cost(10**9, 2 * 2**20),
    )(me, fields)


def observe_kernel(variables, near, me, own, *rest):
    sides, rest = rest[:near], rest[near:]
    coef, centre, cells, fields = rest[:4]
    outs = rest[4:-6]
    slab, side_slabs, grid, region, packed, sems = rest[-6:]
    levels, rows, span, columns = slab.shape
    members = rows // variables
    slots = cells.shape[1]
    width = 2 * EDGE + SPAN
    pairs = (2 * EDGE + span) // 2
    copies = fetch(
        [own, *sides],
        [slab] + [side_slabs.at[i] for i in range(near)],
        [sems.at[i] for i in range(1 + near)],
    )
    orders = jnp.concatenate(
        [permutation(columns, -EDGE), permutation(columns, SPAN - EDGE)], axis=0
    )

    def put(level, r, var, value):
        half, pair = divmod(r + EDGE, pairs)
        at = half * rows + var * members
        grid[level, pair, at : at + members, :] = value

    for level in range(levels):
        for copy in copies[level]:
            copy.wait()
        coefficients = coefficients_of(coef, level)
        for var in range(variables):

            def write(r, value):
                value = value.astype(jnp.bfloat16)
                put(level, r, var, value)
                if 0 <= r < span:
                    pair, half = divmod(r if r < STEPS else r - span + 2 * STEPS, 2)
                    at = half * rows + var * members
                    fields[level, pair, at : at + members, :] = value

            low, high = side_slabs.at[0], side_slabs.at[near - 1]
            read = row_reader(level, var, variables, slab, low, high)
            forecast_rows(read, -EDGE, STEPS, coefficients, write)
            forecast_rows(read, span - STEPS, span + EDGE, coefficients, write)
            for r in range(STEPS, span - STEPS):
                pair, half = divmod(r - STEPS, 2)
                at = half * rows + var * members
                put(level, r, var, centre[level, pair, at : at + members, :])
        for pair in range(pairs):
            turned = dot_rows(orders, grid[level, pair]).astype(jnp.bfloat16)
            at = (level * pairs + pair) * width
            for first in range(2):
                for j in range(columns // width):
                    row = first * columns + j * width
                    region[2 * j + first, at : at + width, :] = turned[row : row + width, :]

    part = pairs * width
    entries = levels * part
    left = lax.broadcasted_iota(jnp.int32, (slots // 2, rows), 1) < members
    lane = lax.broadcasted_iota(jnp.int32, (slots, entries), 1)

    @pl.loop(0, columns // SPAN)
    def _(block):
        cell = column_of(cells[pl.ds(block, 1), :].astype(jnp.float32)).astype(jnp.int32)
        second = cell >= 2 * entries
        cell = jnp.where(second, cell - 2 * entries, cell)
        level = lax.shift_right_logical(cell, (2 * part).bit_length() - 1)
        inside = cell - level * (2 * part)
        lower = inside >= part
        at = level * part + jnp.where(lower, inside - part, inside)
        pick = jnp.where(lane == at, 1.0, 0.0).astype(jnp.bfloat16)
        found = dot(pick, region[block])
        total = jnp.where(lower, found[:, rows:], found[:, :rows])
        other = pltpu.roll(total, members, 1)
        to_left = jnp.where(second, other, total)[: slots // 2]
        to_right = jnp.where(second, total, other)[slots // 2 :]
        packed[block] = jnp.where(left, to_left, to_right).astype(jnp.bfloat16)

    hand_out(me[0], packed, outs)


def observe(dims, me, own, sides, coef, centre, cells):
    members, variables, levels, span, columns = dims
    lanes = members * variables
    blocks, slots = cells.shape
    near = len(sides)
    pairs = (2 * EDGE + span) // 2
    share = (slots // 2, lanes)
    return pl.pallas_call(
        functools.partial(observe_kernel, variables, near),
        out_shape=[jax.ShapeDtypeStruct((levels, STEPS, 2 * lanes, columns), jnp.bfloat16)]
        + [jax.ShapeDtypeStruct(share, jnp.bfloat16)] * blocks,
        in_specs=smem(1) + hbm(1 + near) + vmem(3),
        out_specs=vmem(1 + blocks),
        scratch_shapes=[
            pltpu.VMEM((levels, lanes, span, columns), jnp.float32),
            pltpu.VMEM((near, levels, lanes, span, columns), jnp.float32),
            pltpu.VMEM((levels, pairs, 2 * lanes, columns), jnp.bfloat16),
            pltpu.VMEM((blocks, levels * pairs * (2 * EDGE + SPAN), 2 * lanes), jnp.bfloat16),
            pltpu.VMEM((blocks,) + share, jnp.bfloat16),
            pltpu.SemaphoreType.DMA((1 + near, levels)),
        ],
        compiler_params=params(24),
        cost_estimate=cost(6 * 10**9, 8 * 2**20),
    )(me, own, *sides, coef, centre, cells)


def join(a, b, left, members):
    return (
        jnp.where(left, a, pltpu.roll(b, members, 1)),
        jnp.where(left, pltpu.roll(a, members, 1), b),
    )


def left_lanes(shape):
    return lax.broadcasted_iota(jnp.int32, shape, 1) < shape[1] // 2


def update(states, outs, raw, dev, high, low, poly, gain, alpha, factor):
    groups = len(states)
    half, lanes = states[0].shape
    members = lanes // 2
    left = left_lanes((half, lanes))
    sums = [jnp.zeros((half, lanes), jnp.float32)] * 2
    for j in range(groups // 2):
        here = slice(j * lanes, (j + 1) * lanes)
        pair = join(
            states[2 * j][...].astype(jnp.float32),
            states[2 * j + 1][...].astype(jnp.float32),
            left,
            members,
        )
        raw[:half, here] = pair[0]
        raw[half:, here] = pair[1]
        sums = [sums[0] + pair[0], sums[1] + pair[1]]
    centre = jnp.concatenate([jnp.sum(x, axis=1, keepdims=True) for x in sums], axis=0)
    centre = centre * (1.0 / (groups * members))
    dev[...] = (raw[...] - centre).astype(jnp.bfloat16)
    cross = dot_rows(dev[...], high[...]) + dot_rows(dev[...], low[...])
    shift = centre + jnp.sum(cross * gain, axis=1, keepdims=True)
    mix = (dot(cross, poly, precision=HIGH) * factor).astype(jnp.bfloat16)
    for j in range(groups // 2):
        here = slice(j * lanes, (j + 1) * lanes)
        new = dot(mix, high[:, here]) + alpha * dev[:, here].astype(jnp.float32) + shift
        x, y = join(new[:half], new[half:], left, members)
        outs[2 * j][...] = x.astype(jnp.bfloat16)
        outs[2 * j + 1][...] = y.astype(jnp.bfloat16)


def weigh_kernel(groups, *refs):
    seen, states = refs[:groups], refs[groups : 2 * groups]
    count, value, weight = refs[2 * groups : 2 * groups + 3]
    high, low, poly_ref, gain_ref, scalars = refs[2 * groups + 3 : 2 * groups + 8]
    outs = refs[2 * groups + 8 : 3 * groups + 8]
    raw, dev, obs = refs[3 * groups + 8 :]
    half, lanes = seen[0].shape
    slots = 2 * half
    members = lanes // 2
    total_members = groups * members
    left = left_lanes((half, lanes))

    for j in range(groups // 2):
        here = slice(j * lanes, (j + 1) * lanes)
        obs[:half, here], obs[half:, here] = join(
            seen[2 * j][...].astype(jnp.float32),
            seen[2 * j + 1][...].astype(jnp.float32),
            left,
            members,
        )

    used = lax.broadcasted_iota(jnp.int32, (1, slots), 1) < count[0, 0]
    root = column_of(jnp.where(used, jnp.sqrt(weight[...]), 0.0))
    observed = obs[...]
    mean = jnp.sum(observed, axis=1, keepdims=True) * (1.0 / total_members)
    scaled = (observed - mean) * root
    energy = jnp.sum(jnp.sum(scaled * scaled, axis=1, keepdims=True), axis=0, keepdims=True)
    top = scaled.astype(jnp.bfloat16)
    high[...] = top
    low[...] = (scaled - top.astype(jnp.float32)).astype(jnp.bfloat16)
    misfit = row_of(root * (column_of(value[...]) - mean))

    c = total_members - 1.0
    s = energy * (1.0 / total_members) + c
    inverse = 1.0 / s
    a = c * inverse
    p = 1.5 - 0.5 * a
    p2 = p * p
    p3 = p2 * p
    base = 1.5 * p - 0.5 * a * p3
    q0 = -0.75 - 0.5 * (p3 - 1.5 * a * p2)
    q1 = -0.5 * (0.75 * a * p - 1.5 * p2)
    q2 = -0.5 * (0.75 * p - 0.125 * a)
    small = (
        dot_rows(high[...], high[...])
        + dot_rows(high[...], low[...])
        + dot_rows(low[...], high[...])
    ) * inverse
    diagonal = eye(slots)
    square = dot(small, small, precision=HIGH)
    tail = dot(square, jnp.where(diagonal, q2, 0.0) + 0.0625 * small, precision=HIGH)
    poly = jnp.where(diagonal, q0, 0.0) + q1 * small + tail

    def apply(vector):
        inner_part = jnp.sum(poly * vector, axis=1, keepdims=True)
        return jnp.sum(small * inner_part, axis=0, keepdims=True) + base * vector

    gain = apply(apply(misfit)) * inverse
    stretch = jnp.sqrt(a)
    alpha, factor = stretch * base, stretch * inverse
    poly_ref[...] = poly
    gain_ref[...] = gain
    scalars[0:1, :] = jnp.broadcast_to(alpha, (1, scalars.shape[1]))
    scalars[1:2, :] = jnp.broadcast_to(factor, (1, scalars.shape[1]))
    update(states, outs, raw, dev, high, low, poly, gain, alpha, factor)


def weigh(seen, states, count, value, weight):
    groups = len(states)
    half, lanes = states[0].shape
    slots = 2 * seen[0].shape[0]
    total = groups * lanes // 2
    return pl.pallas_call(
        functools.partial(weigh_kernel, groups),
        out_shape=[
            jax.ShapeDtypeStruct((slots, total), jnp.bfloat16),
            jax.ShapeDtypeStruct((slots, total), jnp.bfloat16),
            jax.ShapeDtypeStruct((slots, slots), jnp.float32),
            jax.ShapeDtypeStruct((1, slots), jnp.float32),
            jax.ShapeDtypeStruct((8, 128), jnp.float32),
        ]
        + [jax.ShapeDtypeStruct((half, lanes), jnp.bfloat16)] * groups,
        in_specs=vmem(2 * groups) + smem(1) + vmem(2),
        out_specs=vmem(5 + groups),
        scratch_shapes=[
            pltpu.VMEM((2 * half, total), jnp.float32),
            pltpu.VMEM((2 * half, total), jnp.bfloat16),
            pltpu.VMEM((slots, total), jnp.float32),
        ],
        compiler_params=params(14),
        cost_estimate=cost(4 * 10**9, 4 * 2**20),
    )(*seen, *states, count, value, weight)


def rest_kernel(groups, *refs):
    states = refs[:groups]
    high, low, poly, gain, scalars = refs[groups : groups + 5]
    outs = refs[groups + 5 : 2 * groups + 5]
    raw, dev = refs[2 * groups + 5 :]
    alpha, factor = scalars[0:1, 0:1], scalars[1:2, 0:1]
    update(states, outs, raw, dev, high, low, poly[...], gain[...], alpha, factor)


def analyse_rest(states, shared):
    groups = len(states)
    half, lanes = states[0].shape
    total = groups * lanes // 2
    return pl.pallas_call(
        functools.partial(rest_kernel, groups),
        out_shape=[jax.ShapeDtypeStruct((half, lanes), jnp.bfloat16)] * groups,
        in_specs=vmem(groups + 5),
        out_specs=vmem(groups),
        scratch_shapes=[
            pltpu.VMEM((2 * half, total), jnp.float32),
            pltpu.VMEM((2 * half, total), jnp.bfloat16),
        ],
        compiler_params=params(10),
        cost_estimate=cost(2 * 10**9, 4 * 2**20),
    )(*states, *shared)


def restore_kernel(blocks, me, *refs):
    shares = (refs[blocks : 2 * blocks], refs[:blocks])
    out, gathered, turned = refs[2 * blocks :]
    members, variables, levels, span, columns = out.shape
    lanes = members * variables
    identity = permutation(lanes, 0)
    for part in range(2):
        for d in range(blocks):
            gathered[part, me[0] ^ d] = shares[part][d][...]
    for level in range(levels):
        for pair in range(span // 2):
            r = 2 * pair
            inside = STEPS <= r < span - STEPS
            first = r - STEPS if inside else r if r < STEPS else r - span + 2 * STEPS
            size = span - 2 * STEPS if inside else 2 * STEPS
            at = (level * size + first) * SPAN
            both = gathered[int(inside), :, at : at + 2 * SPAN, :].astype(jnp.float32)
            for i in range(2):
                one = both[:, i * SPAN : (i + 1) * SPAN, :].reshape(columns, lanes)
                rows = dot_rows(identity, one.astype(jnp.bfloat16))
                turned[level % 2, pl.ds(r + i, lanes, stride=span), :] = rows
        for var in range(variables):
            half = turned[level % 2, var * members * span : (var + 1) * members * span, :]
            out[:, var, level] = half.reshape(members, span, columns).astype(jnp.bfloat16)


def restore(dims, me, inner_shares, outer_shares):
    members, variables, levels, span, columns = dims
    blocks = len(inner_shares)
    return pl.pallas_call(
        functools.partial(restore_kernel, blocks),
        out_shape=jax.ShapeDtypeStruct((members, variables, levels, span, columns), jnp.bfloat16),
        in_specs=smem(1) + vmem(2 * blocks),
        out_specs=pl.BlockSpec(memory_space=pltpu.VMEM),
        scratch_shapes=[
            pltpu.VMEM((2, blocks) + inner_shares[0].shape, jnp.bfloat16),
            pltpu.VMEM((2, variables * members * span, columns), jnp.float32),
        ],
        compiler_params=params(10),
        cost_estimate=cost(2 * 10**9, 2 * 2**20),
    )(me, *inner_shares, *outer_shares)


def neighbours(field, axis):
    count = lax.axis_size(axis)
    low = lax.ppermute(field, axis, [(i, (i + 1) % count) for i in range(count)])
    if count == 2:
        return (low,)
    return low, lax.ppermute(field, axis, [((i + 1) % count, i) for i in range(count)])


def exchange(shares):
    count = len(shares)
    got = list(shares)
    for d in range(count - 1, 0, -1):
        got[d] = lax.ppermute(shares[d], "grp", [(i, i ^ d) for i in range(count)])
    return got


def on_device(start, diffusivity, eastward, northward, cells, count, value, weight):
    members, variables, levels, span, columns = dims = start.shape
    me = lax.axis_index("grp").astype(jnp.int32).reshape(1)
    own = start.reshape(members * variables, levels, span, columns)
    sides = neighbours(own, "tile")
    coef = model_coefficients(diffusivity, eastward, northward)
    centre, *near_shares = inner(dims, me, own, coef)
    near = exchange(near_shares)
    rim, *seen_shares = observe(dims, me, own, sides, coef, centre, cells[0])
    seen = exchange(seen_shares)
    far = exchange(outer(me, rim))
    *shared, near_new = (lambda r: (*r[:5], r[5:]))(
        weigh(seen, near, count, value[0], weight[0])
    )
    near_back = exchange(near_new)
    far_back = exchange(analyse_rest(far, shared))
    return restore(dims, me, near_back, far_back)


def solution(mesh):
    return jax.shard_map(
        on_device,
        mesh=mesh,
        in_specs=(
            P("grp", None, None, "tile", None),
            P(),
            P(),
            P(),
            P("tile", None, None),
            P("tile", "grp"),
            P("tile", "grp", None),
            P("tile", "grp", None),
        ),
        out_specs=P("grp", None, None, "tile", None),
        check_vma=False,
    )
```

```python
import functools

import jax
import jax.numpy as jnp
from jax import lax
from jax.experimental import pallas as pl
from jax.experimental.pallas import tpu as pltpu
from jax.sharding import PartitionSpec as P

SPAN = 8
STEPS = 2
EDGE = SPAN // 2

HIGH = lax.Precision.HIGHEST
ROWS = (((1,), (1,)), ((), ()))


def params(mebibytes):
    return pltpu.CompilerParams(vmem_limit_bytes=mebibytes * 2**20)


def cost(flops, size):
    return pl.CostEstimate(flops=flops, bytes_accessed=size, transcendentals=0)


def vmem(count):
    return [pl.BlockSpec(memory_space=pltpu.VMEM)] * count


def hbm(count):
    return [pl.BlockSpec(memory_space=pltpu.HBM)] * count


def smem(count):
    return [pl.BlockSpec(memory_space=pltpu.SMEM)] * count


def dot(a, b, **kw):
    return jnp.dot(a, b, preferred_element_type=jnp.float32, **kw)


def dot_rows(a, b):
    return lax.dot_general(a, b, ROWS, preferred_element_type=jnp.float32)


def permutation(size, shift):
    row = lax.broadcasted_iota(jnp.int32, (size, size), 0)
    column = lax.broadcasted_iota(jnp.int32, (size, size), 1)
    return (lax.rem(row + shift + size, size) == column).astype(jnp.bfloat16)


def eye(size):
    row = lax.broadcasted_iota(jnp.int32, (size, size), 0)
    column = lax.broadcasted_iota(jnp.int32, (size, size), 1)
    return row == column


def column_of(row):
    return jnp.sum(jnp.where(eye(row.shape[1]), row, 0.0), axis=1, keepdims=True)


def row_of(column):
    return jnp.sum(jnp.where(eye(column.shape[0]), column, 0.0), axis=0, keepdims=True)


def forecast_rows(read, first, last, coefficients, write):
    middle, east, west, north, south = coefficients

    def step(below, here, above):
        columns = here.shape[1]
        return (
            middle * here
            + east * above
            + west * below
            + north * pltpu.roll(here, columns - 1, 1)
            + south * pltpu.roll(here, 1, 1)
        )

    start = [read(first - 2), read(first - 1), read(first)]
    once = [None, None, None]
    for r in range(first - 1, last + 1):
        once = [once[1], once[2], step(*start)]
        if r >= first + 1:
            write(r - 1, step(*once))
        if r < last:
            start = [start[1], start[2], read(r + 2)]


def model_coefficients(diffusivity, eastward, northward):
    u = 0.5 * eastward[:, None]
    w = 0.5 * northward[:, None]
    d = diffusivity
    return jnp.stack([1.0 - 4.0 * d, d - u, d + u, d - w, d + w], axis=1)


def coefficients_of(ref, level):
    return [ref[level, i : i + 1, :] for i in range(5)]


def row_reader(level, var, variables, own, low, high):
    span = own.shape[2]
    rows = own.shape[1] * span
    members = own.shape[1] // variables

    def read(r):
        ref, at = (low, r + span) if r < 0 else (own, r) if r < span else (high, r - span)
        view = ref.at[level].reshape(rows, ref.shape[3])
        return view[pl.ds(var * span + at, members, stride=variables * span), :]

    return read


def fetch(sources, slabs, sems):
    copies = [
        [
            pltpu.make_async_copy(source.at[:, level], slab.at[level], sem.at[level])
            for source, slab, sem in zip(sources, slabs, sems)
        ]
        for level in range(slabs[0].shape[0])
    ]
    for level in copies:
        for copy in level:
            copy.start()
    return copies


def pack_rows(pair, identity, store, at):
    lanes = pair.shape[0] // 2
    turned = dot_rows(identity, pair)
    parts = [turned[:, i * lanes : (i + 1) * lanes].reshape(-1, SPAN, lanes) for i in range(2)]
    store[:, at : at + 2 * SPAN, :] = jnp.concatenate(parts, axis=1).astype(jnp.bfloat16)


def inner_kernel(variables, own, coef, fields, packed, slab, sem):
    levels, rows, span, columns = slab.shape
    members = rows // variables
    copies = fetch([own], [slab], [sem])
    identity = permutation(columns, 0)
    count = span - 2 * STEPS
    for level in range(levels):
        copies[level][0].wait()
        coefficients = coefficients_of(coef, level)
        for var in range(variables):

            def write(r, value):
                pair, half = divmod(r - STEPS, 2)
                at = half * rows + var * members
                fields[level, pair, at : at + members, :] = value.astype(jnp.bfloat16)

            read = row_reader(level, var, variables, slab, None, None)
            forecast_rows(read, STEPS, span - STEPS, coefficients, write)
        for pair in range(count // 2):
            at = (level * count + 2 * pair) * SPAN
            pack_rows(fields[level, pair], identity, packed, at)


def inner(dims, own, coef):
    members, variables, levels, span, columns = dims
    lanes = members * variables
    count = span - 2 * STEPS
    return pl.pallas_call(
        functools.partial(inner_kernel, variables),
        out_shape=[
            jax.ShapeDtypeStruct((levels, count // 2, 2 * lanes, columns), jnp.bfloat16),
            jax.ShapeDtypeStruct((columns // SPAN, levels * count * SPAN, lanes), jnp.bfloat16),
        ],
        in_specs=hbm(1) + vmem(1),
        out_specs=vmem(2),
        scratch_shapes=[
            pltpu.VMEM((levels, lanes, span, columns), jnp.float32),
            pltpu.SemaphoreType.DMA((levels,)),
        ],
        compiler_params=params(8),
        cost_estimate=cost(2 * 10**9, 4 * 2**20),
    )(own, coef)


def observe_kernel(variables, near, own, *rest):
    sides, rest = rest[:near], rest[near:]
    coef, centre, cells, packed, fields, slab, side_slabs, grid, region, sems = rest
    levels, rows, span, columns = slab.shape
    members = rows // variables
    slots = cells.shape[1]
    width = 2 * EDGE + SPAN
    pairs = (2 * EDGE + span) // 2
    copies = fetch(
        [own, *sides],
        [slab] + [side_slabs.at[i] for i in range(near)],
        [sems.at[i] for i in range(1 + near)],
    )
    identity = permutation(columns, 0)
    orders = jnp.concatenate(
        [permutation(columns, -EDGE), permutation(columns, SPAN - EDGE)], axis=0
    )

    def put(level, r, var, value):
        half, pair = divmod(r + EDGE, pairs)
        at = half * rows + var * members
        grid[level, pair, at : at + members, :] = value

    for level in range(levels):
        for copy in copies[level]:
            copy.wait()
        coefficients = coefficients_of(coef, level)
        for var in range(variables):

            def write(r, value):
                value = value.astype(jnp.bfloat16)
                put(level, r, var, value)
                if 0 <= r < span:
                    pair, half = divmod(r if r < STEPS else r - span + 2 * STEPS, 2)
                    at = half * rows + var * members
                    fields[pair, at : at + members, :] = value

            low, high = side_slabs.at[0], side_slabs.at[near - 1]
            read = row_reader(level, var, variables, slab, low, high)
            forecast_rows(read, -EDGE, STEPS, coefficients, write)
            forecast_rows(read, span - STEPS, span + EDGE, coefficients, write)
            for r in range(STEPS, span - STEPS):
                pair, half = divmod(r - STEPS, 2)
                at = half * rows + var * members
                put(level, r, var, centre[level, pair, at : at + members, :])
        for pair in range(STEPS):
            pack_rows(fields[pair], identity, packed, (level * STEPS + pair) * 2 * SPAN)
        for pair in range(pairs):
            turned = dot_rows(orders, grid[level, pair]).astype(jnp.bfloat16)
            at = (level * pairs + pair) * width
            for first in range(2):
                for j in range(columns // width):
                    row = first * columns + j * width
                    region[2 * j + first, at : at + width, :] = turned[row : row + width, :]

    part = pairs * width
    entries = levels * part
    left = lax.broadcasted_iota(jnp.int32, (slots // 2, rows), 1) < members
    lane = lax.broadcasted_iota(jnp.int32, (slots, entries), 1)

    @pl.loop(0, columns // SPAN)
    def _(block):
        cell = column_of(cells[pl.ds(block, 1), :].astype(jnp.float32)).astype(jnp.int32)
        second = cell >= 2 * entries
        cell = jnp.where(second, cell - 2 * entries, cell)
        level = lax.shift_right_logical(cell, (2 * part).bit_length() - 1)
        inside = cell - level * (2 * part)
        lower = inside >= part
        at = level * part + jnp.where(lower, inside - part, inside)
        pick = jnp.where(lane == at, 1.0, 0.0).astype(jnp.bfloat16)
        found = dot(pick, region[block])
        total = jnp.where(lower, found[:, rows:], found[:, :rows])
        other = pltpu.roll(total, members, 1)
        to_left = jnp.where(second, other, total)[: slots // 2]
        to_right = jnp.where(second, total, other)[slots // 2 :]
        seen = jnp.where(left, to_left, to_right).astype(jnp.bfloat16)
        packed[block, levels * 2 * STEPS * SPAN :, :] = seen


def observe(dims, own, sides, coef, centre, cells):
    members, variables, levels, span, columns = dims
    lanes = members * variables
    blocks, slots = cells.shape
    near = len(sides)
    pairs = (2 * EDGE + span) // 2
    share = levels * 2 * STEPS * SPAN + slots // 2
    return pl.pallas_call(
        functools.partial(observe_kernel, variables, near),
        out_shape=jax.ShapeDtypeStruct((blocks, share, lanes), jnp.bfloat16),
        in_specs=hbm(1 + near) + vmem(3),
        out_specs=pl.BlockSpec(memory_space=pltpu.VMEM),
        scratch_shapes=[
            pltpu.VMEM((STEPS, 2 * lanes, columns), jnp.bfloat16),
            pltpu.VMEM((levels, lanes, span, columns), jnp.float32),
            pltpu.VMEM((near, levels, lanes, span, columns), jnp.float32),
            pltpu.VMEM((levels, pairs, 2 * lanes, columns), jnp.bfloat16),
            pltpu.VMEM((blocks, levels * pairs * (2 * EDGE + SPAN), 2 * lanes), jnp.bfloat16),
            pltpu.SemaphoreType.DMA((1 + near, levels)),
        ],
        compiler_params=params(24),
        cost_estimate=cost(6 * 10**9, 8 * 2**20),
    )(own, *sides, coef, centre, cells)


def join(a, b, left, members):
    return (
        jnp.where(left, a, pltpu.roll(b, members, 1)),
        jnp.where(left, pltpu.roll(a, members, 1), b),
    )


def left_lanes(shape):
    return lax.broadcasted_iota(jnp.int32, shape, 1) < shape[1] // 2


def analyse_kernel(first, second, count, value, weight, out, raw, dev, obs, high, low):
    groups, near, lanes = first.shape
    half = obs.shape[0] // 2
    far = second.shape[1] - half
    slots = 2 * half
    members = lanes // 2
    total_members = groups * members
    left = left_lanes((half, lanes))

    parts = ((first, near, 0), (second, far, near))
    sums = [jnp.zeros((size, lanes), jnp.float32) for _, size, _ in parts for _ in range(2)]
    side = near + far
    for j in range(groups // 2):
        here = slice(j * lanes, (j + 1) * lanes)
        for i, (ref, size, start) in enumerate(parts):
            pair = join(
                ref[2 * j, :size, :].astype(jnp.float32),
                ref[2 * j + 1, :size, :].astype(jnp.float32),
                left_lanes((size, lanes)),
                members,
            )
            for var in range(2):
                at = var * side + start
                raw[at : at + size, here] = pair[var]
                sums[2 * var + i] = sums[2 * var + i] + pair[var]
    centre = jnp.concatenate([jnp.sum(x, axis=1, keepdims=True) for x in sums], axis=0)
    centre = centre * (1.0 / total_members)
    dev[...] = (raw[...] - centre).astype(jnp.bfloat16)

    for j in range(groups // 2):
        here = slice(j * lanes, (j + 1) * lanes)
        obs[:half, here], obs[half:, here] = join(
            second[2 * j, far:, :].astype(jnp.float32),
            second[2 * j + 1, far:, :].astype(jnp.float32),
            left,
            members,
        )

    used = lax.broadcasted_iota(jnp.int32, (1, slots), 1) < count[0, 0]
    root = column_of(jnp.where(used, jnp.sqrt(weight[...]), 0.0))
    observed = obs[...]
    mean = jnp.sum(observed, axis=1, keepdims=True) * (1.0 / total_members)
    scaled = (observed - mean) * root
    energy = jnp.sum(jnp.sum(scaled * scaled, axis=1, keepdims=True), axis=0, keepdims=True)
    top = scaled.astype(jnp.bfloat16)
    high[...] = top
    low[...] = (scaled - top.astype(jnp.float32)).astype(jnp.bfloat16)
    misfit = row_of(root * (column_of(value[...]) - mean))

    c = total_members - 1.0
    s = energy * (1.0 / total_members) + c
    inverse = 1.0 / s
    a = c * inverse
    p = 1.5 - 0.5 * a
    p2 = p * p
    p3 = p2 * p
    base = 1.5 * p - 0.5 * a * p3
    q0 = -0.75 - 0.5 * (p3 - 1.5 * a * p2)
    q1 = -0.5 * (0.75 * a * p - 1.5 * p2)
    q2 = -0.5 * (0.75 * p - 0.125 * a)
    small = (
        dot_rows(high[...], high[...])
        + dot_rows(high[...], low[...])
        + dot_rows(low[...], high[...])
    ) * inverse
    diagonal = eye(slots)
    square = dot(small, small, precision=HIGH)
    tail = dot(square, jnp.where(diagonal, q2, 0.0) + 0.0625 * small, precision=HIGH)
    poly = jnp.where(diagonal, q0, 0.0) + q1 * small + tail

    def apply(vector):
        inner_part = jnp.sum(poly * vector, axis=1, keepdims=True)
        return jnp.sum(small * inner_part, axis=0, keepdims=True) + base * vector

    gain = apply(apply(misfit)) * inverse
    stretch = jnp.sqrt(a)
    alpha, factor = stretch * base, stretch * inverse
    cross = dot_rows(dev[...], high[...]) + dot_rows(dev[...], low[...])
    shift = centre + jnp.sum(cross * gain, axis=1, keepdims=True)
    mix = (dot(cross, poly, precision=HIGH) * factor).astype(jnp.bfloat16)
    left = left_lanes((side, lanes))
    for j in range(groups // 2):
        here = slice(j * lanes, (j + 1) * lanes)
        new = dot(mix, high[:, here]) + alpha * dev[:, here].astype(jnp.float32) + shift
        x, y = join(new[:side], new[side:], left, members)
        out[2 * j] = x.astype(jnp.bfloat16)
        out[2 * j + 1] = y.astype(jnp.bfloat16)


def analyse(first, second, count, value, weight):
    groups, near, lanes = first.shape
    slots = value.shape[1]
    side = near + second.shape[1] - slots // 2
    total = groups * lanes // 2
    return pl.pallas_call(
        analyse_kernel,
        out_shape=jax.ShapeDtypeStruct((groups, side, lanes), jnp.bfloat16),
        in_specs=vmem(2) + smem(1) + vmem(2),
        out_specs=pl.BlockSpec(memory_space=pltpu.VMEM),
        scratch_shapes=[
            pltpu.VMEM((2 * side, total), jnp.float32),
            pltpu.VMEM((2 * side, total), jnp.bfloat16),
            pltpu.VMEM((slots, total), jnp.float32),
            pltpu.VMEM((slots, total), jnp.bfloat16),
            pltpu.VMEM((slots, total), jnp.bfloat16),
        ],
        compiler_params=params(16),
        cost_estimate=cost(4 * 10**9, 4 * 2**20),
    )(first, second, count, value, weight)


def restore_kernel(blocks, out, turned):
    members, variables, levels, span, columns = out.shape
    lanes = members * variables
    identity = permutation(lanes, 0)
    near = span - 2 * STEPS
    for level in range(levels):
        for r in range(0, span, 2):
            if STEPS <= r < span - STEPS:
                at = level * near + r - STEPS
            else:
                at = levels * near + level * 2 * STEPS + (r if r < STEPS else r - near)
            both = blocks[:, at * SPAN : (at + 2) * SPAN, :].astype(jnp.float32)
            for i in range(2):
                one = both[:, i * SPAN : (i + 1) * SPAN, :].reshape(columns, lanes)
                rows = dot_rows(identity, one.astype(jnp.bfloat16))
                turned[level % 2, pl.ds(r + i, lanes, stride=span), :] = rows
        for var in range(variables):
            half = turned[level % 2, var * members * span : (var + 1) * members * span, :]
            out[:, var, level] = half.reshape(members, span, columns).astype(jnp.bfloat16)


def restore(dims, blocks):
    members, variables, levels, span, columns = dims
    return pl.pallas_call(
        restore_kernel,
        out_shape=jax.ShapeDtypeStruct((members, variables, levels, span, columns), jnp.bfloat16),
        in_specs=vmem(1),
        out_specs=pl.BlockSpec(memory_space=pltpu.VMEM),
        scratch_shapes=[pltpu.VMEM((2, variables * members * span, columns), jnp.float32)],
        compiler_params=params(8),
        cost_estimate=cost(2 * 10**9, 2 * 2**20),
    )(blocks)


def neighbours(field, axis):
    count = lax.axis_size(axis)
    low = lax.ppermute(field, axis, [(i, (i + 1) % count) for i in range(count)])
    if count == 2:
        return (low,)
    return low, lax.ppermute(field, axis, [((i + 1) % count, i) for i in range(count)])


def exchange(blocks):
    return lax.all_to_all(blocks, "grp", split_axis=0, concat_axis=0, tiled=True)


def on_device(start, diffusivity, eastward, northward, cells, count, value, weight):
    members, variables, levels, span, columns = dims = start.shape
    own = start.reshape(members * variables, levels, span, columns)
    sides = neighbours(own, "tile")
    coef = model_coefficients(diffusivity, eastward, northward)
    centre, near = inner(dims, own, coef)
    first = exchange(near)
    second = exchange(observe(dims, own, sides, coef, centre, cells[0]))
    updated = analyse(first, second, count, value[0], weight[0])
    return restore(dims, exchange(updated))


def solution(mesh):
    return jax.shard_map(
        on_device,
        mesh=mesh,
        in_specs=(
            P("grp", None, None, "tile", None),
            P(),
            P(),
            P(),
            P("tile", None, None),
            P("tile", "grp"),
            P("tile", "grp", None),
            P("tile", "grp", None),
        ),
        out_specs=P("grp", None, None, "tile", None),
        check_vma=False,
    )
```

```python
import functools

import jax
import jax.numpy as jnp
from jax import lax
from jax.experimental import pallas as pl
from jax.experimental.pallas import tpu as pltpu
from jax.sharding import PartitionSpec as P

SPAN = 8
STEPS = 2
EDGE = SPAN // 2

HIGH = lax.Precision.HIGHEST
ROWS = (((1,), (1,)), ((), ()))


def params(mebibytes):
    return pltpu.CompilerParams(vmem_limit_bytes=mebibytes * 2**20)


def cost(flops, size):
    return pl.CostEstimate(flops=flops, bytes_accessed=size, transcendentals=0)


def vmem(count):
    return [pl.BlockSpec(memory_space=pltpu.VMEM)] * count


def hbm(count):
    return [pl.BlockSpec(memory_space=pltpu.HBM)] * count


def smem(count):
    return [pl.BlockSpec(memory_space=pltpu.SMEM)] * count


def dot(a, b, **kw):
    return jnp.dot(a, b, preferred_element_type=jnp.float32, **kw)


def dot_rows(a, b):
    return lax.dot_general(a, b, ROWS, preferred_element_type=jnp.float32)


def permutation(size, shift):
    row = lax.broadcasted_iota(jnp.int32, (size, size), 0)
    column = lax.broadcasted_iota(jnp.int32, (size, size), 1)
    return (lax.rem(row + shift + size, size) == column).astype(jnp.bfloat16)


def eye(size):
    row = lax.broadcasted_iota(jnp.int32, (size, size), 0)
    column = lax.broadcasted_iota(jnp.int32, (size, size), 1)
    return row == column


def column_of(row):
    return jnp.sum(jnp.where(eye(row.shape[1]), row, 0.0), axis=1, keepdims=True)


def row_of(column):
    return jnp.sum(jnp.where(eye(column.shape[0]), column, 0.0), axis=0, keepdims=True)


def forecast_rows(read, first, last, coefficients, write):
    middle, east, west, north, south = coefficients

    def step(below, here, above):
        columns = here.shape[1]
        return (
            middle * here
            + east * above
            + west * below
            + north * pltpu.roll(here, columns - 1, 1)
            + south * pltpu.roll(here, 1, 1)
        )

    start = [read(first - 2), read(first - 1), read(first)]
    once = [None, None, None]
    for r in range(first - 1, last + 1):
        once = [once[1], once[2], step(*start)]
        if r >= first + 1:
            write(r - 1, step(*once))
        if r < last:
            start = [start[1], start[2], read(r + 2)]


def model_coefficients(diffusivity, eastward, northward):
    place = lax.broadcasted_iota(jnp.int32, (1, 5, 1), 1)
    own = jnp.where(place == 0, -4.0, 1.0) * diffusivity[:, None, :] + jnp.where(place == 0, 1.0, 0.0)
    side = jnp.where(place == 1, -0.5, jnp.where(place == 2, 0.5, 0.0)) * eastward[:, None, None]
    front = jnp.where(place == 3, -0.5, jnp.where(place == 4, 0.5, 0.0)) * northward[:, None, None]
    return own + side + front


def coefficients_of(ref, level):
    return [ref[level, i : i + 1, :] for i in range(5)]


def row_reader(level, var, variables, own, low, high):
    span = own.shape[2]
    rows = own.shape[1] * span
    members = own.shape[1] // variables

    def read(r):
        ref, at = (low, r + span) if r < 0 else (own, r) if r < span else (high, r - span)
        view = ref.at[level].reshape(rows, ref.shape[3])
        return view[pl.ds(var * span + at, members, stride=variables * span), :]

    return read


def fetch(sources, slabs, sems):
    copies = [
        [
            pltpu.make_async_copy(source.at[:, level], slab.at[level], sem.at[level])
            for source, slab, sem in zip(sources, slabs, sems)
        ]
        for level in range(slabs[0].shape[0])
    ]
    for level in copies:
        for copy in level:
            copy.start()
    return copies


def pack_rows(pair, identity, store, at):
    lanes = pair.shape[0] // 2
    turned = dot_rows(identity, pair)
    parts = [turned[:, i * lanes : (i + 1) * lanes].reshape(-1, SPAN, lanes) for i in range(2)]
    store[:, at : at + 2 * SPAN, :] = jnp.concatenate(parts, axis=1).astype(jnp.bfloat16)


def inner_kernel(variables, own, coef, fields, packed, slab, sem):
    levels, rows, span, columns = slab.shape
    members = rows // variables
    copies = fetch([own], [slab], [sem])
    identity = permutation(columns, 0)
    count = span - 2 * STEPS
    for level in range(levels):
        copies[level][0].wait()
        coefficients = coefficients_of(coef, level)
        for var in range(variables):

            def write(r, value):
                pair, half = divmod(r - STEPS, 2)
                at = half * rows + var * members
                fields[level, pair, at : at + members, :] = value.astype(jnp.bfloat16)

            read = row_reader(level, var, variables, slab, None, None)
            forecast_rows(read, STEPS, span - STEPS, coefficients, write)
        for pair in range(count // 2):
            at = (level * count + 2 * pair) * SPAN
            pack_rows(fields[level, pair], identity, packed, at)


def inner(dims, own, coef):
    members, variables, levels, span, columns = dims
    lanes = members * variables
    count = span - 2 * STEPS
    return pl.pallas_call(
        functools.partial(inner_kernel, variables),
        out_shape=[
            jax.ShapeDtypeStruct((levels, count // 2, 2 * lanes, columns), jnp.bfloat16),
            jax.ShapeDtypeStruct((columns // SPAN, levels * count * SPAN, lanes), jnp.bfloat16),
        ],
        in_specs=hbm(1) + vmem(1),
        out_specs=vmem(2),
        scratch_shapes=[
            pltpu.VMEM((levels, lanes, span, columns), jnp.float32),
            pltpu.SemaphoreType.DMA((levels,)),
        ],
        compiler_params=params(60),
        cost_estimate=cost(2 * 10**9, 4 * 2**20),
    )(own, coef)


def observe_kernel(variables, near, own, *rest):
    sides, rest = rest[:near], rest[near:]
    coef, centre, cells, packed, seen, fields, slab, side_slabs, grid, region, sems = rest
    levels, rows, span, columns = slab.shape
    members = rows // variables
    slots = cells.shape[1]
    width = 2 * EDGE + SPAN
    pairs = (2 * EDGE + span) // 2
    copies = fetch(
        [own, *sides],
        [slab] + [side_slabs.at[i] for i in range(near)],
        [sems.at[i] for i in range(1 + near)],
    )
    identity = permutation(columns, 0)
    orders = jnp.concatenate(
        [permutation(columns, -EDGE), permutation(columns, SPAN - EDGE)], axis=0
    )

    def put(level, r, var, value):
        half, pair = divmod(r + EDGE, pairs)
        at = half * rows + var * members
        grid[level, pair, at : at + members, :] = value

    for level in range(levels):
        for copy in copies[level]:
            copy.wait()
        coefficients = coefficients_of(coef, level)
        for var in range(variables):

            def write(r, value):
                value = value.astype(jnp.bfloat16)
                put(level, r, var, value)
                if 0 <= r < span:
                    pair, half = divmod(r if r < STEPS else r - span + 2 * STEPS, 2)
                    at = half * rows + var * members
                    fields[pair, at : at + members, :] = value

            low, high = side_slabs.at[0], side_slabs.at[near - 1]
            read = row_reader(level, var, variables, slab, low, high)
            forecast_rows(read, -EDGE, STEPS, coefficients, write)
            forecast_rows(read, span - STEPS, span + EDGE, coefficients, write)
            for r in range(STEPS, span - STEPS):
                pair, half = divmod(r - STEPS, 2)
                at = half * rows + var * members
                put(level, r, var, centre[level, pair, at : at + members, :])
        for pair in range(STEPS):
            pack_rows(fields[pair], identity, packed, (level * STEPS + pair) * 2 * SPAN)
        for pair in range(pairs):
            turned = dot_rows(orders, grid[level, pair]).astype(jnp.bfloat16)
            at = (level * pairs + pair) * width
            for first in range(2):
                for j in range(columns // width):
                    row = first * columns + j * width
                    region[2 * j + first, at : at + width, :] = turned[row : row + width, :]

    part = pairs * width
    entries = levels * part
    left = lax.broadcasted_iota(jnp.int32, (slots // 2, rows), 1) < members
    lane = lax.broadcasted_iota(jnp.int32, (slots, entries), 1)

    @pl.loop(0, columns // SPAN)
    def _(block):
        cell = column_of(cells[pl.ds(block, 1), :].astype(jnp.float32)).astype(jnp.int32)
        second = cell >= 2 * entries
        cell = jnp.where(second, cell - 2 * entries, cell)
        level = lax.shift_right_logical(cell, (2 * part).bit_length() - 1)
        inside = cell - level * (2 * part)
        lower = inside >= part
        at = level * part + jnp.where(lower, inside - part, inside)
        pick = jnp.where(lane == at, 1.0, 0.0).astype(jnp.bfloat16)
        found = dot(pick, region[block])
        total = jnp.where(lower, found[:, rows:], found[:, :rows])
        other = pltpu.roll(total, members, 1)
        to_left = jnp.where(second, other, total)[: slots // 2]
        to_right = jnp.where(second, total, other)[slots // 2 :]
        seen[block] = jnp.where(left, to_left, to_right).astype(jnp.bfloat16)


def observe(dims, own, sides, coef, centre, cells):
    members, variables, levels, span, columns = dims
    lanes = members * variables
    blocks, slots = cells.shape
    near = len(sides)
    pairs = (2 * EDGE + span) // 2
    return pl.pallas_call(
        functools.partial(observe_kernel, variables, near),
        out_shape=[
            jax.ShapeDtypeStruct((blocks, levels * 2 * STEPS * SPAN, lanes), jnp.bfloat16),
            jax.ShapeDtypeStruct((blocks, slots // 2, lanes), jnp.bfloat16),
        ],
        in_specs=hbm(1 + near) + vmem(3),
        out_specs=vmem(2),
        scratch_shapes=[
            pltpu.VMEM((STEPS, 2 * lanes, columns), jnp.bfloat16),
            pltpu.VMEM((levels, lanes, span, columns), jnp.float32),
            pltpu.VMEM((near, levels, lanes, span, columns), jnp.float32),
            pltpu.VMEM((levels, pairs, 2 * lanes, columns), jnp.bfloat16),
            pltpu.VMEM((blocks, levels * pairs * (2 * EDGE + SPAN), 2 * lanes), jnp.bfloat16),
            pltpu.SemaphoreType.DMA((1 + near, levels)),
        ],
        compiler_params=params(60),
        cost_estimate=cost(6 * 10**9, 8 * 2**20),
    )(own, *sides, coef, centre, cells)


def join(a, b, left, members):
    return (
        jnp.where(left, a, pltpu.roll(b, members, 1)),
        jnp.where(left, pltpu.roll(a, members, 1), b),
    )


def left_lanes(shape):
    return lax.broadcasted_iota(jnp.int32, shape, 1) < shape[1] // 2


def update(states, out, raw, dev, high, low, poly, gain, alpha, factor):
    groups, half, lanes = states.shape
    members = lanes // 2
    left = left_lanes((half, lanes))
    sums = [jnp.zeros((half, lanes), jnp.float32)] * 2
    for j in range(groups // 2):
        here = slice(j * lanes, (j + 1) * lanes)
        pair = join(
            states[2 * j].astype(jnp.float32),
            states[2 * j + 1].astype(jnp.float32),
            left,
            members,
        )
        raw[:half, here] = pair[0]
        raw[half:, here] = pair[1]
        sums = [sums[0] + pair[0], sums[1] + pair[1]]
    centre = jnp.concatenate([jnp.sum(x, axis=1, keepdims=True) for x in sums], axis=0)
    centre = centre * (1.0 / (groups * members))
    dev[...] = (raw[...] - centre).astype(jnp.bfloat16)
    cross = dot_rows(dev[...], high[...]) + dot_rows(dev[...], low[...])
    shift = centre + jnp.sum(cross * gain, axis=1, keepdims=True)
    mix = (dot(cross, poly, precision=HIGH) * factor).astype(jnp.bfloat16)
    for j in range(groups // 2):
        here = slice(j * lanes, (j + 1) * lanes)
        new = dot(mix, high[:, here]) + alpha * dev[:, here].astype(jnp.float32) + shift
        x, y = join(new[:half], new[half:], left, members)
        out[2 * j] = x.astype(jnp.bfloat16)
        out[2 * j + 1] = y.astype(jnp.bfloat16)


def weigh_kernel(seen, states, count, value, weight, high, low, poly_ref, gain_ref, scalars, out, raw, dev, obs):
    groups, half, lanes = seen.shape
    slots = 2 * half
    members = lanes // 2
    total_members = groups * members
    left = left_lanes((half, lanes))

    for j in range(groups // 2):
        here = slice(j * lanes, (j + 1) * lanes)
        obs[:half, here], obs[half:, here] = join(
            seen[2 * j].astype(jnp.float32),
            seen[2 * j + 1].astype(jnp.float32),
            left,
            members,
        )

    used = lax.broadcasted_iota(jnp.int32, (1, slots), 1) < count[0, 0]
    root = column_of(jnp.where(used, jnp.sqrt(weight[...]), 0.0))
    observed = obs[...]
    mean = jnp.sum(observed, axis=1, keepdims=True) * (1.0 / total_members)
    scaled = (observed - mean) * root
    energy = jnp.sum(jnp.sum(scaled * scaled, axis=1, keepdims=True), axis=0, keepdims=True)
    top = scaled.astype(jnp.bfloat16)
    high[...] = top
    low[...] = (scaled - top.astype(jnp.float32)).astype(jnp.bfloat16)
    misfit = row_of(root * (column_of(value[...]) - mean))

    c = total_members - 1.0
    s = energy * (1.0 / total_members) + c
    inverse = 1.0 / s
    a = c * inverse
    p = 1.5 - 0.5 * a
    p2 = p * p
    p3 = p2 * p
    base = 1.5 * p - 0.5 * a * p3
    q0 = -0.75 - 0.5 * (p3 - 1.5 * a * p2)
    q1 = -0.5 * (0.75 * a * p - 1.5 * p2)
    q2 = -0.5 * (0.75 * p - 0.125 * a)
    small = (
        dot_rows(high[...], high[...])
        + dot_rows(high[...], low[...])
        + dot_rows(low[...], high[...])
    ) * inverse
    diagonal = eye(slots)
    square = dot(small, small, precision=HIGH)
    tail = dot(square, jnp.where(diagonal, q2, 0.0) + 0.0625 * small, precision=HIGH)
    poly = jnp.where(diagonal, q0, 0.0) + q1 * small + tail

    def apply(vector):
        inner_part = jnp.sum(poly * vector, axis=1, keepdims=True)
        return jnp.sum(small * inner_part, axis=0, keepdims=True) + base * vector

    gain = apply(apply(misfit)) * inverse
    stretch = jnp.sqrt(a)
    alpha, factor = stretch * base, stretch * inverse
    poly_ref[...] = poly
    gain_ref[...] = gain
    scalars[0:1, :] = jnp.broadcast_to(alpha, (1, scalars.shape[1]))
    scalars[1:2, :] = jnp.broadcast_to(factor, (1, scalars.shape[1]))
    update(states, out, raw, dev, high, low, poly, gain, alpha, factor)


def weigh(seen, states, count, value, weight):
    groups, half, lanes = states.shape
    slots = value.shape[1]
    total = groups * lanes // 2
    return pl.pallas_call(
        weigh_kernel,
        out_shape=[
            jax.ShapeDtypeStruct((slots, total), jnp.bfloat16),
            jax.ShapeDtypeStruct((slots, total), jnp.bfloat16),
            jax.ShapeDtypeStruct((slots, slots), jnp.float32),
            jax.ShapeDtypeStruct((1, slots), jnp.float32),
            jax.ShapeDtypeStruct((8, 128), jnp.float32),
            jax.ShapeDtypeStruct(states.shape, jnp.bfloat16),
        ],
        in_specs=vmem(2) + smem(1) + vmem(2),
        out_specs=vmem(6),
        scratch_shapes=[
            pltpu.VMEM((2 * half, total), jnp.float32),
            pltpu.VMEM((2 * half, total), jnp.bfloat16),
            pltpu.VMEM((slots, total), jnp.float32),
        ],
        compiler_params=params(14),
        cost_estimate=cost(4 * 10**9, 4 * 2**20),
    )(seen, states, count, value, weight)


def rest_kernel(states, high, low, poly, gain, scalars, out, raw, dev):
    alpha, factor = scalars[0:1, 0:1], scalars[1:2, 0:1]
    update(states, out, raw, dev, high, low, poly[...], gain[...], alpha, factor)


def analyse_rest(states, shared):
    groups, half, lanes = states.shape
    total = groups * lanes // 2
    return pl.pallas_call(
        rest_kernel,
        out_shape=jax.ShapeDtypeStruct(states.shape, jnp.bfloat16),
        in_specs=vmem(6),
        out_specs=pl.BlockSpec(memory_space=pltpu.VMEM),
        scratch_shapes=[
            pltpu.VMEM((2 * half, total), jnp.float32),
            pltpu.VMEM((2 * half, total), jnp.bfloat16),
        ],
        compiler_params=params(10),
        cost_estimate=cost(2 * 10**9, 4 * 2**20),
    )(states, *shared)


def restore_kernel(inside, outside, out, turned):
    members, variables, levels, span, columns = out.shape
    lanes = members * variables
    identity = permutation(lanes, 0)
    near = span - 2 * STEPS
    for level in range(levels):
        for r in range(0, span, 2):
            if STEPS <= r < span - STEPS:
                blocks, at = inside, level * near + r - STEPS
            else:
                blocks, at = outside, level * 2 * STEPS + (r if r < STEPS else r - near)
            both = blocks[:, at * SPAN : (at + 2) * SPAN, :].astype(jnp.float32)
            for i in range(2):
                one = both[:, i * SPAN : (i + 1) * SPAN, :].reshape(columns, lanes)
                rows = dot_rows(identity, one.astype(jnp.bfloat16))
                turned[level % 2, pl.ds(r + i, lanes, stride=span), :] = rows
        for var in range(variables):
            half = turned[level % 2, var * members * span : (var + 1) * members * span, :]
            out[:, var, level] = half.reshape(members, span, columns).astype(jnp.bfloat16)


def restore(dims, inside, outside):
    members, variables, levels, span, columns = dims
    return pl.pallas_call(
        restore_kernel,
        out_shape=jax.ShapeDtypeStruct((members, variables, levels, span, columns), jnp.bfloat16),
        in_specs=vmem(2),
        out_specs=pl.BlockSpec(memory_space=pltpu.VMEM),
        scratch_shapes=[pltpu.VMEM((2, variables * members * span, columns), jnp.float32)],
        compiler_params=params(8),
        cost_estimate=cost(2 * 10**9, 2 * 2**20),
    )(inside, outside)


def neighbours(field, axis):
    count = lax.axis_size(axis)
    low = lax.ppermute(field, axis, [(i, (i + 1) % count) for i in range(count)])
    if count == 2:
        return (low,)
    return low, lax.ppermute(field, axis, [((i + 1) % count, i) for i in range(count)])


def exchange(blocks):
    return lax.all_to_all(blocks, "grp", split_axis=0, concat_axis=0, tiled=True)


def on_device(start, diffusivity, eastward, northward, cells, count, value, weight):
    members, variables, levels, span, columns = dims = start.shape
    own = start.reshape(members * variables, levels, span, columns)
    sides = neighbours(own, "tile")
    coef = model_coefficients(diffusivity, eastward, northward)
    centre, near = inner(dims, own, coef)
    inside = exchange(near)
    rim, seen = observe(dims, own, sides, coef, centre, cells[0])
    seen = exchange(seen)
    outside = exchange(rim)
    *shared, inside = weigh(seen, inside, count, value[0], weight[0])
    inside = exchange(inside)
    outside = exchange(analyse_rest(outside, shared))
    return restore(dims, inside, outside)


def solution(mesh):
    return jax.shard_map(
        on_device,
        mesh=mesh,
        in_specs=(
            P("grp", None, None, "tile", None),
            P(),
            P(),
            P(),
            P("tile", None, None),
            P("tile", "grp"),
            P("tile", "grp", None),
            P("tile", "grp", None),
        ),
        out_specs=P("grp", None, None, "tile", None),
        check_vma=False,
    )
```

```python
import functools

import jax
import jax.numpy as jnp
from jax import lax
from jax.experimental import pallas as pl
from jax.experimental.pallas import tpu as pltpu
from jax.sharding import PartitionSpec as P

SPAN = 8
STEPS = 2
EDGE = SPAN // 2

ROWS = (((1,), (1,)), ((), ()))


def params(mebibytes, **kw):
    return pltpu.CompilerParams(vmem_limit_bytes=mebibytes * 2**20, **kw)


def cost(flops, size):
    return pl.CostEstimate(flops=flops, bytes_accessed=size, transcendentals=0)


def vmem(count):
    return [pl.BlockSpec(memory_space=pltpu.VMEM)] * count


def hbm(count):
    return [pl.BlockSpec(memory_space=pltpu.HBM)] * count


def smem(count):
    return [pl.BlockSpec(memory_space=pltpu.SMEM)] * count


def dot(a, b, **kw):
    return jnp.dot(a, b, preferred_element_type=jnp.float32, **kw)


def split(x):
    high = x.astype(jnp.bfloat16)
    return high, (x - high.astype(jnp.float32)).astype(jnp.bfloat16)


def dot3(a, b):
    (a_high, a_low), (b_high, b_low) = split(a), split(b)
    return dot(a_high, b_high) + (dot(a_high, b_low) + dot(a_low, b_high))


def dot_rows(a, b):
    return lax.dot_general(a, b, ROWS, preferred_element_type=jnp.float32)


def permutation(size, shift):
    row = lax.broadcasted_iota(jnp.int32, (size, size), 0)
    column = lax.broadcasted_iota(jnp.int32, (size, size), 1)
    return (lax.rem(row + shift + size, size) == column).astype(jnp.bfloat16)


def eye(size):
    row = lax.broadcasted_iota(jnp.int32, (size, size), 0)
    column = lax.broadcasted_iota(jnp.int32, (size, size), 1)
    return row == column


def column_of(row):
    return jnp.sum(jnp.where(eye(row.shape[1]), row, 0.0), axis=1, keepdims=True)


def row_of(column):
    return jnp.sum(jnp.where(eye(column.shape[0]), column, 0.0), axis=0, keepdims=True)


def forecast_rows(read, first, last, coefficients, write):
    middle, east, west, north, south = coefficients

    def step(below, here, above):
        columns = here.shape[2]
        return (
            middle * here
            + east * above
            + west * below
            + north * pltpu.roll(here, columns - 1, 2)
            + south * pltpu.roll(here, 1, 2)
        )

    start = [read(first - 2), read(first - 1), read(first)]
    once = [None, None, None]
    for r in range(first - 1, last + 1):
        once = [once[1], once[2], step(*start)]
        if r >= first + 1:
            write(r - 1, step(*once))
        if r < last:
            start = [start[1], start[2], read(r + 2)]


def coefficients_of(level, diff, east, north):
    spread = jnp.broadcast_to(diff[pl.ds(level, 1), :], (8, diff.shape[1]))
    u = 0.5 * east[level]
    w = 0.5 * north[level]
    return 1.0 - 4.0 * spread, spread - u, spread + u, spread - w, spread + w


def row_reader(var, variables, own, low, high):
    rows, _, span, columns = own.shape

    def read(r):
        ref, at = (low, r + span) if r < 0 else (own, r) if r < span else (high, r - span)
        view = ref.reshape(rows * span, columns)
        here = view[pl.ds(var * span + at, rows // variables, stride=variables * span), :]
        return here.reshape(-1, 8, columns)

    return read


def pack_rows(pair, identity, store, at):
    lanes = pair.shape[0] // 2
    turned = dot_rows(identity, pair)
    parts = [turned[:, i * lanes : (i + 1) * lanes].reshape(-1, SPAN, lanes) for i in range(2)]
    store[:, at : at + 2 * SPAN, :] = jnp.concatenate(parts, axis=1).astype(jnp.bfloat16)


def inner_kernel(variables, own, diff, east, north, fields, packed):
    rows, _, span, columns = own.shape
    members = rows // variables
    coefficients = coefficients_of(pl.program_id(0), diff, east, north)
    for var in range(variables):

        def write(r, value):
            pair, half = divmod(r - STEPS, 2)
            at = half * rows + var * members
            value = value.reshape(members, columns).astype(jnp.bfloat16)
            fields[0, pair, at : at + members, :] = value

        read = row_reader(var, variables, own, None, None)
        forecast_rows(read, STEPS, span - STEPS, coefficients, write)
    identity = permutation(columns, 0)
    for pair in range(span // 2 - STEPS):
        pack_rows(fields[0, pair], identity, packed, 2 * pair * SPAN)


def level_block(rows, span, columns):
    return pl.BlockSpec((rows, 1, span, columns), lambda level: (0, level, 0, 0))


def fields_block(pairs, rows, columns):
    return pl.BlockSpec((1, pairs, rows, columns), lambda level: (level, 0, 0, 0))


def packed_block(blocks, rows, lanes):
    return pl.BlockSpec((blocks, rows, lanes), lambda level: (0, level, 0))


def inner(dims, own, diff, east, north):
    members, variables, levels, span, columns = dims
    lanes = members * variables
    blocks = columns // SPAN
    count = span - 2 * STEPS
    return pl.pallas_call(
        functools.partial(inner_kernel, variables),
        grid=(levels,),
        out_shape=[
            jax.ShapeDtypeStruct((levels, count // 2, 2 * lanes, columns), jnp.bfloat16),
            jax.ShapeDtypeStruct((blocks, levels * count * SPAN, lanes), jnp.bfloat16),
        ],
        in_specs=[level_block(lanes, span, columns)] + vmem(1) + smem(2),
        out_specs=[
            fields_block(count // 2, 2 * lanes, columns),
            packed_block(blocks, count * SPAN, lanes),
        ],
        compiler_params=params(60),
        cost_estimate=cost(2 * 10**9, 4 * 2**20),
    )(own, diff, east, north)


def outer_kernel(variables, near, own, *rest):
    sides, rest = rest[:near], rest[near:]
    diff, east, north, centre, grid, packed, fields = rest
    rows, _, span, columns = own.shape
    members = rows // variables
    pairs = (2 * EDGE + span) // 2
    coefficients = coefficients_of(pl.program_id(0), diff, east, north)

    def put(r, var, value):
        half, pair = divmod(r + EDGE, pairs)
        at = half * rows + var * members
        grid[0, pair, at : at + members, :] = value

    for var in range(variables):

        def write(r, value):
            value = value.reshape(members, columns).astype(jnp.bfloat16)
            put(r, var, value)
            if 0 <= r < span:
                pair, half = divmod(r if r < STEPS else r - span + 2 * STEPS, 2)
                at = half * rows + var * members
                fields[pair, at : at + members, :] = value

        read = row_reader(var, variables, own, sides[0], sides[-1])
        forecast_rows(read, -EDGE, STEPS, coefficients, write)
        forecast_rows(read, span - STEPS, span + EDGE, coefficients, write)
        for r in range(STEPS, span - STEPS):
            pair, half = divmod(r - STEPS, 2)
            at = half * rows + var * members
            put(r, var, centre[0, pair, at : at + members, :])
    identity = permutation(columns, 0)
    for pair in range(STEPS):
        pack_rows(fields[pair], identity, packed, 2 * pair * SPAN)


def outer(dims, own, sides, diff, east, north, centre):
    members, variables, levels, span, columns = dims
    lanes = members * variables
    blocks = columns // SPAN
    near = len(sides)
    pairs = (2 * EDGE + span) // 2
    return pl.pallas_call(
        functools.partial(outer_kernel, variables, near),
        grid=(levels,),
        out_shape=[
            jax.ShapeDtypeStruct((levels, pairs, 2 * lanes, columns), jnp.bfloat16),
            jax.ShapeDtypeStruct((blocks, levels * 2 * STEPS * SPAN, lanes), jnp.bfloat16),
        ],
        in_specs=[level_block(lanes, span, columns)] * (1 + near)
        + vmem(1)
        + smem(2)
        + [fields_block(span // 2 - STEPS, 2 * lanes, columns)],
        out_specs=[
            fields_block(pairs, 2 * lanes, columns),
            packed_block(blocks, 2 * STEPS * SPAN, lanes),
        ],
        scratch_shapes=[pltpu.VMEM((STEPS, 2 * lanes, columns), jnp.bfloat16)],
        compiler_params=params(20),
        cost_estimate=cost(2 * 10**9, 8 * 2**20),
    )(own, *sides, diff, east, north, centre)


def pick_kernel(variables, together, grid, rim, cells, out, region, codes):
    levels, pairs, twice, columns = grid.shape
    rows = twice // 2
    members = rows // variables
    blocks, slots = cells.shape
    width = 2 * EDGE + SPAN
    part = pairs * width
    entries = levels * part
    share = rim.shape[1]

    orders = jnp.concatenate(
        [permutation(columns, -EDGE), permutation(columns, SPAN - EDGE)], axis=0
    )
    for level in range(levels):
        for pair in range(pairs):
            turned = dot_rows(orders, grid[level, pair]).astype(jnp.bfloat16)
            at = (level * pairs + pair) * width
            for first in range(2):
                for j in range(columns // width):
                    row = first * columns + j * width
                    region[2 * j + first, at : at + width, :] = turned[row : row + width, :]

    cell = cells[...]
    second = cell >= 2 * entries
    cell = jnp.where(second, cell - 2 * entries, cell)
    level = lax.shift_right_logical(cell, (2 * part).bit_length() - 1)
    inside = cell - level * (2 * part)
    lower = inside >= part
    code = level * part + jnp.where(lower, inside - part + entries, inside)
    codes[...] = jnp.where(second, code + 2 * entries, code).astype(jnp.float32)

    left = lax.broadcasted_iota(jnp.int32, (slots // 2, rows), 1) < members
    lane = lax.broadcasted_iota(jnp.int32, (slots, entries), 1).astype(jnp.float32)

    @pl.loop(0, blocks // together)
    def _(step):
        for i in range(together):
            block = step * together + i
            at = column_of(codes[pl.ds(block, 1), :])
            second = at >= 2.0 * entries
            at = jnp.where(second, at - 2.0 * entries, at)
            lower = at >= 1.0 * entries
            at = jnp.where(lower, at - 1.0 * entries, at)
            pick = jnp.where(lane == at, 1.0, 0.0).astype(jnp.bfloat16)
            found = dot(pick, region[block])
            total = jnp.where(lower, found[:, rows:], found[:, :rows])
            other = pltpu.roll(total, members, 1)
            to_left = jnp.where(second, other, total)[: slots // 2]
            to_right = jnp.where(second, total, other)[slots // 2 :]
            out[block, share:, :] = jnp.where(left, to_left, to_right).astype(jnp.bfloat16)
            out[block, :share, :] = rim[block]


def pick(variables, grid, rim, cells):
    levels, pairs, twice, columns = grid.shape
    blocks, slots = cells.shape
    _, share, lanes = rim.shape
    together = next(n for n in (4, 2, 1) if blocks % n == 0)
    return pl.pallas_call(
        functools.partial(pick_kernel, variables, together),
        out_shape=jax.ShapeDtypeStruct((blocks, share + slots // 2, lanes), jnp.bfloat16),
        in_specs=vmem(3),
        out_specs=pl.BlockSpec(memory_space=pltpu.VMEM),
        scratch_shapes=[
            pltpu.VMEM((blocks, levels * pairs * (2 * EDGE + SPAN), twice), jnp.bfloat16),
            pltpu.VMEM((blocks, slots), jnp.float32),
        ],
        compiler_params=params(20),
        cost_estimate=cost(4 * 10**9, 4 * 2**20),
    )(grid, rim, cells)


def join(a, b, left, members):
    return (
        jnp.where(left, a, pltpu.roll(b, members, 1)),
        jnp.where(left, pltpu.roll(a, members, 1), b),
    )


def left_lanes(shape):
    return lax.broadcasted_iota(jnp.int32, shape, 1) < shape[1] // 2


def deviations(states, raw, dev, at, size):
    groups, _, lanes = states.shape
    members = lanes // 2
    left = left_lanes((size, lanes))
    sums = [jnp.zeros((size, lanes), jnp.float32)] * 2
    for j in range(groups // 2):
        here = slice(j * lanes, (j + 1) * lanes)
        pair = join(
            states[2 * j, :size, :].astype(jnp.float32),
            states[2 * j + 1, :size, :].astype(jnp.float32),
            left,
            members,
        )
        for var in range(2):
            raw[var * size : (var + 1) * size, here] = pair[var]
        sums = [total + one for total, one in zip(sums, pair)]
    centre = jnp.concatenate([jnp.sum(x, axis=1, keepdims=True) for x in sums], axis=0)
    centre = centre * (1.0 / (groups * members))
    dev[at : at + 2 * size, :] = (raw[...] - centre).astype(jnp.bfloat16)
    return centre


def prepare_kernel(states, dev, centre, raw):
    mean = deviations(states, raw, dev, 0, states.shape[1])
    centre[...] = jnp.broadcast_to(mean, centre.shape)


def prepare(states):
    groups, near, lanes = states.shape
    total = groups * lanes // 2
    return pl.pallas_call(
        prepare_kernel,
        out_shape=[
            jax.ShapeDtypeStruct((2 * near, total), jnp.bfloat16),
            jax.ShapeDtypeStruct((2 * near, lanes), jnp.float32),
        ],
        in_specs=vmem(1),
        out_specs=vmem(2),
        scratch_shapes=[pltpu.VMEM((2 * near, total), jnp.float32)],
        compiler_params=params(6),
        cost_estimate=cost(10**8, 2 * 2**20),
    )(states)


def analyse_kernel(first, means, second, count, value, weight, out, raw, dev, obs, scaled_ref):
    groups, _, lanes = second.shape
    near = first.shape[0] // 2
    half = obs.shape[0] // 2
    far = second.shape[1] - half
    side = near + far
    slots = 2 * half
    members = lanes // 2
    total_members = groups * members
    left = left_lanes((half, lanes))

    for j in range(groups // 2):
        here = slice(j * lanes, (j + 1) * lanes)
        obs[:half, here], obs[half:, here] = join(
            second[2 * j, far:, :].astype(jnp.float32),
            second[2 * j + 1, far:, :].astype(jnp.float32),
            left,
            members,
        )

    used = lax.broadcasted_iota(jnp.int32, (1, slots), 1) < count[0, 0]
    root = column_of(jnp.where(used, jnp.sqrt(weight[...]), 0.0))
    observed = obs[...]
    mean = jnp.sum(observed, axis=1, keepdims=True) * (1.0 / total_members)
    scaled = (observed - mean) * root
    energy = jnp.sum(jnp.sum(scaled * scaled, axis=1, keepdims=True), axis=0, keepdims=True)
    scaled_ref[...] = scaled.astype(jnp.bfloat16)
    misfit = row_of(root * (column_of(value[...]) - mean))

    c = total_members - 1.0
    s = energy * (1.0 / total_members) + c
    inverse = 1.0 / s
    a = c * inverse
    p = 1.5 - 0.5 * a
    p2 = p * p
    p3 = p2 * p
    base = 1.5 * p - 0.5 * a * p3
    q0 = -0.75 - 0.5 * (p3 - 1.5 * a * p2)
    q1 = -0.5 * (0.75 * a * p - 1.5 * p2)
    q2 = -0.5 * (0.75 * p - 0.125 * a)
    small = dot_rows(scaled_ref[...], scaled_ref[...]) * inverse
    diagonal = eye(slots)
    square = dot3(small, small)
    tail = dot3(square, jnp.where(diagonal, q2, 0.0) + 0.0625 * small)
    poly = jnp.where(diagonal, q0, 0.0) + q1 * small + tail

    def apply(vector):
        inner_part = jnp.sum(poly * vector, axis=1, keepdims=True)
        return jnp.sum(small * inner_part, axis=0, keepdims=True) + base * vector

    gain = apply(apply(misfit)) * inverse
    stretch = jnp.sqrt(a)
    alpha, factor = stretch * base, stretch * inverse
    centre = deviations(second, raw, dev, 0, far)
    cross = jnp.concatenate(
        [dot_rows(first[...], scaled_ref[...]), dot_rows(dev[...], scaled_ref[...])], axis=0
    )
    centre = jnp.concatenate([means[:, 0:1], centre], axis=0)
    shift = centre + jnp.sum(cross * gain, axis=1, keepdims=True)
    mix = (dot3(cross, poly) * factor).astype(jnp.bfloat16)
    parts = ((first, 0, near, 0), (dev, 2 * near, far, near))
    for j in range(groups // 2):
        here = slice(j * lanes, (j + 1) * lanes)
        new = dot(mix, scaled_ref[:, here]) + shift
        for ref, at, size, row in parts:
            one = new[at : at + 2 * size] + alpha * ref[:, here].astype(jnp.float32)
            x, y = join(one[:size], one[size:], left_lanes((size, lanes)), members)
            out[2 * j, row : row + size, :] = x.astype(jnp.bfloat16)
            out[2 * j + 1, row : row + size, :] = y.astype(jnp.bfloat16)


def analyse(first, means, second, count, value, weight):
    groups, _, lanes = second.shape
    near = first.shape[0] // 2
    slots = value.shape[1]
    far = second.shape[1] - slots // 2
    total = groups * lanes // 2
    return pl.pallas_call(
        analyse_kernel,
        out_shape=jax.ShapeDtypeStruct((groups, near + far, lanes), jnp.bfloat16),
        in_specs=vmem(3) + smem(1) + vmem(2),
        out_specs=pl.BlockSpec(memory_space=pltpu.VMEM),
        scratch_shapes=[
            pltpu.VMEM((2 * far, total), jnp.float32),
            pltpu.VMEM((2 * far, total), jnp.bfloat16),
            pltpu.VMEM((slots, total), jnp.float32),
            pltpu.VMEM((slots, total), jnp.bfloat16),
        ],
        compiler_params=params(16),
        cost_estimate=cost(4 * 10**9, 4 * 2**20),
    )(first, means, second, count, value, weight)


def restore_kernel(inside, outside, out, turned):
    members, variables, _, span, columns = out.shape
    lanes = members * variables
    identity = permutation(lanes, 0)
    near = span - 2 * STEPS
    for r in range(0, span, 2):
        if STEPS <= r < span - STEPS:
            blocks, at = inside, r - STEPS
        else:
            blocks, at = outside, r if r < STEPS else r - near
        both = blocks[:, at * SPAN : (at + 2) * SPAN, :].astype(jnp.float32)
        for i in range(2):
            one = both[:, i * SPAN : (i + 1) * SPAN, :].reshape(columns, lanes)
            rows = dot_rows(identity, one.astype(jnp.bfloat16))
            turned[pl.ds(r + i, lanes, stride=span), :] = rows
    for var in range(variables):
        half = turned[var * members * span : (var + 1) * members * span, :]
        out[:, var, 0] = half.reshape(members, span, columns).astype(jnp.bfloat16)


def restore(dims, blocks):
    members, variables, levels, span, columns = dims
    lanes = variables * members
    near, far = (span - 2 * STEPS) * SPAN, 2 * STEPS * SPAN
    count = blocks.shape[0]
    return pl.pallas_call(
        restore_kernel,
        grid=(levels,),
        out_shape=jax.ShapeDtypeStruct((members, variables, levels, span, columns), jnp.bfloat16),
        in_specs=[
            pl.BlockSpec((count, near, lanes), lambda level: (0, level, 0)),
            pl.BlockSpec((count, far, lanes), lambda level: (0, levels * near // far + level, 0)),
        ],
        out_specs=pl.BlockSpec(
            (members, variables, 1, span, columns), lambda level: (0, 0, level, 0, 0)
        ),
        scratch_shapes=[pltpu.VMEM((lanes * span, columns), jnp.float32)],
        compiler_params=params(8),
        cost_estimate=cost(2 * 10**9, 2 * 2**20),
    )(blocks, blocks)


def neighbours(field, axis):
    count = lax.axis_size(axis)
    low = lax.ppermute(field, axis, [(i, (i + 1) % count) for i in range(count)])
    if count == 2:
        return (low,)
    return low, lax.ppermute(field, axis, [((i + 1) % count, i) for i in range(count)])


def exchange(blocks):
    return lax.all_to_all(blocks, "grp", split_axis=0, concat_axis=0, tiled=True)


def on_device(start, diffusivity, eastward, northward, cells, count, value, weight):
    members, variables, levels, span, columns = dims = start.shape
    own = start.reshape(members * variables, levels, span, columns)
    sides = neighbours(own, "tile")
    model = (diffusivity, eastward, northward)
    centre, near = inner(dims, own, *model)
    first, means = prepare(exchange(near))
    grid, rim = outer(dims, own, sides, *model, centre)
    second = exchange(pick(variables, grid, rim, cells[0]))
    updated = analyse(first, means, second, count, value[0], weight[0])
    return restore(dims, exchange(updated))


def solution(mesh):
    return jax.shard_map(
        on_device,
        mesh=mesh,
        in_specs=(
            P("grp", None, None, "tile", None),
            P(),
            P(),
            P(),
            P("tile", None, None),
            P("tile", "grp"),
            P("tile", "grp", None),
            P("tile", "grp", None),
        ),
        out_specs=P("grp", None, None, "tile", None),
        check_vma=False,
    )
```

```python
import functools

import jax
import jax.numpy as jnp
from jax import lax
from jax.experimental import pallas as pl
from jax.experimental.pallas import tpu as pltpu
from jax.sharding import PartitionSpec as P

SPAN = 8
STEPS = 2
EDGE = SPAN // 2

ROWS = (((1,), (1,)), ((), ()))


def params(mebibytes, **kw):
    return pltpu.CompilerParams(vmem_limit_bytes=mebibytes * 2**20, **kw)


def cost(flops, size):
    return pl.CostEstimate(flops=flops, bytes_accessed=size, transcendentals=0)


def vmem(count):
    return [pl.BlockSpec(memory_space=pltpu.VMEM)] * count


def hbm(count):
    return [pl.BlockSpec(memory_space=pltpu.HBM)] * count


def smem(count):
    return [pl.BlockSpec(memory_space=pltpu.SMEM)] * count


def dot(a, b, **kw):
    return jnp.dot(a, b, preferred_element_type=jnp.float32, **kw)


def split(x):
    high = x.astype(jnp.bfloat16)
    return high, (x - high.astype(jnp.float32)).astype(jnp.bfloat16)


def dot3(a, b):
    (a_high, a_low), (b_high, b_low) = split(a), split(b)
    return dot(a_high, b_high) + (dot(a_high, b_low) + dot(a_low, b_high))


def dot_rows(a, b):
    return lax.dot_general(a, b, ROWS, preferred_element_type=jnp.float32)


def permutation(size, shift):
    row = lax.broadcasted_iota(jnp.int32, (size, size), 0)
    column = lax.broadcasted_iota(jnp.int32, (size, size), 1)
    return (lax.rem(row + shift + size, size) == column).astype(jnp.bfloat16)


def eye(size):
    row = lax.broadcasted_iota(jnp.int32, (size, size), 0)
    column = lax.broadcasted_iota(jnp.int32, (size, size), 1)
    return row == column


def column_of(row):
    return jnp.sum(jnp.where(eye(row.shape[1]), row, 0.0), axis=1, keepdims=True)


def row_of(column):
    return jnp.sum(jnp.where(eye(column.shape[0]), column, 0.0), axis=0, keepdims=True)


def forecast_rows(read, first, last, coefficients, write):
    middle, east, west, north, south = coefficients

    def step(below, here, above):
        columns = here.shape[2]
        return (
            middle * here
            + east * above
            + west * below
            + north * pltpu.roll(here, columns - 1, 2)
            + south * pltpu.roll(here, 1, 2)
        )

    start = [read(first - 2), read(first - 1), read(first)]
    once = [None, None, None]
    for r in range(first - 1, last + 1):
        once = [once[1], once[2], step(*start)]
        if r >= first + 1:
            write(r - 1, step(*once))
        if r < last:
            start = [start[1], start[2], read(r + 2)]


def coefficients_of(level, diff, east, north):
    spread = jnp.broadcast_to(diff[pl.ds(level, 1), :], (8, diff.shape[1]))
    u = 0.5 * east[level]
    w = 0.5 * north[level]
    return 1.0 - 4.0 * spread, spread - u, spread + u, spread - w, spread + w


def row_reader(level, var, variables, first, size, own, low, high):
    _, levels, span, columns = own.shape
    stride = variables * levels * span

    def read(r):
        ref, at = (low, r + span) if r < 0 else (own, r) if r < span else (high, r - span)
        start = first * stride + (var * levels + level) * span + at
        view = ref.reshape(ref.shape[0] * levels * span, columns)
        return view[pl.ds(start, size, stride=stride), :].reshape(-1, 8, columns)

    return read


def pack_rows(pair, identity, store, at):
    lanes = pair.shape[0] // 2
    turned = dot_rows(identity, pair)
    parts = [turned[:, i * lanes : (i + 1) * lanes].reshape(-1, SPAN, lanes) for i in range(2)]
    store[:, at : at + 2 * SPAN, :] = jnp.concatenate(parts, axis=1).astype(jnp.bfloat16)


def inner_kernel(variables, chunks, own, diff, east, north, fields, packed, slab, sems):
    rows, levels, span, columns = own.shape
    members = rows // variables
    size = members // chunks
    copies = []
    for i in range(chunks):
        here = pl.ds(i * size * variables, size * variables)
        copies.append(pltpu.make_async_copy(own.at[here], slab.at[here], sems.at[i]))
        copies[-1].start()
    coefficients = [coefficients_of(level, diff, east, north) for level in range(levels)]
    for i in range(chunks):
        copies[i].wait()
        for level in range(levels):
            for var in range(variables):

                def write(r, value):
                    at = var * members + i * size
                    value = value.reshape(size, columns).astype(jnp.bfloat16)
                    fields[level, r - STEPS, at : at + size, :] = value

                read = row_reader(level, var, variables, i * size, size, slab, None, None)
                forecast_rows(read, STEPS, span - STEPS, coefficients[level], write)
    identity = permutation(columns, 0)
    count = span - 2 * STEPS
    for level in range(levels):
        for r in range(0, count, 2):
            pair = fields[level, r : r + 2].reshape(2 * rows, columns)
            pack_rows(pair, identity, packed, (level * count + r) * SPAN)


def inner(dims, own, diff, east, north):
    members, variables, levels, span, columns = dims
    lanes = members * variables
    blocks = columns // SPAN
    count = span - 2 * STEPS
    chunks = max(1, members // 16)
    return pl.pallas_call(
        functools.partial(inner_kernel, variables, chunks),
        out_shape=[
            jax.ShapeDtypeStruct((levels, count, lanes, columns), jnp.bfloat16),
            jax.ShapeDtypeStruct((blocks, levels * count * SPAN, lanes), jnp.bfloat16),
        ],
        in_specs=hbm(1) + vmem(1) + smem(2),
        out_specs=vmem(2),
        scratch_shapes=[
            pltpu.VMEM((lanes, levels, span, columns), jnp.float32),
            pltpu.SemaphoreType.DMA((chunks,)),
        ],
        compiler_params=params(56),
        cost_estimate=cost(2 * 10**9, 4 * 2**20),
    )(own, diff, east, north)


def outer_kernel(variables, near, size, own, *rest):
    sides, rest = rest[:near], rest[near:]
    diff, east, north, centre, grid, packed, fields, sems = rest
    rows, levels, span, columns = own.shape
    members = rows // variables
    pairs = (2 * EDGE + span) // 2

    copies = []
    for r in range(STEPS, span - STEPS):
        half, pair = divmod(r + EDGE, pairs)
        place = grid.at[:, pair, pl.ds(half * rows, rows)]
        copies.append(pltpu.make_async_copy(centre.at[:, r - STEPS], place, sems.at[r - STEPS]))
        copies[-1].start()

    for level in range(levels):
        coefficients = coefficients_of(level, diff, east, north)
        for var in range(variables):
            for first in range(0, members, size):

                def write(r, value):
                    value = value.reshape(size, columns).astype(jnp.bfloat16)
                    half, pair = divmod(r + EDGE, pairs)
                    at = half * rows + var * members + first
                    grid[level, pair, at : at + size, :] = value
                    if 0 <= r < span:
                        pair, half = divmod(r if r < STEPS else r - span + 2 * STEPS, 2)
                        at = half * rows + var * members + first
                        fields[level, pair, at : at + size, :] = value

                read = row_reader(
                    level, var, variables, first, size, own, sides[0], sides[-1]
                )
                forecast_rows(read, -EDGE, STEPS, coefficients, write)
                forecast_rows(read, span - STEPS, span + EDGE, coefficients, write)
    identity = permutation(columns, 0)
    for level in range(levels):
        for pair in range(STEPS):
            at = (level * STEPS + pair) * 2 * SPAN
            pack_rows(fields[level, pair], identity, packed, at)
    for copy in copies:
        copy.wait()


def outer(dims, own, sides, diff, east, north, centre):
    members, variables, levels, span, columns = dims
    lanes = members * variables
    blocks = columns // SPAN
    near = len(sides)
    pairs = (2 * EDGE + span) // 2
    size = 32 if members % 32 == 0 else members
    return pl.pallas_call(
        functools.partial(outer_kernel, variables, near, size),
        out_shape=[
            jax.ShapeDtypeStruct((levels, pairs, 2 * lanes, columns), jnp.bfloat16),
            jax.ShapeDtypeStruct((blocks, levels * 2 * STEPS * SPAN, lanes), jnp.bfloat16),
        ],
        in_specs=vmem(2 + near) + smem(2) + hbm(1),
        out_specs=vmem(2),
        scratch_shapes=[
            pltpu.VMEM((levels, STEPS, 2 * lanes, columns), jnp.bfloat16),
            pltpu.SemaphoreType.DMA((span - 2 * STEPS,)),
        ],
        compiler_params=params(16),
        cost_estimate=cost(2 * 10**9, 8 * 2**20),
    )(own, *sides, diff, east, north, centre)


def pick_kernel(variables, together, grid, rim, cells, out, region, codes):
    levels, pairs, twice, columns = grid.shape
    rows = twice // 2
    members = rows // variables
    blocks, slots = cells.shape
    width = 2 * EDGE + SPAN
    part = pairs * width
    entries = levels * part
    share = rim.shape[1]

    orders = jnp.concatenate(
        [permutation(columns, -EDGE), permutation(columns, SPAN - EDGE)], axis=0
    )
    for level in range(levels):
        for pair in range(pairs):
            turned = dot_rows(orders, grid[level, pair]).astype(jnp.bfloat16)
            at = (level * pairs + pair) * width
            for first in range(2):
                for j in range(columns // width):
                    row = first * columns + j * width
                    region[2 * j + first, at : at + width, :] = turned[row : row + width, :]

    cell = cells[...]
    second = cell >= 2 * entries
    cell = jnp.where(second, cell - 2 * entries, cell)
    level = lax.shift_right_logical(cell, (2 * part).bit_length() - 1)
    inside = cell - level * (2 * part)
    lower = inside >= part
    code = level * part + jnp.where(lower, inside - part + entries, inside)
    codes[...] = jnp.where(second, code + 2 * entries, code).astype(jnp.float32)

    left = lax.broadcasted_iota(jnp.int32, (slots // 2, rows), 1) < members
    lane = lax.broadcasted_iota(jnp.int32, (slots, entries), 1).astype(jnp.float32)

    @pl.loop(0, blocks // together)
    def _(step):
        for i in range(together):
            block = step * together + i
            at = column_of(codes[pl.ds(block, 1), :])
            second = at >= 2.0 * entries
            at = jnp.where(second, at - 2.0 * entries, at)
            lower = at >= 1.0 * entries
            at = jnp.where(lower, at - 1.0 * entries, at)
            pick = jnp.where(lane == at, 1.0, 0.0).astype(jnp.bfloat16)
            found = dot(pick, region[block])
            total = jnp.where(lower, found[:, rows:], found[:, :rows])
            other = pltpu.roll(total, members, 1)
            to_left = jnp.where(second, other, total)[: slots // 2]
            to_right = jnp.where(second, total, other)[slots // 2 :]
            out[block, share:, :] = jnp.where(left, to_left, to_right).astype(jnp.bfloat16)
            out[block, :share, :] = rim[block]


def pick(variables, grid, rim, cells):
    levels, pairs, twice, columns = grid.shape
    blocks, slots = cells.shape
    _, share, lanes = rim.shape
    together = next(n for n in (4, 2, 1) if blocks % n == 0)
    return pl.pallas_call(
        functools.partial(pick_kernel, variables, together),
        out_shape=jax.ShapeDtypeStruct((blocks, share + slots // 2, lanes), jnp.bfloat16),
        in_specs=vmem(3),
        out_specs=pl.BlockSpec(memory_space=pltpu.VMEM),
        scratch_shapes=[
            pltpu.VMEM((blocks, levels * pairs * (2 * EDGE + SPAN), twice), jnp.bfloat16),
            pltpu.VMEM((blocks, slots), jnp.float32),
        ],
        compiler_params=params(20),
        cost_estimate=cost(4 * 10**9, 4 * 2**20),
    )(grid, rim, cells)


def join(a, b, left, members):
    return (
        jnp.where(left, a, pltpu.roll(b, members, 1)),
        jnp.where(left, pltpu.roll(a, members, 1), b),
    )


def left_lanes(shape):
    return lax.broadcasted_iota(jnp.int32, shape, 1) < shape[1] // 2


def deviations(states, raw, dev, at, size):
    groups, _, lanes = states.shape
    members = lanes // 2
    left = left_lanes((size, lanes))
    sums = [jnp.zeros((size, lanes), jnp.float32)] * 2
    for j in range(groups // 2):
        here = slice(j * lanes, (j + 1) * lanes)
        pair = join(
            states[2 * j, :size, :].astype(jnp.float32),
            states[2 * j + 1, :size, :].astype(jnp.float32),
            left,
            members,
        )
        for var in range(2):
            raw[var * size : (var + 1) * size, here] = pair[var]
        sums = [total + one for total, one in zip(sums, pair)]
    centre = jnp.concatenate([jnp.sum(x, axis=1, keepdims=True) for x in sums], axis=0)
    centre = centre * (1.0 / (groups * members))
    dev[at : at + 2 * size, :] = (raw[...] - centre).astype(jnp.bfloat16)
    return centre


def prepare_kernel(states, dev, centre, raw):
    mean = deviations(states, raw, dev, 0, states.shape[1])
    centre[...] = jnp.broadcast_to(mean, centre.shape)


def prepare(states):
    groups, near, lanes = states.shape
    total = groups * lanes // 2
    return pl.pallas_call(
        prepare_kernel,
        out_shape=[
            jax.ShapeDtypeStruct((2 * near, total), jnp.bfloat16),
            jax.ShapeDtypeStruct((2 * near, lanes), jnp.float32),
        ],
        in_specs=vmem(1),
        out_specs=vmem(2),
        scratch_shapes=[pltpu.VMEM((2 * near, total), jnp.float32)],
        compiler_params=params(6),
        cost_estimate=cost(10**8, 2 * 2**20),
    )(states)


def analyse_kernel(first, means, second, count, value, weight, out, raw, dev, obs, scaled_ref):
    groups, _, lanes = second.shape
    near = first.shape[0] // 2
    half = obs.shape[0] // 2
    far = second.shape[1] - half
    side = near + far
    slots = 2 * half
    members = lanes // 2
    total_members = groups * members
    left = left_lanes((half, lanes))

    for j in range(groups // 2):
        here = slice(j * lanes, (j + 1) * lanes)
        obs[:half, here], obs[half:, here] = join(
            second[2 * j, far:, :].astype(jnp.float32),
            second[2 * j + 1, far:, :].astype(jnp.float32),
            left,
            members,
        )

    used = lax.broadcasted_iota(jnp.int32, (1, slots), 1) < count[0, 0]
    root = column_of(jnp.where(used, jnp.sqrt(weight[...]), 0.0))
    observed = obs[...]
    mean = jnp.sum(observed, axis=1, keepdims=True) * (1.0 / total_members)
    scaled = (observed - mean) * root
    energy = jnp.sum(jnp.sum(scaled * scaled, axis=1, keepdims=True), axis=0, keepdims=True)
    scaled_ref[...] = scaled.astype(jnp.bfloat16)
    misfit = row_of(root * (column_of(value[...]) - mean))

    c = total_members - 1.0
    s = energy * (1.0 / total_members) + c
    inverse = 1.0 / s
    a = c * inverse
    p = 1.5 - 0.5 * a
    p2 = p * p
    p3 = p2 * p
    base = 1.5 * p - 0.5 * a * p3
    q0 = -0.75 - 0.5 * (p3 - 1.5 * a * p2)
    q1 = -0.5 * (0.75 * a * p - 1.5 * p2)
    q2 = -0.5 * (0.75 * p - 0.125 * a)
    small = dot_rows(scaled_ref[...], scaled_ref[...]) * inverse
    diagonal = eye(slots)
    square = dot3(small, small)
    tail = dot3(square, jnp.where(diagonal, q2, 0.0) + 0.0625 * small)
    poly = jnp.where(diagonal, q0, 0.0) + q1 * small + tail

    def apply(vector):
        inner_part = jnp.sum(poly * vector, axis=1, keepdims=True)
        return jnp.sum(small * inner_part, axis=0, keepdims=True) + base * vector

    gain = apply(apply(misfit)) * inverse
    stretch = jnp.sqrt(a)
    alpha, factor = stretch * base, stretch * inverse
    centre = deviations(second, raw, dev, 0, far)
    cross = jnp.concatenate(
        [dot_rows(first[...], scaled_ref[...]), dot_rows(dev[...], scaled_ref[...])], axis=0
    )
    centre = jnp.concatenate([means[:, 0:1], centre], axis=0)
    shift = centre + jnp.sum(cross * gain, axis=1, keepdims=True)
    mix = (dot3(cross, poly) * factor).astype(jnp.bfloat16)
    parts = ((first, 0, near, 0), (dev, 2 * near, far, near))
    for j in range(groups // 2):
        here = slice(j * lanes, (j + 1) * lanes)
        new = dot(mix, scaled_ref[:, here]) + shift
        for ref, at, size, row in parts:
            one = new[at : at + 2 * size] + alpha * ref[:, here].astype(jnp.float32)
            x, y = join(one[:size], one[size:], left_lanes((size, lanes)), members)
            out[2 * j, row : row + size, :] = x.astype(jnp.bfloat16)
            out[2 * j + 1, row : row + size, :] = y.astype(jnp.bfloat16)


def analyse(first, means, second, count, value, weight):
    groups, _, lanes = second.shape
    near = first.shape[0] // 2
    slots = value.shape[1]
    far = second.shape[1] - slots // 2
    total = groups * lanes // 2
    return pl.pallas_call(
        analyse_kernel,
        out_shape=jax.ShapeDtypeStruct((groups, near + far, lanes), jnp.bfloat16),
        in_specs=vmem(3) + smem(1) + vmem(2),
        out_specs=pl.BlockSpec(memory_space=pltpu.VMEM),
        scratch_shapes=[
            pltpu.VMEM((2 * far, total), jnp.float32),
            pltpu.VMEM((2 * far, total), jnp.bfloat16),
            pltpu.VMEM((slots, total), jnp.float32),
            pltpu.VMEM((slots, total), jnp.bfloat16),
        ],
        compiler_params=params(16),
        cost_estimate=cost(4 * 10**9, 4 * 2**20),
    )(first, means, second, count, value, weight)


def restore_kernel(blocks, out, turned):
    members, variables, levels, span, columns = out.shape
    lanes = members * variables
    identity = permutation(lanes, 0)
    near = span - 2 * STEPS
    for level in range(levels):
        for r in range(0, span, 2):
            if STEPS <= r < span - STEPS:
                at = level * near + r - STEPS
            else:
                at = levels * near + level * 2 * STEPS + (r if r < STEPS else r - near)
            both = blocks[:, at * SPAN : (at + 2) * SPAN, :].astype(jnp.float32)
            for i in range(2):
                one = both[:, i * SPAN : (i + 1) * SPAN, :].reshape(columns, lanes)
                rows = dot_rows(identity, one.astype(jnp.bfloat16))
                turned[level % 2, pl.ds(r + i, lanes, stride=span), :] = rows
        for var in range(variables):
            half = turned[level % 2, var * members * span : (var + 1) * members * span, :]
            out[:, var, level] = half.reshape(members, span, columns).astype(jnp.bfloat16)


def restore(dims, blocks):
    members, variables, levels, span, columns = dims
    return pl.pallas_call(
        restore_kernel,
        out_shape=jax.ShapeDtypeStruct((members, variables, levels, span, columns), jnp.bfloat16),
        in_specs=vmem(1),
        out_specs=pl.BlockSpec(memory_space=pltpu.VMEM),
        scratch_shapes=[pltpu.VMEM((2, variables * members * span, columns), jnp.float32)],
        compiler_params=params(8),
        cost_estimate=cost(2 * 10**9, 2 * 2**20),
    )(blocks)


def neighbours(field, axis):
    count = lax.axis_size(axis)
    low = lax.ppermute(field, axis, [(i, (i + 1) % count) for i in range(count)])
    if count == 2:
        return (low,)
    return low, lax.ppermute(field, axis, [((i + 1) % count, i) for i in range(count)])


def exchange(blocks):
    return lax.all_to_all(blocks, "grp", split_axis=0, concat_axis=0, tiled=True)


def on_device(start, diffusivity, eastward, northward, cells, count, value, weight):
    members, variables, levels, span, columns = dims = start.shape
    own = start.reshape(members * variables, levels, span, columns)
    sides = neighbours(own, "tile")
    model = (diffusivity, eastward, northward)
    centre, near = inner(dims, own, *model)
    first, means = prepare(exchange(near))
    grid, rim = outer(dims, own, sides, *model, centre)
    second = exchange(pick(variables, grid, rim, cells[0]))
    updated = analyse(first, means, second, count, value[0], weight[0])
    return restore(dims, exchange(updated))


def solution(mesh):
    return jax.shard_map(
        on_device,
        mesh=mesh,
        in_specs=(
            P("grp", None, None, "tile", None),
            P(),
            P(),
            P(),
            P("tile", None, None),
            P("tile", "grp"),
            P("tile", "grp", None),
            P("tile", "grp", None),
        ),
        out_specs=P("grp", None, None, "tile", None),
        check_vma=False,
    )
```

```python
import functools

import jax
import jax.numpy as jnp
from jax import lax
from jax.experimental import pallas as pl
from jax.experimental.pallas import tpu as pltpu
from jax.sharding import PartitionSpec as P

SPAN = 8
STEPS = 2
EDGE = SPAN // 2

ROWS = (((1,), (1,)), ((), ()))


def params(mebibytes, **kw):
    return pltpu.CompilerParams(vmem_limit_bytes=mebibytes * 2**20, **kw)


def cost(flops, size):
    return pl.CostEstimate(flops=flops, bytes_accessed=size, transcendentals=0)


def vmem(count):
    return [pl.BlockSpec(memory_space=pltpu.VMEM)] * count


def hbm(count):
    return [pl.BlockSpec(memory_space=pltpu.HBM)] * count


def smem(count):
    return [pl.BlockSpec(memory_space=pltpu.SMEM)] * count


def dot(a, b, **kw):
    return jnp.dot(a, b, preferred_element_type=jnp.float32, **kw)


def split(x):
    high = x.astype(jnp.bfloat16)
    return high, (x - high.astype(jnp.float32)).astype(jnp.bfloat16)


def dot3(a, b):
    (a_high, a_low), (b_high, b_low) = split(a), split(b)
    return dot(a_high, b_high) + (dot(a_high, b_low) + dot(a_low, b_high))


def dot_rows(a, b):
    return lax.dot_general(a, b, ROWS, preferred_element_type=jnp.float32)


def permutation(size, shift):
    row = lax.broadcasted_iota(jnp.int32, (size, size), 0)
    column = lax.broadcasted_iota(jnp.int32, (size, size), 1)
    return (lax.rem(row + shift + size, size) == column).astype(jnp.bfloat16)


def eye(size):
    row = lax.broadcasted_iota(jnp.int32, (size, size), 0)
    column = lax.broadcasted_iota(jnp.int32, (size, size), 1)
    return row == column


def column_of(row):
    return jnp.sum(jnp.where(eye(row.shape[1]), row, 0.0), axis=1, keepdims=True)


def row_of(column):
    return jnp.sum(jnp.where(eye(column.shape[0]), column, 0.0), axis=0, keepdims=True)


def model_step(tiles, coefficients):
    middle, east, west, north, south = coefficients
    _, span, columns = tiles[0].shape
    row = lax.broadcasted_iota(jnp.int32, (1, span, columns), 1)
    new = []
    for i, here in enumerate(tiles):
        after, before = here, here
        if len(tiles) > 1:
            after = jnp.where(row == 0, tiles[(i + 1) % len(tiles)], here)
            before = jnp.where(row == span - 1, tiles[i - 1], here)
        new.append(
            middle * here
            + east * pltpu.roll(after, span - 1, 1)
            + west * pltpu.roll(before, 1, 1)
            + north * pltpu.roll(here, columns - 1, 2)
            + south * pltpu.roll(here, 1, 2)
        )
    return new


def forecast(tiles, coefficients):
    for _ in range(STEPS):
        tiles = model_step(tiles, coefficients)
    return tiles


def separate(row_of_place, count, variables, size, span):
    shape = (count * variables * size, size * variables * span)
    to = lax.broadcasted_iota(jnp.int32, (shape[0], 1), 0)
    place = to // (variables * size)
    rest = to - place * (variables * size)
    var = rest // size
    member = rest - var * size
    source = (member * variables + var) * span + row_of_place(place)
    return (lax.broadcasted_iota(jnp.int32, shape, 1) == source).astype(jnp.bfloat16)


def coefficients_of(level, diff, east, north):
    spread = jnp.broadcast_to(diff[pl.ds(level, 1), :], (8, diff.shape[1]))
    u = 0.5 * east[level]
    w = 0.5 * north[level]
    return 1.0 - 4.0 * spread, spread - u, spread + u, spread - w, spread + w


GROUP = 16
PIECE = 8


def tile_loop(group, level, refs, wide, coefficients):
    rows, _, span, columns = refs[0].shape
    size = wide.shape[1] // span
    for at in range(0, size, PIECE):
        first = group * size + at
        tiles = forecast([ref[pl.ds(first, PIECE), level] for ref in refs], coefficients)
        for i, tile in enumerate(tiles):
            flat = tile.reshape(PIECE * span, columns).astype(jnp.bfloat16)
            wide[i, at * span : (at + PIECE) * span, :] = flat


def pack_rows(pair, identity, store, at):
    lanes = pair.shape[0] // 2
    turned = dot_rows(identity, pair)
    parts = [turned[:, i * lanes : (i + 1) * lanes].reshape(-1, SPAN, lanes) for i in range(2)]
    store[:, at : at + 2 * SPAN, :] = jnp.concatenate(parts, axis=1).astype(jnp.bfloat16)


def inner_kernel(variables, own, diff, east, north, fields, packed, slab, wide, sems):
    rows, levels, span, columns = own.shape
    members = rows // variables
    size = GROUP * variables
    copies = []
    for i in range(members // GROUP):
        here = pl.ds(i * size, size)
        copies.append(pltpu.make_async_copy(own.at[here], slab.at[here], sems.at[i]))
        copies[-1].start()
    count = span - 2 * STEPS
    order = separate(lambda place: place + STEPS, count, variables, GROUP, span)
    for group, copy in enumerate(copies):
        copy.wait()

        @pl.loop(0, levels)
        def _(level):
            slot = lax.rem(level, 2)
            coefficients = coefficients_of(level, diff, east, north)
            tile_loop(group, level, [slab], wide.at[pl.ds(slot, 1)], coefficients)
            rows_apart = dot(order, wide[slot]).astype(jnp.bfloat16)
            for r in range(count):
                for var in range(variables):
                    to = var * members + group * GROUP
                    piece = rows_apart[(r * variables + var) * GROUP :][:GROUP]
                    fields[level, r, to : to + GROUP, :] = piece

    identity = permutation(columns, 0)
    for level in range(levels):
        for r in range(0, count, 2):
            pair = fields[level, r : r + 2].reshape(2 * rows, columns)
            pack_rows(pair, identity, packed, (level * count + r) * SPAN)


def inner(dims, own, diff, east, north):
    members, variables, levels, span, columns = dims
    lanes = members * variables
    blocks = columns // SPAN
    count = span - 2 * STEPS
    return pl.pallas_call(
        functools.partial(inner_kernel, variables),
        out_shape=[
            jax.ShapeDtypeStruct((levels, count, lanes, columns), jnp.bfloat16),
            jax.ShapeDtypeStruct((blocks, levels * count * SPAN, lanes), jnp.bfloat16),
        ],
        in_specs=hbm(1) + vmem(1) + smem(2),
        out_specs=vmem(2),
        scratch_shapes=[
            pltpu.VMEM((lanes, levels, span, columns), jnp.float32),
            pltpu.VMEM((2, GROUP * variables * span, columns), jnp.bfloat16),
            pltpu.SemaphoreType.DMA((members // GROUP,)),
        ],
        compiler_params=params(56),
        cost_estimate=cost(2 * 10**9, 4 * 2**20),
    )(own, diff, east, north)


def outer_kernel(variables, near, own, *rest):
    sides, rest = rest[:near], rest[near:]
    diff, east, north, centre, grid, packed, fields, wide, sems = rest
    rows, levels, span, columns = own.shape
    members = rows // variables
    pairs = (2 * EDGE + span) // 2

    copies = []
    for r in range(STEPS, span - STEPS):
        half, pair = divmod(r + EDGE, pairs)
        place = grid.at[:, pair, pl.ds(half * rows, rows)]
        copies.append(pltpu.make_async_copy(centre.at[:, r - STEPS], place, sems.at[r - STEPS]))
        copies[-1].start()

    tiles = (own, *sides[::-1])
    skip = span - 2 * STEPS
    wanted = (
        (0, separate(lambda place: jnp.where(place < STEPS, place, place + skip), 2 * STEPS, variables, GROUP, span),
         [*range(STEPS), *range(span - STEPS, span)]),
        (1, separate(lambda place: place, EDGE, variables, GROUP, span), range(span, span + EDGE)),
        (near, separate(lambda place: place + span - EDGE, EDGE, variables, GROUP, span), range(-EDGE, 0)),
    )
    groups = members // GROUP

    @pl.loop(0, levels * groups)
    def _(step):
        level = step // groups
        group = step - level * groups
        slot = lax.rem(step, 2)
        coefficients = coefficients_of(level, diff, east, north)
        tile_loop(group, level, tiles, wide.at[slot], coefficients)
        for tile, order, places in wanted:
            rows_apart = dot(order, wide[slot, tile]).astype(jnp.bfloat16)
            for i, r in enumerate(places):
                half, pair = divmod(r + EDGE, pairs)
                for var in range(variables):
                    piece = rows_apart[(i * variables + var) * GROUP :][:GROUP]
                    to = pl.multiple_of(var * members + group * GROUP, GROUP)
                    grid[level, pair, pl.ds(half * rows + to, GROUP), :] = piece
                    if tile == 0:
                        fields[level, i // 2, pl.ds((i % 2) * rows + to, GROUP), :] = piece

    identity = permutation(columns, 0)
    for level in range(levels):
        for pair in range(STEPS):
            at = (level * STEPS + pair) * 2 * SPAN
            pack_rows(fields[level, pair], identity, packed, at)
    for copy in copies:
        copy.wait()


def outer(dims, own, sides, diff, east, north, centre):
    members, variables, levels, span, columns = dims
    lanes = members * variables
    blocks = columns // SPAN
    near = len(sides)
    pairs = (2 * EDGE + span) // 2
    return pl.pallas_call(
        functools.partial(outer_kernel, variables, near),
        out_shape=[
            jax.ShapeDtypeStruct((levels, pairs, 2 * lanes, columns), jnp.bfloat16),
            jax.ShapeDtypeStruct((blocks, levels * 2 * STEPS * SPAN, lanes), jnp.bfloat16),
        ],
        in_specs=vmem(2 + near) + smem(2) + hbm(1),
        out_specs=vmem(2),
        scratch_shapes=[
            pltpu.VMEM((levels, STEPS, 2 * lanes, columns), jnp.bfloat16),
            pltpu.VMEM((2, 1 + near, GROUP * variables * span, columns), jnp.bfloat16),
            pltpu.SemaphoreType.DMA((span - 2 * STEPS,)),
        ],
        compiler_params=params(16),
        cost_estimate=cost(2 * 10**9, 8 * 2**20),
    )(own, *sides, diff, east, north, centre)


def pick_kernel(variables, together, grid, rim, cells, out, region, codes):
    levels, pairs, twice, columns = grid.shape
    rows = twice // 2
    members = rows // variables
    blocks, slots = cells.shape
    width = 2 * EDGE + SPAN
    part = pairs * width
    entries = levels * part
    share = rim.shape[1]

    orders = jnp.concatenate(
        [permutation(columns, -EDGE), permutation(columns, SPAN - EDGE)], axis=0
    )
    for level in range(levels):
        for pair in range(pairs):
            turned = dot_rows(orders, grid[level, pair]).astype(jnp.bfloat16)
            at = (level * pairs + pair) * width
            for first in range(2):
                for j in range(columns // width):
                    row = first * columns + j * width
                    region[2 * j + first, at : at + width, :] = turned[row : row + width, :]

    cell = cells[...]
    second = cell >= 2 * entries
    cell = jnp.where(second, cell - 2 * entries, cell)
    level = lax.shift_right_logical(cell, (2 * part).bit_length() - 1)
    inside = cell - level * (2 * part)
    lower = inside >= part
    code = level * part + jnp.where(lower, inside - part + entries, inside)
    codes[...] = jnp.where(second, code + 2 * entries, code).astype(jnp.float32)

    left = lax.broadcasted_iota(jnp.int32, (slots // 2, rows), 1) < members
    lane = lax.broadcasted_iota(jnp.int32, (slots, entries), 1).astype(jnp.float32)

    @pl.loop(0, blocks // together)
    def _(step):
        for i in range(together):
            block = step * together + i
            at = column_of(codes[pl.ds(block, 1), :])
            second = at >= 2.0 * entries
            at = jnp.where(second, at - 2.0 * entries, at)
            lower = at >= 1.0 * entries
            at = jnp.where(lower, at - 1.0 * entries, at)
            pick = jnp.where(lane == at, 1.0, 0.0).astype(jnp.bfloat16)
            found = dot(pick, region[block])
            total = jnp.where(lower, found[:, rows:], found[:, :rows])
            other = pltpu.roll(total, members, 1)
            to_left = jnp.where(second, other, total)[: slots // 2]
            to_right = jnp.where(second, total, other)[slots // 2 :]
            out[block, share:, :] = jnp.where(left, to_left, to_right).astype(jnp.bfloat16)
            out[block, :share, :] = rim[block]


def pick(variables, grid, rim, cells):
    levels, pairs, twice, columns = grid.shape
    blocks, slots = cells.shape
    _, share, lanes = rim.shape
    together = next(n for n in (4, 2, 1) if blocks % n == 0)
    return pl.pallas_call(
        functools.partial(pick_kernel, variables, together),
        out_shape=jax.ShapeDtypeStruct((blocks, share + slots // 2, lanes), jnp.bfloat16),
        in_specs=vmem(3),
        out_specs=pl.BlockSpec(memory_space=pltpu.VMEM),
        scratch_shapes=[
            pltpu.VMEM((blocks, levels * pairs * (2 * EDGE + SPAN), twice), jnp.bfloat16),
            pltpu.VMEM((blocks, slots), jnp.float32),
        ],
        compiler_params=params(20),
        cost_estimate=cost(4 * 10**9, 4 * 2**20),
    )(grid, rim, cells)


def join(a, b, left, members):
    return (
        jnp.where(left, a, pltpu.roll(b, members, 1)),
        jnp.where(left, pltpu.roll(a, members, 1), b),
    )


def left_lanes(shape):
    return lax.broadcasted_iota(jnp.int32, shape, 1) < shape[1] // 2


def deviations(states, raw, dev, at, size):
    groups, _, lanes = states.shape
    members = lanes // 2
    left = left_lanes((size, lanes))
    sums = [jnp.zeros((size, lanes), jnp.float32)] * 2
    for j in range(groups // 2):
        here = slice(j * lanes, (j + 1) * lanes)
        pair = join(
            states[2 * j, :size, :].astype(jnp.float32),
            states[2 * j + 1, :size, :].astype(jnp.float32),
            left,
            members,
        )
        for var in range(2):
            raw[var * size : (var + 1) * size, here] = pair[var]
        sums = [total + one for total, one in zip(sums, pair)]
    centre = jnp.concatenate([jnp.sum(x, axis=1, keepdims=True) for x in sums], axis=0)
    centre = centre * (1.0 / (groups * members))
    dev[at : at + 2 * size, :] = (raw[...] - centre).astype(jnp.bfloat16)
    return centre


def prepare_kernel(states, dev, centre, raw):
    mean = deviations(states, raw, dev, 0, states.shape[1])
    centre[...] = jnp.broadcast_to(mean, centre.shape)


def prepare(states):
    groups, near, lanes = states.shape
    total = groups * lanes // 2
    return pl.pallas_call(
        prepare_kernel,
        out_shape=[
            jax.ShapeDtypeStruct((2 * near, total), jnp.bfloat16),
            jax.ShapeDtypeStruct((2 * near, lanes), jnp.float32),
        ],
        in_specs=vmem(1),
        out_specs=vmem(2),
        scratch_shapes=[pltpu.VMEM((2 * near, total), jnp.float32)],
        compiler_params=params(6),
        cost_estimate=cost(10**8, 2 * 2**20),
    )(states)


def analyse_kernel(first, means, second, count, value, weight, out, raw, dev, obs, scaled_ref):
    groups, _, lanes = second.shape
    near = first.shape[0] // 2
    half = obs.shape[0] // 2
    far = second.shape[1] - half
    side = near + far
    slots = 2 * half
    members = lanes // 2
    total_members = groups * members
    left = left_lanes((half, lanes))

    for j in range(groups // 2):
        here = slice(j * lanes, (j + 1) * lanes)
        obs[:half, here], obs[half:, here] = join(
            second[2 * j, far:, :].astype(jnp.float32),
            second[2 * j + 1, far:, :].astype(jnp.float32),
            left,
            members,
        )

    used = lax.broadcasted_iota(jnp.int32, (1, slots), 1) < count[0, 0]
    root = column_of(jnp.where(used, jnp.sqrt(weight[...]), 0.0))
    observed = obs[...]
    mean = jnp.sum(observed, axis=1, keepdims=True) * (1.0 / total_members)
    scaled = (observed - mean) * root
    energy = jnp.sum(jnp.sum(scaled * scaled, axis=1, keepdims=True), axis=0, keepdims=True)
    scaled_ref[...] = scaled.astype(jnp.bfloat16)
    misfit = row_of(root * (column_of(value[...]) - mean))

    c = total_members - 1.0
    s = energy * (1.0 / total_members) + c
    inverse = 1.0 / s
    a = c * inverse
    p = 1.5 - 0.5 * a
    p2 = p * p
    p3 = p2 * p
    base = 1.5 * p - 0.5 * a * p3
    q0 = -0.75 - 0.5 * (p3 - 1.5 * a * p2)
    q1 = -0.5 * (0.75 * a * p - 1.5 * p2)
    q2 = -0.5 * (0.75 * p - 0.125 * a)
    small = dot_rows(scaled_ref[...], scaled_ref[...]) * inverse
    diagonal = eye(slots)
    square = dot3(small, small)
    tail = dot3(square, jnp.where(diagonal, q2, 0.0) + 0.0625 * small)
    poly = jnp.where(diagonal, q0, 0.0) + q1 * small + tail

    def apply(vector):
        inner_part = jnp.sum(poly * vector, axis=1, keepdims=True)
        return jnp.sum(small * inner_part, axis=0, keepdims=True) + base * vector

    gain = apply(apply(misfit)) * inverse
    stretch = jnp.sqrt(a)
    alpha, factor = stretch * base, stretch * inverse
    centre = deviations(second, raw, dev, 0, far)
    cross = jnp.concatenate(
        [dot_rows(first[...], scaled_ref[...]), dot_rows(dev[...], scaled_ref[...])], axis=0
    )
    centre = jnp.concatenate([means[:, 0:1], centre], axis=0)
    shift = centre + jnp.sum(cross * gain, axis=1, keepdims=True)
    mix = (dot3(cross, poly) * factor).astype(jnp.bfloat16)
    parts = ((first, 0, near, 0), (dev, 2 * near, far, near))
    for j in range(groups // 2):
        here = slice(j * lanes, (j + 1) * lanes)
        new = dot(mix, scaled_ref[:, here]) + shift
        for ref, at, size, row in parts:
            one = new[at : at + 2 * size] + alpha * ref[:, here].astype(jnp.float32)
            x, y = join(one[:size], one[size:], left_lanes((size, lanes)), members)
            out[2 * j, row : row + size, :] = x.astype(jnp.bfloat16)
            out[2 * j + 1, row : row + size, :] = y.astype(jnp.bfloat16)


def analyse(first, means, second, count, value, weight):
    groups, _, lanes = second.shape
    near = first.shape[0] // 2
    slots = value.shape[1]
    far = second.shape[1] - slots // 2
    total = groups * lanes // 2
    return pl.pallas_call(
        analyse_kernel,
        out_shape=jax.ShapeDtypeStruct((groups, near + far, lanes), jnp.bfloat16),
        in_specs=vmem(3) + smem(1) + vmem(2),
        out_specs=pl.BlockSpec(memory_space=pltpu.VMEM),
        scratch_shapes=[
            pltpu.VMEM((2 * far, total), jnp.float32),
            pltpu.VMEM((2 * far, total), jnp.bfloat16),
            pltpu.VMEM((slots, total), jnp.float32),
            pltpu.VMEM((slots, total), jnp.bfloat16),
        ],
        compiler_params=params(16),
        cost_estimate=cost(4 * 10**9, 4 * 2**20),
    )(first, means, second, count, value, weight)


def restore_kernel(blocks, out, turned):
    members, variables, levels, span, columns = out.shape
    lanes = members * variables
    identity = permutation(lanes, 0)
    near = span - 2 * STEPS
    for level in range(levels):
        for r in range(0, span, 2):
            if STEPS <= r < span - STEPS:
                at = level * near + r - STEPS
            else:
                at = levels * near + level * 2 * STEPS + (r if r < STEPS else r - near)
            both = blocks[:, at * SPAN : (at + 2) * SPAN, :].astype(jnp.float32)
            for i in range(2):
                one = both[:, i * SPAN : (i + 1) * SPAN, :].reshape(columns, lanes)
                rows = dot_rows(identity, one.astype(jnp.bfloat16))
                turned[level % 2, pl.ds(r + i, lanes, stride=span), :] = rows
        for var in range(variables):
            half = turned[level % 2, var * members * span : (var + 1) * members * span, :]
            out[:, var, level] = half.reshape(members, span, columns).astype(jnp.bfloat16)


def restore(dims, blocks):
    members, variables, levels, span, columns = dims
    return pl.pallas_call(
        restore_kernel,
        out_shape=jax.ShapeDtypeStruct((members, variables, levels, span, columns), jnp.bfloat16),
        in_specs=vmem(1),
        out_specs=pl.BlockSpec(memory_space=pltpu.VMEM),
        scratch_shapes=[pltpu.VMEM((2, variables * members * span, columns), jnp.float32)],
        compiler_params=params(8),
        cost_estimate=cost(2 * 10**9, 2 * 2**20),
    )(blocks)


def neighbours(field, axis):
    count = lax.axis_size(axis)
    low = lax.ppermute(field, axis, [(i, (i + 1) % count) for i in range(count)])
    if count == 2:
        return (low,)
    return low, lax.ppermute(field, axis, [((i + 1) % count, i) for i in range(count)])


def exchange(blocks):
    return lax.all_to_all(blocks, "grp", split_axis=0, concat_axis=0, tiled=True)


def on_device(start, diffusivity, eastward, northward, cells, count, value, weight):
    members, variables, levels, span, columns = dims = start.shape
    own = start.reshape(members * variables, levels, span, columns)
    sides = neighbours(own, "tile")
    model = (diffusivity, eastward, northward)
    centre, near = inner(dims, own, *model)
    first, means = prepare(exchange(near))
    grid, rim = outer(dims, own, sides, *model, centre)
    second = exchange(pick(variables, grid, rim, cells[0]))
    updated = analyse(first, means, second, count, value[0], weight[0])
    return restore(dims, exchange(updated))


def solution(mesh):
    return jax.shard_map(
        on_device,
        mesh=mesh,
        in_specs=(
            P("grp", None, None, "tile", None),
            P(),
            P(),
            P(),
            P("tile", None, None),
            P("tile", "grp"),
            P("tile", "grp", None),
            P("tile", "grp", None),
        ),
        out_specs=P("grp", None, None, "tile", None),
        check_vma=False,
    )
```

```python
import functools

import jax
import jax.numpy as jnp
from jax import lax
from jax.experimental import pallas as pl
from jax.experimental.pallas import tpu as pltpu
from jax.sharding import PartitionSpec as P

SPAN = 8
STEPS = 2
EDGE = SPAN // 2

ROWS = (((1,), (1,)), ((), ()))


def params(mebibytes, **kw):
    return pltpu.CompilerParams(vmem_limit_bytes=mebibytes * 2**20, **kw)


def cost(flops, size):
    return pl.CostEstimate(flops=flops, bytes_accessed=size, transcendentals=0)


def vmem(count):
    return [pl.BlockSpec(memory_space=pltpu.VMEM)] * count


def hbm(count):
    return [pl.BlockSpec(memory_space=pltpu.HBM)] * count


def smem(count):
    return [pl.BlockSpec(memory_space=pltpu.SMEM)] * count


def dot(a, b, **kw):
    return jnp.dot(a, b, preferred_element_type=jnp.float32, **kw)


def split(x):
    high = x.astype(jnp.bfloat16)
    return high, (x - high.astype(jnp.float32)).astype(jnp.bfloat16)


def dot3(a, b):
    (a_high, a_low), (b_high, b_low) = split(a), split(b)
    return dot(a_high, b_high) + (dot(a_high, b_low) + dot(a_low, b_high))


def dot_rows(a, b):
    return lax.dot_general(a, b, ROWS, preferred_element_type=jnp.float32)


def permutation(size, shift):
    row = lax.broadcasted_iota(jnp.int32, (size, size), 0)
    column = lax.broadcasted_iota(jnp.int32, (size, size), 1)
    return (lax.rem(row + shift + size, size) == column).astype(jnp.bfloat16)


def eye(size):
    row = lax.broadcasted_iota(jnp.int32, (size, size), 0)
    column = lax.broadcasted_iota(jnp.int32, (size, size), 1)
    return row == column


def column_of(row):
    return jnp.sum(jnp.where(eye(row.shape[1]), row, 0.0), axis=1, keepdims=True)


def row_of(column):
    return jnp.sum(jnp.where(eye(column.shape[0]), column, 0.0), axis=0, keepdims=True)


def forecast_rows(read, first, last, coefficients, write):
    middle, east, west, north, south = coefficients

    def step(below, here, above):
        columns = here.shape[2]
        return (
            middle * here
            + east * above
            + west * below
            + north * pltpu.roll(here, columns - 1, 2)
            + south * pltpu.roll(here, 1, 2)
        )

    start = [read(first - 2), read(first - 1), read(first)]
    once = [None, None, None]
    for r in range(first - 1, last + 1):
        once = [once[1], once[2], step(*start)]
        if r >= first + 1:
            write(r - 1, step(*once))
        if r < last:
            start = [start[1], start[2], read(r + 2)]


def model_rows(diffusivity, eastward, northward):
    levels, columns = diffusivity.shape
    place = lax.broadcasted_iota(jnp.int32, (levels, 3, columns), 1)
    speeds = jnp.where(place == 1, eastward[:, None, None], northward[:, None, None])
    return jnp.where(place == 0, diffusivity[:, None, :], speeds)


def coefficients_of(model, level):
    spread, u, w = (
        jnp.broadcast_to(model[level, i : i + 1, :], (8, model.shape[2])) for i in range(3)
    )
    u, w = 0.5 * u, 0.5 * w
    return 1.0 - 4.0 * spread, spread - u, spread + u, spread - w, spread + w


CHUNK = 32


def row_reader(level, var, first, size, own, low, high):
    span, columns = own.shape[2], own.shape[4]

    def read(r):
        ref, at = (low, r + span) if r < 0 else (own, r) if r < span else (high, r - span)
        return ref[var, level, at, first : first + size, :].reshape(-1, 8, columns)

    return read


def pack_rows(pair, identity, store, at):
    lanes = pair.shape[0] // 2
    turned = dot_rows(identity, pair)
    parts = [turned[:, i * lanes : (i + 1) * lanes].reshape(-1, SPAN, lanes) for i in range(2)]
    store[:, at : at + 2 * SPAN, :] = jnp.concatenate(parts, axis=1).astype(jnp.bfloat16)


def inner_kernel(own, model, fields, packed):
    variables, levels, span, members, columns = own.shape
    rows = variables * members
    count = span - 2 * STEPS

    @pl.loop(0, levels)
    def _(level):
        coefficients = coefficients_of(model, level)
        for var in range(variables):
            for first in range(0, members, CHUNK):

                def write(r, value):
                    at = var * members + first
                    value = value.reshape(CHUNK, columns).astype(jnp.bfloat16)
                    fields[level, r - STEPS, at : at + CHUNK, :] = value

                read = row_reader(level, var, first, CHUNK, own, None, None)
                forecast_rows(read, STEPS, span - STEPS, coefficients, write)

    identity = permutation(columns, 0)
    for level in range(levels):
        for r in range(0, count, 2):
            pair = fields[level, r : r + 2].reshape(2 * rows, columns)
            pack_rows(pair, identity, packed, (level * count + r) * SPAN)


def inner(dims, own, model):
    members, variables, levels, span, columns = dims
    lanes = members * variables
    blocks = columns // SPAN
    count = span - 2 * STEPS
    return pl.pallas_call(
        inner_kernel,
        out_shape=[
            jax.ShapeDtypeStruct((levels, count, lanes, columns), jnp.bfloat16),
            jax.ShapeDtypeStruct((blocks, levels * count * SPAN, lanes), jnp.bfloat16),
        ],
        in_specs=vmem(2),
        out_specs=vmem(2),
        compiler_params=params(8),
        cost_estimate=cost(2 * 10**9, 4 * 2**20),
    )(own, model)


def outer_kernel(near, own, *rest):
    sides, rest = rest[:near], rest[near:]
    model, centre, grid, packed, fields, sems = rest
    variables, levels, span, members, columns = own.shape
    rows = variables * members
    pairs = (2 * EDGE + span) // 2

    copies = []
    for r in range(STEPS, span - STEPS):
        half, pair = divmod(r + EDGE, pairs)
        place = grid.at[:, pair, pl.ds(half * rows, rows)]
        copies.append(pltpu.make_async_copy(centre.at[:, r - STEPS], place, sems.at[r - STEPS]))
        copies[-1].start()

    @pl.loop(0, levels)
    def _(level):
        coefficients = coefficients_of(model, level)
        for var in range(variables):
            for first in range(0, members, CHUNK):

                def write(r, value):
                    value = value.reshape(CHUNK, columns).astype(jnp.bfloat16)
                    half, pair = divmod(r + EDGE, pairs)
                    at = half * rows + var * members + first
                    grid[level, pair, at : at + CHUNK, :] = value
                    if 0 <= r < span:
                        pair, half = divmod(r if r < STEPS else r - span + 2 * STEPS, 2)
                        at = half * rows + var * members + first
                        fields[level, pair, at : at + CHUNK, :] = value

                read = row_reader(level, var, first, CHUNK, own, sides[0], sides[-1])
                forecast_rows(read, -EDGE, STEPS, coefficients, write)
                forecast_rows(read, span - STEPS, span + EDGE, coefficients, write)

    identity = permutation(columns, 0)
    for level in range(levels):
        for pair in range(STEPS):
            at = (level * STEPS + pair) * 2 * SPAN
            pack_rows(fields[level, pair], identity, packed, at)
    for copy in copies:
        copy.wait()


def outer(dims, own, sides, model, centre):
    members, variables, levels, span, columns = dims
    lanes = members * variables
    blocks = columns // SPAN
    near = len(sides)
    pairs = (2 * EDGE + span) // 2
    return pl.pallas_call(
        functools.partial(outer_kernel, near),
        out_shape=[
            jax.ShapeDtypeStruct((levels, pairs, 2 * lanes, columns), jnp.bfloat16),
            jax.ShapeDtypeStruct((blocks, levels * 2 * STEPS * SPAN, lanes), jnp.bfloat16),
        ],
        in_specs=vmem(2 + near) + hbm(1),
        out_specs=vmem(2),
        scratch_shapes=[
            pltpu.VMEM((levels, STEPS, 2 * lanes, columns), jnp.bfloat16),
            pltpu.SemaphoreType.DMA((span - 2 * STEPS,)),
        ],
        compiler_params=params(16),
        cost_estimate=cost(2 * 10**9, 8 * 2**20),
    )(own, *sides, model, centre)


def pick_kernel(variables, together, grid, rim, cells, out, region, codes):
    levels, pairs, twice, columns = grid.shape
    rows = twice // 2
    members = rows // variables
    blocks, slots = cells.shape
    width = 2 * EDGE + SPAN
    part = pairs * width
    entries = levels * part
    share = rim.shape[1]

    orders = jnp.concatenate(
        [permutation(columns, -EDGE), permutation(columns, SPAN - EDGE)], axis=0
    )
    for level in range(levels):
        for pair in range(pairs):
            turned = dot_rows(orders, grid[level, pair]).astype(jnp.bfloat16)
            at = (level * pairs + pair) * width
            for first in range(2):
                for j in range(columns // width):
                    row = first * columns + j * width
                    region[2 * j + first, at : at + width, :] = turned[row : row + width, :]

    cell = cells[...]
    second = cell >= 2 * entries
    cell = jnp.where(second, cell - 2 * entries, cell)
    level = lax.shift_right_logical(cell, (2 * part).bit_length() - 1)
    inside = cell - level * (2 * part)
    lower = inside >= part
    code = level * part + jnp.where(lower, inside - part + entries, inside)
    codes[...] = jnp.where(second, code + 2 * entries, code).astype(jnp.float32)

    left = lax.broadcasted_iota(jnp.int32, (slots // 2, rows), 1) < members
    lane = lax.broadcasted_iota(jnp.int32, (slots, entries), 1).astype(jnp.float32)

    @pl.loop(0, blocks // together)
    def _(step):
        for i in range(together):
            block = step * together + i
            at = column_of(codes[pl.ds(block, 1), :])
            second = at >= 2.0 * entries
            at = jnp.where(second, at - 2.0 * entries, at)
            lower = at >= 1.0 * entries
            at = jnp.where(lower, at - 1.0 * entries, at)
            pick = jnp.where(lane == at, 1.0, 0.0).astype(jnp.bfloat16)
            found = dot(pick, region[block])
            total = jnp.where(lower, found[:, rows:], found[:, :rows])
            other = pltpu.roll(total, members, 1)
            to_left = jnp.where(second, other, total)[: slots // 2]
            to_right = jnp.where(second, total, other)[slots // 2 :]
            out[block, share:, :] = jnp.where(left, to_left, to_right).astype(jnp.bfloat16)
            out[block, :share, :] = rim[block]


def pick(variables, grid, rim, cells):
    levels, pairs, twice, columns = grid.shape
    blocks, slots = cells.shape
    _, share, lanes = rim.shape
    together = next(n for n in (4, 2, 1) if blocks % n == 0)
    return pl.pallas_call(
        functools.partial(pick_kernel, variables, together),
        out_shape=jax.ShapeDtypeStruct((blocks, share + slots // 2, lanes), jnp.bfloat16),
        in_specs=vmem(3),
        out_specs=pl.BlockSpec(memory_space=pltpu.VMEM),
        scratch_shapes=[
            pltpu.VMEM((blocks, levels * pairs * (2 * EDGE + SPAN), twice), jnp.bfloat16),
            pltpu.VMEM((blocks, slots), jnp.float32),
        ],
        compiler_params=params(20),
        cost_estimate=cost(4 * 10**9, 4 * 2**20),
    )(grid, rim, cells)


def join(a, b, left, members):
    return (
        jnp.where(left, a, pltpu.roll(b, members, 1)),
        jnp.where(left, pltpu.roll(a, members, 1), b),
    )


def left_lanes(shape):
    return lax.broadcasted_iota(jnp.int32, shape, 1) < shape[1] // 2


def deviations(states, raw, dev, at, size):
    groups, _, lanes = states.shape
    members = lanes // 2
    left = left_lanes((size, lanes))
    sums = [jnp.zeros((size, lanes), jnp.float32)] * 2
    for j in range(groups // 2):
        here = slice(j * lanes, (j + 1) * lanes)
        pair = join(
            states[2 * j, :size, :].astype(jnp.float32),
            states[2 * j + 1, :size, :].astype(jnp.float32),
            left,
            members,
        )
        for var in range(2):
            raw[var * size : (var + 1) * size, here] = pair[var]
        sums = [total + one for total, one in zip(sums, pair)]
    centre = jnp.concatenate([jnp.sum(x, axis=1, keepdims=True) for x in sums], axis=0)
    centre = centre * (1.0 / (groups * members))
    dev[at : at + 2 * size, :] = (raw[...] - centre).astype(jnp.bfloat16)
    return centre


def prepare_kernel(states, dev, centre, raw):
    mean = deviations(states, raw, dev, 0, states.shape[1])
    centre[...] = jnp.broadcast_to(mean, centre.shape)


def prepare(states):
    groups, near, lanes = states.shape
    total = groups * lanes // 2
    return pl.pallas_call(
        prepare_kernel,
        out_shape=[
            jax.ShapeDtypeStruct((2 * near, total), jnp.bfloat16),
            jax.ShapeDtypeStruct((2 * near, lanes), jnp.float32),
        ],
        in_specs=vmem(1),
        out_specs=vmem(2),
        scratch_shapes=[pltpu.VMEM((2 * near, total), jnp.float32)],
        compiler_params=params(6),
        cost_estimate=cost(10**8, 2 * 2**20),
    )(states)


def analyse_kernel(first, means, second, count, value, weight, out, raw, dev, obs, scaled_ref):
    groups, _, lanes = second.shape
    near = first.shape[0] // 2
    half = obs.shape[0] // 2
    far = second.shape[1] - half
    side = near + far
    slots = 2 * half
    members = lanes // 2
    total_members = groups * members
    left = left_lanes((half, lanes))

    for j in range(groups // 2):
        here = slice(j * lanes, (j + 1) * lanes)
        obs[:half, here], obs[half:, here] = join(
            second[2 * j, far:, :].astype(jnp.float32),
            second[2 * j + 1, far:, :].astype(jnp.float32),
            left,
            members,
        )

    used = lax.broadcasted_iota(jnp.int32, (1, slots), 1) < count[0, 0]
    root = column_of(jnp.where(used, jnp.sqrt(weight[...]), 0.0))
    observed = obs[...]
    mean = jnp.sum(observed, axis=1, keepdims=True) * (1.0 / total_members)
    scaled = (observed - mean) * root
    energy = jnp.sum(jnp.sum(scaled * scaled, axis=1, keepdims=True), axis=0, keepdims=True)
    scaled_ref[...] = scaled.astype(jnp.bfloat16)
    misfit = row_of(root * (column_of(value[...]) - mean))

    c = total_members - 1.0
    s = energy * (1.0 / total_members) + c
    inverse = 1.0 / s
    a = c * inverse
    p = 1.5 - 0.5 * a
    p2 = p * p
    p3 = p2 * p
    base = 1.5 * p - 0.5 * a * p3
    q0 = -0.75 - 0.5 * (p3 - 1.5 * a * p2)
    q1 = -0.5 * (0.75 * a * p - 1.5 * p2)
    q2 = -0.5 * (0.75 * p - 0.125 * a)
    small = dot_rows(scaled_ref[...], scaled_ref[...]) * inverse
    diagonal = eye(slots)
    square = dot3(small, small)
    tail = dot3(square, jnp.where(diagonal, q2, 0.0) + 0.0625 * small)
    poly = jnp.where(diagonal, q0, 0.0) + q1 * small + tail

    def apply(vector):
        inner_part = jnp.sum(poly * vector, axis=1, keepdims=True)
        return jnp.sum(small * inner_part, axis=0, keepdims=True) + base * vector

    gain = apply(apply(misfit)) * inverse
    stretch = jnp.sqrt(a)
    alpha, factor = stretch * base, stretch * inverse
    centre = deviations(second, raw, dev, 0, far)
    cross = jnp.concatenate(
        [dot_rows(first[...], scaled_ref[...]), dot_rows(dev[...], scaled_ref[...])], axis=0
    )
    centre = jnp.concatenate([means[:, 0:1], centre], axis=0)
    shift = centre + jnp.sum(cross * gain, axis=1, keepdims=True)
    mix = (dot3(cross, poly) * factor).astype(jnp.bfloat16)
    parts = ((first, 0, near, 0), (dev, 2 * near, far, near))
    for j in range(groups // 2):
        here = slice(j * lanes, (j + 1) * lanes)
        new = dot(mix, scaled_ref[:, here]) + shift
        for ref, at, size, row in parts:
            one = new[at : at + 2 * size] + alpha * ref[:, here].astype(jnp.float32)
            x, y = join(one[:size], one[size:], left_lanes((size, lanes)), members)
            out[2 * j, row : row + size, :] = x.astype(jnp.bfloat16)
            out[2 * j + 1, row : row + size, :] = y.astype(jnp.bfloat16)


def analyse(first, means, second, count, value, weight):
    groups, _, lanes = second.shape
    near = first.shape[0] // 2
    slots = value.shape[1]
    far = second.shape[1] - slots // 2
    total = groups * lanes // 2
    return pl.pallas_call(
        analyse_kernel,
        out_shape=jax.ShapeDtypeStruct((groups, near + far, lanes), jnp.bfloat16),
        in_specs=vmem(3) + smem(1) + vmem(2),
        out_specs=pl.BlockSpec(memory_space=pltpu.VMEM),
        scratch_shapes=[
            pltpu.VMEM((2 * far, total), jnp.float32),
            pltpu.VMEM((2 * far, total), jnp.bfloat16),
            pltpu.VMEM((slots, total), jnp.float32),
            pltpu.VMEM((slots, total), jnp.bfloat16),
        ],
        compiler_params=params(16),
        cost_estimate=cost(4 * 10**9, 4 * 2**20),
    )(first, means, second, count, value, weight)


def restore_kernel(blocks, out, turned):
    members, variables, levels, span, columns = out.shape
    lanes = members * variables
    identity = permutation(lanes, 0)
    near = span - 2 * STEPS
    for level in range(levels):
        for r in range(0, span, 2):
            if STEPS <= r < span - STEPS:
                at = level * near + r - STEPS
            else:
                at = levels * near + level * 2 * STEPS + (r if r < STEPS else r - near)
            both = blocks[:, at * SPAN : (at + 2) * SPAN, :].astype(jnp.float32)
            for i in range(2):
                one = both[:, i * SPAN : (i + 1) * SPAN, :].reshape(columns, lanes)
                rows = dot_rows(identity, one.astype(jnp.bfloat16))
                turned[level % 2, pl.ds(r + i, lanes, stride=span), :] = rows
        for var in range(variables):
            half = turned[level % 2, var * members * span : (var + 1) * members * span, :]
            out[:, var, level] = half.reshape(members, span, columns).astype(jnp.bfloat16)


def restore(dims, blocks):
    members, variables, levels, span, columns = dims
    return pl.pallas_call(
        restore_kernel,
        out_shape=jax.ShapeDtypeStruct((members, variables, levels, span, columns), jnp.bfloat16),
        in_specs=vmem(1),
        out_specs=pl.BlockSpec(memory_space=pltpu.VMEM),
        scratch_shapes=[pltpu.VMEM((2, variables * members * span, columns), jnp.float32)],
        compiler_params=params(8),
        cost_estimate=cost(2 * 10**9, 2 * 2**20),
    )(blocks)


def neighbours(field, axis):
    count = lax.axis_size(axis)
    low = lax.ppermute(field, axis, [(i, (i + 1) % count) for i in range(count)])
    if count == 2:
        return (low,)
    return low, lax.ppermute(field, axis, [((i + 1) % count, i) for i in range(count)])


def exchange(blocks):
    return lax.all_to_all(blocks, "grp", split_axis=0, concat_axis=0, tiled=True)


def on_device(start, diffusivity, eastward, northward, cells, count, value, weight):
    members, variables, levels, span, columns = dims = start.shape
    own = jnp.transpose(start, (1, 2, 3, 0, 4))
    sides = neighbours(own, "tile")
    model = model_rows(diffusivity, eastward, northward)
    centre, near = inner(dims, own, model)
    first, means = prepare(exchange(near))
    grid, rim = outer(dims, own, sides, model, centre)
    second = exchange(pick(variables, grid, rim, cells[0]))
    updated = analyse(first, means, second, count, value[0], weight[0])
    return restore(dims, exchange(updated))


def solution(mesh):
    return jax.shard_map(
        on_device,
        mesh=mesh,
        in_specs=(
            P("grp", None, None, "tile", None),
            P(),
            P(),
            P(),
            P("tile", None, None),
            P("tile", "grp"),
            P("tile", "grp", None),
            P("tile", "grp", None),
        ),
        out_specs=P("grp", None, None, "tile", None),
        check_vma=False,
    )
```

```python
import functools

import jax
import jax.numpy as jnp
from jax import lax
from jax.experimental import pallas as pl
from jax.experimental.pallas import tpu as pltpu
from jax.sharding import PartitionSpec as P

SPAN = 8
STEPS = 2
EDGE = SPAN // 2

ROWS = (((1,), (1,)), ((), ()))


def params(mebibytes, **kw):
    return pltpu.CompilerParams(vmem_limit_bytes=mebibytes * 2**20, **kw)


def cost(flops, size):
    return pl.CostEstimate(flops=flops, bytes_accessed=size, transcendentals=0)


def vmem(count):
    return [pl.BlockSpec(memory_space=pltpu.VMEM)] * count


def hbm(count):
    return [pl.BlockSpec(memory_space=pltpu.HBM)] * count


def smem(count):
    return [pl.BlockSpec(memory_space=pltpu.SMEM)] * count


def dot(a, b, **kw):
    return jnp.dot(a, b, preferred_element_type=jnp.float32, **kw)


def split(x):
    high = x.astype(jnp.bfloat16)
    return high, (x - high.astype(jnp.float32)).astype(jnp.bfloat16)


def dot3(a, b):
    (a_high, a_low), (b_high, b_low) = split(a), split(b)
    return dot(a_high, b_high) + (dot(a_high, b_low) + dot(a_low, b_high))


def dot_rows(a, b):
    return lax.dot_general(a, b, ROWS, preferred_element_type=jnp.float32)


def permutation(size, shift):
    row = lax.broadcasted_iota(jnp.int32, (size, size), 0)
    column = lax.broadcasted_iota(jnp.int32, (size, size), 1)
    return (lax.rem(row + shift + size, size) == column).astype(jnp.bfloat16)


def eye(size):
    row = lax.broadcasted_iota(jnp.int32, (size, size), 0)
    column = lax.broadcasted_iota(jnp.int32, (size, size), 1)
    return row == column


def column_of(row):
    return jnp.sum(jnp.where(eye(row.shape[1]), row, 0.0), axis=1, keepdims=True)


def row_of(column):
    return jnp.sum(jnp.where(eye(column.shape[0]), column, 0.0), axis=0, keepdims=True)


def forecast_rows(read, first, last, coefficients, write):
    middle, east, west, north, south = coefficients

    def step(below, here, above):
        columns = here.shape[2]
        return (
            middle * here
            + east * above
            + west * below
            + north * pltpu.roll(here, columns - 1, 2)
            + south * pltpu.roll(here, 1, 2)
        )

    start = [read(first - 2), read(first - 1), read(first)]
    once = [None, None, None]
    for r in range(first - 1, last + 1):
        once = [once[1], once[2], step(*start)]
        if r >= first + 1:
            write(r - 1, step(*once))
        if r < last:
            start = [start[1], start[2], read(r + 2)]


def model_rows(diffusivity, eastward, northward):
    levels, columns = diffusivity.shape
    place = lax.broadcasted_iota(jnp.int32, (levels, 3, columns), 1)
    speeds = jnp.where(place == 1, eastward[:, None, None], northward[:, None, None])
    return jnp.where(place == 0, diffusivity[:, None, :], speeds)


def coefficients_of(model, level):
    spread, u, w = (
        jnp.broadcast_to(model[level, i : i + 1, :], (8, model.shape[2])) for i in range(3)
    )
    u, w = 0.5 * u, 0.5 * w
    return 1.0 - 4.0 * spread, spread - u, spread + u, spread - w, spread + w


CHUNK = 64


def row_reader(level, var, first, size, own, low, high):
    span, columns = own.shape[2], own.shape[4]

    def read(r):
        ref, at = (low, r + span) if r < 0 else (own, r) if r < span else (high, r - span)
        return ref[var, level, at, first : first + size, :].reshape(-1, 8, columns)

    return read


def pack_rows(pair, identity, store, at):
    lanes = pair.shape[0] // 2
    turned = dot_rows(identity, pair)
    parts = [turned[:, i * lanes : (i + 1) * lanes].reshape(-1, SPAN, lanes) for i in range(2)]
    store[:, at : at + 2 * SPAN, :] = jnp.concatenate(parts, axis=1).astype(jnp.bfloat16)


def inner_kernel(variables, own, model, slabs, fields, packed):
    lanes, _, span, columns = own.shape
    members = lanes // variables
    count = span - 2 * STEPS
    coefficients = coefficients_of(model, pl.program_id(0))
    view = own.reshape(lanes * span, columns)
    for var in range(variables):

        def read(r):
            rows = view[pl.ds(var * span + r, members, stride=variables * span), :]
            slabs[var, 0, r] = rows
            return rows.reshape(-1, 8, columns)

        def write(r, value):
            at = var * members
            value = value.reshape(members, columns).astype(jnp.bfloat16)
            fields[0, r - STEPS, at : at + members, :] = value

        forecast_rows(read, STEPS, span - STEPS, coefficients, write)
    identity = permutation(columns, 0)
    for r in range(0, count, 2):
        pair = fields[0, r : r + 2].reshape(2 * lanes, columns)
        pack_rows(pair, identity, packed, r * SPAN)


def inner(own, model, variables):
    lanes, levels, span, columns = own.shape
    members = lanes // variables
    blocks = columns // SPAN
    count = span - 2 * STEPS
    return pl.pallas_call(
        functools.partial(inner_kernel, variables),
        grid=(levels,),
        out_shape=[
            jax.ShapeDtypeStruct((variables, levels, span, members, columns), jnp.float32),
            jax.ShapeDtypeStruct((levels, count, lanes, columns), jnp.bfloat16),
            jax.ShapeDtypeStruct((blocks, levels * count * SPAN, lanes), jnp.bfloat16),
        ],
        in_specs=[pl.BlockSpec((lanes, 1, span, columns), lambda level: (0, level, 0, 0))] + vmem(1),
        out_specs=[
            pl.BlockSpec((variables, 1, span, members, columns), lambda level: (0, level, 0, 0, 0)),
            pl.BlockSpec((1, count, lanes, columns), lambda level: (level, 0, 0, 0)),
            pl.BlockSpec((blocks, count * SPAN, lanes), lambda level: (0, level, 0)),
        ],
        compiler_params=params(50),
        cost_estimate=cost(2 * 10**9, 4 * 2**20),
    )(own, model)


def outer_kernel(near, own, *rest):
    sides, rest = rest[:near], rest[near:]
    model, centre, grid, packed, fields, sems = rest
    variables, levels, span, members, columns = own.shape
    rows = variables * members
    pairs = (2 * EDGE + span) // 2

    copies = []
    for r in range(STEPS, span - STEPS):
        half, pair = divmod(r + EDGE, pairs)
        place = grid.at[:, pair, pl.ds(half * rows, rows)]
        copies.append(pltpu.make_async_copy(centre.at[:, r - STEPS], place, sems.at[r - STEPS]))
        copies[-1].start()

    @pl.loop(0, levels)
    def _(level):
        coefficients = coefficients_of(model, level)
        for var in range(variables):
            for first in range(0, members, CHUNK):

                def write(r, value):
                    value = value.reshape(CHUNK, columns).astype(jnp.bfloat16)
                    half, pair = divmod(r + EDGE, pairs)
                    at = half * rows + var * members + first
                    grid[level, pair, at : at + CHUNK, :] = value
                    if 0 <= r < span:
                        pair, half = divmod(r if r < STEPS else r - span + 2 * STEPS, 2)
                        at = half * rows + var * members + first
                        fields[level, pair, at : at + CHUNK, :] = value

                read = row_reader(level, var, first, CHUNK, own, sides[0], sides[-1])
                forecast_rows(read, -EDGE, STEPS, coefficients, write)
                forecast_rows(read, span - STEPS, span + EDGE, coefficients, write)

    identity = permutation(columns, 0)
    for level in range(levels):
        for pair in range(STEPS):
            at = (level * STEPS + pair) * 2 * SPAN
            pack_rows(fields[level, pair], identity, packed, at)
    for copy in copies:
        copy.wait()


def outer(dims, own, sides, model, centre):
    members, variables, levels, span, columns = dims
    lanes = members * variables
    blocks = columns // SPAN
    near = len(sides)
    pairs = (2 * EDGE + span) // 2
    return pl.pallas_call(
        functools.partial(outer_kernel, near),
        out_shape=[
            jax.ShapeDtypeStruct((levels, pairs, 2 * lanes, columns), jnp.bfloat16),
            jax.ShapeDtypeStruct((blocks, levels * 2 * STEPS * SPAN, lanes), jnp.bfloat16),
        ],
        in_specs=vmem(2 + near) + hbm(1),
        out_specs=vmem(2),
        scratch_shapes=[
            pltpu.VMEM((levels, STEPS, 2 * lanes, columns), jnp.bfloat16),
            pltpu.SemaphoreType.DMA((span - 2 * STEPS,)),
        ],
        compiler_params=params(16),
        cost_estimate=cost(2 * 10**9, 8 * 2**20),
    )(own, *sides, model, centre)


def pick_kernel(variables, together, grid, rim, cells, out, region, codes):
    levels, pairs, twice, columns = grid.shape
    rows = twice // 2
    members = rows // variables
    blocks, slots = cells.shape
    width = 2 * EDGE + SPAN
    part = pairs * width
    entries = levels * part
    share = rim.shape[1]

    orders = jnp.concatenate(
        [permutation(columns, -EDGE), permutation(columns, SPAN - EDGE)], axis=0
    )
    for level in range(levels):
        for pair in range(pairs):
            turned = dot_rows(orders, grid[level, pair]).astype(jnp.bfloat16)
            at = (level * pairs + pair) * width
            for first in range(2):
                for j in range(columns // width):
                    row = first * columns + j * width
                    region[2 * j + first, at : at + width, :] = turned[row : row + width, :]

    cell = cells[...]
    second = cell >= 2 * entries
    cell = jnp.where(second, cell - 2 * entries, cell)
    level = lax.shift_right_logical(cell, (2 * part).bit_length() - 1)
    inside = cell - level * (2 * part)
    lower = inside >= part
    code = level * part + jnp.where(lower, inside - part + entries, inside)
    codes[...] = jnp.where(second, code + 2 * entries, code).astype(jnp.float32)

    left = lax.broadcasted_iota(jnp.int32, (slots // 2, rows), 1) < members
    lane = lax.broadcasted_iota(jnp.int32, (slots, entries), 1).astype(jnp.float32)

    @pl.loop(0, blocks // together)
    def _(step):
        for i in range(together):
            block = step * together + i
            at = column_of(codes[pl.ds(block, 1), :])
            second = at >= 2.0 * entries
            at = jnp.where(second, at - 2.0 * entries, at)
            lower = at >= 1.0 * entries
            at = jnp.where(lower, at - 1.0 * entries, at)
            pick = jnp.where(lane == at, 1.0, 0.0).astype(jnp.bfloat16)
            found = dot(pick, region[block])
            total = jnp.where(lower, found[:, rows:], found[:, :rows])
            other = pltpu.roll(total, members, 1)
            to_left = jnp.where(second, other, total)[: slots // 2]
            to_right = jnp.where(second, total, other)[slots // 2 :]
            out[block, share:, :] = jnp.where(left, to_left, to_right).astype(jnp.bfloat16)
            out[block, :share, :] = rim[block]


def pick(variables, grid, rim, cells):
    levels, pairs, twice, columns = grid.shape
    blocks, slots = cells.shape
    _, share, lanes = rim.shape
    together = next(n for n in (4, 2, 1) if blocks % n == 0)
    return pl.pallas_call(
        functools.partial(pick_kernel, variables, together),
        out_shape=jax.ShapeDtypeStruct((blocks, share + slots // 2, lanes), jnp.bfloat16),
        in_specs=vmem(3),
        out_specs=pl.BlockSpec(memory_space=pltpu.VMEM),
        scratch_shapes=[
            pltpu.VMEM((blocks, levels * pairs * (2 * EDGE + SPAN), twice), jnp.bfloat16),
            pltpu.VMEM((blocks, slots), jnp.float32),
        ],
        compiler_params=params(20),
        cost_estimate=cost(4 * 10**9, 4 * 2**20),
    )(grid, rim, cells)


def join(a, b, left, members):
    return (
        jnp.where(left, a, pltpu.roll(b, members, 1)),
        jnp.where(left, pltpu.roll(a, members, 1), b),
    )


def left_lanes(shape):
    return lax.broadcasted_iota(jnp.int32, shape, 1) < shape[1] // 2


def deviations(states, raw, dev, at, size):
    groups, _, lanes = states.shape
    members = lanes // 2
    left = left_lanes((size, lanes))
    sums = [jnp.zeros((size, lanes), jnp.float32)] * 2
    for j in range(groups // 2):
        here = slice(j * lanes, (j + 1) * lanes)
        pair = join(
            states[2 * j, :size, :].astype(jnp.float32),
            states[2 * j + 1, :size, :].astype(jnp.float32),
            left,
            members,
        )
        for var in range(2):
            raw[var * size : (var + 1) * size, here] = pair[var]
        sums = [total + one for total, one in zip(sums, pair)]
    centre = jnp.concatenate([jnp.sum(x, axis=1, keepdims=True) for x in sums], axis=0)
    centre = centre * (1.0 / (groups * members))
    dev[at : at + 2 * size, :] = (raw[...] - centre).astype(jnp.bfloat16)
    return centre


def prepare_kernel(states, dev, centre, raw):
    mean = deviations(states, raw, dev, 0, states.shape[1])
    centre[...] = jnp.broadcast_to(mean, centre.shape)


def prepare(states):
    groups, near, lanes = states.shape
    total = groups * lanes // 2
    return pl.pallas_call(
        prepare_kernel,
        out_shape=[
            jax.ShapeDtypeStruct((2 * near, total), jnp.bfloat16),
            jax.ShapeDtypeStruct((2 * near, lanes), jnp.float32),
        ],
        in_specs=vmem(1),
        out_specs=vmem(2),
        scratch_shapes=[pltpu.VMEM((2 * near, total), jnp.float32)],
        compiler_params=params(6),
        cost_estimate=cost(10**8, 2 * 2**20),
    )(states)


def analyse_kernel(first, means, second, count, value, weight, out, raw, dev, obs, scaled_ref):
    groups, _, lanes = second.shape
    near = first.shape[0] // 2
    half = obs.shape[0] // 2
    far = second.shape[1] - half
    side = near + far
    slots = 2 * half
    members = lanes // 2
    total_members = groups * members
    left = left_lanes((half, lanes))

    for j in range(groups // 2):
        here = slice(j * lanes, (j + 1) * lanes)
        obs[:half, here], obs[half:, here] = join(
            second[2 * j, far:, :].astype(jnp.float32),
            second[2 * j + 1, far:, :].astype(jnp.float32),
            left,
            members,
        )

    used = lax.broadcasted_iota(jnp.int32, (1, slots), 1) < count[0, 0]
    root = column_of(jnp.where(used, jnp.sqrt(weight[...]), 0.0))
    observed = obs[...]
    mean = jnp.sum(observed, axis=1, keepdims=True) * (1.0 / total_members)
    scaled = (observed - mean) * root
    energy = jnp.sum(jnp.sum(scaled * scaled, axis=1, keepdims=True), axis=0, keepdims=True)
    scaled_ref[...] = scaled.astype(jnp.bfloat16)
    misfit = row_of(root * (column_of(value[...]) - mean))

    c = total_members - 1.0
    s = energy * (1.0 / total_members) + c
    inverse = 1.0 / s
    a = c * inverse
    p = 1.5 - 0.5 * a
    p2 = p * p
    p3 = p2 * p
    base = 1.5 * p - 0.5 * a * p3
    q0 = -0.75 - 0.5 * (p3 - 1.5 * a * p2)
    q1 = -0.5 * (0.75 * a * p - 1.5 * p2)
    q2 = -0.5 * (0.75 * p - 0.125 * a)
    small = dot_rows(scaled_ref[...], scaled_ref[...]) * inverse
    diagonal = eye(slots)
    square = dot3(small, small)
    tail = dot3(square, jnp.where(diagonal, q2, 0.0) + 0.0625 * small)
    poly = jnp.where(diagonal, q0, 0.0) + q1 * small + tail

    def apply(vector):
        inner_part = jnp.sum(poly * vector, axis=1, keepdims=True)
        return jnp.sum(small * inner_part, axis=0, keepdims=True) + base * vector

    gain = apply(apply(misfit)) * inverse
    stretch = jnp.sqrt(a)
    alpha, factor = stretch * base, stretch * inverse
    centre = deviations(second, raw, dev, 0, far)
    cross = jnp.concatenate(
        [dot_rows(first[...], scaled_ref[...]), dot_rows(dev[...], scaled_ref[...])], axis=0
    )
    centre = jnp.concatenate([means[:, 0:1], centre], axis=0)
    shift = centre + jnp.sum(cross * gain, axis=1, keepdims=True)
    mix = (dot3(cross, poly) * factor).astype(jnp.bfloat16)
    parts = ((first, 0, near, 0), (dev, 2 * near, far, near))
    for j in range(groups // 2):
        here = slice(j * lanes, (j + 1) * lanes)
        new = dot(mix, scaled_ref[:, here]) + shift
        for ref, at, size, row in parts:
            one = new[at : at + 2 * size] + alpha * ref[:, here].astype(jnp.float32)
            x, y = join(one[:size], one[size:], left_lanes((size, lanes)), members)
            out[2 * j, row : row + size, :] = x.astype(jnp.bfloat16)
            out[2 * j + 1, row : row + size, :] = y.astype(jnp.bfloat16)


def analyse(first, means, second, count, value, weight):
    groups, _, lanes = second.shape
    near = first.shape[0] // 2
    slots = value.shape[1]
    far = second.shape[1] - slots // 2
    total = groups * lanes // 2
    return pl.pallas_call(
        analyse_kernel,
        out_shape=jax.ShapeDtypeStruct((groups, near + far, lanes), jnp.bfloat16),
        in_specs=vmem(3) + smem(1) + vmem(2),
        out_specs=pl.BlockSpec(memory_space=pltpu.VMEM),
        scratch_shapes=[
            pltpu.VMEM((2 * far, total), jnp.float32),
            pltpu.VMEM((2 * far, total), jnp.bfloat16),
            pltpu.VMEM((slots, total), jnp.float32),
            pltpu.VMEM((slots, total), jnp.bfloat16),
        ],
        compiler_params=params(16),
        cost_estimate=cost(4 * 10**9, 4 * 2**20),
    )(first, means, second, count, value, weight)


def restore_kernel(blocks, out, turned):
    members, variables, levels, span, columns = out.shape
    lanes = members * variables
    identity = permutation(lanes, 0)
    near = span - 2 * STEPS
    for level in range(levels):
        for r in range(0, span, 2):
            if STEPS <= r < span - STEPS:
                at = level * near + r - STEPS
            else:
                at = levels * near + level * 2 * STEPS + (r if r < STEPS else r - near)
            both = blocks[:, at * SPAN : (at + 2) * SPAN, :].astype(jnp.float32)
            for i in range(2):
                one = both[:, i * SPAN : (i + 1) * SPAN, :].reshape(columns, lanes)
                rows = dot_rows(identity, one.astype(jnp.bfloat16))
                turned[level % 2, pl.ds(r + i, lanes, stride=span), :] = rows
        for var in range(variables):
            half = turned[level % 2, var * members * span : (var + 1) * members * span, :]
            out[:, var, level] = half.reshape(members, span, columns).astype(jnp.bfloat16)


def restore(dims, blocks):
    members, variables, levels, span, columns = dims
    return pl.pallas_call(
        restore_kernel,
        out_shape=jax.ShapeDtypeStruct((members, variables, levels, span, columns), jnp.bfloat16),
        in_specs=vmem(1),
        out_specs=pl.BlockSpec(memory_space=pltpu.VMEM),
        scratch_shapes=[pltpu.VMEM((2, variables * members * span, columns), jnp.float32)],
        compiler_params=params(8),
        cost_estimate=cost(2 * 10**9, 2 * 2**20),
    )(blocks)


def neighbours(field, axis):
    count = lax.axis_size(axis)
    low = lax.ppermute(field, axis, [(i, (i + 1) % count) for i in range(count)])
    if count == 2:
        return (low,)
    return low, lax.ppermute(field, axis, [((i + 1) % count, i) for i in range(count)])


def exchange(blocks):
    return lax.all_to_all(blocks, "grp", split_axis=0, concat_axis=0, tiled=True)


def on_device(start, diffusivity, eastward, northward, cells, count, value, weight):
    members, variables, levels, span, columns = dims = start.shape
    model = model_rows(diffusivity, eastward, northward)
    whole = start.reshape(members * variables, levels, span, columns)
    own, centre, near = inner(whole, model, variables)
    sides = neighbours(own, "tile")
    first, means = prepare(exchange(near))
    grid, rim = outer(dims, own, sides, model, centre)
    second = exchange(pick(variables, grid, rim, cells[0]))
    updated = analyse(first, means, second, count, value[0], weight[0])
    return restore(dims, exchange(updated))


def solution(mesh):
    return jax.shard_map(
        on_device,
        mesh=mesh,
        in_specs=(
            P("grp", None, None, "tile", None),
            P(),
            P(),
            P(),
            P("tile", None, None),
            P("tile", "grp"),
            P("tile", "grp", None),
            P("tile", "grp", None),
        ),
        out_specs=P("grp", None, None, "tile", None),
        check_vma=False,
    )
```

```python
import functools

import jax
import jax.numpy as jnp
from jax import lax
from jax.experimental import pallas as pl
from jax.experimental.pallas import tpu as pltpu
from jax.sharding import PartitionSpec as P

SPAN = 8
STEPS = 2
EDGE = SPAN // 2

ROWS = (((1,), (1,)), ((), ()))


def params(mebibytes, **kw):
    return pltpu.CompilerParams(vmem_limit_bytes=mebibytes * 2**20, **kw)


def cost(flops, size):
    return pl.CostEstimate(flops=flops, bytes_accessed=size, transcendentals=0)


def vmem(count):
    return [pl.BlockSpec(memory_space=pltpu.VMEM)] * count


def hbm(count):
    return [pl.BlockSpec(memory_space=pltpu.HBM)] * count


def smem(count):
    return [pl.BlockSpec(memory_space=pltpu.SMEM)] * count


def dot(a, b, **kw):
    return jnp.dot(a, b, preferred_element_type=jnp.float32, **kw)


def split(x):
    high = x.astype(jnp.bfloat16)
    return high, (x - high.astype(jnp.float32)).astype(jnp.bfloat16)


def dot3(a, b):
    (a_high, a_low), (b_high, b_low) = split(a), split(b)
    return dot(a_high, b_high) + (dot(a_high, b_low) + dot(a_low, b_high))


def dot_rows(a, b):
    return lax.dot_general(a, b, ROWS, preferred_element_type=jnp.float32)


def permutation(size, shift):
    row = lax.broadcasted_iota(jnp.int32, (size, size), 0)
    column = lax.broadcasted_iota(jnp.int32, (size, size), 1)
    return (lax.rem(row + shift + size, size) == column).astype(jnp.bfloat16)


def eye(size):
    row = lax.broadcasted_iota(jnp.int32, (size, size), 0)
    column = lax.broadcasted_iota(jnp.int32, (size, size), 1)
    return row == column


def column_of(row):
    return jnp.sum(jnp.where(eye(row.shape[1]), row, 0.0), axis=1, keepdims=True)


def row_of(column):
    return jnp.sum(jnp.where(eye(column.shape[0]), column, 0.0), axis=0, keepdims=True)


def model_step(rows, factors):
    middle, east, west, sideways = factors
    members, columns = rows[0].shape
    inside = rows[1:-1]
    high, low = split(jnp.concatenate(inside, axis=0))
    across = dot(jnp.concatenate([high, low], axis=1), sideways)
    new = []
    for i, here in enumerate(inside):
        below, above = rows[i], rows[i + 2]
        moved = (
            middle * here.reshape(-1, 8, columns)
            + east * above.reshape(-1, 8, columns)
            + west * below.reshape(-1, 8, columns)
        )
        new.append(moved.reshape(members, columns) + across[i * members : (i + 1) * members])
    return new


def forecast_rows(read, first, last, factors, write):
    rows = [read(r) for r in range(first - STEPS, last + STEPS)]
    for _ in range(STEPS):
        rows = model_step(rows, factors)
    for i, row in enumerate(rows):
        write(first + i, row.astype(jnp.bfloat16))


def model_rows(diffusivity, eastward, northward):
    levels, columns = diffusivity.shape
    place = lax.broadcasted_iota(jnp.int32, (levels, 3, columns), 1)
    speeds = jnp.where(place == 1, eastward[:, None, None], northward[:, None, None])
    return jnp.where(place == 0, diffusivity[:, None, :], speeds)


def factors_of(model, level):
    columns = model.shape[2]
    spread, u, w = (
        jnp.broadcast_to(model[level, i : i + 1, :], (8, columns)) for i in range(3)
    )
    u, w = 0.5 * u, 0.5 * w
    source = lax.broadcasted_iota(jnp.int32, (columns, columns), 0)
    target = lax.broadcasted_iota(jnp.int32, (columns, columns), 1)
    ahead = jnp.where(source == 0, columns - 1, source - 1)
    behind = jnp.where(source == columns - 1, 0, source + 1)
    matrix = jnp.where(target == ahead, (spread - w)[0:1], 0.0)
    matrix += jnp.where(target == behind, (spread + w)[0:1], 0.0)
    matrix = matrix.astype(jnp.bfloat16)
    return 1.0 - 4.0 * spread, spread - u, spread + u, jnp.concatenate([matrix, matrix], axis=0)


CHUNK = 64


def row_reader(level, var, first, size, own, low, high):
    span = own.shape[2]

    def read(r):
        ref, at = (low, r + span) if r < 0 else (own, r) if r < span else (high, r - span)
        return ref[var, level, at, first : first + size, :]

    return read


def pack_rows(pair, identity, store, at):
    lanes = pair.shape[0] // 2
    turned = dot_rows(identity, pair)
    parts = [turned[:, i * lanes : (i + 1) * lanes].reshape(-1, SPAN, lanes) for i in range(2)]
    store[:, at : at + 2 * SPAN, :] = jnp.concatenate(parts, axis=1).astype(jnp.bfloat16)


def inner_kernel(variables, own, model, slabs, fields, packed):
    lanes, _, span, columns = own.shape
    members = lanes // variables
    count = span - 2 * STEPS
    factors = factors_of(model, pl.program_id(0))
    view = own.reshape(lanes * span, columns)
    for var in range(variables):

        def read(r):
            rows = view[pl.ds(var * span + r, members, stride=variables * span), :]
            slabs[var, 0, r] = rows
            return rows

        def write(r, value):
            at = var * members
            fields[0, r - STEPS, at : at + members, :] = value

        forecast_rows(read, STEPS, span - STEPS, factors, write)
    identity = permutation(columns, 0)
    for r in range(0, count, 2):
        pair = fields[0, r : r + 2].reshape(2 * lanes, columns)
        pack_rows(pair, identity, packed, r * SPAN)


def inner(own, model, variables):
    lanes, levels, span, columns = own.shape
    members = lanes // variables
    blocks = columns // SPAN
    count = span - 2 * STEPS
    return pl.pallas_call(
        functools.partial(inner_kernel, variables),
        grid=(levels,),
        out_shape=[
            jax.ShapeDtypeStruct((variables, levels, span, members, columns), jnp.float32),
            jax.ShapeDtypeStruct((levels, count, lanes, columns), jnp.bfloat16),
            jax.ShapeDtypeStruct((blocks, levels * count * SPAN, lanes), jnp.bfloat16),
        ],
        in_specs=[pl.BlockSpec((lanes, 1, span, columns), lambda level: (0, level, 0, 0))] + vmem(1),
        out_specs=[
            pl.BlockSpec((variables, 1, span, members, columns), lambda level: (0, level, 0, 0, 0)),
            pl.BlockSpec((1, count, lanes, columns), lambda level: (level, 0, 0, 0)),
            pl.BlockSpec((blocks, count * SPAN, lanes), lambda level: (0, level, 0)),
        ],
        compiler_params=params(50),
        cost_estimate=cost(2 * 10**9, 4 * 2**20),
    )(own, model)


def outer_kernel(near, own, *rest):
    sides, rest = rest[:near], rest[near:]
    model, centre, grid, packed, fields, sems = rest
    variables, levels, span, members, columns = own.shape
    rows = variables * members
    pairs = (2 * EDGE + span) // 2

    copies = []
    for r in range(STEPS, span - STEPS):
        half, pair = divmod(r + EDGE, pairs)
        place = grid.at[:, pair, pl.ds(half * rows, rows)]
        copies.append(pltpu.make_async_copy(centre.at[:, r - STEPS], place, sems.at[r - STEPS]))
        copies[-1].start()

    @pl.loop(0, levels)
    def _(level):
        factors = factors_of(model, level)
        for var in range(variables):
            for first in range(0, members, CHUNK):

                def write(r, value):
                    half, pair = divmod(r + EDGE, pairs)
                    at = half * rows + var * members + first
                    grid[level, pair, at : at + CHUNK, :] = value
                    if 0 <= r < span:
                        pair, half = divmod(r if r < STEPS else r - span + 2 * STEPS, 2)
                        at = half * rows + var * members + first
                        fields[level, pair, at : at + CHUNK, :] = value

                read = row_reader(level, var, first, CHUNK, own, sides[0], sides[-1])
                forecast_rows(read, -EDGE, STEPS, factors, write)
                forecast_rows(read, span - STEPS, span + EDGE, factors, write)

    identity = permutation(columns, 0)
    for level in range(levels):
        for pair in range(STEPS):
            at = (level * STEPS + pair) * 2 * SPAN
            pack_rows(fields[level, pair], identity, packed, at)
    for copy in copies:
        copy.wait()


def outer(dims, own, sides, model, centre):
    members, variables, levels, span, columns = dims
    lanes = members * variables
    blocks = columns // SPAN
    near = len(sides)
    pairs = (2 * EDGE + span) // 2
    return pl.pallas_call(
        functools.partial(outer_kernel, near),
        out_shape=[
            jax.ShapeDtypeStruct((levels, pairs, 2 * lanes, columns), jnp.bfloat16),
            jax.ShapeDtypeStruct((blocks, levels * 2 * STEPS * SPAN, lanes), jnp.bfloat16),
        ],
        in_specs=vmem(2 + near) + hbm(1),
        out_specs=vmem(2),
        scratch_shapes=[
            pltpu.VMEM((levels, STEPS, 2 * lanes, columns), jnp.bfloat16),
            pltpu.SemaphoreType.DMA((span - 2 * STEPS,)),
        ],
        compiler_params=params(16),
        cost_estimate=cost(2 * 10**9, 8 * 2**20),
    )(own, *sides, model, centre)


def pick_kernel(variables, together, grid, rim, cells, out, region, codes):
    levels, pairs, twice, columns = grid.shape
    rows = twice // 2
    members = rows // variables
    blocks, slots = cells.shape
    width = 2 * EDGE + SPAN
    part = pairs * width
    entries = levels * part
    share = rim.shape[1]

    orders = jnp.concatenate(
        [permutation(columns, -EDGE), permutation(columns, SPAN - EDGE)], axis=0
    )
    for level in range(levels):
        for pair in range(pairs):
            turned = dot_rows(orders, grid[level, pair]).astype(jnp.bfloat16)
            at = (level * pairs + pair) * width
            for first in range(2):
                for j in range(columns // width):
                    row = first * columns + j * width
                    region[2 * j + first, at : at + width, :] = turned[row : row + width, :]

    cell = cells[...]
    second = cell >= 2 * entries
    cell = jnp.where(second, cell - 2 * entries, cell)
    level = lax.shift_right_logical(cell, (2 * part).bit_length() - 1)
    inside = cell - level * (2 * part)
    lower = inside >= part
    code = level * part + jnp.where(lower, inside - part + entries, inside)
    codes[...] = jnp.where(second, code + 2 * entries, code).astype(jnp.float32)

    left = lax.broadcasted_iota(jnp.int32, (slots // 2, rows), 1) < members
    lane = lax.broadcasted_iota(jnp.int32, (slots, entries), 1).astype(jnp.float32)

    @pl.loop(0, blocks // together)
    def _(step):
        for i in range(together):
            block = step * together + i
            at = column_of(codes[pl.ds(block, 1), :])
            second = at >= 2.0 * entries
            at = jnp.where(second, at - 2.0 * entries, at)
            lower = at >= 1.0 * entries
            at = jnp.where(lower, at - 1.0 * entries, at)
            pick = jnp.where(lane == at, 1.0, 0.0).astype(jnp.bfloat16)
            found = dot(pick, region[block])
            total = jnp.where(lower, found[:, rows:], found[:, :rows])
            other = pltpu.roll(total, members, 1)
            to_left = jnp.where(second, other, total)[: slots // 2]
            to_right = jnp.where(second, total, other)[slots // 2 :]
            out[block, share:, :] = jnp.where(left, to_left, to_right).astype(jnp.bfloat16)
            out[block, :share, :] = rim[block]


def pick(variables, grid, rim, cells):
    levels, pairs, twice, columns = grid.shape
    blocks, slots = cells.shape
    _, share, lanes = rim.shape
    together = next(n for n in (4, 2, 1) if blocks % n == 0)
    return pl.pallas_call(
        functools.partial(pick_kernel, variables, together),
        out_shape=jax.ShapeDtypeStruct((blocks, share + slots // 2, lanes), jnp.bfloat16),
        in_specs=vmem(3),
        out_specs=pl.BlockSpec(memory_space=pltpu.VMEM),
        scratch_shapes=[
            pltpu.VMEM((blocks, levels * pairs * (2 * EDGE + SPAN), twice), jnp.bfloat16),
            pltpu.VMEM((blocks, slots), jnp.float32),
        ],
        compiler_params=params(20),
        cost_estimate=cost(4 * 10**9, 4 * 2**20),
    )(grid, rim, cells)


def join(a, b, left, members):
    return (
        jnp.where(left, a, pltpu.roll(b, members, 1)),
        jnp.where(left, pltpu.roll(a, members, 1), b),
    )


def left_lanes(shape):
    return lax.broadcasted_iota(jnp.int32, shape, 1) < shape[1] // 2


def deviations(states, raw, dev, at, size):
    groups, _, lanes = states.shape
    members = lanes // 2
    left = left_lanes((size, lanes))
    sums = [jnp.zeros((size, lanes), jnp.float32)] * 2
    for j in range(groups // 2):
        here = slice(j * lanes, (j + 1) * lanes)
        pair = join(
            states[2 * j, :size, :].astype(jnp.float32),
            states[2 * j + 1, :size, :].astype(jnp.float32),
            left,
            members,
        )
        for var in range(2):
            raw[var * size : (var + 1) * size, here] = pair[var]
        sums = [total + one for total, one in zip(sums, pair)]
    centre = jnp.concatenate([jnp.sum(x, axis=1, keepdims=True) for x in sums], axis=0)
    centre = centre * (1.0 / (groups * members))
    dev[at : at + 2 * size, :] = (raw[...] - centre).astype(jnp.bfloat16)
    return centre


def prepare_kernel(states, dev, centre, raw):
    mean = deviations(states, raw, dev, 0, states.shape[1])
    centre[...] = jnp.broadcast_to(mean, centre.shape)


def prepare(states):
    groups, near, lanes = states.shape
    total = groups * lanes // 2
    return pl.pallas_call(
        prepare_kernel,
        out_shape=[
            jax.ShapeDtypeStruct((2 * near, total), jnp.bfloat16),
            jax.ShapeDtypeStruct((2 * near, lanes), jnp.float32),
        ],
        in_specs=vmem(1),
        out_specs=vmem(2),
        scratch_shapes=[pltpu.VMEM((2 * near, total), jnp.float32)],
        compiler_params=params(6),
        cost_estimate=cost(10**8, 2 * 2**20),
    )(states)


def analyse_kernel(first, means, second, count, value, weight, out, raw, dev, obs, scaled_ref):
    groups, _, lanes = second.shape
    near = first.shape[0] // 2
    half = obs.shape[0] // 2
    far = second.shape[1] - half
    side = near + far
    slots = 2 * half
    members = lanes // 2
    total_members = groups * members
    left = left_lanes((half, lanes))

    for j in range(groups // 2):
        here = slice(j * lanes, (j + 1) * lanes)
        obs[:half, here], obs[half:, here] = join(
            second[2 * j, far:, :].astype(jnp.float32),
            second[2 * j + 1, far:, :].astype(jnp.float32),
            left,
            members,
        )

    used = lax.broadcasted_iota(jnp.int32, (1, slots), 1) < count[0, 0]
    root = column_of(jnp.where(used, jnp.sqrt(weight[...]), 0.0))
    observed = obs[...]
    mean = jnp.sum(observed, axis=1, keepdims=True) * (1.0 / total_members)
    scaled = (observed - mean) * root
    energy = jnp.sum(jnp.sum(scaled * scaled, axis=1, keepdims=True), axis=0, keepdims=True)
    scaled_ref[...] = scaled.astype(jnp.bfloat16)
    misfit = row_of(root * (column_of(value[...]) - mean))

    c = total_members - 1.0
    s = energy * (1.0 / total_members) + c
    inverse = 1.0 / s
    a = c * inverse
    p = 1.5 - 0.5 * a
    p2 = p * p
    p3 = p2 * p
    base = 1.5 * p - 0.5 * a * p3
    q0 = -0.75 - 0.5 * (p3 - 1.5 * a * p2)
    q1 = -0.5 * (0.75 * a * p - 1.5 * p2)
    q2 = -0.5 * (0.75 * p - 0.125 * a)
    small = dot_rows(scaled_ref[...], scaled_ref[...]) * inverse
    diagonal = eye(slots)
    square = dot3(small, small)
    tail = dot3(square, jnp.where(diagonal, q2, 0.0) + 0.0625 * small)
    poly = jnp.where(diagonal, q0, 0.0) + q1 * small + tail

    def apply(vector):
        inner_part = jnp.sum(poly * vector, axis=1, keepdims=True)
        return jnp.sum(small * inner_part, axis=0, keepdims=True) + base * vector

    gain = apply(apply(misfit)) * inverse
    stretch = jnp.sqrt(a)
    alpha, factor = stretch * base, stretch * inverse
    centre = deviations(second, raw, dev, 0, far)
    cross = jnp.concatenate(
        [dot_rows(first[...], scaled_ref[...]), dot_rows(dev[...], scaled_ref[...])], axis=0
    )
    centre = jnp.concatenate([means[:, 0:1], centre], axis=0)
    shift = centre + jnp.sum(cross * gain, axis=1, keepdims=True)
    mix = (dot3(cross, poly) * factor).astype(jnp.bfloat16)
    parts = ((first, 0, near, 0), (dev, 2 * near, far, near))
    for j in range(groups // 2):
        here = slice(j * lanes, (j + 1) * lanes)
        new = dot(mix, scaled_ref[:, here]) + shift
        for ref, at, size, row in parts:
            one = new[at : at + 2 * size] + alpha * ref[:, here].astype(jnp.float32)
            x, y = join(one[:size], one[size:], left_lanes((size, lanes)), members)
            out[2 * j, row : row + size, :] = x.astype(jnp.bfloat16)
            out[2 * j + 1, row : row + size, :] = y.astype(jnp.bfloat16)


def analyse(first, means, second, count, value, weight):
    groups, _, lanes = second.shape
    near = first.shape[0] // 2
    slots = value.shape[1]
    far = second.shape[1] - slots // 2
    total = groups * lanes // 2
    return pl.pallas_call(
        analyse_kernel,
        out_shape=jax.ShapeDtypeStruct((groups, near + far, lanes), jnp.bfloat16),
        in_specs=vmem(3) + smem(1) + vmem(2),
        out_specs=pl.BlockSpec(memory_space=pltpu.VMEM),
        scratch_shapes=[
            pltpu.VMEM((2 * far, total), jnp.float32),
            pltpu.VMEM((2 * far, total), jnp.bfloat16),
            pltpu.VMEM((slots, total), jnp.float32),
            pltpu.VMEM((slots, total), jnp.bfloat16),
        ],
        compiler_params=params(16),
        cost_estimate=cost(4 * 10**9, 4 * 2**20),
    )(first, means, second, count, value, weight)


def restore_kernel(blocks, out, turned):
    members, variables, levels, span, columns = out.shape
    lanes = members * variables
    identity = permutation(lanes, 0)
    near = span - 2 * STEPS
    for level in range(levels):
        for r in range(0, span, 2):
            if STEPS <= r < span - STEPS:
                at = level * near + r - STEPS
            else:
                at = levels * near + level * 2 * STEPS + (r if r < STEPS else r - near)
            both = blocks[:, at * SPAN : (at + 2) * SPAN, :].astype(jnp.float32)
            for i in range(2):
                one = both[:, i * SPAN : (i + 1) * SPAN, :].reshape(columns, lanes)
                rows = dot_rows(identity, one.astype(jnp.bfloat16))
                turned[level % 2, pl.ds(r + i, lanes, stride=span), :] = rows
        for var in range(variables):
            half = turned[level % 2, var * members * span : (var + 1) * members * span, :]
            out[:, var, level] = half.reshape(members, span, columns).astype(jnp.bfloat16)


def restore(dims, blocks):
    members, variables, levels, span, columns = dims
    return pl.pallas_call(
        restore_kernel,
        out_shape=jax.ShapeDtypeStruct((members, variables, levels, span, columns), jnp.bfloat16),
        in_specs=vmem(1),
        out_specs=pl.BlockSpec(memory_space=pltpu.VMEM),
        scratch_shapes=[pltpu.VMEM((2, variables * members * span, columns), jnp.float32)],
        compiler_params=params(8),
        cost_estimate=cost(2 * 10**9, 2 * 2**20),
    )(blocks)


def neighbours(field, axis):
    count = lax.axis_size(axis)
    low = lax.ppermute(field, axis, [(i, (i + 1) % count) for i in range(count)])
    if count == 2:
        return (low,)
    return low, lax.ppermute(field, axis, [((i + 1) % count, i) for i in range(count)])


def exchange(blocks):
    return lax.all_to_all(blocks, "grp", split_axis=0, concat_axis=0, tiled=True)


def on_device(start, diffusivity, eastward, northward, cells, count, value, weight):
    members, variables, levels, span, columns = dims = start.shape
    model = model_rows(diffusivity, eastward, northward)
    whole = start.reshape(members * variables, levels, span, columns)
    own, centre, near = inner(whole, model, variables)
    sides = neighbours(own, "tile")
    first, means = prepare(exchange(near))
    grid, rim = outer(dims, own, sides, model, centre)
    second = exchange(pick(variables, grid, rim, cells[0]))
    updated = analyse(first, means, second, count, value[0], weight[0])
    return restore(dims, exchange(updated))


def solution(mesh):
    return jax.shard_map(
        on_device,
        mesh=mesh,
        in_specs=(
            P("grp", None, None, "tile", None),
            P(),
            P(),
            P(),
            P("tile", None, None),
            P("tile", "grp"),
            P("tile", "grp", None),
            P("tile", "grp", None),
        ),
        out_specs=P("grp", None, None, "tile", None),
        check_vma=False,
    )
```

```python
import functools

import jax
import jax.numpy as jnp
from jax import lax
from jax.experimental import pallas as pl
from jax.experimental.pallas import tpu as pltpu
from jax.sharding import PartitionSpec as P

SPAN = 8
STEPS = 2
EDGE = SPAN // 2

ROWS = (((1,), (1,)), ((), ()))


def params(mebibytes, **kw):
    return pltpu.CompilerParams(vmem_limit_bytes=mebibytes * 2**20, **kw)


def cost(flops, size):
    return pl.CostEstimate(flops=flops, bytes_accessed=size, transcendentals=0)


def vmem(count):
    return [pl.BlockSpec(memory_space=pltpu.VMEM)] * count


def hbm(count):
    return [pl.BlockSpec(memory_space=pltpu.HBM)] * count


def smem(count):
    return [pl.BlockSpec(memory_space=pltpu.SMEM)] * count


def dot(a, b, **kw):
    return jnp.dot(a, b, preferred_element_type=jnp.float32, **kw)


def split(x):
    high = x.astype(jnp.bfloat16)
    return high, (x - high.astype(jnp.float32)).astype(jnp.bfloat16)


def dot3(a, b):
    (a_high, a_low), (b_high, b_low) = split(a), split(b)
    return dot(a_high, b_high) + (dot(a_high, b_low) + dot(a_low, b_high))


def dot_rows(a, b):
    return lax.dot_general(a, b, ROWS, preferred_element_type=jnp.float32)


def permutation(size, shift):
    row = lax.broadcasted_iota(jnp.int32, (size, size), 0)
    column = lax.broadcasted_iota(jnp.int32, (size, size), 1)
    return (lax.rem(row + shift + size, size) == column).astype(jnp.bfloat16)


def eye(size):
    row = lax.broadcasted_iota(jnp.int32, (size, size), 0)
    column = lax.broadcasted_iota(jnp.int32, (size, size), 1)
    return row == column


def column_of(row):
    return jnp.sum(jnp.where(eye(row.shape[1]), row, 0.0), axis=1, keepdims=True)


def row_of(column):
    return jnp.sum(jnp.where(eye(column.shape[0]), column, 0.0), axis=0, keepdims=True)


def forecast_rows(read, first, last, coefficients, write):
    middle, east, west, north, south = coefficients

    def step(below, here, above):
        columns = here.shape[2]
        return (
            middle * here
            + east * above
            + west * below
            + north * pltpu.roll(here, columns - 1, 2)
            + south * pltpu.roll(here, 1, 2)
        )

    start = [read(first - 2), read(first - 1), read(first)]
    once = [None, None, None]
    for r in range(first - 1, last + 1):
        once = [once[1], once[2], step(*start)]
        if r >= first + 1:
            write(r - 1, step(*once))
        if r < last:
            start = [start[1], start[2], read(r + 2)]


def model_rows(diffusivity, eastward, northward):
    levels, columns = diffusivity.shape
    place = lax.broadcasted_iota(jnp.int32, (levels, 3, columns), 1)
    speeds = jnp.where(place == 1, eastward[:, None, None], northward[:, None, None])
    return jnp.where(place == 0, diffusivity[:, None, :], speeds)


def coefficients_of(model, level):
    spread, u, w = (
        jnp.broadcast_to(model[level, i : i + 1, :], (8, model.shape[2])) for i in range(3)
    )
    u, w = 0.5 * u, 0.5 * w
    return 1.0 - 4.0 * spread, spread - u, spread + u, spread - w, spread + w


CHUNK = 64


def row_reader(level, var, first, size, own, low, high):
    span, columns = own.shape[2], own.shape[4]

    def read(r):
        ref, at = (low, r + span) if r < 0 else (own, r) if r < span else (high, r - span)
        return ref[var, level, at, first : first + size, :].reshape(-1, 8, columns)

    return read


def pack_rows(pair, identity, store, at):
    lanes = pair.shape[0] // 2
    turned = dot_rows(identity, pair)
    parts = [turned[:, i * lanes : (i + 1) * lanes].reshape(-1, SPAN, lanes) for i in range(2)]
    store[:, at : at + 2 * SPAN, :] = jnp.concatenate(parts, axis=1).astype(jnp.bfloat16)


def inner_kernel(variables, chunks, own, model, slabs, fields, packed, whole, sems):
    lanes, levels, span, columns = own.shape
    members = lanes // variables
    count = span - 2 * STEPS
    part = lanes // chunks
    copies = []
    for i in range(chunks):
        here = pl.ds(i * part, part)
        copies.append(pltpu.make_async_copy(own.at[here], whole.at[here], sems.at[i]))
        copies[-1].start()
    for copy in copies:
        copy.wait()
    view = whole.reshape(lanes * levels * span, columns)
    stride = variables * levels * span

    @pl.loop(0, levels)
    def _(level):
        coefficients = coefficients_of(model, level)
        for var in range(variables):

            def read(r):
                at = (var * levels + level) * span + r
                rows = view[pl.ds(at, members, stride=stride), :]
                slabs[var, level, r] = rows
                return rows.reshape(-1, 8, columns)

            def write(r, value):
                at = var * members
                value = value.reshape(members, columns).astype(jnp.bfloat16)
                fields[level, r - STEPS, at : at + members, :] = value

            forecast_rows(read, STEPS, span - STEPS, coefficients, write)

    identity = permutation(columns, 0)
    for level in range(levels):
        for r in range(0, count, 2):
            pair = fields[level, r : r + 2].reshape(2 * lanes, columns)
            pack_rows(pair, identity, packed, (level * count + r) * SPAN)


def inner(own, model, variables):
    lanes, levels, span, columns = own.shape
    members = lanes // variables
    blocks = columns // SPAN
    count = span - 2 * STEPS
    chunks = next(n for n in (4, 2, 1) if lanes % n == 0)
    return pl.pallas_call(
        functools.partial(inner_kernel, variables, chunks),
        out_shape=[
            jax.ShapeDtypeStruct((variables, levels, span, members, columns), jnp.float32),
            jax.ShapeDtypeStruct((levels, count, lanes, columns), jnp.bfloat16),
            jax.ShapeDtypeStruct((blocks, levels * count * SPAN, lanes), jnp.bfloat16),
        ],
        in_specs=hbm(1) + vmem(1),
        out_specs=vmem(3),
        scratch_shapes=[
            pltpu.VMEM((lanes, levels, span, columns), jnp.float32),
            pltpu.SemaphoreType.DMA((chunks,)),
        ],
        compiler_params=params(50),
        cost_estimate=cost(2 * 10**9, 4 * 2**20),
    )(own, model)


def outer_kernel(near, own, *rest):
    sides, rest = rest[:near], rest[near:]
    model, centre, grid, packed, fields, sems = rest
    variables, levels, span, members, columns = own.shape
    rows = variables * members
    pairs = (2 * EDGE + span) // 2

    copies = []
    for r in range(STEPS, span - STEPS):
        half, pair = divmod(r + EDGE, pairs)
        place = grid.at[:, pair, pl.ds(half * rows, rows)]
        copies.append(pltpu.make_async_copy(centre.at[:, r - STEPS], place, sems.at[r - STEPS]))
        copies[-1].start()

    @pl.loop(0, levels)
    def _(level):
        coefficients = coefficients_of(model, level)
        for var in range(variables):
            for first in range(0, members, CHUNK):

                def write(r, value):
                    value = value.reshape(CHUNK, columns).astype(jnp.bfloat16)
                    half, pair = divmod(r + EDGE, pairs)
                    at = half * rows + var * members + first
                    grid[level, pair, at : at + CHUNK, :] = value
                    if 0 <= r < span:
                        pair, half = divmod(r if r < STEPS else r - span + 2 * STEPS, 2)
                        at = half * rows + var * members + first
                        fields[level, pair, at : at + CHUNK, :] = value

                read = row_reader(level, var, first, CHUNK, own, sides[0], sides[-1])
                forecast_rows(read, -EDGE, STEPS, coefficients, write)
                forecast_rows(read, span - STEPS, span + EDGE, coefficients, write)

    identity = permutation(columns, 0)
    for level in range(levels):
        for pair in range(STEPS):
            at = (level * STEPS + pair) * 2 * SPAN
            pack_rows(fields[level, pair], identity, packed, at)
    for copy in copies:
        copy.wait()


def outer(dims, own, sides, model, centre):
    members, variables, levels, span, columns = dims
    lanes = members * variables
    blocks = columns // SPAN
    near = len(sides)
    pairs = (2 * EDGE + span) // 2
    return pl.pallas_call(
        functools.partial(outer_kernel, near),
        out_shape=[
            jax.ShapeDtypeStruct((levels, pairs, 2 * lanes, columns), jnp.bfloat16),
            jax.ShapeDtypeStruct((blocks, levels * 2 * STEPS * SPAN, lanes), jnp.bfloat16),
        ],
        in_specs=vmem(2 + near) + hbm(1),
        out_specs=vmem(2),
        scratch_shapes=[
            pltpu.VMEM((levels, STEPS, 2 * lanes, columns), jnp.bfloat16),
            pltpu.SemaphoreType.DMA((span - 2 * STEPS,)),
        ],
        compiler_params=params(16),
        cost_estimate=cost(2 * 10**9, 8 * 2**20),
    )(own, *sides, model, centre)


def pick_kernel(variables, together, grid, rim, cells, out, region, codes):
    levels, pairs, twice, columns = grid.shape
    rows = twice // 2
    members = rows // variables
    blocks, slots = cells.shape
    width = 2 * EDGE + SPAN
    part = pairs * width
    entries = levels * part
    share = rim.shape[1]

    orders = jnp.concatenate(
        [permutation(columns, -EDGE), permutation(columns, SPAN - EDGE)], axis=0
    )
    for level in range(levels):
        for pair in range(pairs):
            turned = dot_rows(orders, grid[level, pair]).astype(jnp.bfloat16)
            at = (level * pairs + pair) * width
            for first in range(2):
                for j in range(columns // width):
                    row = first * columns + j * width
                    region[2 * j + first, at : at + width, :] = turned[row : row + width, :]

    cell = cells[...]
    second = cell >= 2 * entries
    cell = jnp.where(second, cell - 2 * entries, cell)
    level = lax.shift_right_logical(cell, (2 * part).bit_length() - 1)
    inside = cell - level * (2 * part)
    lower = inside >= part
    code = level * part + jnp.where(lower, inside - part + entries, inside)
    codes[...] = jnp.where(second, code + 2 * entries, code).astype(jnp.float32)

    left = lax.broadcasted_iota(jnp.int32, (slots // 2, rows), 1) < members
    lane = lax.broadcasted_iota(jnp.int32, (slots, entries), 1).astype(jnp.float32)

    @pl.loop(0, blocks // together)
    def _(step):
        for i in range(together):
            block = step * together + i
            at = column_of(codes[pl.ds(block, 1), :])
            second = at >= 2.0 * entries
            at = jnp.where(second, at - 2.0 * entries, at)
            lower = at >= 1.0 * entries
            at = jnp.where(lower, at - 1.0 * entries, at)
            pick = jnp.where(lane == at, 1.0, 0.0).astype(jnp.bfloat16)
            found = dot(pick, region[block])
            total = jnp.where(lower, found[:, rows:], found[:, :rows])
            other = pltpu.roll(total, members, 1)
            to_left = jnp.where(second, other, total)[: slots // 2]
            to_right = jnp.where(second, total, other)[slots // 2 :]
            out[block, share:, :] = jnp.where(left, to_left, to_right).astype(jnp.bfloat16)
            out[block, :share, :] = rim[block]


def pick(variables, grid, rim, cells):
    levels, pairs, twice, columns = grid.shape
    blocks, slots = cells.shape
    _, share, lanes = rim.shape
    together = next(n for n in (4, 2, 1) if blocks % n == 0)
    return pl.pallas_call(
        functools.partial(pick_kernel, variables, together),
        out_shape=jax.ShapeDtypeStruct((blocks, share + slots // 2, lanes), jnp.bfloat16),
        in_specs=vmem(3),
        out_specs=pl.BlockSpec(memory_space=pltpu.VMEM),
        scratch_shapes=[
            pltpu.VMEM((blocks, levels * pairs * (2 * EDGE + SPAN), twice), jnp.bfloat16),
            pltpu.VMEM((blocks, slots), jnp.float32),
        ],
        compiler_params=params(20),
        cost_estimate=cost(4 * 10**9, 4 * 2**20),
    )(grid, rim, cells)


def join(a, b, left, members):
    return (
        jnp.where(left, a, pltpu.roll(b, members, 1)),
        jnp.where(left, pltpu.roll(a, members, 1), b),
    )


def left_lanes(shape):
    return lax.broadcasted_iota(jnp.int32, shape, 1) < shape[1] // 2


def deviations(states, raw, dev, at, size):
    groups, _, lanes = states.shape
    members = lanes // 2
    left = left_lanes((size, lanes))
    sums = [jnp.zeros((size, lanes), jnp.float32)] * 2
    for j in range(groups // 2):
        here = slice(j * lanes, (j + 1) * lanes)
        pair = join(
            states[2 * j, :size, :].astype(jnp.float32),
            states[2 * j + 1, :size, :].astype(jnp.float32),
            left,
            members,
        )
        for var in range(2):
            raw[var * size : (var + 1) * size, here] = pair[var]
        sums = [total + one for total, one in zip(sums, pair)]
    centre = jnp.concatenate([jnp.sum(x, axis=1, keepdims=True) for x in sums], axis=0)
    centre = centre * (1.0 / (groups * members))
    dev[at : at + 2 * size, :] = (raw[...] - centre).astype(jnp.bfloat16)
    return centre


def prepare_kernel(states, dev, centre, raw):
    mean = deviations(states, raw, dev, 0, states.shape[1])
    centre[...] = jnp.broadcast_to(mean, centre.shape)


def prepare(states):
    groups, near, lanes = states.shape
    total = groups * lanes // 2
    return pl.pallas_call(
        prepare_kernel,
        out_shape=[
            jax.ShapeDtypeStruct((2 * near, total), jnp.bfloat16),
            jax.ShapeDtypeStruct((2 * near, lanes), jnp.float32),
        ],
        in_specs=vmem(1),
        out_specs=vmem(2),
        scratch_shapes=[pltpu.VMEM((2 * near, total), jnp.float32)],
        compiler_params=params(6),
        cost_estimate=cost(10**8, 2 * 2**20),
    )(states)


def analyse_kernel(first, means, second, count, value, weight, out, raw, dev, obs, scaled_ref):
    groups, _, lanes = second.shape
    near = first.shape[0] // 2
    half = obs.shape[0] // 2
    far = second.shape[1] - half
    side = near + far
    slots = 2 * half
    members = lanes // 2
    total_members = groups * members
    left = left_lanes((half, lanes))

    for j in range(groups // 2):
        here = slice(j * lanes, (j + 1) * lanes)
        obs[:half, here], obs[half:, here] = join(
            second[2 * j, far:, :].astype(jnp.float32),
            second[2 * j + 1, far:, :].astype(jnp.float32),
            left,
            members,
        )

    used = lax.broadcasted_iota(jnp.int32, (1, slots), 1) < count[0, 0]
    root = column_of(jnp.where(used, jnp.sqrt(weight[...]), 0.0))
    observed = obs[...]
    mean = jnp.sum(observed, axis=1, keepdims=True) * (1.0 / total_members)
    scaled = (observed - mean) * root
    energy = jnp.sum(jnp.sum(scaled * scaled, axis=1, keepdims=True), axis=0, keepdims=True)
    scaled_ref[...] = scaled.astype(jnp.bfloat16)
    misfit = row_of(root * (column_of(value[...]) - mean))

    c = total_members - 1.0
    s = energy * (1.0 / total_members) + c
    inverse = 1.0 / s
    a = c * inverse
    p = 1.5 - 0.5 * a
    p2 = p * p
    p3 = p2 * p
    base = 1.5 * p - 0.5 * a * p3
    q0 = -0.75 - 0.5 * (p3 - 1.5 * a * p2)
    q1 = -0.5 * (0.75 * a * p - 1.5 * p2)
    q2 = -0.5 * (0.75 * p - 0.125 * a)
    small = dot_rows(scaled_ref[...], scaled_ref[...]) * inverse
    diagonal = eye(slots)
    square = dot3(small, small)
    tail = dot3(square, jnp.where(diagonal, q2, 0.0) + 0.0625 * small)
    poly = jnp.where(diagonal, q0, 0.0) + q1 * small + tail

    def apply(vector):
        inner_part = jnp.sum(poly * vector, axis=1, keepdims=True)
        return jnp.sum(small * inner_part, axis=0, keepdims=True) + base * vector

    gain = apply(apply(misfit)) * inverse
    stretch = jnp.sqrt(a)
    alpha, factor = stretch * base, stretch * inverse
    centre = deviations(second, raw, dev, 0, far)
    cross = jnp.concatenate(
        [dot_rows(first[...], scaled_ref[...]), dot_rows(dev[...], scaled_ref[...])], axis=0
    )
    centre = jnp.concatenate([means[:, 0:1], centre], axis=0)
    shift = centre + jnp.sum(cross * gain, axis=1, keepdims=True)
    mix = (dot3(cross, poly) * factor).astype(jnp.bfloat16)
    parts = ((first, 0, near, 0), (dev, 2 * near, far, near))
    for j in range(groups // 2):
        here = slice(j * lanes, (j + 1) * lanes)
        new = dot(mix, scaled_ref[:, here]) + shift
        for ref, at, size, row in parts:
            one = new[at : at + 2 * size] + alpha * ref[:, here].astype(jnp.float32)
            x, y = join(one[:size], one[size:], left_lanes((size, lanes)), members)
            out[2 * j, row : row + size, :] = x.astype(jnp.bfloat16)
            out[2 * j + 1, row : row + size, :] = y.astype(jnp.bfloat16)


def analyse(first, means, second, count, value, weight):
    groups, _, lanes = second.shape
    near = first.shape[0] // 2
    slots = value.shape[1]
    far = second.shape[1] - slots // 2
    total = groups * lanes // 2
    return pl.pallas_call(
        analyse_kernel,
        out_shape=jax.ShapeDtypeStruct((groups, near + far, lanes), jnp.bfloat16),
        in_specs=vmem(3) + smem(1) + vmem(2),
        out_specs=pl.BlockSpec(memory_space=pltpu.VMEM),
        scratch_shapes=[
            pltpu.VMEM((2 * far, total), jnp.float32),
            pltpu.VMEM((2 * far, total), jnp.bfloat16),
            pltpu.VMEM((slots, total), jnp.float32),
            pltpu.VMEM((slots, total), jnp.bfloat16),
        ],
        compiler_params=params(16),
        cost_estimate=cost(4 * 10**9, 4 * 2**20),
    )(first, means, second, count, value, weight)


def restore_kernel(blocks, out, turned):
    members, variables, levels, span, columns = out.shape
    lanes = members * variables
    identity = permutation(lanes, 0)
    near = span - 2 * STEPS
    for level in range(levels):
        for r in range(0, span, 2):
            if STEPS <= r < span - STEPS:
                at = level * near + r - STEPS
            else:
                at = levels * near + level * 2 * STEPS + (r if r < STEPS else r - near)
            both = blocks[:, at * SPAN : (at + 2) * SPAN, :].astype(jnp.float32)
            for i in range(2):
                one = both[:, i * SPAN : (i + 1) * SPAN, :].reshape(columns, lanes)
                rows = dot_rows(identity, one.astype(jnp.bfloat16))
                turned[level % 2, pl.ds(r + i, lanes, stride=span), :] = rows
        for var in range(variables):
            half = turned[level % 2, var * members * span : (var + 1) * members * span, :]
            out[:, var, level] = half.reshape(members, span, columns).astype(jnp.bfloat16)


def restore(dims, blocks):
    members, variables, levels, span, columns = dims
    return pl.pallas_call(
        restore_kernel,
        out_shape=jax.ShapeDtypeStruct((members, variables, levels, span, columns), jnp.bfloat16),
        in_specs=vmem(1),
        out_specs=pl.BlockSpec(memory_space=pltpu.VMEM),
        scratch_shapes=[pltpu.VMEM((2, variables * members * span, columns), jnp.float32)],
        compiler_params=params(8),
        cost_estimate=cost(2 * 10**9, 2 * 2**20),
    )(blocks)


def neighbours(field, axis):
    count = lax.axis_size(axis)
    low = lax.ppermute(field, axis, [(i, (i + 1) % count) for i in range(count)])
    if count == 2:
        return (low,)
    return low, lax.ppermute(field, axis, [((i + 1) % count, i) for i in range(count)])


def exchange(blocks):
    return lax.all_to_all(blocks, "grp", split_axis=0, concat_axis=0, tiled=True)


def on_device(start, diffusivity, eastward, northward, cells, count, value, weight):
    members, variables, levels, span, columns = dims = start.shape
    model = model_rows(diffusivity, eastward, northward)
    whole = start.reshape(members * variables, levels, span, columns)
    own, centre, near = inner(whole, model, variables)
    sides = neighbours(own, "tile")
    first, means = prepare(exchange(near))
    grid, rim = outer(dims, own, sides, model, centre)
    second = exchange(pick(variables, grid, rim, cells[0]))
    updated = analyse(first, means, second, count, value[0], weight[0])
    return restore(dims, exchange(updated))


def solution(mesh):
    return jax.shard_map(
        on_device,
        mesh=mesh,
        in_specs=(
            P("grp", None, None, "tile", None),
            P(),
            P(),
            P(),
            P("tile", None, None),
            P("tile", "grp"),
            P("tile", "grp", None),
            P("tile", "grp", None),
        ),
        out_specs=P("grp", None, None, "tile", None),
        check_vma=False,
    )
```

```python
import functools

import jax
import jax.numpy as jnp
from jax import lax
from jax.experimental import pallas as pl
from jax.experimental.pallas import tpu as pltpu
from jax.sharding import PartitionSpec as P

SPAN = 8
STEPS = 2
EDGE = SPAN // 2

ROWS = (((1,), (1,)), ((), ()))


def params(mebibytes, **kw):
    return pltpu.CompilerParams(vmem_limit_bytes=mebibytes * 2**20, **kw)


def cost(flops, size):
    return pl.CostEstimate(flops=flops, bytes_accessed=size, transcendentals=0)


def vmem(count):
    return [pl.BlockSpec(memory_space=pltpu.VMEM)] * count


def hbm(count):
    return [pl.BlockSpec(memory_space=pltpu.HBM)] * count


def smem(count):
    return [pl.BlockSpec(memory_space=pltpu.SMEM)] * count


def dot(a, b, **kw):
    return jnp.dot(a, b, preferred_element_type=jnp.float32, **kw)


def split(x):
    high = x.astype(jnp.bfloat16)
    return high, (x - high.astype(jnp.float32)).astype(jnp.bfloat16)


def dot3(a, b):
    (a_high, a_low), (b_high, b_low) = split(a), split(b)
    return dot(a_high, b_high) + (dot(a_high, b_low) + dot(a_low, b_high))


def dot_rows(a, b):
    return lax.dot_general(a, b, ROWS, preferred_element_type=jnp.float32)


def permutation(size, shift):
    row = lax.broadcasted_iota(jnp.int32, (size, size), 0)
    column = lax.broadcasted_iota(jnp.int32, (size, size), 1)
    return (lax.rem(row + shift + size, size) == column).astype(jnp.bfloat16)


def eye(size):
    row = lax.broadcasted_iota(jnp.int32, (size, size), 0)
    column = lax.broadcasted_iota(jnp.int32, (size, size), 1)
    return row == column


def column_of(row):
    return jnp.sum(jnp.where(eye(row.shape[1]), row, 0.0), axis=1, keepdims=True)


def row_of(column):
    return jnp.sum(jnp.where(eye(column.shape[0]), column, 0.0), axis=0, keepdims=True)


def forecast_rows(read, first, last, coefficients):
    middle, east, west, north, south = coefficients

    def step(below, here, above):
        columns = here.shape[2]
        return (
            middle * here
            + east * above
            + west * below
            + north * pltpu.roll(here, columns - 1, 2)
            + south * pltpu.roll(here, 1, 2)
        )

    rows, once, twice = [read(first - 2), read(first - 1)], [], []
    for r in range(first - 1, last + 1):
        rows.append(read(r + 1))
        once.append(step(*rows[-3:]))
        if r >= first + 1:
            new = step(*once[-3:])
            twice.append((r - 1, new.reshape(-1, new.shape[2]).astype(jnp.bfloat16)))
    return twice


def model_rows(diffusivity, eastward, northward):
    levels, columns = diffusivity.shape
    place = lax.broadcasted_iota(jnp.int32, (levels, 3, columns), 1)
    speeds = jnp.where(place == 1, eastward[:, None, None], northward[:, None, None])
    return jnp.where(place == 0, diffusivity[:, None, :], speeds)


def coefficients_of(model, level):
    spread, u, w = (
        jnp.broadcast_to(model[level, i : i + 1, :], (8, model.shape[2])) for i in range(3)
    )
    u, w = 0.5 * u, 0.5 * w
    return 1.0 - 4.0 * spread, spread - u, spread + u, spread - w, spread + w


def row_reader(level, var, own, low, high):
    span, columns = own.shape[2], own.shape[4]

    def read(r):
        ref, at = (low, r + span) if r < 0 else (own, r) if r < span else (high, r - span)
        return ref[var, level, at].reshape(-1, 8, columns)

    return read


def pack_rows(pairs, identity, store, first):
    lanes = pairs[0].shape[0] // 2
    packed = []
    for pair in pairs:
        turned = dot_rows(identity, pair)
        parts = [turned[:, i * lanes : (i + 1) * lanes].reshape(-1, SPAN, lanes) for i in range(2)]
        packed.append(jnp.concatenate(parts, axis=1).astype(jnp.bfloat16))
    for i, value in enumerate(packed):
        at = first + i * 2 * SPAN
        store[:, at : at + 2 * SPAN, :] = value


def inner_kernel(variables, own, model, slabs, fields, packed):
    lanes, _, span, columns = own.shape
    members = lanes // variables
    count = span - 2 * STEPS
    coefficients = coefficients_of(model, pl.program_id(0))
    view = own.reshape(lanes * span, columns)
    reads, made = [], []
    for var in range(variables):

        def read(r):
            rows = view[pl.ds(var * span + r, members, stride=variables * span), :]
            reads.append((var, r, rows))
            return rows.reshape(-1, 8, columns)

        for r, value in forecast_rows(read, STEPS, span - STEPS, coefficients):
            made.append((var, r, value))
    identity = permutation(columns, 0)
    pairs = []
    for first in range(STEPS, span - STEPS, 2):
        rows = [one for r in (first, first + 1) for _, at, one in made if at == r]
        pairs.append(jnp.concatenate(rows, axis=0))
    pack_rows(pairs, identity, packed, 0)
    for var, r, value in made:
        fields[0, r - STEPS, var * members : (var + 1) * members, :] = value
    for var, r, rows in reads:
        slabs[var, 0, r] = rows


def inner(own, model, variables):
    lanes, levels, span, columns = own.shape
    members = lanes // variables
    blocks = columns // SPAN
    count = span - 2 * STEPS
    return pl.pallas_call(
        functools.partial(inner_kernel, variables),
        grid=(levels,),
        out_shape=[
            jax.ShapeDtypeStruct((variables, levels, span, members, columns), jnp.float32),
            jax.ShapeDtypeStruct((levels, count, lanes, columns), jnp.bfloat16),
            jax.ShapeDtypeStruct((blocks, levels * count * SPAN, lanes), jnp.bfloat16),
        ],
        in_specs=[pl.BlockSpec((lanes, 1, span, columns), lambda level: (0, level, 0, 0))] + vmem(1),
        out_specs=[
            pl.BlockSpec((variables, 1, span, members, columns), lambda level: (0, level, 0, 0, 0)),
            pl.BlockSpec((1, count, lanes, columns), lambda level: (level, 0, 0, 0)),
            pl.BlockSpec((blocks, count * SPAN, lanes), lambda level: (0, level, 0)),
        ],
        compiler_params=params(50),
        cost_estimate=cost(2 * 10**9, 4 * 2**20),
    )(own, model)


def outer_kernel(near, own, *rest):
    sides, rest = rest[:near], rest[near:]
    model, centre, grid, packed, fields, sems = rest
    variables, levels, span, members, columns = own.shape
    rows = variables * members
    pairs = (2 * EDGE + span) // 2

    copies = []
    for r in range(STEPS, span - STEPS):
        half, pair = divmod(r + EDGE, pairs)
        place = grid.at[:, pair, pl.ds(half * rows, rows)]
        copies.append(pltpu.make_async_copy(centre.at[:, r - STEPS], place, sems.at[r - STEPS]))
        copies[-1].start()

    @pl.loop(0, levels)
    def _(level):
        coefficients = coefficients_of(model, level)
        made = []
        for var in range(variables):
            read = row_reader(level, var, own, sides[0], sides[-1])
            for first, last in ((-EDGE, STEPS), (span - STEPS, span + EDGE)):
                for r, value in forecast_rows(read, first, last, coefficients):
                    made.append((var, r, value))
        for var, r, value in made:
            half, pair = divmod(r + EDGE, pairs)
            at = half * rows + var * members
            grid[level, pair, at : at + members, :] = value
            if 0 <= r < span:
                pair, half = divmod(r if r < STEPS else r - span + 2 * STEPS, 2)
                at = half * rows + var * members
                fields[level, pair, at : at + members, :] = value

    identity = permutation(columns, 0)
    for level in range(0, levels, 2):
        batch = [fields[at, pair] for at in range(level, min(levels, level + 2)) for pair in range(STEPS)]
        pack_rows(batch, identity, packed, level * STEPS * 2 * SPAN)
    for copy in copies:
        copy.wait()


def outer(dims, own, sides, model, centre):
    members, variables, levels, span, columns = dims
    lanes = members * variables
    blocks = columns // SPAN
    near = len(sides)
    pairs = (2 * EDGE + span) // 2
    return pl.pallas_call(
        functools.partial(outer_kernel, near),
        out_shape=[
            jax.ShapeDtypeStruct((levels, pairs, 2 * lanes, columns), jnp.bfloat16),
            jax.ShapeDtypeStruct((blocks, levels * 2 * STEPS * SPAN, lanes), jnp.bfloat16),
        ],
        in_specs=vmem(2 + near) + hbm(1),
        out_specs=vmem(2),
        scratch_shapes=[
            pltpu.VMEM((levels, STEPS, 2 * lanes, columns), jnp.bfloat16),
            pltpu.SemaphoreType.DMA((span - 2 * STEPS,)),
        ],
        compiler_params=params(16),
        cost_estimate=cost(2 * 10**9, 8 * 2**20),
    )(own, *sides, model, centre)


def pick_kernel(variables, together, grid, rim, cells, out, region, codes):
    levels, pairs, twice, columns = grid.shape
    rows = twice // 2
    members = rows // variables
    blocks, slots = cells.shape
    width = 2 * EDGE + SPAN
    part = pairs * width
    entries = levels * part
    share = rim.shape[1]

    orders = jnp.concatenate(
        [permutation(columns, -EDGE), permutation(columns, SPAN - EDGE)], axis=0
    )
    batch = next(n for n in (4, 2, 1) if pairs % n == 0)
    for level in range(levels):
        for start in range(0, pairs, batch):
            turned = [
                dot_rows(orders, grid[level, start + i]).astype(jnp.bfloat16) for i in range(batch)
            ]
            for i, value in enumerate(turned):
                at = (level * pairs + start + i) * width
                for first in range(2):
                    for j in range(columns // width):
                        row = first * columns + j * width
                        region[2 * j + first, at : at + width, :] = value[row : row + width, :]

    cell = cells[...]
    second = cell >= 2 * entries
    cell = jnp.where(second, cell - 2 * entries, cell)
    level = lax.shift_right_logical(cell, (2 * part).bit_length() - 1)
    inside = cell - level * (2 * part)
    lower = inside >= part
    code = level * part + jnp.where(lower, inside - part + entries, inside)
    codes[...] = jnp.where(second, code + 2 * entries, code).astype(jnp.float32)

    left = lax.broadcasted_iota(jnp.int32, (slots // 2, rows), 1) < members
    lane = lax.broadcasted_iota(jnp.int32, (slots, entries), 1).astype(jnp.float32)

    @pl.loop(0, blocks // together)
    def _(step):
        made = []
        for i in range(together):
            block = step * together + i
            at = column_of(codes[pl.ds(block, 1), :])
            second = at >= 2.0 * entries
            at = jnp.where(second, at - 2.0 * entries, at)
            lower = at >= 1.0 * entries
            at = jnp.where(lower, at - 1.0 * entries, at)
            pick = jnp.where(lane == at, 1.0, 0.0).astype(jnp.bfloat16)
            found = dot(pick, region[block])
            total = jnp.where(lower, found[:, rows:], found[:, :rows])
            other = pltpu.roll(total, members, 1)
            to_left = jnp.where(second, other, total)[: slots // 2]
            to_right = jnp.where(second, total, other)[slots // 2 :]
            made.append(jnp.where(left, to_left, to_right).astype(jnp.bfloat16))
        for i, value in enumerate(made):
            block = step * together + i
            out[block, share:, :] = value
            out[block, :share, :] = rim[block]


def pick(variables, grid, rim, cells):
    levels, pairs, twice, columns = grid.shape
    blocks, slots = cells.shape
    _, share, lanes = rim.shape
    together = next(n for n in (4, 2, 1) if blocks % n == 0)
    return pl.pallas_call(
        functools.partial(pick_kernel, variables, together),
        out_shape=jax.ShapeDtypeStruct((blocks, share + slots // 2, lanes), jnp.bfloat16),
        in_specs=vmem(3),
        out_specs=pl.BlockSpec(memory_space=pltpu.VMEM),
        scratch_shapes=[
            pltpu.VMEM((blocks, levels * pairs * (2 * EDGE + SPAN), twice), jnp.bfloat16),
            pltpu.VMEM((blocks, slots), jnp.float32),
        ],
        compiler_params=params(20),
        cost_estimate=cost(4 * 10**9, 4 * 2**20),
    )(grid, rim, cells)


def join(a, b, left, members):
    return (
        jnp.where(left, a, pltpu.roll(b, members, 1)),
        jnp.where(left, pltpu.roll(a, members, 1), b),
    )


def batches(count, size):
    return [range(at, min(count, at + size)) for at in range(0, count, size)]


def left_lanes(shape):
    return lax.broadcasted_iota(jnp.int32, shape, 1) < shape[1] // 2


def deviations(states, raw, dev, at, size):
    groups, _, lanes = states.shape
    members = lanes // 2
    left = left_lanes((size, lanes))
    sums = [jnp.zeros((size, lanes), jnp.float32)] * 2
    for batch in batches(groups // 2, 4):
        made = [
            join(
                states[2 * j, :size, :].astype(jnp.float32),
                states[2 * j + 1, :size, :].astype(jnp.float32),
                left,
                members,
            )
            for j in batch
        ]
        for j, pair in zip(batch, made):
            here = slice(j * lanes, (j + 1) * lanes)
            for var in range(2):
                raw[var * size : (var + 1) * size, here] = pair[var]
            sums = [total + one for total, one in zip(sums, pair)]
    centre = jnp.concatenate([jnp.sum(x, axis=1, keepdims=True) for x in sums], axis=0)
    centre = centre * (1.0 / (groups * members))
    dev[at : at + 2 * size, :] = (raw[...] - centre).astype(jnp.bfloat16)
    return centre


def prepare_kernel(states, dev, centre, raw):
    mean = deviations(states, raw, dev, 0, states.shape[1])
    centre[...] = jnp.broadcast_to(mean, centre.shape)


def prepare(states):
    groups, near, lanes = states.shape
    total = groups * lanes // 2
    return pl.pallas_call(
        prepare_kernel,
        out_shape=[
            jax.ShapeDtypeStruct((2 * near, total), jnp.bfloat16),
            jax.ShapeDtypeStruct((2 * near, lanes), jnp.float32),
        ],
        in_specs=vmem(1),
        out_specs=vmem(2),
        scratch_shapes=[pltpu.VMEM((2 * near, total), jnp.float32)],
        compiler_params=params(6),
        cost_estimate=cost(10**8, 2 * 2**20),
    )(states)


def analyse_kernel(first, means, second, count, value, weight, out, raw, dev, obs, scaled_ref):
    groups, _, lanes = second.shape
    near = first.shape[0] // 2
    half = obs.shape[0] // 2
    far = second.shape[1] - half
    side = near + far
    slots = 2 * half
    members = lanes // 2
    total_members = groups * members
    left = left_lanes((half, lanes))

    for batch in batches(groups // 2, 4):
        made = [
            join(
                second[2 * j, far:, :].astype(jnp.float32),
                second[2 * j + 1, far:, :].astype(jnp.float32),
                left,
                members,
            )
            for j in batch
        ]
        for j, pair in zip(batch, made):
            here = slice(j * lanes, (j + 1) * lanes)
            obs[:half, here], obs[half:, here] = pair

    used = lax.broadcasted_iota(jnp.int32, (1, slots), 1) < count[0, 0]
    root = column_of(jnp.where(used, jnp.sqrt(weight[...]), 0.0))
    observed = obs[...]
    mean = jnp.sum(observed, axis=1, keepdims=True) * (1.0 / total_members)
    scaled = (observed - mean) * root
    energy = jnp.sum(jnp.sum(scaled * scaled, axis=1, keepdims=True), axis=0, keepdims=True)
    scaled_ref[...] = scaled.astype(jnp.bfloat16)
    misfit = row_of(root * (column_of(value[...]) - mean))

    c = total_members - 1.0
    s = energy * (1.0 / total_members) + c
    inverse = 1.0 / s
    a = c * inverse
    p = 1.5 - 0.5 * a
    p2 = p * p
    p3 = p2 * p
    base = 1.5 * p - 0.5 * a * p3
    q0 = -0.75 - 0.5 * (p3 - 1.5 * a * p2)
    q1 = -0.5 * (0.75 * a * p - 1.5 * p2)
    q2 = -0.5 * (0.75 * p - 0.125 * a)
    small = dot_rows(scaled_ref[...], scaled_ref[...]) * inverse
    diagonal = eye(slots)
    square = dot3(small, small)
    tail = dot3(square, jnp.where(diagonal, q2, 0.0) + 0.0625 * small)
    poly = jnp.where(diagonal, q0, 0.0) + q1 * small + tail

    def apply(vector):
        inner_part = jnp.sum(poly * vector, axis=1, keepdims=True)
        return jnp.sum(small * inner_part, axis=0, keepdims=True) + base * vector

    gain = apply(apply(misfit)) * inverse
    stretch = jnp.sqrt(a)
    alpha, factor = stretch * base, stretch * inverse
    centre = deviations(second, raw, dev, 0, far)
    cross = jnp.concatenate(
        [dot_rows(first[...], scaled_ref[...]), dot_rows(dev[...], scaled_ref[...])], axis=0
    )
    centre = jnp.concatenate([means[:, 0:1], centre], axis=0)
    shift = centre + jnp.sum(cross * gain, axis=1, keepdims=True)
    mix = (dot3(cross, poly) * factor).astype(jnp.bfloat16)
    parts = ((first, 0, near, 0), (dev, 2 * near, far, near))
    for batch in batches(groups // 2, 2):
        made = []
        for j in batch:
            here = slice(j * lanes, (j + 1) * lanes)
            new = dot(mix, scaled_ref[:, here]) + shift
            for ref, at, size, row in parts:
                one = new[at : at + 2 * size] + alpha * ref[:, here].astype(jnp.float32)
                pair = join(one[:size], one[size:], left_lanes((size, lanes)), members)
                made += [(2 * j + i, row, x.astype(jnp.bfloat16)) for i, x in enumerate(pair)]
        for group, row, value in made:
            out[group, row : row + value.shape[0], :] = value


def analyse(first, means, second, count, value, weight):
    groups, _, lanes = second.shape
    near = first.shape[0] // 2
    slots = value.shape[1]
    far = second.shape[1] - slots // 2
    total = groups * lanes // 2
    return pl.pallas_call(
        analyse_kernel,
        out_shape=jax.ShapeDtypeStruct((groups, near + far, lanes), jnp.bfloat16),
        in_specs=vmem(3) + smem(1) + vmem(2),
        out_specs=pl.BlockSpec(memory_space=pltpu.VMEM),
        scratch_shapes=[
            pltpu.VMEM((2 * far, total), jnp.float32),
            pltpu.VMEM((2 * far, total), jnp.bfloat16),
            pltpu.VMEM((slots, total), jnp.float32),
            pltpu.VMEM((slots, total), jnp.bfloat16),
        ],
        compiler_params=params(16),
        cost_estimate=cost(4 * 10**9, 4 * 2**20),
    )(first, means, second, count, value, weight)


def restore_kernel(blocks, out, turned):
    members, variables, levels, span, columns = out.shape
    lanes = members * variables
    identity = permutation(lanes, 0)
    near = span - 2 * STEPS
    for level in range(levels):
        made = []
        for r in range(0, span, 2):
            if STEPS <= r < span - STEPS:
                at = level * near + r - STEPS
            else:
                at = levels * near + level * 2 * STEPS + (r if r < STEPS else r - near)
            both = blocks[:, at * SPAN : (at + 2) * SPAN, :].astype(jnp.float32)
            for i in range(2):
                one = both[:, i * SPAN : (i + 1) * SPAN, :].reshape(columns, lanes)
                made.append((r + i, dot_rows(identity, one.astype(jnp.bfloat16))))
        for r, rows in made:
            turned[level % 2, pl.ds(r, lanes, stride=span), :] = rows
        for var in range(variables):
            half = turned[level % 2, var * members * span : (var + 1) * members * span, :]
            out[:, var, level] = half.reshape(members, span, columns).astype(jnp.bfloat16)


def restore(dims, blocks):
    members, variables, levels, span, columns = dims
    return pl.pallas_call(
        restore_kernel,
        out_shape=jax.ShapeDtypeStruct((members, variables, levels, span, columns), jnp.bfloat16),
        in_specs=vmem(1),
        out_specs=pl.BlockSpec(memory_space=pltpu.VMEM),
        scratch_shapes=[pltpu.VMEM((2, variables * members * span, columns), jnp.float32)],
        compiler_params=params(8),
        cost_estimate=cost(2 * 10**9, 2 * 2**20),
    )(blocks)


def neighbours(field, axis):
    count = lax.axis_size(axis)
    low = lax.ppermute(field, axis, [(i, (i + 1) % count) for i in range(count)])
    if count == 2:
        return (low,)
    return low, lax.ppermute(field, axis, [((i + 1) % count, i) for i in range(count)])


def exchange(blocks):
    return lax.all_to_all(blocks, "grp", split_axis=0, concat_axis=0, tiled=True)


def on_device(start, diffusivity, eastward, northward, cells, count, value, weight):
    members, variables, levels, span, columns = dims = start.shape
    model = model_rows(diffusivity, eastward, northward)
    whole = start.reshape(members * variables, levels, span, columns)
    own, centre, near = inner(whole, model, variables)
    sides = neighbours(own, "tile")
    first, means = prepare(exchange(near))
    grid, rim = outer(dims, own, sides, model, centre)
    second = exchange(pick(variables, grid, rim, cells[0]))
    updated = analyse(first, means, second, count, value[0], weight[0])
    return restore(dims, exchange(updated))


def solution(mesh):
    return jax.shard_map(
        on_device,
        mesh=mesh,
        in_specs=(
            P("grp", None, None, "tile", None),
            P(),
            P(),
            P(),
            P("tile", None, None),
            P("tile", "grp"),
            P("tile", "grp", None),
            P("tile", "grp", None),
        ),
        out_specs=P("grp", None, None, "tile", None),
        check_vma=False,
    )
```

```python
import functools

import jax
import jax.numpy as jnp
from jax import lax
from jax.experimental import pallas as pl
from jax.experimental.pallas import tpu as pltpu
from jax.sharding import PartitionSpec as P

SPAN = 8
STEPS = 2
EDGE = SPAN // 2

ROWS = (((1,), (1,)), ((), ()))


def params(mebibytes, **kw):
    return pltpu.CompilerParams(vmem_limit_bytes=mebibytes * 2**20, **kw)


def cost(flops, size):
    return pl.CostEstimate(flops=flops, bytes_accessed=size, transcendentals=0)


def vmem(count):
    return [pl.BlockSpec(memory_space=pltpu.VMEM)] * count


def hbm(count):
    return [pl.BlockSpec(memory_space=pltpu.HBM)] * count


def smem(count):
    return [pl.BlockSpec(memory_space=pltpu.SMEM)] * count


def dot(a, b, **kw):
    return jnp.dot(a, b, preferred_element_type=jnp.float32, **kw)


def split(x):
    high = x.astype(jnp.bfloat16)
    return high, (x - high.astype(jnp.float32)).astype(jnp.bfloat16)


def dot3(a, b):
    (a_high, a_low), (b_high, b_low) = split(a), split(b)
    return dot(a_high, b_high) + (dot(a_high, b_low) + dot(a_low, b_high))


def dot_rows(a, b):
    return lax.dot_general(a, b, ROWS, preferred_element_type=jnp.float32)


def permutation(size, shift):
    row = lax.broadcasted_iota(jnp.int32, (size, size), 0)
    column = lax.broadcasted_iota(jnp.int32, (size, size), 1)
    return (lax.rem(row + shift + size, size) == column).astype(jnp.bfloat16)


def eye(size):
    row = lax.broadcasted_iota(jnp.int32, (size, size), 0)
    column = lax.broadcasted_iota(jnp.int32, (size, size), 1)
    return row == column


def column_of(row):
    return jnp.sum(jnp.where(eye(row.shape[1]), row, 0.0), axis=1, keepdims=True)


def row_of(column):
    return jnp.sum(jnp.where(eye(column.shape[0]), column, 0.0), axis=0, keepdims=True)


def forecast_rows(read, first, last, coefficients):
    middle, east, west, north, south = coefficients

    def step(below, here, above):
        columns = here.shape[2]
        return (
            middle * here
            + east * above
            + west * below
            + north * pltpu.roll(here, columns - 1, 2)
            + south * pltpu.roll(here, 1, 2)
        )

    rows, once, twice = [read(first - 2), read(first - 1)], [], []
    for r in range(first - 1, last + 1):
        rows.append(read(r + 1))
        once.append(step(*rows[-3:]))
        if r >= first + 1:
            new = step(*once[-3:])
            twice.append((r - 1, new.reshape(-1, new.shape[2]).astype(jnp.bfloat16)))
    return twice


def model_rows(diffusivity, eastward, northward):
    levels, columns = diffusivity.shape
    place = lax.broadcasted_iota(jnp.int32, (levels, 3, columns), 1)
    speeds = jnp.where(place == 1, eastward[:, None, None], northward[:, None, None])
    return jnp.where(place == 0, diffusivity[:, None, :], speeds)


def coefficients_of(model, level):
    spread, u, w = (
        jnp.broadcast_to(model[level, i : i + 1, :], (8, model.shape[2])) for i in range(3)
    )
    u, w = 0.5 * u, 0.5 * w
    return 1.0 - 4.0 * spread, spread - u, spread + u, spread - w, spread + w


def row_reader(level, var, own, low, high):
    span, columns = own.shape[2], own.shape[4]

    def read(r):
        ref, at = (low, r + span) if r < 0 else (own, r) if r < span else (high, r - span)
        return ref[var, level, at].reshape(-1, 8, columns)

    return read


def pack_rows(pairs, identity, store, first):
    lanes = pairs[0].shape[0] // 2
    packed = []
    for pair in pairs:
        turned = dot_rows(identity, pair)
        parts = [turned[:, i * lanes : (i + 1) * lanes].reshape(-1, SPAN, lanes) for i in range(2)]
        packed.append(jnp.concatenate(parts, axis=1).astype(jnp.bfloat16))
    for i, value in enumerate(packed):
        at = first + i * 2 * SPAN
        store[:, at : at + 2 * SPAN, :] = value


def inner_kernel(own, model, slabs, fields, packed):
    members, _, _, span, columns = own.shape
    variables = fields.shape[2] // members
    level, var = pl.program_id(0), pl.program_id(1)
    coefficients = coefficients_of(model, level)
    view = own.reshape(members * span, columns)
    reads = []

    def read(r):
        reads.append((r, view[pl.ds(r, members, stride=span), :]))
        return reads[-1][1].reshape(-1, 8, columns)

    made = forecast_rows(read, STEPS, span - STEPS, coefficients)
    at = pl.multiple_of(var * members, members)
    for r, value in made:
        fields[0, r - STEPS, pl.ds(at, members), :] = value
    for r, rows in reads:
        slabs[0, 0, r] = rows

    @pl.when(var == variables - 1)
    def _():
        identity = permutation(columns, 0)
        pairs = [
            fields[0, r : r + 2].reshape(2 * variables * members, columns)
            for r in range(0, span - 2 * STEPS, 2)
        ]
        pack_rows(pairs, identity, packed, 0)


def inner(own, model):
    members, variables, levels, span, columns = own.shape
    lanes = variables * members
    blocks = columns // SPAN
    count = span - 2 * STEPS
    return pl.pallas_call(
        inner_kernel,
        grid=(levels, variables),
        out_shape=[
            jax.ShapeDtypeStruct((variables, levels, span, members, columns), jnp.float32),
            jax.ShapeDtypeStruct((levels, count, lanes, columns), jnp.bfloat16),
            jax.ShapeDtypeStruct((blocks, levels * count * SPAN, lanes), jnp.bfloat16),
        ],
        in_specs=[pl.BlockSpec((members, 1, 1, span, columns), lambda level, var: (0, var, level, 0, 0))]
        + vmem(1),
        out_specs=[
            pl.BlockSpec((1, 1, span, members, columns), lambda level, var: (var, level, 0, 0, 0)),
            pl.BlockSpec((1, count, lanes, columns), lambda level, var: (level, 0, 0, 0)),
            pl.BlockSpec((blocks, count * SPAN, lanes), lambda level, var: (0, level, 0)),
        ],
        compiler_params=params(50),
        cost_estimate=cost(2 * 10**9, 4 * 2**20),
    )(own, model)


def outer_kernel(near, own, *rest):
    sides, rest = rest[:near], rest[near:]
    model, centre, grid, packed, fields, sems = rest
    variables, levels, span, members, columns = own.shape
    rows = variables * members
    pairs = (2 * EDGE + span) // 2

    copies = []
    for r in range(STEPS, span - STEPS):
        half, pair = divmod(r + EDGE, pairs)
        place = grid.at[:, pair, pl.ds(half * rows, rows)]
        copies.append(pltpu.make_async_copy(centre.at[:, r - STEPS], place, sems.at[r - STEPS]))
        copies[-1].start()

    @pl.loop(0, levels)
    def _(level):
        coefficients = coefficients_of(model, level)
        made = []
        for var in range(variables):
            read = row_reader(level, var, own, sides[0], sides[-1])
            for first, last in ((-EDGE, STEPS), (span - STEPS, span + EDGE)):
                for r, value in forecast_rows(read, first, last, coefficients):
                    made.append((var, r, value))
        for var, r, value in made:
            half, pair = divmod(r + EDGE, pairs)
            at = half * rows + var * members
            grid[level, pair, at : at + members, :] = value
            if 0 <= r < span:
                pair, half = divmod(r if r < STEPS else r - span + 2 * STEPS, 2)
                at = half * rows + var * members
                fields[level, pair, at : at + members, :] = value

    identity = permutation(columns, 0)
    for level in range(0, levels, 2):
        batch = [fields[at, pair] for at in range(level, min(levels, level + 2)) for pair in range(STEPS)]
        pack_rows(batch, identity, packed, level * STEPS * 2 * SPAN)
    for copy in copies:
        copy.wait()


def outer(dims, own, sides, model, centre):
    members, variables, levels, span, columns = dims
    lanes = members * variables
    blocks = columns // SPAN
    near = len(sides)
    pairs = (2 * EDGE + span) // 2
    return pl.pallas_call(
        functools.partial(outer_kernel, near),
        out_shape=[
            jax.ShapeDtypeStruct((levels, pairs, 2 * lanes, columns), jnp.bfloat16),
            jax.ShapeDtypeStruct((blocks, levels * 2 * STEPS * SPAN, lanes), jnp.bfloat16),
        ],
        in_specs=vmem(2 + near) + hbm(1),
        out_specs=vmem(2),
        scratch_shapes=[
            pltpu.VMEM((levels, STEPS, 2 * lanes, columns), jnp.bfloat16),
            pltpu.SemaphoreType.DMA((span - 2 * STEPS,)),
        ],
        compiler_params=params(16),
        cost_estimate=cost(2 * 10**9, 8 * 2**20),
    )(own, *sides, model, centre)


def pick_kernel(variables, together, grid, rim, cells, out, region, codes):
    levels, pairs, twice, columns = grid.shape
    rows = twice // 2
    members = rows // variables
    blocks, slots = cells.shape
    width = 2 * EDGE + SPAN
    part = pairs * width
    entries = levels * part
    share = rim.shape[1]

    orders = jnp.concatenate(
        [permutation(columns, -EDGE), permutation(columns, SPAN - EDGE)], axis=0
    )
    batch = next(n for n in (4, 2, 1) if pairs % n == 0)
    for level in range(levels):
        for start in range(0, pairs, batch):
            turned = [
                dot_rows(orders, grid[level, start + i]).astype(jnp.bfloat16) for i in range(batch)
            ]
            for i, value in enumerate(turned):
                at = (level * pairs + start + i) * width
                for first in range(2):
                    for j in range(columns // width):
                        row = first * columns + j * width
                        region[2 * j + first, at : at + width, :] = value[row : row + width, :]

    cell = cells[...]
    second = cell >= 2 * entries
    cell = jnp.where(second, cell - 2 * entries, cell)
    level = lax.shift_right_logical(cell, (2 * part).bit_length() - 1)
    inside = cell - level * (2 * part)
    lower = inside >= part
    code = level * part + jnp.where(lower, inside - part + entries, inside)
    codes[...] = jnp.where(second, code + 2 * entries, code).astype(jnp.float32)

    left = lax.broadcasted_iota(jnp.int32, (slots // 2, rows), 1) < members
    lane = lax.broadcasted_iota(jnp.int32, (slots, entries), 1).astype(jnp.float32)

    @pl.loop(0, blocks // together)
    def _(step):
        made = []
        for i in range(together):
            block = step * together + i
            at = column_of(codes[pl.ds(block, 1), :])
            second = at >= 2.0 * entries
            at = jnp.where(second, at - 2.0 * entries, at)
            lower = at >= 1.0 * entries
            at = jnp.where(lower, at - 1.0 * entries, at)
            pick = jnp.where(lane == at, 1.0, 0.0).astype(jnp.bfloat16)
            found = dot(pick, region[block])
            total = jnp.where(lower, found[:, rows:], found[:, :rows])
            other = pltpu.roll(total, members, 1)
            to_left = jnp.where(second, other, total)[: slots // 2]
            to_right = jnp.where(second, total, other)[slots // 2 :]
            made.append(jnp.where(left, to_left, to_right).astype(jnp.bfloat16))
        for i, value in enumerate(made):
            block = step * together + i
            out[block, share:, :] = value
            out[block, :share, :] = rim[block]


def pick(variables, grid, rim, cells):
    levels, pairs, twice, columns = grid.shape
    blocks, slots = cells.shape
    _, share, lanes = rim.shape
    together = next(n for n in (4, 2, 1) if blocks % n == 0)
    return pl.pallas_call(
        functools.partial(pick_kernel, variables, together),
        out_shape=jax.ShapeDtypeStruct((blocks, share + slots // 2, lanes), jnp.bfloat16),
        in_specs=vmem(3),
        out_specs=pl.BlockSpec(memory_space=pltpu.VMEM),
        scratch_shapes=[
            pltpu.VMEM((blocks, levels * pairs * (2 * EDGE + SPAN), twice), jnp.bfloat16),
            pltpu.VMEM((blocks, slots), jnp.float32),
        ],
        compiler_params=params(20),
        cost_estimate=cost(4 * 10**9, 4 * 2**20),
    )(grid, rim, cells)


def batches(count, size):
    return [range(at, min(count, at + size)) for at in range(0, count, size)]


def left_lanes(shape):
    return lax.broadcasted_iota(jnp.int32, shape, 1) < shape[1] // 2


def half_sums(total, left):
    return (
        jnp.sum(jnp.where(left, total, 0.0), axis=1, keepdims=True),
        jnp.sum(jnp.where(left, 0.0, total), axis=1, keepdims=True),
    )


def deviations(states, size, dev):
    groups, _, lanes = states.shape
    left = left_lanes((size, lanes))
    total = jnp.zeros((size, lanes), jnp.float32)
    for group in range(groups):
        total += states[group, :size, :].astype(jnp.float32)
    means = [x * (2.0 / (groups * lanes)) for x in half_sums(total, left)]
    mean = jnp.where(left, *means)
    for group in range(groups):
        here = slice(group * lanes, (group + 1) * lanes)
        one = states[group, :size, :].astype(jnp.float32) - mean
        dev[:, here] = one.astype(jnp.bfloat16)
    return mean


def prepare_kernel(states, dev, mean):
    mean[...] = deviations(states, states.shape[1], dev)


def prepare(states):
    groups, near, lanes = states.shape
    return pl.pallas_call(
        prepare_kernel,
        out_shape=[
            jax.ShapeDtypeStruct((near, groups * lanes), jnp.bfloat16),
            jax.ShapeDtypeStruct((near, lanes), jnp.float32),
        ],
        in_specs=vmem(1),
        out_specs=vmem(2),
        compiler_params=params(6),
        cost_estimate=cost(10**8, 2 * 2**20),
    )(states)


def analyse_kernel(first, first_mean, second, count, value, weight, out, dev, scaled_ref):
    groups, _, lanes = second.shape
    near = first.shape[0]
    slots = value.shape[1]
    half = slots // 2
    far = second.shape[1] - half
    members = lanes // 2
    total_members = groups * members
    left = left_lanes((half, lanes))

    used = lax.broadcasted_iota(jnp.int32, (1, slots), 1) < count[0, 0]
    root = column_of(jnp.where(used, jnp.sqrt(weight[...]), 0.0))
    total = jnp.zeros((half, lanes), jnp.float32)
    for group in range(groups):
        total += second[group, far:, :].astype(jnp.float32)
    means = [x * (1.0 / total_members) for x in half_sums(total, left)]
    mean = jnp.concatenate(means, axis=0)
    mean_lane = jnp.where(left, *means)
    root_lane = jnp.where(left, root[:half], root[half:])
    squares = jnp.zeros((half, lanes), jnp.float32)
    for batch in batches(groups, 4):
        made = []
        for group in batch:
            one = (second[group, far:, :].astype(jnp.float32) - mean_lane) * root_lane
            squares += one * one
            made.append((group, one, pltpu.roll(one, members, 1)))
        for group, one, turned in made:
            here = slice(group * lanes, (group + 1) * lanes)
            rows = (
                jnp.where(left, one, 0.0),
                jnp.where(left, turned, 0.0),
                jnp.where(left, 0.0, turned),
                jnp.where(left, 0.0, one),
            )
            for i, row in enumerate(rows):
                scaled_ref[i * half : (i + 1) * half, here] = row.astype(jnp.bfloat16)
    energy = jnp.sum(jnp.sum(squares, axis=1, keepdims=True), axis=0, keepdims=True)
    misfit = row_of(root * (column_of(value[...]) - mean))

    c = total_members - 1.0
    s = energy * (1.0 / total_members) + c
    inverse = 1.0 / s
    a = c * inverse
    p = 1.5 - 0.5 * a
    p2 = p * p
    p3 = p2 * p
    base = 1.5 * p - 0.5 * a * p3
    q0 = -0.75 - 0.5 * (p3 - 1.5 * a * p2)
    q1 = -0.5 * (0.75 * a * p - 1.5 * p2)
    q2 = -0.5 * (0.75 * p - 0.125 * a)
    small = dot_rows(scaled_ref[:slots, :], scaled_ref[:slots, :]) * inverse
    diagonal = eye(slots)
    square = dot3(small, small)
    tail = dot3(square, jnp.where(diagonal, q2, 0.0) + 0.0625 * small)
    poly = jnp.where(diagonal, q0, 0.0) + q1 * small + tail

    def apply(vector):
        inner_part = jnp.sum(poly * vector, axis=1, keepdims=True)
        return jnp.sum(small * inner_part, axis=0, keepdims=True) + base * vector

    gain = apply(apply(misfit)) * inverse
    stretch = jnp.sqrt(a)
    alpha, factor = stretch * base, stretch * inverse

    far_mean = deviations(second, far, dev)
    cross = jnp.concatenate(
        [dot_rows(first[...], scaled_ref[...]), dot_rows(dev[...], scaled_ref[...])], axis=0
    )
    crosses = [cross[:, i * slots : (i + 1) * slots] for i in range(2)]
    mixes = [(dot3(x, poly) * factor).astype(jnp.bfloat16) for x in crosses]
    mix = jnp.concatenate(mixes, axis=1)
    moved = [jnp.sum(x * gain, axis=1, keepdims=True) for x in crosses]
    shift = jnp.where(left_lanes((near + far, lanes)), *moved)
    shift += jnp.concatenate([first_mean[...], far_mean], axis=0)
    for batch in batches(groups, 4):
        made = []
        for group in batch:
            here = slice(group * lanes, (group + 1) * lanes)
            old = jnp.concatenate([first[:, here], dev[:, here]], axis=0).astype(jnp.float32)
            new = dot(mix, scaled_ref[:, here]) + alpha * old + shift
            made.append((group, new.astype(jnp.bfloat16)))
        for group, new in made:
            out[group] = new


def analyse(first, first_mean, second, count, value, weight):
    groups, rows, lanes = second.shape
    slots = value.shape[1]
    far = rows - slots // 2
    return pl.pallas_call(
        analyse_kernel,
        out_shape=jax.ShapeDtypeStruct((groups, first.shape[0] + far, lanes), jnp.bfloat16),
        in_specs=vmem(3) + smem(1) + vmem(2),
        out_specs=pl.BlockSpec(memory_space=pltpu.VMEM),
        scratch_shapes=[
            pltpu.VMEM((far, groups * lanes), jnp.bfloat16),
            pltpu.VMEM((2 * slots, groups * lanes), jnp.bfloat16),
        ],
        compiler_params=params(16),
        cost_estimate=cost(4 * 10**9, 4 * 2**20),
    )(first, first_mean, second, count, value, weight)


def restore_kernel(blocks, out, turned):
    members, variables, levels, span, columns = out.shape
    lanes = members * variables
    identity = permutation(lanes, 0)
    near = span - 2 * STEPS
    for level in range(levels):
        made = []
        for r in range(0, span, 2):
            if STEPS <= r < span - STEPS:
                at = level * near + r - STEPS
            else:
                at = levels * near + level * 2 * STEPS + (r if r < STEPS else r - near)
            both = blocks[:, at * SPAN : (at + 2) * SPAN, :].astype(jnp.float32)
            for i in range(2):
                one = both[:, i * SPAN : (i + 1) * SPAN, :].reshape(columns, lanes)
                made.append((r + i, dot_rows(identity, one.astype(jnp.bfloat16))))
        for r, rows in made:
            turned[level % 2, pl.ds(r, lanes, stride=span), :] = rows
        for var in range(variables):
            half = turned[level % 2, var * members * span : (var + 1) * members * span, :]
            out[:, var, level] = half.reshape(members, span, columns).astype(jnp.bfloat16)


def restore(dims, blocks):
    members, variables, levels, span, columns = dims
    return pl.pallas_call(
        restore_kernel,
        out_shape=jax.ShapeDtypeStruct((members, variables, levels, span, columns), jnp.bfloat16),
        in_specs=vmem(1),
        out_specs=pl.BlockSpec(memory_space=pltpu.VMEM),
        scratch_shapes=[pltpu.VMEM((2, variables * members * span, columns), jnp.float32)],
        compiler_params=params(8),
        cost_estimate=cost(2 * 10**9, 2 * 2**20),
    )(blocks)


def neighbours(field, axis):
    count = lax.axis_size(axis)
    low = lax.ppermute(field, axis, [(i, (i + 1) % count) for i in range(count)])
    if count == 2:
        return (low,)
    return low, lax.ppermute(field, axis, [((i + 1) % count, i) for i in range(count)])


def exchange(blocks):
    return lax.all_to_all(blocks, "grp", split_axis=0, concat_axis=0, tiled=True)


def on_device(start, diffusivity, eastward, northward, cells, count, value, weight):
    members, variables, levels, span, columns = dims = start.shape
    model = model_rows(diffusivity, eastward, northward)
    own, centre, near = inner(start, model)
    sides = neighbours(own, "tile")
    first, first_mean = prepare(exchange(near))
    grid, rim = outer(dims, own, sides, model, centre)
    second = exchange(pick(variables, grid, rim, cells[0]))
    updated = analyse(first, first_mean, second, count, value[0], weight[0])
    return restore(dims, exchange(updated))


def solution(mesh):
    return jax.shard_map(
        on_device,
        mesh=mesh,
        in_specs=(
            P("grp", None, None, "tile", None),
            P(),
            P(),
            P(),
            P("tile", None, None),
            P("tile", "grp"),
            P("tile", "grp", None),
            P("tile", "grp", None),
        ),
        out_specs=P("grp", None, None, "tile", None),
        check_vma=False,
    )
```

```python
import functools

import jax
import jax.numpy as jnp
from jax import lax
from jax.experimental import pallas as pl
from jax.experimental.pallas import tpu as pltpu
from jax.sharding import PartitionSpec as P

SPAN = 8
STEPS = 2
EDGE = SPAN // 2

ROWS = (((1,), (1,)), ((), ()))


def params(mebibytes, **kw):
    return pltpu.CompilerParams(vmem_limit_bytes=mebibytes * 2**20, **kw)


def cost(flops, size):
    return pl.CostEstimate(flops=flops, bytes_accessed=size, transcendentals=0)


def vmem(count):
    return [pl.BlockSpec(memory_space=pltpu.VMEM)] * count


def hbm(count):
    return [pl.BlockSpec(memory_space=pltpu.HBM)] * count


def smem(count):
    return [pl.BlockSpec(memory_space=pltpu.SMEM)] * count


def dot(a, b, **kw):
    return jnp.dot(a, b, preferred_element_type=jnp.float32, **kw)


def split(x):
    high = x.astype(jnp.bfloat16)
    return high, (x - high.astype(jnp.float32)).astype(jnp.bfloat16)


def dot3(a, b):
    (a_high, a_low), (b_high, b_low) = split(a), split(b)
    return dot(a_high, b_high) + (dot(a_high, b_low) + dot(a_low, b_high))


def dot_rows(a, b):
    return lax.dot_general(a, b, ROWS, preferred_element_type=jnp.float32)


def permutation(size, shift):
    row = lax.broadcasted_iota(jnp.int32, (size, size), 0)
    column = lax.broadcasted_iota(jnp.int32, (size, size), 1)
    return (lax.rem(row + shift + size, size) == column).astype(jnp.bfloat16)


def eye(size):
    row = lax.broadcasted_iota(jnp.int32, (size, size), 0)
    column = lax.broadcasted_iota(jnp.int32, (size, size), 1)
    return row == column


def column_of(row):
    return jnp.sum(jnp.where(eye(row.shape[1]), row, 0.0), axis=1, keepdims=True)


def row_of(column):
    return jnp.sum(jnp.where(eye(column.shape[0]), column, 0.0), axis=0, keepdims=True)


def forecast_rows(read, first, last, coefficients):
    middle, east, west, north, south = coefficients

    def step(below, here, above):
        columns = here.shape[2]
        return (
            middle * here
            + east * above
            + west * below
            + north * pltpu.roll(here, columns - 1, 2)
            + south * pltpu.roll(here, 1, 2)
        )

    rows, once, twice = [read(first - 2), read(first - 1)], [], []
    for r in range(first - 1, last + 1):
        rows.append(read(r + 1))
        once.append(step(*rows[-3:]))
        if r >= first + 1:
            new = step(*once[-3:])
            twice.append((r - 1, new.reshape(-1, new.shape[2]).astype(jnp.bfloat16)))
    return twice


def coefficients_of(level, diff, east, north):
    spread = jnp.broadcast_to(diff[level : level + 1, :], (8, diff.shape[1]))
    u = 0.5 * east[level]
    w = 0.5 * north[level]
    return 1.0 - 4.0 * spread, spread - u, spread + u, spread - w, spread + w


def row_reader(level, var, own, low, high):
    span, columns = own.shape[2], own.shape[4]

    def read(r):
        ref, at = (low, r + span) if r < 0 else (own, r) if r < span else (high, r - span)
        return ref[var, level, at].reshape(-1, 8, columns)

    return read


def pack_rows(pairs, identity, store, first):
    lanes = pairs[0].shape[0] // 2
    packed = []
    for pair in pairs:
        turned = dot_rows(identity, pair)
        parts = [turned[:, i * lanes : (i + 1) * lanes].reshape(-1, SPAN, lanes) for i in range(2)]
        packed.append(jnp.concatenate(parts, axis=1).astype(jnp.bfloat16))
    for i, value in enumerate(packed):
        at = first + i * 2 * SPAN
        store[:, at : at + 2 * SPAN, :] = value


def inner_kernel(variables, own, *refs):
    raw, (slabs, fields, packed, model) = refs[:3], refs[3:7]
    local, (whole, staged, in_sems, raw_sems, out_sems) = refs[7:10], refs[10:]
    lanes, levels, span, columns = own.shape
    members = lanes // variables
    count = span - 2 * STEPS
    copies = [pltpu.make_async_copy(x, y, raw_sems.at[i]) for i, (x, y) in enumerate(zip(raw, local))]
    arrivals = [
        pltpu.make_async_copy(own.at[:, level], whole.at[level], in_sems.at[level])
        for level in range(levels)
    ]
    for copy in copies + arrivals:
        copy.start()
    for copy in copies:
        copy.wait()
    identity = permutation(columns, 0)
    leaving = []
    for level in range(levels):
        coefficients = coefficients_of(level, *local)
        for i, one in enumerate(coefficients):
            model[level, i] = one
        arrivals[level].wait()
        view = whole.at[level].reshape(lanes * span, columns)
        reads, made = [], []
        for var in range(variables):

            def read(r):
                rows = view[pl.ds(var * span + r, members, stride=variables * span), :]
                reads.append((var, r, rows))
                return rows.reshape(-1, 8, columns)

            for r, value in forecast_rows(read, STEPS, span - STEPS, coefficients):
                made.append((var, r, value))
        pairs = []
        for first in range(STEPS, span - STEPS, 2):
            rows = [one for r in (first, first + 1) for _, at, one in made if at == r]
            pairs.append(jnp.concatenate(rows, axis=0))
        pack_rows(pairs, identity, staged.at[level], 0)
        here = pl.ds(level * count * SPAN, count * SPAN)
        leaving.append(pltpu.make_async_copy(staged.at[level], packed.at[:, here], out_sems.at[level]))
        leaving[-1].start()
        for var, r, value in made:
            fields[level, r - STEPS, var * members : (var + 1) * members, :] = value
        for var, r, rows in reads:
            slabs[var, level, r] = rows
    for copy in leaving:
        copy.wait()


def inner(own, raw, variables):
    lanes, levels, span, columns = own.shape
    members = lanes // variables
    blocks = columns // SPAN
    count = span - 2 * STEPS
    fixed = [pltpu.with_memory_space_constraint(x, pltpu.HBM) for x in (own, *raw)]
    return pl.pallas_call(
        functools.partial(inner_kernel, variables),
        out_shape=[
            jax.ShapeDtypeStruct((variables, levels, span, members, columns), jnp.float32),
            jax.ShapeDtypeStruct((levels, count, lanes, columns), jnp.bfloat16),
            jax.ShapeDtypeStruct((blocks, levels * count * SPAN, lanes), jnp.bfloat16),
            jax.ShapeDtypeStruct((levels, 5, 8, columns), jnp.float32),
        ],
        in_specs=hbm(4),
        out_specs=vmem(2) + hbm(1) + vmem(1),
        scratch_shapes=[
            pltpu.VMEM(raw[0].shape, jnp.float32),
            pltpu.SMEM(raw[1].shape, jnp.float32),
            pltpu.SMEM(raw[2].shape, jnp.float32),
            pltpu.VMEM((levels, lanes, span, columns), jnp.float32),
            pltpu.VMEM((levels, blocks, count * SPAN, lanes), jnp.bfloat16),
            pltpu.SemaphoreType.DMA((levels,)),
            pltpu.SemaphoreType.DMA((3,)),
            pltpu.SemaphoreType.DMA((levels,)),
        ],
        compiler_params=params(10),
        cost_estimate=cost(2 * 10**9, 4 * 2**20),
    )(*fixed)


def outer_kernel(near, own, *rest):
    sides, rest = rest[:near], rest[near:]
    model, centre, grid, packed, fields, sems = rest
    variables, levels, span, members, columns = own.shape
    rows = variables * members
    pairs = (2 * EDGE + span) // 2

    copies = []
    for r in range(STEPS, span - STEPS):
        half, pair = divmod(r + EDGE, pairs)
        place = grid.at[:, pair, pl.ds(half * rows, rows)]
        copies.append(pltpu.make_async_copy(centre.at[:, r - STEPS], place, sems.at[r - STEPS]))
        copies[-1].start()

    @pl.loop(0, levels)
    def _(level):
        coefficients = [model[level, i] for i in range(5)]
        made = []
        for var in range(variables):
            read = row_reader(level, var, own, sides[0], sides[-1])
            for first, last in ((-EDGE, STEPS), (span - STEPS, span + EDGE)):
                for r, value in forecast_rows(read, first, last, coefficients):
                    made.append((var, r, value))
        for var, r, value in made:
            half, pair = divmod(r + EDGE, pairs)
            at = half * rows + var * members
            grid[level, pair, at : at + members, :] = value
            if 0 <= r < span:
                pair, half = divmod(r if r < STEPS else r - span + 2 * STEPS, 2)
                at = half * rows + var * members
                fields[level, pair, at : at + members, :] = value

    identity = permutation(columns, 0)
    for level in range(0, levels, 2):
        batch = [fields[at, pair] for at in range(level, min(levels, level + 2)) for pair in range(STEPS)]
        pack_rows(batch, identity, packed, level * STEPS * 2 * SPAN)
    for copy in copies:
        copy.wait()


def outer(dims, own, sides, model, centre):
    members, variables, levels, span, columns = dims
    lanes = members * variables
    blocks = columns // SPAN
    near = len(sides)
    pairs = (2 * EDGE + span) // 2
    return pl.pallas_call(
        functools.partial(outer_kernel, near),
        out_shape=[
            jax.ShapeDtypeStruct((levels, pairs, 2 * lanes, columns), jnp.bfloat16),
            jax.ShapeDtypeStruct((blocks, levels * 2 * STEPS * SPAN, lanes), jnp.bfloat16),
        ],
        in_specs=vmem(2 + near) + hbm(1),
        out_specs=vmem(2),
        scratch_shapes=[
            pltpu.VMEM((levels, STEPS, 2 * lanes, columns), jnp.bfloat16),
            pltpu.SemaphoreType.DMA((span - 2 * STEPS,)),
        ],
        compiler_params=params(16),
        cost_estimate=cost(2 * 10**9, 8 * 2**20),
    )(own, *sides, model, centre)


def pick_kernel(variables, together, grid, rim, cells, out, region, codes):
    levels, pairs, twice, columns = grid.shape
    rows = twice // 2
    members = rows // variables
    blocks, slots = cells.shape
    width = 2 * EDGE + SPAN
    part = pairs * width
    entries = levels * part
    share = rim.shape[1]

    orders = jnp.concatenate(
        [permutation(columns, -EDGE), permutation(columns, SPAN - EDGE)], axis=0
    )
    batch = next(n for n in (4, 2, 1) if pairs % n == 0)
    for level in range(levels):
        for start in range(0, pairs, batch):
            turned = [
                dot_rows(orders, grid[level, start + i]).astype(jnp.bfloat16) for i in range(batch)
            ]
            for i, value in enumerate(turned):
                at = (level * pairs + start + i) * width
                for first in range(2):
                    for j in range(columns // width):
                        row = first * columns + j * width
                        region[2 * j + first, at : at + width, :] = value[row : row + width, :]

    cell = cells[...]
    second = cell >= 2 * entries
    cell = jnp.where(second, cell - 2 * entries, cell)
    level = lax.shift_right_logical(cell, (2 * part).bit_length() - 1)
    inside = cell - level * (2 * part)
    lower = inside >= part
    code = level * part + jnp.where(lower, inside - part + entries, inside)
    codes[...] = jnp.where(second, code + 2 * entries, code).astype(jnp.float32)

    left = lax.broadcasted_iota(jnp.int32, (slots // 2, rows), 1) < members
    lane = lax.broadcasted_iota(jnp.int32, (slots, entries), 1).astype(jnp.float32)

    @pl.loop(0, blocks // together)
    def _(step):
        made = []
        for i in range(together):
            block = step * together + i
            at = column_of(codes[pl.ds(block, 1), :])
            second = at >= 2.0 * entries
            at = jnp.where(second, at - 2.0 * entries, at)
            lower = at >= 1.0 * entries
            at = jnp.where(lower, at - 1.0 * entries, at)
            pick = jnp.where(lane == at, 1.0, 0.0).astype(jnp.bfloat16)
            found = dot(pick, region[block])
            total = jnp.where(lower, found[:, rows:], found[:, :rows])
            other = pltpu.roll(total, members, 1)
            to_left = jnp.where(second, other, total)[: slots // 2]
            to_right = jnp.where(second, total, other)[slots // 2 :]
            made.append(jnp.where(left, to_left, to_right).astype(jnp.bfloat16))
        for i, value in enumerate(made):
            block = step * together + i
            out[block, share:, :] = value
            out[block, :share, :] = rim[block]


def pick(variables, grid, rim, cells):
    levels, pairs, twice, columns = grid.shape
    blocks, slots = cells.shape
    _, share, lanes = rim.shape
    together = next(n for n in (4, 2, 1) if blocks % n == 0)
    return pl.pallas_call(
        functools.partial(pick_kernel, variables, together),
        out_shape=jax.ShapeDtypeStruct((blocks, share + slots // 2, lanes), jnp.bfloat16),
        in_specs=vmem(3),
        out_specs=pl.BlockSpec(memory_space=pltpu.VMEM),
        scratch_shapes=[
            pltpu.VMEM((blocks, levels * pairs * (2 * EDGE + SPAN), twice), jnp.bfloat16),
            pltpu.VMEM((blocks, slots), jnp.float32),
        ],
        compiler_params=params(20),
        cost_estimate=cost(4 * 10**9, 4 * 2**20),
    )(grid, rim, cells)


def join(a, b, left, members):
    return (
        jnp.where(left, a, pltpu.roll(b, members, 1)),
        jnp.where(left, pltpu.roll(a, members, 1), b),
    )


def batches(count, size):
    return [range(at, min(count, at + size)) for at in range(0, count, size)]


def left_lanes(shape):
    return lax.broadcasted_iota(jnp.int32, shape, 1) < shape[1] // 2


def deviations(states, raw, dev, at, size):
    groups, _, lanes = states.shape
    members = lanes // 2
    left = left_lanes((size, lanes))
    sums = [jnp.zeros((size, lanes), jnp.float32)] * 2
    for batch in batches(groups // 2, 4):
        made = [
            join(
                states[2 * j, :size, :].astype(jnp.float32),
                states[2 * j + 1, :size, :].astype(jnp.float32),
                left,
                members,
            )
            for j in batch
        ]
        for j, pair in zip(batch, made):
            here = slice(j * lanes, (j + 1) * lanes)
            for var in range(2):
                raw[var * size : (var + 1) * size, here] = pair[var]
            sums = [total + one for total, one in zip(sums, pair)]
    centre = jnp.concatenate([jnp.sum(x, axis=1, keepdims=True) for x in sums], axis=0)
    centre = centre * (1.0 / (groups * members))
    dev[at : at + 2 * size, :] = (raw[...] - centre).astype(jnp.bfloat16)
    return centre


def prepare_kernel(states, dev, centre, raw):
    mean = deviations(states, raw, dev, 0, states.shape[1])
    centre[...] = jnp.broadcast_to(mean, centre.shape)


def prepare(states):
    groups, near, lanes = states.shape
    total = groups * lanes // 2
    return pl.pallas_call(
        prepare_kernel,
        out_shape=[
            jax.ShapeDtypeStruct((2 * near, total), jnp.bfloat16),
            jax.ShapeDtypeStruct((2 * near, lanes), jnp.float32),
        ],
        in_specs=vmem(1),
        out_specs=vmem(2),
        scratch_shapes=[pltpu.VMEM((2 * near, total), jnp.float32)],
        compiler_params=params(6),
        cost_estimate=cost(10**8, 2 * 2**20),
    )(states)


def analyse_kernel(first, means, second, count, value, weight, out, raw, dev, obs, scaled_ref):
    groups, _, lanes = second.shape
    near = first.shape[0] // 2
    half = obs.shape[0] // 2
    far = second.shape[1] - half
    side = near + far
    slots = 2 * half
    members = lanes // 2
    total_members = groups * members
    left = left_lanes((half, lanes))

    for batch in batches(groups // 2, 4):
        made = [
            join(
                second[2 * j, far:, :].astype(jnp.float32),
                second[2 * j + 1, far:, :].astype(jnp.float32),
                left,
                members,
            )
            for j in batch
        ]
        for j, pair in zip(batch, made):
            here = slice(j * lanes, (j + 1) * lanes)
            obs[:half, here], obs[half:, here] = pair

    used = lax.broadcasted_iota(jnp.int32, (1, slots), 1) < count[0, 0]
    root = column_of(jnp.where(used, jnp.sqrt(weight[...]), 0.0))
    observed = obs[...]
    mean = jnp.sum(observed, axis=1, keepdims=True) * (1.0 / total_members)
    scaled = (observed - mean) * root
    energy = jnp.sum(jnp.sum(scaled * scaled, axis=1, keepdims=True), axis=0, keepdims=True)
    scaled_ref[...] = scaled.astype(jnp.bfloat16)
    misfit = row_of(root * (column_of(value[...]) - mean))

    c = total_members - 1.0
    s = energy * (1.0 / total_members) + c
    inverse = 1.0 / s
    a = c * inverse
    p = 1.5 - 0.5 * a
    p2 = p * p
    p3 = p2 * p
    base = 1.5 * p - 0.5 * a * p3
    q0 = -0.75 - 0.5 * (p3 - 1.5 * a * p2)
    q1 = -0.5 * (0.75 * a * p - 1.5 * p2)
    q2 = -0.5 * (0.75 * p - 0.125 * a)
    small = dot_rows(scaled_ref[...], scaled_ref[...]) * inverse
    diagonal = eye(slots)
    square = dot3(small, small)
    tail = dot3(square, jnp.where(diagonal, q2, 0.0) + 0.0625 * small)
    poly = jnp.where(diagonal, q0, 0.0) + q1 * small + tail

    def apply(vector):
        inner_part = jnp.sum(poly * vector, axis=1, keepdims=True)
        return jnp.sum(small * inner_part, axis=0, keepdims=True) + base * vector

    gain = apply(apply(misfit)) * inverse
    stretch = jnp.sqrt(a)
    alpha, factor = stretch * base, stretch * inverse
    centre = deviations(second, raw, dev, 0, far)
    cross = jnp.concatenate(
        [dot_rows(first[...], scaled_ref[...]), dot_rows(dev[...], scaled_ref[...])], axis=0
    )
    centre = jnp.concatenate([means[:, 0:1], centre], axis=0)
    shift = centre + jnp.sum(cross * gain, axis=1, keepdims=True)
    mix = (dot3(cross, poly) * factor).astype(jnp.bfloat16)
    parts = ((first, 0, near, 0), (dev, 2 * near, far, near))
    for batch in batches(groups // 2, 2):
        made = []
        wide = slice(batch[0] * lanes, (batch[-1] + 1) * lanes)
        both = dot(mix, scaled_ref[:, wide]) + shift
        for j in batch:
            here = slice(j * lanes, (j + 1) * lanes)
            new = both[:, (j - batch[0]) * lanes :][:, :lanes]
            for ref, at, size, row in parts:
                one = new[at : at + 2 * size] + alpha * ref[:, here].astype(jnp.float32)
                pair = join(one[:size], one[size:], left_lanes((size, lanes)), members)
                made += [(2 * j + i, row, x.astype(jnp.bfloat16)) for i, x in enumerate(pair)]
        for group, row, value in made:
            out[group, row : row + value.shape[0], :] = value


def analyse(first, means, second, count, value, weight):
    groups, _, lanes = second.shape
    near = first.shape[0] // 2
    slots = value.shape[1]
    far = second.shape[1] - slots // 2
    total = groups * lanes // 2
    return pl.pallas_call(
        analyse_kernel,
        out_shape=jax.ShapeDtypeStruct((groups, near + far, lanes), jnp.bfloat16),
        in_specs=vmem(3) + smem(1) + vmem(2),
        out_specs=pl.BlockSpec(memory_space=pltpu.VMEM),
        scratch_shapes=[
            pltpu.VMEM((2 * far, total), jnp.float32),
            pltpu.VMEM((2 * far, total), jnp.bfloat16),
            pltpu.VMEM((slots, total), jnp.float32),
            pltpu.VMEM((slots, total), jnp.bfloat16),
        ],
        compiler_params=params(16),
        cost_estimate=cost(4 * 10**9, 4 * 2**20),
    )(first, means, second, count, value, weight)


def restore_kernel(blocks, out, turned):
    members, variables, levels, span, columns = out.shape
    lanes = members * variables
    identity = permutation(lanes, 0)
    near = span - 2 * STEPS
    for level in range(levels):
        made = []
        for r in range(0, span, 2):
            if STEPS <= r < span - STEPS:
                at = level * near + r - STEPS
            else:
                at = levels * near + level * 2 * STEPS + (r if r < STEPS else r - near)
            both = blocks[:, at * SPAN : (at + 2) * SPAN, :].astype(jnp.float32)
            for i in range(2):
                one = both[:, i * SPAN : (i + 1) * SPAN, :].reshape(columns, lanes)
                made.append((r + i, dot_rows(identity, one.astype(jnp.bfloat16))))
        for r, rows in made:
            turned[level % 2, pl.ds(r, lanes, stride=span), :] = rows
        for var in range(variables):
            half = turned[level % 2, var * members * span : (var + 1) * members * span, :]
            out[:, var, level] = half.reshape(members, span, columns).astype(jnp.bfloat16)


def restore(dims, blocks):
    members, variables, levels, span, columns = dims
    return pl.pallas_call(
        restore_kernel,
        out_shape=jax.ShapeDtypeStruct((members, variables, levels, span, columns), jnp.bfloat16),
        in_specs=vmem(1),
        out_specs=pl.BlockSpec(memory_space=pltpu.VMEM),
        scratch_shapes=[pltpu.VMEM((2, variables * members * span, columns), jnp.float32)],
        compiler_params=params(8),
        cost_estimate=cost(2 * 10**9, 2 * 2**20),
    )(blocks)


def neighbours(field, axis):
    count = lax.axis_size(axis)
    low = lax.ppermute(field, axis, [(i, (i + 1) % count) for i in range(count)])
    if count == 2:
        return (low,)
    return low, lax.ppermute(field, axis, [((i + 1) % count, i) for i in range(count)])


def exchange(blocks):
    return lax.all_to_all(blocks, "grp", split_axis=0, concat_axis=0, tiled=True)


def on_device(start, diffusivity, eastward, northward, cells, count, value, weight):
    members, variables, levels, span, columns = dims = start.shape
    whole = start.reshape(members * variables, levels, span, columns)
    own, centre, near, model = inner(whole, (diffusivity, eastward, northward), variables)
    sides = neighbours(own, "tile")
    first, means = prepare(exchange(near))
    grid, rim = outer(dims, own, sides, model, centre)
    second = exchange(pick(variables, grid, rim, cells[0]))
    updated = analyse(first, means, second, count, value[0], weight[0])
    return restore(dims, exchange(updated))


def solution(mesh):
    return jax.shard_map(
        on_device,
        mesh=mesh,
        in_specs=(
            P("grp", None, None, "tile", None),
            P(),
            P(),
            P(),
            P("tile", None, None),
            P("tile", "grp"),
            P("tile", "grp", None),
            P("tile", "grp", None),
        ),
        out_specs=P("grp", None, None, "tile", None),
        check_vma=False,
    )
```

```python
import functools

import jax
import jax.numpy as jnp
from jax import lax
from jax.experimental import pallas as pl
from jax.experimental.pallas import tpu as pltpu
from jax.sharding import PartitionSpec as P

SPAN = 8
STEPS = 2
EDGE = SPAN // 2

ROWS = (((1,), (1,)), ((), ()))


def params(mebibytes, **kw):
    return pltpu.CompilerParams(vmem_limit_bytes=mebibytes * 2**20, **kw)


def cost(flops, size):
    return pl.CostEstimate(flops=flops, bytes_accessed=size, transcendentals=0)


def vmem(count):
    return [pl.BlockSpec(memory_space=pltpu.VMEM)] * count


def hbm(count):
    return [pl.BlockSpec(memory_space=pltpu.HBM)] * count


def smem(count):
    return [pl.BlockSpec(memory_space=pltpu.SMEM)] * count


def dot(a, b, **kw):
    return jnp.dot(a, b, preferred_element_type=jnp.float32, **kw)


def split(x):
    high = x.astype(jnp.bfloat16)
    return high, (x - high.astype(jnp.float32)).astype(jnp.bfloat16)


def dot_rows(a, b):
    return lax.dot_general(a, b, ROWS, preferred_element_type=jnp.float32)


def permutation(size, shift):
    row = lax.broadcasted_iota(jnp.int32, (size, size), 0)
    column = lax.broadcasted_iota(jnp.int32, (size, size), 1)
    return (lax.rem(row + shift + size, size) == column).astype(jnp.bfloat16)


def eye(size):
    row = lax.broadcasted_iota(jnp.int32, (size, size), 0)
    column = lax.broadcasted_iota(jnp.int32, (size, size), 1)
    return row == column


def column_of(row):
    return jnp.sum(jnp.where(eye(row.shape[1]), row, 0.0), axis=1, keepdims=True)


def row_of(column):
    return jnp.sum(jnp.where(eye(column.shape[0]), column, 0.0), axis=0, keepdims=True)


def forecast_rows(read, first, last, coefficients):
    middle, east, west, north, south = coefficients

    def step(below, here, above):
        columns = here.shape[2]
        return (
            middle * here
            + east * above
            + west * below
            + north * pltpu.roll(here, columns - 1, 2)
            + south * pltpu.roll(here, 1, 2)
        )

    rows, once, twice = [read(first - 2), read(first - 1)], [], []
    for r in range(first - 1, last + 1):
        rows.append(read(r + 1))
        once.append(step(*rows[-3:]))
        if r >= first + 1:
            new = step(*once[-3:])
            twice.append((r - 1, new.reshape(-1, new.shape[2]).astype(jnp.bfloat16)))
    return twice


def coefficients_of(level, diff, east, north):
    spread = jnp.broadcast_to(diff[level : level + 1, :], (8, diff.shape[1]))
    u = 0.5 * east[level]
    w = 0.5 * north[level]
    return 1.0 - 4.0 * spread, spread - u, spread + u, spread - w, spread + w


def row_reader(level, var, own, low, high):
    span, columns = own.shape[2], own.shape[4]

    def read(r):
        ref, at = (low, r + span) if r < 0 else (own, r) if r < span else (high, r - span)
        return ref[var, level, at].reshape(-1, 8, columns)

    return read


def pack_rows(pairs, identity, store, first):
    lanes = pairs[0].shape[0] // 2
    packed = []
    for pair in pairs:
        turned = dot_rows(identity, pair)
        parts = [turned[:, i * lanes : (i + 1) * lanes].reshape(-1, SPAN, lanes) for i in range(2)]
        packed.append(jnp.concatenate(parts, axis=1).astype(jnp.bfloat16))
    for i, value in enumerate(packed):
        at = first + i * 2 * SPAN
        store[:, at : at + 2 * SPAN, :] = value


def inner_kernel(variables, own, *refs):
    raw, (slabs, fields, packed, model) = refs[:3], refs[3:7]
    local, (whole, staged, in_sems, raw_sems, out_sems) = refs[7:10], refs[10:]
    lanes, levels, span, columns = own.shape
    members = lanes // variables
    count = span - 2 * STEPS
    copies = [pltpu.make_async_copy(x, y, raw_sems.at[i]) for i, (x, y) in enumerate(zip(raw, local))]
    together = whole.shape[2]
    arrivals = []
    for i in range(levels // together):
        for part in range(2):
            here = pl.ds(part * (lanes // 2), lanes // 2)
            source = own.at[here, pl.ds(i * together, together)]
            arrivals.append(
                pltpu.make_async_copy(source, whole.at[i, here], in_sems.at[2 * i + part])
            )
    for copy in copies + arrivals:
        copy.start()
    for copy in copies:
        copy.wait()
    identity = permutation(columns, 0)
    leaving = []
    for level in range(levels):
        coefficients = coefficients_of(level, *local)
        for i, one in enumerate(coefficients):
            model[level, i] = one
        step, inside = divmod(level, together)
        if inside == 0:
            arrivals[2 * step].wait()
            arrivals[2 * step + 1].wait()
        view = whole.at[step].reshape(lanes * together * span, columns)
        reads, made = [], []
        for var in range(variables):

            def read(r):
                at = (var * together + inside) * span + r
                rows = view[pl.ds(at, members, stride=variables * together * span), :]
                reads.append((var, r, rows))
                return rows.reshape(-1, 8, columns)

            for r, value in forecast_rows(read, STEPS, span - STEPS, coefficients):
                made.append((var, r, value))
        pairs = []
        for first in range(STEPS, span - STEPS, 2):
            rows = [one for r in (first, first + 1) for _, at, one in made if at == r]
            pairs.append(jnp.concatenate(rows, axis=0))
        pack_rows(pairs, identity, staged.at[level], 0)
        here = pl.ds(level * count * SPAN, count * SPAN)
        leaving.append(pltpu.make_async_copy(staged.at[level], packed.at[:, here], out_sems.at[level]))
        leaving[-1].start()
        for var, r, value in made:
            fields[level, r - STEPS, var * members : (var + 1) * members, :] = value
        for var, r, rows in reads:
            slabs[var, level, r] = rows
    for copy in leaving:
        copy.wait()


def inner(own, raw, variables):
    lanes, levels, span, columns = own.shape
    members = lanes // variables
    blocks = columns // SPAN
    count = span - 2 * STEPS
    together = 2 if levels % 2 == 0 else 1
    fixed = [pltpu.with_memory_space_constraint(x, pltpu.HBM) for x in (own, *raw)]
    return pl.pallas_call(
        functools.partial(inner_kernel, variables),
        out_shape=[
            jax.ShapeDtypeStruct((variables, levels, span, members, columns), jnp.float32),
            jax.ShapeDtypeStruct((levels, count, lanes, columns), jnp.bfloat16),
            jax.ShapeDtypeStruct((blocks, levels * count * SPAN, lanes), jnp.bfloat16),
            jax.ShapeDtypeStruct((levels, 5, 8, columns), jnp.float32),
        ],
        in_specs=hbm(4),
        out_specs=vmem(2) + hbm(1) + vmem(1),
        scratch_shapes=[
            pltpu.VMEM(raw[0].shape, jnp.float32),
            pltpu.SMEM(raw[1].shape, jnp.float32),
            pltpu.SMEM(raw[2].shape, jnp.float32),
            pltpu.VMEM((levels // together, lanes, together, span, columns), jnp.float32),
            pltpu.VMEM((levels, blocks, count * SPAN, lanes), jnp.bfloat16),
            pltpu.SemaphoreType.DMA((2 * levels // together,)),
            pltpu.SemaphoreType.DMA((3,)),
            pltpu.SemaphoreType.DMA((levels,)),
        ],
        compiler_params=params(10),
        cost_estimate=cost(2 * 10**9, 4 * 2**20),
    )(*fixed)


def outer_kernel(near, own, *rest):
    sides, rest = rest[:near], rest[near:]
    model, centre, grid, packed, fields, sems = rest
    variables, levels, span, members, columns = own.shape
    rows = variables * members
    pairs = (2 * EDGE + span) // 2

    copies = []
    for r in range(STEPS, span - STEPS):
        half, pair = divmod(r + EDGE, pairs)
        place = grid.at[:, pair, pl.ds(half * rows, rows)]
        copies.append(pltpu.make_async_copy(centre.at[:, r - STEPS], place, sems.at[r - STEPS]))
        copies[-1].start()

    @pl.loop(0, levels)
    def _(level):
        coefficients = [model[level, i] for i in range(5)]
        made = []
        for var in range(variables):
            read = row_reader(level, var, own, sides[0], sides[-1])
            for first, last in ((-EDGE, STEPS), (span - STEPS, span + EDGE)):
                for r, value in forecast_rows(read, first, last, coefficients):
                    made.append((var, r, value))
        for var, r, value in made:
            half, pair = divmod(r + EDGE, pairs)
            at = half * rows + var * members
            grid[level, pair, at : at + members, :] = value
            if 0 <= r < span:
                pair, half = divmod(r if r < STEPS else r - span + 2 * STEPS, 2)
                at = half * rows + var * members
                fields[level, pair, at : at + members, :] = value

    identity = permutation(columns, 0)
    for level in range(0, levels, 2):
        batch = [fields[at, pair] for at in range(level, min(levels, level + 2)) for pair in range(STEPS)]
        pack_rows(batch, identity, packed, level * STEPS * 2 * SPAN)
    for copy in copies:
        copy.wait()


def outer(dims, own, sides, model, centre):
    members, variables, levels, span, columns = dims
    lanes = members * variables
    blocks = columns // SPAN
    near = len(sides)
    pairs = (2 * EDGE + span) // 2
    return pl.pallas_call(
        functools.partial(outer_kernel, near),
        out_shape=[
            jax.ShapeDtypeStruct((levels, pairs, 2 * lanes, columns), jnp.bfloat16),
            jax.ShapeDtypeStruct((blocks, levels * 2 * STEPS * SPAN, lanes), jnp.bfloat16),
        ],
        in_specs=vmem(2 + near) + hbm(1),
        out_specs=vmem(2),
        scratch_shapes=[
            pltpu.VMEM((levels, STEPS, 2 * lanes, columns), jnp.bfloat16),
            pltpu.SemaphoreType.DMA((span - 2 * STEPS,)),
        ],
        compiler_params=params(16),
        cost_estimate=cost(2 * 10**9, 8 * 2**20),
    )(own, *sides, model, centre)


def pick_kernel(variables, together, grid, rim, cells, out, region, codes):
    levels, pairs, twice, columns = grid.shape
    rows = twice // 2
    members = rows // variables
    blocks, slots = cells.shape
    width = 2 * EDGE + SPAN
    part = pairs * width
    entries = levels * part
    share = rim.shape[1]

    orders = jnp.concatenate(
        [permutation(columns, -EDGE), permutation(columns, SPAN - EDGE)], axis=0
    )
    batch = next(n for n in (4, 2, 1) if pairs % n == 0)
    for level in range(levels):
        for start in range(0, pairs, batch):
            turned = [
                dot_rows(orders, grid[level, start + i]).astype(jnp.bfloat16) for i in range(batch)
            ]
            for i, value in enumerate(turned):
                at = (level * pairs + start + i) * width
                for first in range(2):
                    for j in range(columns // width):
                        row = first * columns + j * width
                        region[2 * j + first, at : at + width, :] = value[row : row + width, :]

    cell = cells[...]
    second = cell >= 2 * entries
    cell = jnp.where(second, cell - 2 * entries, cell)
    level = lax.shift_right_logical(cell, (2 * part).bit_length() - 1)
    inside = cell - level * (2 * part)
    lower = inside >= part
    code = level * part + jnp.where(lower, inside - part + entries, inside)
    codes[...] = jnp.where(second, code + 2 * entries, code).astype(jnp.float32)

    left = lax.broadcasted_iota(jnp.int32, (slots // 2, rows), 1) < members
    lane = lax.broadcasted_iota(jnp.int32, (slots, entries), 1).astype(jnp.float32)

    @pl.loop(0, blocks // together)
    def _(step):
        made = []
        for i in range(together):
            block = step * together + i
            at = column_of(codes[pl.ds(block, 1), :])
            second = at >= 2.0 * entries
            at = jnp.where(second, at - 2.0 * entries, at)
            lower = at >= 1.0 * entries
            at = jnp.where(lower, at - 1.0 * entries, at)
            pick = jnp.where(lane == at, 1.0, 0.0).astype(jnp.bfloat16)
            found = dot(pick, region[block])
            total = jnp.where(lower, found[:, rows:], found[:, :rows])
            other = pltpu.roll(total, members, 1)
            to_left = jnp.where(second, other, total)[: slots // 2]
            to_right = jnp.where(second, total, other)[slots // 2 :]
            made.append(jnp.where(left, to_left, to_right).astype(jnp.bfloat16))
        for i, value in enumerate(made):
            block = step * together + i
            out[block, share:, :] = value
            out[block, :share, :] = rim[block]


def pick(variables, grid, rim, cells):
    levels, pairs, twice, columns = grid.shape
    blocks, slots = cells.shape
    _, share, lanes = rim.shape
    together = next(n for n in (4, 2, 1) if blocks % n == 0)
    return pl.pallas_call(
        functools.partial(pick_kernel, variables, together),
        out_shape=jax.ShapeDtypeStruct((blocks, share + slots // 2, lanes), jnp.bfloat16),
        in_specs=vmem(3),
        out_specs=pl.BlockSpec(memory_space=pltpu.VMEM),
        scratch_shapes=[
            pltpu.VMEM((blocks, levels * pairs * (2 * EDGE + SPAN), twice), jnp.bfloat16),
            pltpu.VMEM((blocks, slots), jnp.float32),
        ],
        compiler_params=params(20),
        cost_estimate=cost(4 * 10**9, 4 * 2**20),
    )(grid, rim, cells)


def join(a, b, left, members):
    return (
        jnp.where(left, a, pltpu.roll(b, members, 1)),
        jnp.where(left, pltpu.roll(a, members, 1), b),
    )


def batches(count, size):
    return [range(at, min(count, at + size)) for at in range(0, count, size)]


def left_lanes(shape):
    return lax.broadcasted_iota(jnp.int32, shape, 1) < shape[1] // 2


def deviations(states, raw, dev, at, size):
    groups, _, lanes = states.shape
    members = lanes // 2
    left = left_lanes((size, lanes))
    sums = [jnp.zeros((size, lanes), jnp.float32)] * 2
    for batch in batches(groups // 2, 4):
        made = [
            join(
                states[2 * j, :size, :].astype(jnp.float32),
                states[2 * j + 1, :size, :].astype(jnp.float32),
                left,
                members,
            )
            for j in batch
        ]
        for j, pair in zip(batch, made):
            here = slice(j * lanes, (j + 1) * lanes)
            for var in range(2):
                raw[var * size : (var + 1) * size, here] = pair[var]
            sums = [total + one for total, one in zip(sums, pair)]
    centre = jnp.concatenate([jnp.sum(x, axis=1, keepdims=True) for x in sums], axis=0)
    centre = centre * (1.0 / (groups * members))
    dev[at : at + 2 * size, :] = (raw[...] - centre).astype(jnp.bfloat16)
    return centre


def prepare_kernel(states, dev, centre, raw):
    mean = deviations(states, raw, dev, 0, states.shape[1])
    centre[...] = jnp.broadcast_to(mean, centre.shape)


def prepare(states):
    groups, near, lanes = states.shape
    total = groups * lanes // 2
    return pl.pallas_call(
        prepare_kernel,
        out_shape=[
            jax.ShapeDtypeStruct((2 * near, total), jnp.bfloat16),
            jax.ShapeDtypeStruct((2 * near, lanes), jnp.float32),
        ],
        in_specs=vmem(1),
        out_specs=vmem(2),
        scratch_shapes=[pltpu.VMEM((2 * near, total), jnp.float32)],
        compiler_params=params(6),
        cost_estimate=cost(10**8, 2 * 2**20),
    )(states)


def analyse_kernel(first, means, second, count, value, weight, out, raw, dev, obs, scaled_ref):
    groups, _, lanes = second.shape
    near = first.shape[0] // 2
    half = obs.shape[0] // 2
    far = second.shape[1] - half
    side = near + far
    slots = 2 * half
    members = lanes // 2
    total_members = groups * members
    left = left_lanes((half, lanes))

    for batch in batches(groups // 2, 4):
        made = [
            join(
                second[2 * j, far:, :].astype(jnp.float32),
                second[2 * j + 1, far:, :].astype(jnp.float32),
                left,
                members,
            )
            for j in batch
        ]
        for j, pair in zip(batch, made):
            here = slice(j * lanes, (j + 1) * lanes)
            obs[:half, here], obs[half:, here] = pair

    used = lax.broadcasted_iota(jnp.int32, (1, slots), 1) < count[0, 0]
    root = column_of(jnp.where(used, jnp.sqrt(weight[...]), 0.0))
    observed = obs[...]
    mean = jnp.sum(observed, axis=1, keepdims=True) * (1.0 / total_members)
    scaled = (observed - mean) * root
    energy = jnp.sum(jnp.sum(scaled * scaled, axis=1, keepdims=True), axis=0, keepdims=True)
    scaled_ref[...] = scaled.astype(jnp.bfloat16)
    misfit = row_of(root * (column_of(value[...]) - mean))

    c = total_members - 1.0
    s = energy * (1.0 / total_members) + c
    inverse = 1.0 / s
    a = c * inverse
    p = 1.5 - 0.5 * a
    p2 = p * p
    p3 = p2 * p
    base = 1.5 * p - 0.5 * a * p3
    q0 = -0.75 - 0.5 * (p3 - 1.5 * a * p2)
    q1 = -0.5 * (0.75 * a * p - 1.5 * p2)
    q2 = -0.5 * (0.75 * p - 0.125 * a)
    small = dot_rows(scaled_ref[...], scaled_ref[...]) * inverse
    diagonal = eye(slots)
    once = small.astype(jnp.bfloat16)
    square = dot(once, once).astype(jnp.bfloat16)
    tail = dot(square, (jnp.where(diagonal, q2, 0.0) + 0.0625 * small).astype(jnp.bfloat16))
    poly = jnp.where(diagonal, q0, 0.0) + q1 * small + tail

    def apply(vector):
        inner_part = jnp.sum(poly * vector, axis=1, keepdims=True)
        return jnp.sum(small * inner_part, axis=0, keepdims=True) + base * vector

    gain = apply(apply(misfit)) * inverse
    stretch = jnp.sqrt(a)
    alpha, factor = stretch * base, stretch * inverse
    centre = deviations(second, raw, dev, 0, far)
    cross = jnp.concatenate(
        [dot_rows(first[...], scaled_ref[...]), dot_rows(dev[...], scaled_ref[...])], axis=0
    )
    centre = jnp.concatenate([means[:, 0:1], centre], axis=0)
    shift = centre + jnp.sum(cross * gain, axis=1, keepdims=True)
    once = cross.astype(jnp.bfloat16)
    mix = sum(dot(once, part) for part in split(poly))
    mix = (mix * factor).astype(jnp.bfloat16)
    parts = ((first, 0, near, 0), (dev, 2 * near, far, near))
    for batch in batches(groups // 2, 2):
        made = []
        wide = slice(batch[0] * lanes, (batch[-1] + 1) * lanes)
        both = dot(mix, scaled_ref[:, wide]) + shift
        for j in batch:
            here = slice(j * lanes, (j + 1) * lanes)
            new = both[:, (j - batch[0]) * lanes :][:, :lanes]
            for ref, at, size, row in parts:
                one = new[at : at + 2 * size] + alpha * ref[:, here].astype(jnp.float32)
                pair = join(one[:size], one[size:], left_lanes((size, lanes)), members)
                made += [(2 * j + i, row, x.astype(jnp.bfloat16)) for i, x in enumerate(pair)]
        for group, row, value in made:
            out[group, row : row + value.shape[0], :] = value


def analyse(first, means, second, count, value, weight):
    groups, _, lanes = second.shape
    near = first.shape[0] // 2
    slots = value.shape[1]
    far = second.shape[1] - slots // 2
    total = groups * lanes // 2
    return pl.pallas_call(
        analyse_kernel,
        out_shape=jax.ShapeDtypeStruct((groups, near + far, lanes), jnp.bfloat16),
        in_specs=vmem(3) + smem(1) + vmem(2),
        out_specs=pl.BlockSpec(memory_space=pltpu.VMEM),
        scratch_shapes=[
            pltpu.VMEM((2 * far, total), jnp.float32),
            pltpu.VMEM((2 * far, total), jnp.bfloat16),
            pltpu.VMEM((slots, total), jnp.float32),
            pltpu.VMEM((slots, total), jnp.bfloat16),
        ],
        compiler_params=params(16),
        cost_estimate=cost(4 * 10**9, 4 * 2**20),
    )(first, means, second, count, value, weight)


def restore_kernel(blocks, out, turned):
    members, variables, levels, span, columns = out.shape
    lanes = members * variables
    identity = permutation(lanes, 0)
    near = span - 2 * STEPS
    for level in range(levels):
        made = []
        for r in range(0, span, 2):
            if STEPS <= r < span - STEPS:
                at = level * near + r - STEPS
            else:
                at = levels * near + level * 2 * STEPS + (r if r < STEPS else r - near)
            both = blocks[:, at * SPAN : (at + 2) * SPAN, :].astype(jnp.float32)
            for i in range(2):
                one = both[:, i * SPAN : (i + 1) * SPAN, :].reshape(columns, lanes)
                made.append((r + i, dot_rows(identity, one.astype(jnp.bfloat16))))
        for r, rows in made:
            turned[level % 2, pl.ds(r, lanes, stride=span), :] = rows
        for var in range(variables):
            half = turned[level % 2, var * members * span : (var + 1) * members * span, :]
            out[:, var, level] = half.reshape(members, span, columns).astype(jnp.bfloat16)


def restore(dims, blocks):
    members, variables, levels, span, columns = dims
    return pl.pallas_call(
        restore_kernel,
        out_shape=jax.ShapeDtypeStruct((members, variables, levels, span, columns), jnp.bfloat16),
        in_specs=vmem(1),
        out_specs=pl.BlockSpec(memory_space=pltpu.VMEM),
        scratch_shapes=[pltpu.VMEM((2, variables * members * span, columns), jnp.float32)],
        compiler_params=params(8),
        cost_estimate=cost(2 * 10**9, 2 * 2**20),
    )(blocks)


def neighbours(field, axis):
    count = lax.axis_size(axis)
    low = lax.ppermute(field, axis, [(i, (i + 1) % count) for i in range(count)])
    if count == 2:
        return (low,)
    return low, lax.ppermute(field, axis, [((i + 1) % count, i) for i in range(count)])


def exchange(blocks):
    return lax.all_to_all(blocks, "grp", split_axis=0, concat_axis=0, tiled=True)


def on_device(start, diffusivity, eastward, northward, cells, count, value, weight):
    members, variables, levels, span, columns = dims = start.shape
    whole = start.reshape(members * variables, levels, span, columns)
    own, centre, near, model = inner(whole, (diffusivity, eastward, northward), variables)
    sides = neighbours(own, "tile")
    first, means = prepare(exchange(near))
    grid, rim = outer(dims, own, sides, model, centre)
    second = exchange(pick(variables, grid, rim, cells[0]))
    updated = analyse(first, means, second, count, value[0], weight[0])
    return restore(dims, exchange(updated))


def solution(mesh):
    return jax.shard_map(
        on_device,
        mesh=mesh,
        in_specs=(
            P("grp", None, None, "tile", None),
            P(),
            P(),
            P(),
            P("tile", None, None),
            P("tile", "grp"),
            P("tile", "grp", None),
            P("tile", "grp", None),
        ),
        out_specs=P("grp", None, None, "tile", None),
        check_vma=False,
    )
```

```python
import functools

import jax
import jax.numpy as jnp
from jax import lax
from jax.experimental import pallas as pl
from jax.experimental.pallas import tpu as pltpu
from jax.sharding import PartitionSpec as P

SPAN = 8
STEPS = 2
EDGE = SPAN // 2

ROWS = (((1,), (1,)), ((), ()))


def params(mebibytes, **kw):
    return pltpu.CompilerParams(vmem_limit_bytes=mebibytes * 2**20, **kw)


def cost(flops, size):
    return pl.CostEstimate(flops=flops, bytes_accessed=size, transcendentals=0)


def vmem(count):
    return [pl.BlockSpec(memory_space=pltpu.VMEM)] * count


def hbm(count):
    return [pl.BlockSpec(memory_space=pltpu.HBM)] * count


def smem(count):
    return [pl.BlockSpec(memory_space=pltpu.SMEM)] * count


def dot(a, b, **kw):
    return jnp.dot(a, b, preferred_element_type=jnp.float32, **kw)


def split(x):
    high = x.astype(jnp.bfloat16)
    return high, (x - high.astype(jnp.float32)).astype(jnp.bfloat16)


def dot_rows(a, b):
    return lax.dot_general(a, b, ROWS, preferred_element_type=jnp.float32)


def permutation(size, shift):
    row = lax.broadcasted_iota(jnp.int32, (size, size), 0)
    column = lax.broadcasted_iota(jnp.int32, (size, size), 1)
    return (lax.rem(row + shift + size, size) == column).astype(jnp.bfloat16)


def eye(size):
    row = lax.broadcasted_iota(jnp.int32, (size, size), 0)
    column = lax.broadcasted_iota(jnp.int32, (size, size), 1)
    return row == column


def column_of(row):
    return jnp.sum(jnp.where(eye(row.shape[1]), row, 0.0), axis=1, keepdims=True)


def row_of(column):
    return jnp.sum(jnp.where(eye(column.shape[0]), column, 0.0), axis=0, keepdims=True)


def forecast_rows(read, first, last, coefficients):
    middle, east, west, north, south = coefficients

    def step(below, here, above):
        columns = here.shape[2]
        return (
            middle * here
            + east * above
            + west * below
            + north * pltpu.roll(here, columns - 1, 2)
            + south * pltpu.roll(here, 1, 2)
        )

    rows, once, twice = [read(first - 2), read(first - 1)], [], []
    for r in range(first - 1, last + 1):
        rows.append(read(r + 1))
        once.append(step(*rows[-3:]))
        if r >= first + 1:
            new = step(*once[-3:])
            twice.append((r - 1, new.reshape(-1, new.shape[2]).astype(jnp.bfloat16)))
    return twice


def coefficients_of(level, diff, east, north):
    spread = jnp.broadcast_to(diff[level : level + 1, :], (8, diff.shape[1]))
    u = 0.5 * east[level]
    w = 0.5 * north[level]
    return 1.0 - 4.0 * spread, spread - u, spread + u, spread - w, spread + w


def row_reader(level, var, own, low, high):
    span, columns = own.shape[2], own.shape[4]

    def read(r):
        ref, at = (low, r + span) if r < 0 else (own, r) if r < span else (high, r - span)
        return ref[var, level, at].reshape(-1, 8, columns)

    return read


def pack_rows(pairs, identity, store, first):
    lanes = pairs[0].shape[0] // 2
    packed = []
    for pair in pairs:
        turned = dot_rows(identity, pair)
        parts = [turned[:, i * lanes : (i + 1) * lanes].reshape(-1, SPAN, lanes) for i in range(2)]
        packed.append(jnp.concatenate(parts, axis=1).astype(jnp.bfloat16))
    for i, value in enumerate(packed):
        at = first + i * 2 * SPAN
        store[:, at : at + 2 * SPAN, :] = value


def inner_kernel(variables, own, *refs):
    raw, (slabs, fields, packed, model) = refs[:3], refs[3:7]
    local, (whole, staged, in_sems, raw_sems, out_sems) = refs[7:10], refs[10:]
    lanes, levels, span, columns = own.shape
    members = lanes // variables
    count = span - 2 * STEPS
    copies = [pltpu.make_async_copy(x, y, raw_sems.at[i]) for i, (x, y) in enumerate(zip(raw, local))]
    together = whole.shape[2]
    arrivals = []
    for i in range(levels // together):
        for part in range(2):
            here = pl.ds(part * (lanes // 2), lanes // 2)
            source = own.at[here, pl.ds(i * together, together)]
            arrivals.append(
                pltpu.make_async_copy(source, whole.at[i, here], in_sems.at[2 * i + part])
            )
    for copy in copies + arrivals:
        copy.start()
    for copy in copies:
        copy.wait()
    identity = permutation(columns, 0)
    leaving = []
    for level in range(levels):
        coefficients = coefficients_of(level, *local)
        for i, one in enumerate(coefficients):
            model[level, i] = one
        step, inside = divmod(level, together)
        if inside == 0:
            arrivals[2 * step].wait()
            arrivals[2 * step + 1].wait()
        view = whole.at[step].reshape(lanes * together * span, columns)
        reads, made = [], []
        for var in range(variables):

            def read(r):
                at = (var * together + inside) * span + r
                rows = view[pl.ds(at, members, stride=variables * together * span), :]
                reads.append((var, r, rows))
                return rows.reshape(-1, 8, columns)

            for r, value in forecast_rows(read, STEPS, span - STEPS, coefficients):
                made.append((var, r, value))
        pairs = []
        for first in range(STEPS, span - STEPS, 2):
            rows = [one for r in (first, first + 1) for _, at, one in made if at == r]
            pairs.append(jnp.concatenate(rows, axis=0))
        pack_rows(pairs, identity, staged.at[level], 0)
        here = pl.ds(level * count * SPAN, count * SPAN)
        leaving.append(pltpu.make_async_copy(staged.at[level], packed.at[:, here], out_sems.at[level]))
        leaving[-1].start()
        for var, r, value in made:
            fields[level, r - STEPS, var * members : (var + 1) * members, :] = value
        for var, r, rows in reads:
            slabs[var, level, r] = rows
    for copy in leaving:
        copy.wait()


def inner(own, raw, variables):
    lanes, levels, span, columns = own.shape
    members = lanes // variables
    blocks = columns // SPAN
    count = span - 2 * STEPS
    together = 1
    fixed = [pltpu.with_memory_space_constraint(x, pltpu.HBM) for x in (own, *raw)]
    return pl.pallas_call(
        functools.partial(inner_kernel, variables),
        out_shape=[
            jax.ShapeDtypeStruct((variables, levels, span, members, columns), jnp.float32),
            jax.ShapeDtypeStruct((levels, count, lanes, columns), jnp.bfloat16),
            jax.ShapeDtypeStruct((blocks, levels * count * SPAN, lanes), jnp.bfloat16),
            jax.ShapeDtypeStruct((levels, 5, 8, columns), jnp.float32),
        ],
        in_specs=hbm(4),
        out_specs=vmem(2) + hbm(1) + vmem(1),
        scratch_shapes=[
            pltpu.VMEM(raw[0].shape, jnp.float32),
            pltpu.SMEM(raw[1].shape, jnp.float32),
            pltpu.SMEM(raw[2].shape, jnp.float32),
            pltpu.VMEM((levels // together, lanes, together, span, columns), jnp.float32),
            pltpu.VMEM((levels, blocks, count * SPAN, lanes), jnp.bfloat16),
            pltpu.SemaphoreType.DMA((2 * levels // together,)),
            pltpu.SemaphoreType.DMA((3,)),
            pltpu.SemaphoreType.DMA((levels,)),
        ],
        compiler_params=params(10),
        cost_estimate=cost(2 * 10**9, 4 * 2**20),
    )(*fixed)


def outer_kernel(near, own, *rest):
    sides, rest = rest[:near], rest[near:]
    model, centre, grid, packed, staged, sems, out_sems = rest
    variables, levels, span, members, columns = own.shape
    rows_each = variables * members
    pairs = (2 * EDGE + span) // 2
    size = STEPS * 2 * SPAN
    identity = permutation(columns, 0)

    def leave(level):
        here = pl.ds(pl.multiple_of(level * size, size), size)
        return pltpu.make_async_copy(staged.at[level], packed.at[:, here], out_sems.at[level])

    copies = []
    for r in range(STEPS, span - STEPS):
        half, pair = divmod(r + EDGE, pairs)
        place = grid.at[:, pair, pl.ds(half * rows_each, rows_each)]
        copies.append(pltpu.make_async_copy(centre.at[:, r - STEPS], place, sems.at[r - STEPS]))
        copies[-1].start()

    @pl.loop(0, levels)
    def _(level):
        coefficients = [model[level, i] for i in range(5)]
        made = []
        for var in range(variables):
            read = row_reader(level, var, own, sides[0], sides[-1])
            for first, last in ((-EDGE, STEPS), (span - STEPS, span + EDGE)):
                for r, value in forecast_rows(read, first, last, coefficients):
                    made.append((var, r, value))
        sheets = []
        for first in (0, span - STEPS):
            rows = [one for r in range(first, first + STEPS) for _, at, one in made if at == r]
            sheets.append(jnp.concatenate(rows, axis=0))
        pack_rows(sheets, identity, staged.at[level], 0)
        leave(level).start()
        for var, r, value in made:
            half, pair = divmod(r + EDGE, pairs)
            at = half * rows_each + var * members
            grid[level, pair, at : at + members, :] = value

    for level in range(levels):
        leave(level).wait()
    for copy in copies:
        copy.wait()


def outer(dims, own, sides, model, centre, slots):
    members, variables, levels, span, columns = dims
    lanes = members * variables
    blocks = columns // SPAN
    near = len(sides)
    pairs = (2 * EDGE + span) // 2
    return pl.pallas_call(
        functools.partial(outer_kernel, near),
        out_shape=[
            jax.ShapeDtypeStruct((levels, pairs, 2 * lanes, columns), jnp.bfloat16),
            jax.ShapeDtypeStruct(
                (blocks, levels * 2 * STEPS * SPAN + slots // 2, lanes), jnp.bfloat16
            ),
        ],
        in_specs=vmem(2 + near) + hbm(1),
        out_specs=vmem(1) + hbm(1),
        scratch_shapes=[
            pltpu.VMEM((levels, blocks, 2 * STEPS * SPAN, lanes), jnp.bfloat16),
            pltpu.SemaphoreType.DMA((span - 2 * STEPS,)),
            pltpu.SemaphoreType.DMA((levels,)),
        ],
        compiler_params=params(16),
        cost_estimate=cost(2 * 10**9, 8 * 2**20),
    )(own, *sides, model, centre)


def pick_kernel(variables, together, grid, _, cells, out, region, codes, staged, sems):
    levels, pairs, twice, columns = grid.shape
    rows = twice // 2
    members = rows // variables
    blocks, slots = cells.shape
    width = 2 * EDGE + SPAN
    part = pairs * width
    entries = levels * part
    share = out.shape[1] - slots // 2

    order = permutation(columns, -EDGE)
    batch = next(n for n in (4, 2, 1) if pairs % n == 0)
    for level in range(levels):
        for start in range(0, pairs, batch):
            made = []
            for i in range(batch):
                even = dot_rows(order, grid[level, start + i])
                odd = jnp.concatenate([even[SPAN:], even[:SPAN]], axis=0)
                made.append((even.astype(jnp.bfloat16), odd.astype(jnp.bfloat16)))
            for i, both in enumerate(made):
                at = (level * pairs + start + i) * width
                for first, value in enumerate(both):
                    for j in range(columns // width):
                        piece = value[j * width : (j + 1) * width, :]
                        region[2 * j + first, at : at + width, :] = piece

    cell = cells[...]
    second = cell >= 2 * entries
    cell = jnp.where(second, cell - 2 * entries, cell)
    level = lax.shift_right_logical(cell, (2 * part).bit_length() - 1)
    inside = cell - level * (2 * part)
    lower = inside >= part
    code = level * part + jnp.where(lower, inside - part + entries, inside)
    codes[...] = jnp.where(second, code + 2 * entries, code).astype(jnp.float32)

    left = lax.broadcasted_iota(jnp.int32, (slots // 2, rows), 1) < members
    lane = lax.broadcasted_iota(jnp.int32, (slots, entries), 1).astype(jnp.float32)

    def leave(step):
        here = pl.ds(step * together, together)
        place = out.at[here, pl.ds(share, slots // 2)]
        return pltpu.make_async_copy(staged.at[here], place, sems.at[step])

    @pl.loop(0, blocks // together)
    def _(step):
        made = []
        for i in range(together):
            block = step * together + i
            at = column_of(codes[pl.ds(block, 1), :])
            second = at >= 2.0 * entries
            at = jnp.where(second, at - 2.0 * entries, at)
            lower = at >= 1.0 * entries
            at = jnp.where(lower, at - 1.0 * entries, at)
            pick = jnp.where(lane == at, 1.0, 0.0).astype(jnp.bfloat16)
            found = dot(pick, region[block])
            total = jnp.where(lower, found[:, rows:], found[:, :rows])
            other = pltpu.roll(total, members, 1)
            to_left = jnp.where(second, other, total)[: slots // 2]
            to_right = jnp.where(second, total, other)[slots // 2 :]
            made.append(jnp.where(left, to_left, to_right).astype(jnp.bfloat16))
        for i, value in enumerate(made):
            staged[step * together + i] = value
        leave(step).start()

    for step in range(blocks // together):
        leave(step).wait()


def pick(variables, grid, packed, cells):
    levels, pairs, twice, columns = grid.shape
    blocks, slots = cells.shape
    together = next(n for n in (4, 2, 1) if blocks % n == 0)
    return pl.pallas_call(
        functools.partial(pick_kernel, variables, together),
        out_shape=jax.ShapeDtypeStruct(packed.shape, packed.dtype),
        in_specs=vmem(1) + hbm(1) + vmem(1),
        out_specs=pl.BlockSpec(memory_space=pltpu.HBM),
        scratch_shapes=[
            pltpu.VMEM((blocks, levels * pairs * (2 * EDGE + SPAN), twice), jnp.bfloat16),
            pltpu.VMEM((blocks, slots), jnp.float32),
            pltpu.VMEM((blocks, slots // 2, packed.shape[2]), jnp.bfloat16),
            pltpu.SemaphoreType.DMA((blocks // together,)),
        ],
        input_output_aliases={1: 0},
        compiler_params=params(20),
        cost_estimate=cost(4 * 10**9, 4 * 2**20),
    )(grid, packed, cells)


def join(a, b, left, members):
    return (
        jnp.where(left, a, pltpu.roll(b, members, 1)),
        jnp.where(left, pltpu.roll(a, members, 1), b),
    )


def batches(count, size):
    return [range(at, min(count, at + size)) for at in range(0, count, size)]


def left_lanes(shape):
    return lax.broadcasted_iota(jnp.int32, shape, 1) < shape[1] // 2


def deviations(states, raw, dev, at, size):
    groups, _, lanes = states.shape
    members = lanes // 2
    left = left_lanes((size, lanes))
    sums = [jnp.zeros((size, lanes), jnp.float32)] * 2
    for batch in batches(groups // 2, 4):
        made = [
            join(
                states[2 * j, :size, :].astype(jnp.float32),
                states[2 * j + 1, :size, :].astype(jnp.float32),
                left,
                members,
            )
            for j in batch
        ]
        for j, pair in zip(batch, made):
            here = slice(j * lanes, (j + 1) * lanes)
            for var in range(2):
                raw[var * size : (var + 1) * size, here] = pair[var]
            sums = [total + one for total, one in zip(sums, pair)]
    centre = jnp.concatenate([jnp.sum(x, axis=1, keepdims=True) for x in sums], axis=0)
    centre = centre * (1.0 / (groups * members))
    dev[at : at + 2 * size, :] = (raw[...] - centre).astype(jnp.bfloat16)
    return centre


def prepare_kernel(states, dev, centre, raw):
    mean = deviations(states, raw, dev, 0, states.shape[1])
    centre[...] = jnp.broadcast_to(mean, centre.shape)


def prepare(states):
    groups, near, lanes = states.shape
    total = groups * lanes // 2
    return pl.pallas_call(
        prepare_kernel,
        out_shape=[
            jax.ShapeDtypeStruct((2 * near, total), jnp.bfloat16),
            jax.ShapeDtypeStruct((2 * near, lanes), jnp.float32),
        ],
        in_specs=vmem(1),
        out_specs=vmem(2),
        scratch_shapes=[pltpu.VMEM((2 * near, total), jnp.float32)],
        compiler_params=params(6),
        cost_estimate=cost(10**8, 2 * 2**20),
    )(states)


def analyse_kernel(first, means, second, count, value, weight, out, raw, dev, obs, scaled_ref):
    groups, _, lanes = second.shape
    near = first.shape[0] // 2
    half = obs.shape[0] // 2
    far = second.shape[1] - half
    side = near + far
    slots = 2 * half
    members = lanes // 2
    total_members = groups * members
    left = left_lanes((half, lanes))

    for batch in batches(groups // 2, 4):
        made = [
            join(
                second[2 * j, far:, :].astype(jnp.float32),
                second[2 * j + 1, far:, :].astype(jnp.float32),
                left,
                members,
            )
            for j in batch
        ]
        for j, pair in zip(batch, made):
            here = slice(j * lanes, (j + 1) * lanes)
            obs[:half, here], obs[half:, here] = pair

    used = lax.broadcasted_iota(jnp.int32, (1, slots), 1) < count[0, 0]
    root = column_of(jnp.where(used, jnp.sqrt(weight[...]), 0.0))
    observed = obs[...]
    mean = jnp.sum(observed, axis=1, keepdims=True) * (1.0 / total_members)
    scaled = (observed - mean) * root
    energy = jnp.sum(jnp.sum(scaled * scaled, axis=1, keepdims=True), axis=0, keepdims=True)
    scaled_ref[...] = scaled.astype(jnp.bfloat16)
    misfit = row_of(root * (column_of(value[...]) - mean))

    c = total_members - 1.0
    s = energy * (1.0 / total_members) + c
    inverse = 1.0 / s
    a = c * inverse
    p = 1.5 - 0.5 * a
    p2 = p * p
    p3 = p2 * p
    base = 1.5 * p - 0.5 * a * p3
    q0 = -0.75 - 0.5 * (p3 - 1.5 * a * p2)
    q1 = -0.5 * (0.75 * a * p - 1.5 * p2)
    q2 = -0.5 * (0.75 * p - 0.125 * a)
    small = dot_rows(scaled_ref[...], scaled_ref[...]) * inverse
    diagonal = eye(slots)
    once = small.astype(jnp.bfloat16)
    square = dot(once, once).astype(jnp.bfloat16)
    tail = dot(square, (jnp.where(diagonal, q2, 0.0) + 0.0625 * small).astype(jnp.bfloat16))
    poly = jnp.where(diagonal, q0, 0.0) + q1 * small + tail

    def apply(vector):
        inner_part = jnp.sum(poly * vector, axis=1, keepdims=True)
        return jnp.sum(small * inner_part, axis=0, keepdims=True) + base * vector

    gain = apply(apply(misfit)) * inverse
    stretch = jnp.sqrt(a)
    alpha, factor = stretch * base, stretch * inverse
    centre = deviations(second, raw, dev, 0, far)
    cross = jnp.concatenate(
        [dot_rows(first[...], scaled_ref[...]), dot_rows(dev[...], scaled_ref[...])], axis=0
    )
    centre = jnp.concatenate([means[:, 0:1], centre], axis=0)
    shift = centre + jnp.sum(cross * gain, axis=1, keepdims=True)
    once = cross.astype(jnp.bfloat16)
    mix = sum(dot(once, part) for part in split(poly))
    mix = (mix * factor).astype(jnp.bfloat16)
    parts = ((first, 0, near, 0), (dev, 2 * near, far, near))
    for batch in batches(groups // 2, 2):
        made = []
        wide = slice(batch[0] * lanes, (batch[-1] + 1) * lanes)
        both = dot(mix, scaled_ref[:, wide]) + shift
        for j in batch:
            here = slice(j * lanes, (j + 1) * lanes)
            new = both[:, (j - batch[0]) * lanes :][:, :lanes]
            for ref, at, size, row in parts:
                one = new[at : at + 2 * size] + alpha * ref[:, here].astype(jnp.float32)
                pair = join(one[:size], one[size:], left_lanes((size, lanes)), members)
                made += [(2 * j + i, row, x.astype(jnp.bfloat16)) for i, x in enumerate(pair)]
        for group, row, value in made:
            out[group, row : row + value.shape[0], :] = value


def analyse(first, means, second, count, value, weight):
    groups, _, lanes = second.shape
    near = first.shape[0] // 2
    slots = value.shape[1]
    far = second.shape[1] - slots // 2
    total = groups * lanes // 2
    return pl.pallas_call(
        analyse_kernel,
        out_shape=jax.ShapeDtypeStruct((groups, near + far, lanes), jnp.bfloat16),
        in_specs=vmem(3) + smem(1) + vmem(2),
        out_specs=pl.BlockSpec(memory_space=pltpu.VMEM),
        scratch_shapes=[
            pltpu.VMEM((2 * far, total), jnp.float32),
            pltpu.VMEM((2 * far, total), jnp.bfloat16),
            pltpu.VMEM((slots, total), jnp.float32),
            pltpu.VMEM((slots, total), jnp.bfloat16),
        ],
        compiler_params=params(16),
        cost_estimate=cost(4 * 10**9, 4 * 2**20),
    )(first, means, second, count, value, weight)


def restore_kernel(blocks, out, turned):
    members, variables, levels, span, columns = out.shape
    lanes = members * variables
    identity = permutation(lanes, 0)
    near = span - 2 * STEPS
    for level in range(levels):
        made = []
        for r in range(0, span, 2):
            if STEPS <= r < span - STEPS:
                at = level * near + r - STEPS
            else:
                at = levels * near + level * 2 * STEPS + (r if r < STEPS else r - near)
            both = blocks[:, at * SPAN : (at + 2) * SPAN, :].astype(jnp.float32)
            for i in range(2):
                one = both[:, i * SPAN : (i + 1) * SPAN, :].reshape(columns, lanes)
                made.append((r + i, dot_rows(identity, one.astype(jnp.bfloat16))))
        for r, rows in made:
            turned[level % 2, pl.ds(r, lanes, stride=span), :] = rows
        for var in range(variables):
            half = turned[level % 2, var * members * span : (var + 1) * members * span, :]
            out[:, var, level] = half.reshape(members, span, columns).astype(jnp.bfloat16)


def restore(dims, blocks):
    members, variables, levels, span, columns = dims
    return pl.pallas_call(
        restore_kernel,
        out_shape=jax.ShapeDtypeStruct((members, variables, levels, span, columns), jnp.bfloat16),
        in_specs=vmem(1),
        out_specs=pl.BlockSpec(memory_space=pltpu.VMEM),
        scratch_shapes=[pltpu.VMEM((2, variables * members * span, columns), jnp.float32)],
        compiler_params=params(8),
        cost_estimate=cost(2 * 10**9, 2 * 2**20),
    )(blocks)


def neighbours(field, axis):
    count = lax.axis_size(axis)
    low = lax.ppermute(field, axis, [(i, (i + 1) % count) for i in range(count)])
    if count == 2:
        return (low,)
    return low, lax.ppermute(field, axis, [((i + 1) % count, i) for i in range(count)])


def exchange(blocks):
    return lax.all_to_all(blocks, "grp", split_axis=0, concat_axis=0, tiled=True)


def on_device(start, diffusivity, eastward, northward, cells, count, value, weight):
    members, variables, levels, span, columns = dims = start.shape
    whole = start.reshape(members * variables, levels, span, columns)
    own, centre, near, model = inner(whole, (diffusivity, eastward, northward), variables)
    sides = neighbours(own, "tile")
    first, means = prepare(exchange(near))
    grid, packed = outer(dims, own, sides, model, centre, cells.shape[2])
    second = exchange(pick(variables, grid, packed, cells[0]))
    updated = analyse(first, means, second, count, value[0], weight[0])
    return restore(dims, exchange(updated))


def solution(mesh):
    return jax.shard_map(
        on_device,
        mesh=mesh,
        in_specs=(
            P("grp", None, None, "tile", None),
            P(),
            P(),
            P(),
            P("tile", None, None),
            P("tile", "grp"),
            P("tile", "grp", None),
            P("tile", "grp", None),
        ),
        out_specs=P("grp", None, None, "tile", None),
        check_vma=False,
    )
```

```python
import functools

import jax
import jax.numpy as jnp
from jax import lax
from jax.experimental import pallas as pl
from jax.experimental.pallas import tpu as pltpu
from jax.sharding import PartitionSpec as P

SPAN = 8
STEPS = 2
EDGE = SPAN // 2

ROWS = (((1,), (1,)), ((), ()))


def params(mebibytes, **kw):
    return pltpu.CompilerParams(vmem_limit_bytes=mebibytes * 2**20, **kw)


def cost(flops, size):
    return pl.CostEstimate(flops=flops, bytes_accessed=size, transcendentals=0)


def vmem(count):
    return [pl.BlockSpec(memory_space=pltpu.VMEM)] * count


def hbm(count):
    return [pl.BlockSpec(memory_space=pltpu.HBM)] * count


def smem(count):
    return [pl.BlockSpec(memory_space=pltpu.SMEM)] * count


def dot(a, b, **kw):
    return jnp.dot(a, b, preferred_element_type=jnp.float32, **kw)


def split(x):
    high = x.astype(jnp.bfloat16)
    return high, (x - high.astype(jnp.float32)).astype(jnp.bfloat16)


def dot_rows(a, b):
    return lax.dot_general(a, b, ROWS, preferred_element_type=jnp.float32)


def permutation(size, shift):
    row = lax.broadcasted_iota(jnp.int32, (size, size), 0)
    column = lax.broadcasted_iota(jnp.int32, (size, size), 1)
    return (lax.rem(row + shift + size, size) == column).astype(jnp.bfloat16)


def eye(size):
    row = lax.broadcasted_iota(jnp.int32, (size, size), 0)
    column = lax.broadcasted_iota(jnp.int32, (size, size), 1)
    return row == column


def column_of(row):
    return jnp.sum(jnp.where(eye(row.shape[1]), row, 0.0), axis=1, keepdims=True)


def row_of(column):
    return jnp.sum(jnp.where(eye(column.shape[0]), column, 0.0), axis=0, keepdims=True)


def both_ways(columns):
    pair = jnp.concatenate([permutation(columns, -1), permutation(columns, 1)], axis=1)
    return jnp.concatenate([pair, pair], axis=0)


def forecast_rows(read, first, last, coefficients, shifts):
    middle, east, west, north, south = coefficients

    def step(below, here, above, ahead, behind):
        return middle * here + east * above + west * below + north * ahead + south * behind

    rows = [read(r) for r in range(first - 2, last + 2)]
    tiles, _, columns = rows[0].shape
    flat = jnp.concatenate(rows[1:-1], axis=0).reshape(-1, columns)
    moved = dot(jnp.concatenate(split(flat), axis=1), shifts)
    ahead = moved[:, :columns].reshape(-1, 8, columns)
    behind = moved[:, columns:].reshape(-1, 8, columns)
    once, twice = [], []
    for i, r in enumerate(range(first - 1, last + 1)):
        here = slice(i * tiles, (i + 1) * tiles)
        once.append(step(*rows[i : i + 3], ahead[here], behind[here]))
        if i >= 2:
            one = once[-2]
            new = step(*once[-3:], pltpu.roll(one, columns - 1, 2), pltpu.roll(one, 1, 2))
            twice.append((r - 1, new.reshape(-1, columns).astype(jnp.bfloat16)))
    return twice


def coefficients_of(level, diff, east, north):
    spread = jnp.broadcast_to(diff[level : level + 1, :], (8, diff.shape[1]))
    u = 0.5 * east[level]
    w = 0.5 * north[level]
    return 1.0 - 4.0 * spread, spread - u, spread + u, spread - w, spread + w


def row_reader(level, var, own, low, high):
    span, columns = own.shape[2], own.shape[4]

    def read(r):
        ref, at = (low, r + span) if r < 0 else (own, r) if r < span else (high, r - span)
        return ref[var, level, at].reshape(-1, 8, columns)

    return read


def pack_rows(pairs, identity, store, first):
    lanes = pairs[0].shape[0] // 2
    packed = []
    for pair in pairs:
        turned = dot_rows(identity, pair)
        parts = [turned[:, i * lanes : (i + 1) * lanes].reshape(-1, SPAN, lanes) for i in range(2)]
        packed.append(jnp.concatenate(parts, axis=1).astype(jnp.bfloat16))
    for i, value in enumerate(packed):
        at = first + i * 2 * SPAN
        store[:, at : at + 2 * SPAN, :] = value


def inner_kernel(variables, own, *refs):
    raw, (slabs, fields, packed, model) = refs[:3], refs[3:7]
    local, (whole, staged, in_sems, raw_sems, out_sems) = refs[7:10], refs[10:]
    lanes, levels, span, columns = own.shape
    members = lanes // variables
    count = span - 2 * STEPS
    copies = [pltpu.make_async_copy(x, y, raw_sems.at[i]) for i, (x, y) in enumerate(zip(raw, local))]
    together = whole.shape[2]
    arrivals = []
    for i in range(levels // together):
        for part in range(2):
            here = pl.ds(part * (lanes // 2), lanes // 2)
            source = own.at[here, pl.ds(i * together, together)]
            arrivals.append(
                pltpu.make_async_copy(source, whole.at[i, here], in_sems.at[2 * i + part])
            )
    for copy in copies + arrivals:
        copy.start()
    for copy in copies:
        copy.wait()
    identity = permutation(columns, 0)
    shifts = both_ways(columns)
    leaving = []
    for level in range(levels):
        coefficients = coefficients_of(level, *local)
        for i, one in enumerate(coefficients):
            model[level, i] = one
        step, inside = divmod(level, together)
        if inside == 0:
            arrivals[2 * step].wait()
            arrivals[2 * step + 1].wait()
        view = whole.at[step].reshape(lanes * together * span, columns)
        reads, made = [], []
        for var in range(variables):

            def read(r):
                at = (var * together + inside) * span + r
                rows = view[pl.ds(at, members, stride=variables * together * span), :]
                reads.append((var, r, rows))
                return rows.reshape(-1, 8, columns)

            for r, value in forecast_rows(read, STEPS, span - STEPS, coefficients, shifts):
                made.append((var, r, value))
        pairs = []
        for first in range(STEPS, span - STEPS, 2):
            rows = [one for r in (first, first + 1) for _, at, one in made if at == r]
            pairs.append(jnp.concatenate(rows, axis=0))
        pack_rows(pairs, identity, staged.at[level], 0)
        here = pl.ds(level * count * SPAN, count * SPAN)
        leaving.append(pltpu.make_async_copy(staged.at[level], packed.at[:, here], out_sems.at[level]))
        leaving[-1].start()
        for var, r, value in made:
            fields[level, r - STEPS, var * members : (var + 1) * members, :] = value
        for var, r, rows in reads:
            slabs[var, level, r] = rows
    for copy in leaving:
        copy.wait()


def inner(own, raw, variables):
    lanes, levels, span, columns = own.shape
    members = lanes // variables
    blocks = columns // SPAN
    count = span - 2 * STEPS
    together = 1
    fixed = [pltpu.with_memory_space_constraint(x, pltpu.HBM) for x in (own, *raw)]
    return pl.pallas_call(
        functools.partial(inner_kernel, variables),
        out_shape=[
            jax.ShapeDtypeStruct((variables, levels, span, members, columns), jnp.float32),
            jax.ShapeDtypeStruct((levels, count, lanes, columns), jnp.bfloat16),
            jax.ShapeDtypeStruct((blocks, levels * count * SPAN, lanes), jnp.bfloat16),
            jax.ShapeDtypeStruct((levels, 5, 8, columns), jnp.float32),
        ],
        in_specs=hbm(4),
        out_specs=vmem(2) + hbm(1) + vmem(1),
        scratch_shapes=[
            pltpu.VMEM(raw[0].shape, jnp.float32),
            pltpu.SMEM(raw[1].shape, jnp.float32),
            pltpu.SMEM(raw[2].shape, jnp.float32),
            pltpu.VMEM((levels // together, lanes, together, span, columns), jnp.float32),
            pltpu.VMEM((levels, blocks, count * SPAN, lanes), jnp.bfloat16),
            pltpu.SemaphoreType.DMA((2 * levels // together,)),
            pltpu.SemaphoreType.DMA((3,)),
            pltpu.SemaphoreType.DMA((levels,)),
        ],
        compiler_params=params(10),
        cost_estimate=cost(2 * 10**9, 4 * 2**20),
    )(*fixed)


def outer_kernel(near, own, *rest):
    sides, rest = rest[:near], rest[near:]
    model, centre, grid, packed, staged, near_tiles, sems, out_sems, near_sems = rest
    variables, levels, span, members, columns = own.shape
    rows_each = variables * members
    pairs = (2 * EDGE + span) // 2
    size = STEPS * 2 * SPAN
    identity = permutation(columns, 0)
    shifts = both_ways(columns)

    def arrive(level):
        return [
            pltpu.make_async_copy(
                side.at[:, level], near_tiles.at[i, :, level], near_sems.at[i, level]
            )
            for i, side in enumerate(sides)
        ]

    for level in range(levels):
        for copy in arrive(level):
            copy.start()

    def leave(level):
        here = pl.ds(pl.multiple_of(level * size, size), size)
        return pltpu.make_async_copy(staged.at[level], packed.at[:, here], out_sems.at[level])

    copies = []
    for r in range(STEPS, span - STEPS):
        half, pair = divmod(r + EDGE, pairs)
        place = grid.at[:, pair, pl.ds(half * rows_each, rows_each)]
        copies.append(pltpu.make_async_copy(centre.at[:, r - STEPS], place, sems.at[r - STEPS]))
        copies[-1].start()

    @pl.loop(0, levels)
    def _(level):
        for copy in arrive(level):
            copy.wait()
        coefficients = [model[level, i] for i in range(5)]
        made = []
        for var in range(variables):
            read = row_reader(level, var, own, near_tiles.at[0], near_tiles.at[near - 1])
            for first, last in ((-EDGE, STEPS), (span - STEPS, span + EDGE)):
                for r, value in forecast_rows(read, first, last, coefficients, shifts):
                    made.append((var, r, value))
        sheets = []
        for first in (0, span - STEPS):
            rows = [one for r in range(first, first + STEPS) for _, at, one in made if at == r]
            sheets.append(jnp.concatenate(rows, axis=0))
        pack_rows(sheets, identity, staged.at[level], 0)
        leave(level).start()
        for var, r, value in made:
            half, pair = divmod(r + EDGE, pairs)
            at = half * rows_each + var * members
            grid[level, pair, at : at + members, :] = value

    for level in range(levels):
        leave(level).wait()
    for copy in copies:
        copy.wait()


def outer(dims, own, sides, model, centre, slots):
    members, variables, levels, span, columns = dims
    lanes = members * variables
    blocks = columns // SPAN
    near = len(sides)
    pairs = (2 * EDGE + span) // 2
    return pl.pallas_call(
        functools.partial(outer_kernel, near),
        out_shape=[
            jax.ShapeDtypeStruct((levels, pairs, 2 * lanes, columns), jnp.bfloat16),
            jax.ShapeDtypeStruct(
                (blocks, levels * 2 * STEPS * SPAN + slots // 2, lanes), jnp.bfloat16
            ),
        ],
        in_specs=vmem(1) + hbm(near) + vmem(1) + hbm(1),
        out_specs=vmem(1) + hbm(1),
        scratch_shapes=[
            pltpu.VMEM((levels, blocks, 2 * STEPS * SPAN, lanes), jnp.bfloat16),
            pltpu.VMEM((near, *own.shape), jnp.float32),
            pltpu.SemaphoreType.DMA((span - 2 * STEPS,)),
            pltpu.SemaphoreType.DMA((levels,)),
            pltpu.SemaphoreType.DMA((near, levels)),
        ],
        compiler_params=params(16),
        cost_estimate=cost(2 * 10**9, 8 * 2**20),
    )(own, *(pltpu.with_memory_space_constraint(x, pltpu.HBM) for x in sides), model, centre)


def pick_kernel(variables, together, grid, _, cells, out, region, codes, staged, sems):
    levels, pairs, twice, columns = grid.shape
    rows = twice // 2
    members = rows // variables
    blocks, slots = cells.shape
    width = 2 * EDGE + SPAN
    part = pairs * width
    entries = levels * part
    share = out.shape[1] - slots // 2

    order = permutation(columns, -EDGE)
    batch = next(n for n in (4, 2, 1) if pairs % n == 0)
    for level in range(levels):
        for start in range(0, pairs, batch):
            made = []
            for i in range(batch):
                even = dot_rows(order, grid[level, start + i])
                odd = jnp.concatenate([even[SPAN:], even[:SPAN]], axis=0)
                made.append((even.astype(jnp.bfloat16), odd.astype(jnp.bfloat16)))
            for i, both in enumerate(made):
                at = (level * pairs + start + i) * width
                for first, value in enumerate(both):
                    for j in range(columns // width):
                        piece = value[j * width : (j + 1) * width, :]
                        region[2 * j + first, at : at + width, :] = piece

    cell = cells[...]
    second = cell >= 2 * entries
    cell = jnp.where(second, cell - 2 * entries, cell)
    level = lax.shift_right_logical(cell, (2 * part).bit_length() - 1)
    inside = cell - level * (2 * part)
    lower = inside >= part
    code = level * part + jnp.where(lower, inside - part + entries, inside)
    codes[...] = jnp.where(second, code + 2 * entries, code).astype(jnp.float32)

    left = lax.broadcasted_iota(jnp.int32, (slots // 2, rows), 1) < members
    lane = lax.broadcasted_iota(jnp.int32, (slots, entries), 1).astype(jnp.float32)

    def leave(step):
        here = pl.ds(step * together, together)
        place = out.at[here, pl.ds(share, slots // 2)]
        return pltpu.make_async_copy(staged.at[here], place, sems.at[step])

    @pl.loop(0, blocks // together)
    def _(step):
        made = []
        for i in range(together):
            block = step * together + i
            at = column_of(codes[pl.ds(block, 1), :])
            second = at >= 2.0 * entries
            at = jnp.where(second, at - 2.0 * entries, at)
            lower = at >= 1.0 * entries
            at = jnp.where(lower, at - 1.0 * entries, at)
            pick = jnp.where(lane == at, 1.0, 0.0).astype(jnp.bfloat16)
            found = dot(pick, region[block])
            total = jnp.where(lower, found[:, rows:], found[:, :rows])
            other = pltpu.roll(total, members, 1)
            to_left = jnp.where(second, other, total)[: slots // 2]
            to_right = jnp.where(second, total, other)[slots // 2 :]
            made.append(jnp.where(left, to_left, to_right).astype(jnp.bfloat16))
        for i, value in enumerate(made):
            staged[step * together + i] = value
        leave(step).start()

    for step in range(blocks // together):
        leave(step).wait()


def pick(variables, grid, packed, cells):
    levels, pairs, twice, columns = grid.shape
    blocks, slots = cells.shape
    together = next(n for n in (4, 2, 1) if blocks % n == 0)
    return pl.pallas_call(
        functools.partial(pick_kernel, variables, together),
        out_shape=jax.ShapeDtypeStruct(packed.shape, packed.dtype),
        in_specs=vmem(1) + hbm(1) + vmem(1),
        out_specs=pl.BlockSpec(memory_space=pltpu.HBM),
        scratch_shapes=[
            pltpu.VMEM((blocks, levels * pairs * (2 * EDGE + SPAN), twice), jnp.bfloat16),
            pltpu.VMEM((blocks, slots), jnp.float32),
            pltpu.VMEM((blocks, slots // 2, packed.shape[2]), jnp.bfloat16),
            pltpu.SemaphoreType.DMA((blocks // together,)),
        ],
        input_output_aliases={1: 0},
        compiler_params=params(20),
        cost_estimate=cost(4 * 10**9, 4 * 2**20),
    )(grid, packed, cells)


def join(a, b, left, members):
    return (
        jnp.where(left, a, pltpu.roll(b, members, 1)),
        jnp.where(left, pltpu.roll(a, members, 1), b),
    )


def batches(count, size):
    return [range(at, min(count, at + size)) for at in range(0, count, size)]


def left_lanes(shape):
    return lax.broadcasted_iota(jnp.int32, shape, 1) < shape[1] // 2


def deviations(states, raw, dev, at, size):
    groups, _, lanes = states.shape
    members = lanes // 2
    left = left_lanes((size, lanes))
    sums = [jnp.zeros((size, lanes), jnp.float32)] * 2
    for batch in batches(groups // 2, 4):
        made = [
            join(
                states[2 * j, :size, :].astype(jnp.float32),
                states[2 * j + 1, :size, :].astype(jnp.float32),
                left,
                members,
            )
            for j in batch
        ]
        for j, pair in zip(batch, made):
            here = slice(j * lanes, (j + 1) * lanes)
            for var in range(2):
                raw[var * size : (var + 1) * size, here] = pair[var]
            sums = [total + one for total, one in zip(sums, pair)]
    centre = jnp.concatenate([jnp.sum(x, axis=1, keepdims=True) for x in sums], axis=0)
    centre = centre * (1.0 / (groups * members))
    dev[at : at + 2 * size, :] = (raw[...] - centre).astype(jnp.bfloat16)
    return centre


def prepare_kernel(states, dev, centre, raw):
    mean = deviations(states, raw, dev, 0, states.shape[1])
    centre[...] = jnp.broadcast_to(mean, centre.shape)


def prepare(states):
    groups, near, lanes = states.shape
    total = groups * lanes // 2
    return pl.pallas_call(
        prepare_kernel,
        out_shape=[
            jax.ShapeDtypeStruct((2 * near, total), jnp.bfloat16),
            jax.ShapeDtypeStruct((2 * near, lanes), jnp.float32),
        ],
        in_specs=vmem(1),
        out_specs=vmem(2),
        scratch_shapes=[pltpu.VMEM((2 * near, total), jnp.float32)],
        compiler_params=params(6),
        cost_estimate=cost(10**8, 2 * 2**20),
    )(states)


def analyse_kernel(first, means, second, count, value, weight, out, raw, dev, obs, scaled_ref):
    groups, _, lanes = second.shape
    near = first.shape[0] // 2
    half = obs.shape[0] // 2
    far = second.shape[1] - half
    side = near + far
    slots = 2 * half
    members = lanes // 2
    total_members = groups * members
    left = left_lanes((half, lanes))

    for batch in batches(groups // 2, 4):
        made = [
            join(
                second[2 * j, far:, :].astype(jnp.float32),
                second[2 * j + 1, far:, :].astype(jnp.float32),
                left,
                members,
            )
            for j in batch
        ]
        for j, pair in zip(batch, made):
            here = slice(j * lanes, (j + 1) * lanes)
            obs[:half, here], obs[half:, here] = pair

    used = lax.broadcasted_iota(jnp.int32, (1, slots), 1) < count[0, 0]
    root = column_of(jnp.where(used, jnp.sqrt(weight[...]), 0.0))
    observed = obs[...]
    mean = jnp.sum(observed, axis=1, keepdims=True) * (1.0 / total_members)
    scaled = (observed - mean) * root
    energy = jnp.sum(jnp.sum(scaled * scaled, axis=1, keepdims=True), axis=0, keepdims=True)
    scaled_ref[...] = scaled.astype(jnp.bfloat16)
    misfit = row_of(root * (column_of(value[...]) - mean))

    c = total_members - 1.0
    s = energy * (1.0 / total_members) + c
    inverse = 1.0 / s
    a = c * inverse
    p = 1.5 - 0.5 * a
    p2 = p * p
    p3 = p2 * p
    base = 1.5 * p - 0.5 * a * p3
    q0 = -0.75 - 0.5 * (p3 - 1.5 * a * p2)
    q1 = -0.5 * (0.75 * a * p - 1.5 * p2)
    q2 = -0.5 * (0.75 * p - 0.125 * a)
    small = dot_rows(scaled_ref[...], scaled_ref[...]) * inverse
    diagonal = eye(slots)
    once = small.astype(jnp.bfloat16)
    square = dot(once, once).astype(jnp.bfloat16)
    tail = dot(square, (jnp.where(diagonal, q2, 0.0) + 0.0625 * small).astype(jnp.bfloat16))
    poly = jnp.where(diagonal, q0, 0.0) + q1 * small + tail

    def apply(vector):
        inner_part = jnp.sum(poly * vector, axis=1, keepdims=True)
        return jnp.sum(small * inner_part, axis=0, keepdims=True) + base * vector

    gain = apply(apply(misfit)) * inverse
    stretch = jnp.sqrt(a)
    alpha, factor = stretch * base, stretch * inverse
    centre = deviations(second, raw, dev, 0, far)
    cross = jnp.concatenate(
        [dot_rows(first[...], scaled_ref[...]), dot_rows(dev[...], scaled_ref[...])], axis=0
    )
    centre = jnp.concatenate([means[:, 0:1], centre], axis=0)
    shift = centre + jnp.sum(cross * gain, axis=1, keepdims=True)
    once = cross.astype(jnp.bfloat16)
    mix = sum(dot(once, part) for part in split(poly))
    mix = (mix * factor).astype(jnp.bfloat16)
    parts = ((first, 0, near, 0), (dev, 2 * near, far, near))
    for batch in batches(groups // 2, 2):
        made = []
        wide = slice(batch[0] * lanes, (batch[-1] + 1) * lanes)
        both = dot(mix, scaled_ref[:, wide]) + shift
        for j in batch:
            here = slice(j * lanes, (j + 1) * lanes)
            new = both[:, (j - batch[0]) * lanes :][:, :lanes]
            for ref, at, size, row in parts:
                one = new[at : at + 2 * size] + alpha * ref[:, here].astype(jnp.float32)
                pair = join(one[:size], one[size:], left_lanes((size, lanes)), members)
                made += [(2 * j + i, row, x.astype(jnp.bfloat16)) for i, x in enumerate(pair)]
        for group, row, value in made:
            out[group, row : row + value.shape[0], :] = value


def analyse(first, means, second, count, value, weight):
    groups, _, lanes = second.shape
    near = first.shape[0] // 2
    slots = value.shape[1]
    far = second.shape[1] - slots // 2
    total = groups * lanes // 2
    return pl.pallas_call(
        analyse_kernel,
        out_shape=jax.ShapeDtypeStruct((groups, near + far, lanes), jnp.bfloat16),
        in_specs=vmem(3) + smem(1) + vmem(2),
        out_specs=pl.BlockSpec(memory_space=pltpu.VMEM),
        scratch_shapes=[
            pltpu.VMEM((2 * far, total), jnp.float32),
            pltpu.VMEM((2 * far, total), jnp.bfloat16),
            pltpu.VMEM((slots, total), jnp.float32),
            pltpu.VMEM((slots, total), jnp.bfloat16),
        ],
        compiler_params=params(16),
        cost_estimate=cost(4 * 10**9, 4 * 2**20),
    )(first, means, second, count, value, weight)


def restore_kernel(blocks, out, turned):
    members, variables, levels, span, columns = out.shape
    lanes = members * variables
    identity = permutation(lanes, 0)
    near = span - 2 * STEPS
    for level in range(levels):
        made = []
        for r in range(0, span, 2):
            if STEPS <= r < span - STEPS:
                at = level * near + r - STEPS
            else:
                at = levels * near + level * 2 * STEPS + (r if r < STEPS else r - near)
            both = blocks[:, at * SPAN : (at + 2) * SPAN, :].astype(jnp.float32)
            for i in range(2):
                one = both[:, i * SPAN : (i + 1) * SPAN, :].reshape(columns, lanes)
                made.append((r + i, dot_rows(identity, one.astype(jnp.bfloat16))))
        for r, rows in made:
            turned[level % 2, pl.ds(r, lanes, stride=span), :] = rows
        for var in range(variables):
            half = turned[level % 2, var * members * span : (var + 1) * members * span, :]
            out[:, var, level] = half.reshape(members, span, columns).astype(jnp.bfloat16)


def restore(dims, blocks):
    members, variables, levels, span, columns = dims
    return pl.pallas_call(
        restore_kernel,
        out_shape=jax.ShapeDtypeStruct((members, variables, levels, span, columns), jnp.bfloat16),
        in_specs=vmem(1),
        out_specs=pl.BlockSpec(memory_space=pltpu.VMEM),
        scratch_shapes=[pltpu.VMEM((2, variables * members * span, columns), jnp.float32)],
        compiler_params=params(8),
        cost_estimate=cost(2 * 10**9, 2 * 2**20),
    )(blocks)


def neighbours(field, axis):
    count = lax.axis_size(axis)
    low = lax.ppermute(field, axis, [(i, (i + 1) % count) for i in range(count)])
    if count == 2:
        return (low,)
    return low, lax.ppermute(field, axis, [((i + 1) % count, i) for i in range(count)])


def exchange(blocks):
    return lax.all_to_all(blocks, "grp", split_axis=0, concat_axis=0, tiled=True)


def on_device(start, diffusivity, eastward, northward, cells, count, value, weight):
    members, variables, levels, span, columns = dims = start.shape
    whole = start.reshape(members * variables, levels, span, columns)
    own, centre, near, model = inner(whole, (diffusivity, eastward, northward), variables)
    sides = neighbours(own, "tile")
    first, means = prepare(exchange(near))
    grid, packed = outer(dims, own, sides, model, centre, cells.shape[2])
    second = exchange(pick(variables, grid, packed, cells[0]))
    updated = analyse(first, means, second, count, value[0], weight[0])
    return restore(dims, exchange(updated))


def solution(mesh):
    return jax.shard_map(
        on_device,
        mesh=mesh,
        in_specs=(
            P("grp", None, None, "tile", None),
            P(),
            P(),
            P(),
            P("tile", None, None),
            P("tile", "grp"),
            P("tile", "grp", None),
            P("tile", "grp", None),
        ),
        out_specs=P("grp", None, None, "tile", None),
        check_vma=False,
    )
```

```python
import functools

import jax
import jax.numpy as jnp
from jax import lax
from jax.experimental import pallas as pl
from jax.experimental.pallas import tpu as pltpu
from jax.sharding import PartitionSpec as P

SPAN = 8
STEPS = 2
EDGE = SPAN // 2

ROWS = (((1,), (1,)), ((), ()))


def params(mebibytes, **kw):
    return pltpu.CompilerParams(vmem_limit_bytes=mebibytes * 2**20, **kw)


def cost(flops, size):
    return pl.CostEstimate(flops=flops, bytes_accessed=size, transcendentals=0)


def vmem(count):
    return [pl.BlockSpec(memory_space=pltpu.VMEM)] * count


def hbm(count):
    return [pl.BlockSpec(memory_space=pltpu.HBM)] * count


def smem(count):
    return [pl.BlockSpec(memory_space=pltpu.SMEM)] * count


def dot(a, b, **kw):
    return jnp.dot(a, b, preferred_element_type=jnp.float32, **kw)


def split(x):
    high = x.astype(jnp.bfloat16)
    return high, (x - high.astype(jnp.float32)).astype(jnp.bfloat16)


def dot_rows(a, b):
    return lax.dot_general(a, b, ROWS, preferred_element_type=jnp.float32)


def permutation(size, shift):
    row = lax.broadcasted_iota(jnp.int32, (size, size), 0)
    column = lax.broadcasted_iota(jnp.int32, (size, size), 1)
    return (lax.rem(row + shift + size, size) == column).astype(jnp.bfloat16)


def eye(size):
    row = lax.broadcasted_iota(jnp.int32, (size, size), 0)
    column = lax.broadcasted_iota(jnp.int32, (size, size), 1)
    return row == column


def column_of(row):
    return jnp.sum(jnp.where(eye(row.shape[1]), row, 0.0), axis=1, keepdims=True)


def row_of(column):
    return jnp.sum(jnp.where(eye(column.shape[0]), column, 0.0), axis=0, keepdims=True)


def both_ways(columns):
    pair = jnp.concatenate([permutation(columns, -1), permutation(columns, 1)], axis=1)
    return jnp.concatenate([pair, pair], axis=0)


def forecast_rows(read, first, last, coefficients, shifts):
    middle, east, west, north, south = coefficients

    def step(below, here, above, ahead, behind):
        return middle * here + east * above + west * below + north * ahead + south * behind

    rows = [read(r) for r in range(first - 2, last + 2)]
    tiles, _, columns = rows[0].shape
    flat = jnp.concatenate(rows[1:-1], axis=0).reshape(-1, columns)
    moved = dot(jnp.concatenate(split(flat), axis=1), shifts)
    ahead = moved[:, :columns].reshape(-1, 8, columns)
    behind = moved[:, columns:].reshape(-1, 8, columns)
    once, twice = [], []
    for i, r in enumerate(range(first - 1, last + 1)):
        here = slice(i * tiles, (i + 1) * tiles)
        once.append(step(*rows[i : i + 3], ahead[here], behind[here]))
        if i >= 2:
            one = once[-2]
            new = step(*once[-3:], pltpu.roll(one, columns - 1, 2), pltpu.roll(one, 1, 2))
            twice.append((r - 1, new.reshape(-1, columns).astype(jnp.bfloat16)))
    return twice


def coefficients_of(level, diff, east, north):
    spread = jnp.broadcast_to(diff[pl.ds(level, 1), :], (8, diff.shape[1]))
    u = 0.5 * east[level]
    w = 0.5 * north[level]
    return 1.0 - 4.0 * spread, spread - u, spread + u, spread - w, spread + w


def row_reader(level, var, own, low, high):
    span, columns = own.shape[2], own.shape[4]

    def read(r):
        ref, at = (low, r + span) if r < 0 else (own, r) if r < span else (high, r - span)
        return ref[var, level, at].reshape(-1, 8, columns)

    return read


def pack_rows(pairs, identity, store, first):
    lanes = pairs[0].shape[0] // 2
    packed = []
    for pair in pairs:
        turned = dot_rows(identity, pair)
        parts = [turned[:, i * lanes : (i + 1) * lanes].reshape(-1, SPAN, lanes) for i in range(2)]
        packed.append(jnp.concatenate(parts, axis=1).astype(jnp.bfloat16))
    for i, value in enumerate(packed):
        at = first + i * 2 * SPAN
        store[:, at : at + 2 * SPAN, :] = value


def inner_kernel(variables, own, *refs):
    raw, (slabs, fields, packed, model) = refs[:3], refs[3:7]
    local, (whole, staged, in_sems, raw_sems, out_sems) = refs[7:10], refs[10:]
    lanes, levels, span, columns = own.shape
    members = lanes // variables
    count = span - 2 * STEPS
    def arrive(level):
        return pltpu.make_async_copy(own.at[:, level], whole.at[level], in_sems.at[level])

    def leave(level):
        size = count * SPAN
        here = pl.ds(pl.multiple_of(level * size, size), size)
        return pltpu.make_async_copy(staged.at[level], packed.at[:, here], out_sems.at[level])

    copies = [pltpu.make_async_copy(x, y, raw_sems.at[i]) for i, (x, y) in enumerate(zip(raw, local))]
    for copy in copies:
        copy.start()
    for level in range(levels):
        arrive(level).start()
    identity = permutation(columns, 0)
    shifts = both_ways(columns)
    for copy in copies:
        copy.wait()

    @pl.loop(0, levels)
    def _(level):
        coefficients = coefficients_of(level, *local)
        for i, one in enumerate(coefficients):
            model[level, i] = one
        arrive(level).wait()
        view = whole.at[level].reshape(lanes * span, columns)
        reads, made = [], []
        for var in range(variables):

            def read(r):
                rows = view[pl.ds(var * span + r, members, stride=variables * span), :]
                reads.append((var, r, rows))
                return rows.reshape(-1, 8, columns)

            for r, value in forecast_rows(read, STEPS, span - STEPS, coefficients, shifts):
                made.append((var, r, value))
        pairs = []
        for first in range(STEPS, span - STEPS, 2):
            rows = [one for r in (first, first + 1) for _, at, one in made if at == r]
            pairs.append(jnp.concatenate(rows, axis=0))
        pack_rows(pairs, identity, staged.at[level], 0)
        leave(level).start()
        for var, r, value in made:
            fields[level, r - STEPS, var * members : (var + 1) * members, :] = value
        for var, r, rows in reads:
            slabs[var, level, r] = rows

    for level in range(levels):
        leave(level).wait()


def inner(own, raw, variables):
    lanes, levels, span, columns = own.shape
    members = lanes // variables
    blocks = columns // SPAN
    count = span - 2 * STEPS
    fixed = [pltpu.with_memory_space_constraint(x, pltpu.HBM) for x in (own, *raw)]
    return pl.pallas_call(
        functools.partial(inner_kernel, variables),
        out_shape=[
            jax.ShapeDtypeStruct((variables, levels, span, members, columns), jnp.float32),
            jax.ShapeDtypeStruct((levels, count, lanes, columns), jnp.bfloat16),
            jax.ShapeDtypeStruct((blocks, levels * count * SPAN, lanes), jnp.bfloat16),
            jax.ShapeDtypeStruct((levels, 5, 8, columns), jnp.float32),
        ],
        in_specs=hbm(4),
        out_specs=vmem(2) + hbm(1) + vmem(1),
        scratch_shapes=[
            pltpu.VMEM(raw[0].shape, jnp.float32),
            pltpu.SMEM(raw[1].shape, jnp.float32),
            pltpu.SMEM(raw[2].shape, jnp.float32),
            pltpu.VMEM((levels, lanes, span, columns), jnp.float32),
            pltpu.VMEM((levels, blocks, count * SPAN, lanes), jnp.bfloat16),
            pltpu.SemaphoreType.DMA((levels,)),
            pltpu.SemaphoreType.DMA((3,)),
            pltpu.SemaphoreType.DMA((levels,)),
        ],
        compiler_params=params(10),
        cost_estimate=cost(2 * 10**9, 4 * 2**20),
    )(*fixed)


def outer_kernel(near, own, *rest):
    sides, rest = rest[:near], rest[near:]
    model, centre, grid, packed, staged, near_tiles, sems, out_sems, near_sems = rest
    variables, levels, span, members, columns = own.shape
    rows_each = variables * members
    pairs = (2 * EDGE + span) // 2
    size = STEPS * 2 * SPAN
    identity = permutation(columns, 0)
    shifts = both_ways(columns)

    def arrive(level):
        return [
            pltpu.make_async_copy(
                side.at[:, level], near_tiles.at[i, :, level], near_sems.at[i, level]
            )
            for i, side in enumerate(sides)
        ]

    for level in range(levels):
        for copy in arrive(level):
            copy.start()

    def leave(level):
        here = pl.ds(pl.multiple_of(level * size, size), size)
        return pltpu.make_async_copy(staged.at[level], packed.at[:, here], out_sems.at[level])

    copies = []
    for r in range(STEPS, span - STEPS):
        half, pair = divmod(r + EDGE, pairs)
        place = grid.at[:, pair, pl.ds(half * rows_each, rows_each)]
        copies.append(pltpu.make_async_copy(centre.at[:, r - STEPS], place, sems.at[r - STEPS]))
        copies[-1].start()

    @pl.loop(0, levels)
    def _(level):
        for copy in arrive(level):
            copy.wait()
        coefficients = [model[level, i] for i in range(5)]
        made = []
        for var in range(variables):
            read = row_reader(level, var, own, near_tiles.at[0], near_tiles.at[near - 1])
            for first, last in ((-EDGE, STEPS), (span - STEPS, span + EDGE)):
                for r, value in forecast_rows(read, first, last, coefficients, shifts):
                    made.append((var, r, value))
        sheets = []
        for first in (0, span - STEPS):
            rows = [one for r in range(first, first + STEPS) for _, at, one in made if at == r]
            sheets.append(jnp.concatenate(rows, axis=0))
        pack_rows(sheets, identity, staged.at[level], 0)
        leave(level).start()
        for var, r, value in made:
            half, pair = divmod(r + EDGE, pairs)
            at = half * rows_each + var * members
            grid[level, pair, at : at + members, :] = value

    for level in range(levels):
        leave(level).wait()
    for copy in copies:
        copy.wait()


def outer(dims, own, sides, model, centre, slots):
    members, variables, levels, span, columns = dims
    lanes = members * variables
    blocks = columns // SPAN
    near = len(sides)
    pairs = (2 * EDGE + span) // 2
    return pl.pallas_call(
        functools.partial(outer_kernel, near),
        out_shape=[
            jax.ShapeDtypeStruct((levels, pairs, 2 * lanes, columns), jnp.bfloat16),
            jax.ShapeDtypeStruct(
                (blocks, levels * 2 * STEPS * SPAN + slots // 2, lanes), jnp.bfloat16
            ),
        ],
        in_specs=vmem(1) + hbm(near) + vmem(1) + hbm(1),
        out_specs=vmem(1) + hbm(1),
        scratch_shapes=[
            pltpu.VMEM((levels, blocks, 2 * STEPS * SPAN, lanes), jnp.bfloat16),
            pltpu.VMEM((near, *own.shape), jnp.float32),
            pltpu.SemaphoreType.DMA((span - 2 * STEPS,)),
            pltpu.SemaphoreType.DMA((levels,)),
            pltpu.SemaphoreType.DMA((near, levels)),
        ],
        compiler_params=params(16),
        cost_estimate=cost(2 * 10**9, 8 * 2**20),
    )(own, *(pltpu.with_memory_space_constraint(x, pltpu.HBM) for x in sides), model, centre)


def pick_kernel(variables, together, grid, _, cells, out, region, codes, staged, sems):
    levels, pairs, twice, columns = grid.shape
    rows = twice // 2
    members = rows // variables
    blocks, slots = cells.shape
    width = 2 * EDGE + SPAN
    part = pairs * width
    entries = levels * part
    share = out.shape[1] - slots // 2

    order = permutation(columns, -EDGE)
    batch = next(n for n in (4, 2, 1) if pairs % n == 0)

    @pl.loop(0, levels)
    def _(level):
        for start in range(0, pairs, batch):
            made = []
            for i in range(batch):
                even = dot_rows(order, grid[level, start + i])
                odd = jnp.concatenate([even[SPAN:], even[:SPAN]], axis=0)
                made.append((even.astype(jnp.bfloat16), odd.astype(jnp.bfloat16)))
            for i, both in enumerate(made):
                at = pl.multiple_of((level * pairs + start + i) * width, width)
                for first, value in enumerate(both):
                    for j in range(columns // width):
                        piece = value[j * width : (j + 1) * width, :]
                        region[2 * j + first, pl.ds(at, width), :] = piece

    cell = cells[...]
    second = cell >= 2 * entries
    cell = jnp.where(second, cell - 2 * entries, cell)
    level = lax.shift_right_logical(cell, (2 * part).bit_length() - 1)
    inside = cell - level * (2 * part)
    lower = inside >= part
    code = level * part + jnp.where(lower, inside - part + entries, inside)
    codes[...] = jnp.where(second, code + 2 * entries, code).astype(jnp.float32)

    left = lax.broadcasted_iota(jnp.int32, (slots // 2, rows), 1) < members
    lane = lax.broadcasted_iota(jnp.int32, (slots, entries), 1).astype(jnp.float32)

    def leave(step):
        here = pl.ds(step * together, together)
        place = out.at[here, pl.ds(share, slots // 2)]
        return pltpu.make_async_copy(staged.at[here], place, sems.at[step])

    @pl.loop(0, blocks // together)
    def _(step):
        made = []
        for i in range(together):
            block = step * together + i
            at = column_of(codes[pl.ds(block, 1), :])
            second = at >= 2.0 * entries
            at = jnp.where(second, at - 2.0 * entries, at)
            lower = at >= 1.0 * entries
            at = jnp.where(lower, at - 1.0 * entries, at)
            pick = jnp.where(lane == at, 1.0, 0.0).astype(jnp.bfloat16)
            found = dot(pick, region[block])
            total = jnp.where(lower, found[:, rows:], found[:, :rows])
            other = pltpu.roll(total, members, 1)
            to_left = jnp.where(second, other, total)[: slots // 2]
            to_right = jnp.where(second, total, other)[slots // 2 :]
            made.append(jnp.where(left, to_left, to_right).astype(jnp.bfloat16))
        for i, value in enumerate(made):
            staged[step * together + i] = value
        leave(step).start()

    for step in range(blocks // together):
        leave(step).wait()


def pick(variables, grid, packed, cells):
    levels, pairs, twice, columns = grid.shape
    blocks, slots = cells.shape
    together = next(n for n in (4, 2, 1) if blocks % n == 0)
    return pl.pallas_call(
        functools.partial(pick_kernel, variables, together),
        out_shape=jax.ShapeDtypeStruct(packed.shape, packed.dtype),
        in_specs=vmem(1) + hbm(1) + vmem(1),
        out_specs=pl.BlockSpec(memory_space=pltpu.HBM),
        scratch_shapes=[
            pltpu.VMEM((blocks, levels * pairs * (2 * EDGE + SPAN), twice), jnp.bfloat16),
            pltpu.VMEM((blocks, slots), jnp.float32),
            pltpu.VMEM((blocks, slots // 2, packed.shape[2]), jnp.bfloat16),
            pltpu.SemaphoreType.DMA((blocks // together,)),
        ],
        input_output_aliases={1: 0},
        compiler_params=params(20),
        cost_estimate=cost(4 * 10**9, 4 * 2**20),
    )(grid, packed, cells)


def join(a, b, left, members):
    return (
        jnp.where(left, a, pltpu.roll(b, members, 1)),
        jnp.where(left, pltpu.roll(a, members, 1), b),
    )


def batches(count, size):
    return [range(at, min(count, at + size)) for at in range(0, count, size)]


def left_lanes(shape):
    return lax.broadcasted_iota(jnp.int32, shape, 1) < shape[1] // 2


def deviations(states, raw, dev, at, size):
    groups, _, lanes = states.shape
    members = lanes // 2
    left = left_lanes((size, lanes))
    sums = [jnp.zeros((size, lanes), jnp.float32)] * 2
    for batch in batches(groups // 2, 4):
        made = [
            join(
                states[2 * j, :size, :].astype(jnp.float32),
                states[2 * j + 1, :size, :].astype(jnp.float32),
                left,
                members,
            )
            for j in batch
        ]
        for j, pair in zip(batch, made):
            here = slice(j * lanes, (j + 1) * lanes)
            for var in range(2):
                raw[var * size : (var + 1) * size, here] = pair[var]
            sums = [total + one for total, one in zip(sums, pair)]
    centre = jnp.concatenate([jnp.sum(x, axis=1, keepdims=True) for x in sums], axis=0)
    centre = centre * (1.0 / (groups * members))
    dev[at : at + 2 * size, :] = (raw[...] - centre).astype(jnp.bfloat16)
    return centre


def prepare_kernel(states, dev, centre, raw):
    mean = deviations(states, raw, dev, 0, states.shape[1])
    centre[...] = jnp.broadcast_to(mean, centre.shape)


def prepare(states):
    groups, near, lanes = states.shape
    total = groups * lanes // 2
    return pl.pallas_call(
        prepare_kernel,
        out_shape=[
            jax.ShapeDtypeStruct((2 * near, total), jnp.bfloat16),
            jax.ShapeDtypeStruct((2 * near, lanes), jnp.float32),
        ],
        in_specs=vmem(1),
        out_specs=vmem(2),
        scratch_shapes=[pltpu.VMEM((2 * near, total), jnp.float32)],
        compiler_params=params(6),
        cost_estimate=cost(10**8, 2 * 2**20),
    )(states)


def analyse_kernel(first, means, second, count, value, weight, out, raw, dev, obs, scaled_ref):
    groups, _, lanes = second.shape
    near = first.shape[0] // 2
    half = obs.shape[0] // 2
    far = second.shape[1] - half
    side = near + far
    slots = 2 * half
    members = lanes // 2
    total_members = groups * members
    left = left_lanes((half, lanes))

    for batch in batches(groups // 2, 4):
        made = [
            join(
                second[2 * j, far:, :].astype(jnp.float32),
                second[2 * j + 1, far:, :].astype(jnp.float32),
                left,
                members,
            )
            for j in batch
        ]
        for j, pair in zip(batch, made):
            here = slice(j * lanes, (j + 1) * lanes)
            obs[:half, here], obs[half:, here] = pair

    used = lax.broadcasted_iota(jnp.int32, (1, slots), 1) < count[0, 0]
    root = column_of(jnp.where(used, jnp.sqrt(weight[...]), 0.0))
    observed = obs[...]
    mean = jnp.sum(observed, axis=1, keepdims=True) * (1.0 / total_members)
    scaled = (observed - mean) * root
    energy = jnp.sum(jnp.sum(scaled * scaled, axis=1, keepdims=True), axis=0, keepdims=True)
    scaled_ref[...] = scaled.astype(jnp.bfloat16)
    misfit = row_of(root * (column_of(value[...]) - mean))

    c = total_members - 1.0
    s = energy * (1.0 / total_members) + c
    inverse = 1.0 / s
    a = c * inverse
    p = 1.5 - 0.5 * a
    p2 = p * p
    p3 = p2 * p
    base = 1.5 * p - 0.5 * a * p3
    q0 = -0.75 - 0.5 * (p3 - 1.5 * a * p2)
    q1 = -0.5 * (0.75 * a * p - 1.5 * p2)
    q2 = -0.5 * (0.75 * p - 0.125 * a)
    small = dot_rows(scaled_ref[...], scaled_ref[...]) * inverse
    diagonal = eye(slots)
    once = small.astype(jnp.bfloat16)
    square = dot(once, once).astype(jnp.bfloat16)
    tail = dot(square, (jnp.where(diagonal, q2, 0.0) + 0.0625 * small).astype(jnp.bfloat16))
    poly = jnp.where(diagonal, q0, 0.0) + q1 * small + tail

    def apply(vector):
        inner_part = jnp.sum(poly * vector, axis=1, keepdims=True)
        return jnp.sum(small * inner_part, axis=0, keepdims=True) + base * vector

    gain = apply(apply(misfit)) * inverse
    stretch = jnp.sqrt(a)
    alpha, factor = stretch * base, stretch * inverse
    centre = deviations(second, raw, dev, 0, far)
    cross = jnp.concatenate(
        [dot_rows(first[...], scaled_ref[...]), dot_rows(dev[...], scaled_ref[...])], axis=0
    )
    centre = jnp.concatenate([means[:, 0:1], centre], axis=0)
    shift = centre + jnp.sum(cross * gain, axis=1, keepdims=True)
    once = cross.astype(jnp.bfloat16)
    mix = sum(dot(once, part) for part in split(poly))
    mix = (mix * factor).astype(jnp.bfloat16)
    parts = ((first, 0, near, 0), (dev, 2 * near, far, near))
    for batch in batches(groups // 2, 2):
        made = []
        wide = slice(batch[0] * lanes, (batch[-1] + 1) * lanes)
        both = dot(mix, scaled_ref[:, wide]) + shift
        for j in batch:
            here = slice(j * lanes, (j + 1) * lanes)
            new = both[:, (j - batch[0]) * lanes :][:, :lanes]
            for ref, at, size, row in parts:
                one = new[at : at + 2 * size] + alpha * ref[:, here].astype(jnp.float32)
                pair = join(one[:size], one[size:], left_lanes((size, lanes)), members)
                made += [(2 * j + i, row, x.astype(jnp.bfloat16)) for i, x in enumerate(pair)]
        for group, row, value in made:
            out[group, row : row + value.shape[0], :] = value


def analyse(first, means, second, count, value, weight):
    groups, _, lanes = second.shape
    near = first.shape[0] // 2
    slots = value.shape[1]
    far = second.shape[1] - slots // 2
    total = groups * lanes // 2
    return pl.pallas_call(
        analyse_kernel,
        out_shape=jax.ShapeDtypeStruct((groups, near + far, lanes), jnp.bfloat16),
        in_specs=vmem(3) + smem(1) + vmem(2),
        out_specs=pl.BlockSpec(memory_space=pltpu.VMEM),
        scratch_shapes=[
            pltpu.VMEM((2 * far, total), jnp.float32),
            pltpu.VMEM((2 * far, total), jnp.bfloat16),
            pltpu.VMEM((slots, total), jnp.float32),
            pltpu.VMEM((slots, total), jnp.bfloat16),
        ],
        compiler_params=params(16),
        cost_estimate=cost(4 * 10**9, 4 * 2**20),
    )(first, means, second, count, value, weight)


def restore_kernel(blocks, out, turned):
    members, variables, levels, span, columns = out.shape
    lanes = members * variables
    identity = permutation(lanes, 0)
    near = span - 2 * STEPS

    @pl.loop(0, levels)
    def _(level):
        slot = lax.rem(level, 2)
        made = []
        for r in range(0, span, 2):
            if STEPS <= r < span - STEPS:
                at = level * near + r - STEPS
            else:
                at = levels * near + level * 2 * STEPS + (r if r < STEPS else r - near)
            here = pl.ds(pl.multiple_of(at * SPAN, 2 * SPAN), 2 * SPAN)
            both = blocks[:, here, :].astype(jnp.float32)
            for i in range(2):
                one = both[:, i * SPAN : (i + 1) * SPAN, :].reshape(columns, lanes)
                made.append((r + i, dot_rows(identity, one.astype(jnp.bfloat16))))
        for r, rows in made:
            turned[slot, pl.ds(r, lanes, stride=span), :] = rows
        for var in range(variables):
            half = turned[slot, var * members * span : (var + 1) * members * span, :]
            out[:, var, level] = half.reshape(members, span, columns).astype(jnp.bfloat16)


def restore(dims, blocks):
    members, variables, levels, span, columns = dims
    return pl.pallas_call(
        restore_kernel,
        out_shape=jax.ShapeDtypeStruct((members, variables, levels, span, columns), jnp.bfloat16),
        in_specs=vmem(1),
        out_specs=pl.BlockSpec(memory_space=pltpu.VMEM),
        scratch_shapes=[pltpu.VMEM((2, variables * members * span, columns), jnp.float32)],
        compiler_params=params(8),
        cost_estimate=cost(2 * 10**9, 2 * 2**20),
    )(blocks)


def neighbours(field, axis):
    count = lax.axis_size(axis)
    low = lax.ppermute(field, axis, [(i, (i + 1) % count) for i in range(count)])
    if count == 2:
        return (low,)
    return low, lax.ppermute(field, axis, [((i + 1) % count, i) for i in range(count)])


def exchange(blocks):
    return lax.all_to_all(blocks, "grp", split_axis=0, concat_axis=0, tiled=True)


def on_device(start, diffusivity, eastward, northward, cells, count, value, weight):
    members, variables, levels, span, columns = dims = start.shape
    whole = start.reshape(members * variables, levels, span, columns)
    own, centre, near, model = inner(whole, (diffusivity, eastward, northward), variables)
    sides = neighbours(own, "tile")
    first, means = prepare(exchange(near))
    grid, packed = outer(dims, own, sides, model, centre, cells.shape[2])
    second = exchange(pick(variables, grid, packed, cells[0]))
    updated = analyse(first, means, second, count, value[0], weight[0])
    return restore(dims, exchange(updated))


def solution(mesh):
    return jax.shard_map(
        on_device,
        mesh=mesh,
        in_specs=(
            P("grp", None, None, "tile", None),
            P(),
            P(),
            P(),
            P("tile", None, None),
            P("tile", "grp"),
            P("tile", "grp", None),
            P("tile", "grp", None),
        ),
        out_specs=P("grp", None, None, "tile", None),
        check_vma=False,
    )
```

```python
import functools

import jax
import jax.numpy as jnp
from jax import lax
from jax.experimental import pallas as pl
from jax.experimental.pallas import tpu as pltpu
from jax.sharding import PartitionSpec as P

SPAN = 8
STEPS = 2
EDGE = SPAN // 2

ROWS = (((1,), (1,)), ((), ()))


def params(mebibytes, **kw):
    return pltpu.CompilerParams(vmem_limit_bytes=mebibytes * 2**20, **kw)


def cost(flops, size):
    return pl.CostEstimate(flops=flops, bytes_accessed=size, transcendentals=0)


def vmem(count):
    return [pl.BlockSpec(memory_space=pltpu.VMEM)] * count


def hbm(count):
    return [pl.BlockSpec(memory_space=pltpu.HBM)] * count


def smem(count):
    return [pl.BlockSpec(memory_space=pltpu.SMEM)] * count


def dot(a, b, **kw):
    return jnp.dot(a, b, preferred_element_type=jnp.float32, **kw)


def split(x):
    high = x.astype(jnp.bfloat16)
    return high, (x - high.astype(jnp.float32)).astype(jnp.bfloat16)


def dot_rows(a, b):
    return lax.dot_general(a, b, ROWS, preferred_element_type=jnp.float32)


def permutation(size, shift):
    row = lax.broadcasted_iota(jnp.int32, (size, size), 0)
    column = lax.broadcasted_iota(jnp.int32, (size, size), 1)
    return (lax.rem(row + shift + size, size) == column).astype(jnp.bfloat16)


def eye(size):
    row = lax.broadcasted_iota(jnp.int32, (size, size), 0)
    column = lax.broadcasted_iota(jnp.int32, (size, size), 1)
    return row == column


def column_of(row):
    return jnp.sum(jnp.where(eye(row.shape[1]), row, 0.0), axis=1, keepdims=True)


def row_of(column):
    return jnp.sum(jnp.where(eye(column.shape[0]), column, 0.0), axis=0, keepdims=True)


def both_ways(columns):
    pair = jnp.concatenate([permutation(columns, -1), permutation(columns, 1)], axis=1)
    return jnp.concatenate([pair, pair], axis=0)


def forecast_rows(read, first, last, coefficients, shifts):
    middle, east, west, north, south = coefficients

    def step(below, here, above, ahead, behind):
        return middle * here + east * above + west * below + north * ahead + south * behind

    rows = [read(r) for r in range(first - 2, last + 2)]
    tiles, _, columns = rows[0].shape
    flat = jnp.concatenate(rows[1:-1], axis=0).reshape(-1, columns)
    moved = dot(jnp.concatenate(split(flat), axis=1), shifts)
    ahead = moved[:, :columns].reshape(-1, 8, columns)
    behind = moved[:, columns:].reshape(-1, 8, columns)
    once, twice = [], []
    for i, r in enumerate(range(first - 1, last + 1)):
        here = slice(i * tiles, (i + 1) * tiles)
        once.append(step(*rows[i : i + 3], ahead[here], behind[here]))
        if i >= 2:
            one = once[-2]
            new = step(*once[-3:], pltpu.roll(one, columns - 1, 2), pltpu.roll(one, 1, 2))
            twice.append((r - 1, new.reshape(-1, columns).astype(jnp.bfloat16)))
    return twice


def coefficients_of(level, diff, east, north):
    spread = jnp.broadcast_to(diff[pl.ds(level, 1), :], (8, diff.shape[1]))
    u = 0.5 * east[level]
    w = 0.5 * north[level]
    return 1.0 - 4.0 * spread, spread - u, spread + u, spread - w, spread + w


def row_reader(level, var, own, low, high):
    span, columns = own.shape[2], own.shape[4]

    def read(r):
        ref, at = (low, r + span) if r < 0 else (own, r) if r < span else (high, r - span)
        return ref[var, level, at].reshape(-1, 8, columns)

    return read


def pack_rows(pairs, identity, store, first):
    lanes = pairs[0].shape[0] // 2
    packed = []
    for pair in pairs:
        turned = dot_rows(identity, pair)
        parts = [turned[:, i * lanes : (i + 1) * lanes].reshape(-1, SPAN, lanes) for i in range(2)]
        packed.append(jnp.concatenate(parts, axis=1).astype(jnp.bfloat16))
    for i, value in enumerate(packed):
        at = first + i * 2 * SPAN
        store[:, at : at + 2 * SPAN, :] = value


def inner_kernel(variables, own, *refs):
    raw, (slabs, fields, packed, model) = refs[:3], refs[3:7]
    local, (whole, staged, in_sems, raw_sems, out_sems) = refs[7:10], refs[10:]
    lanes, levels, span, columns = own.shape
    members = lanes // variables
    count = span - 2 * STEPS
    def arrive(level):
        return pltpu.make_async_copy(own.at[:, level], whole.at[level], in_sems.at[level])

    def leave(level):
        size = count * SPAN
        here = pl.ds(pl.multiple_of(level * size, size), size)
        return pltpu.make_async_copy(staged.at[level], packed.at[:, here], out_sems.at[level])

    copies = [pltpu.make_async_copy(x, y, raw_sems.at[i]) for i, (x, y) in enumerate(zip(raw, local))]
    for copy in copies:
        copy.start()
    for level in range(min(2, levels)):
        arrive(level).start()
    identity = permutation(columns, 0)
    shifts = both_ways(columns)
    for copy in copies:
        copy.wait()

    @pl.loop(0, levels)
    def _(level):
        coefficients = coefficients_of(level, *local)
        for i, one in enumerate(coefficients):
            model[level, i] = one
        arrive(level).wait()

        @pl.when(level + 2 < levels)
        def _():
            arrive(level + 2).start()

        view = whole.at[level].reshape(lanes * span, columns)
        reads, made = [], []
        for var in range(variables):

            def read(r):
                rows = view[pl.ds(var * span + r, members, stride=variables * span), :]
                reads.append((var, r, rows))
                return rows.reshape(-1, 8, columns)

            for r, value in forecast_rows(read, STEPS, span - STEPS, coefficients, shifts):
                made.append((var, r, value))
        pairs = []
        for first in range(STEPS, span - STEPS, 2):
            rows = [one for r in (first, first + 1) for _, at, one in made if at == r]
            pairs.append(jnp.concatenate(rows, axis=0))
        pack_rows(pairs, identity, staged.at[level], 0)
        leave(level).start()
        for var, r, value in made:
            fields[level, r - STEPS, var * members : (var + 1) * members, :] = value
        for var, r, rows in reads:
            slabs[var, level, r] = rows

    for level in range(levels):
        leave(level).wait()


def inner(own, raw, variables):
    lanes, levels, span, columns = own.shape
    members = lanes // variables
    blocks = columns // SPAN
    count = span - 2 * STEPS
    fixed = [pltpu.with_memory_space_constraint(x, pltpu.HBM) for x in (own, *raw)]
    return pl.pallas_call(
        functools.partial(inner_kernel, variables),
        out_shape=[
            jax.ShapeDtypeStruct((variables, levels, span, members, columns), jnp.float32),
            jax.ShapeDtypeStruct((levels, count, lanes, columns), jnp.bfloat16),
            jax.ShapeDtypeStruct((blocks, levels * count * SPAN, lanes), jnp.bfloat16),
            jax.ShapeDtypeStruct((levels, 5, 8, columns), jnp.float32),
        ],
        in_specs=hbm(4),
        out_specs=vmem(2) + hbm(1) + vmem(1),
        scratch_shapes=[
            pltpu.VMEM(raw[0].shape, jnp.float32),
            pltpu.SMEM(raw[1].shape, jnp.float32),
            pltpu.SMEM(raw[2].shape, jnp.float32),
            pltpu.VMEM((levels, lanes, span, columns), jnp.float32),
            pltpu.VMEM((levels, blocks, count * SPAN, lanes), jnp.bfloat16),
            pltpu.SemaphoreType.DMA((levels,)),
            pltpu.SemaphoreType.DMA((3,)),
            pltpu.SemaphoreType.DMA((levels,)),
        ],
        compiler_params=params(10),
        cost_estimate=cost(2 * 10**9, 4 * 2**20),
    )(*fixed)


def outer_kernel(near, own, *rest):
    sides, rest = rest[:near], rest[near:]
    model, centre, grid, packed, staged, near_tiles, sems, out_sems, near_sems = rest
    variables, levels, span, members, columns = own.shape
    rows_each = variables * members
    pairs = (2 * EDGE + span) // 2
    size = STEPS * 2 * SPAN
    identity = permutation(columns, 0)
    shifts = both_ways(columns)

    def arrive(level):
        return [
            pltpu.make_async_copy(
                side.at[:, level], near_tiles.at[i, :, level], near_sems.at[i, level]
            )
            for i, side in enumerate(sides)
        ]

    for level in range(levels):
        for copy in arrive(level):
            copy.start()

    def leave(level):
        here = pl.ds(pl.multiple_of(level * size, size), size)
        return pltpu.make_async_copy(staged.at[level], packed.at[:, here], out_sems.at[level])

    copies = []
    for r in range(STEPS, span - STEPS):
        half, pair = divmod(r + EDGE, pairs)
        place = grid.at[:, pair, pl.ds(half * rows_each, rows_each)]
        copies.append(pltpu.make_async_copy(centre.at[:, r - STEPS], place, sems.at[r - STEPS]))
        copies[-1].start()

    @pl.loop(0, levels)
    def _(level):
        for copy in arrive(level):
            copy.wait()
        coefficients = [model[level, i] for i in range(5)]
        made = []
        for var in range(variables):
            read = row_reader(level, var, own, near_tiles.at[0], near_tiles.at[near - 1])
            for first, last in ((-EDGE, STEPS), (span - STEPS, span + EDGE)):
                for r, value in forecast_rows(read, first, last, coefficients, shifts):
                    made.append((var, r, value))
        sheets = []
        for first in (0, span - STEPS):
            rows = [one for r in range(first, first + STEPS) for _, at, one in made if at == r]
            sheets.append(jnp.concatenate(rows, axis=0))
        pack_rows(sheets, identity, staged.at[level], 0)
        leave(level).start()
        for var, r, value in made:
            half, pair = divmod(r + EDGE, pairs)
            at = half * rows_each + var * members
            grid[level, pair, at : at + members, :] = value

    for level in range(levels):
        leave(level).wait()
    for copy in copies:
        copy.wait()


def outer(dims, own, sides, model, centre, slots):
    members, variables, levels, span, columns = dims
    lanes = members * variables
    blocks = columns // SPAN
    near = len(sides)
    pairs = (2 * EDGE + span) // 2
    return pl.pallas_call(
        functools.partial(outer_kernel, near),
        out_shape=[
            jax.ShapeDtypeStruct((levels, pairs, 2 * lanes, columns), jnp.bfloat16),
            jax.ShapeDtypeStruct(
                (blocks, levels * 2 * STEPS * SPAN + slots // 2, lanes), jnp.bfloat16
            ),
        ],
        in_specs=vmem(1) + hbm(near) + vmem(1) + hbm(1),
        out_specs=vmem(1) + hbm(1),
        scratch_shapes=[
            pltpu.VMEM((levels, blocks, 2 * STEPS * SPAN, lanes), jnp.bfloat16),
            pltpu.VMEM((near, *own.shape), jnp.float32),
            pltpu.SemaphoreType.DMA((span - 2 * STEPS,)),
            pltpu.SemaphoreType.DMA((levels,)),
            pltpu.SemaphoreType.DMA((near, levels)),
        ],
        compiler_params=params(16),
        cost_estimate=cost(2 * 10**9, 8 * 2**20),
    )(own, *(pltpu.with_memory_space_constraint(x, pltpu.HBM) for x in sides), model, centre)


def pick_kernel(variables, together, grid, _, cells, out, region, codes, staged, sems):
    levels, pairs, twice, columns = grid.shape
    rows = twice // 2
    members = rows // variables
    blocks, slots = cells.shape
    width = 2 * EDGE + SPAN
    part = pairs * width
    entries = levels * part
    share = out.shape[1] - slots // 2

    order = permutation(columns, -EDGE)
    batch = next(n for n in (4, 2, 1) if pairs % n == 0)
    for level in range(levels):
        for start in range(0, pairs, batch):
            made = []
            for i in range(batch):
                even = dot_rows(order, grid[level, start + i])
                odd = jnp.concatenate([even[SPAN:], even[:SPAN]], axis=0)
                made.append((even.astype(jnp.bfloat16), odd.astype(jnp.bfloat16)))
            for i, both in enumerate(made):
                at = (level * pairs + start + i) * width
                for first, value in enumerate(both):
                    for j in range(columns // width):
                        piece = value[j * width : (j + 1) * width, :]
                        region[2 * j + first, at : at + width, :] = piece

    cell = cells[...]
    second = cell >= 2 * entries
    cell = jnp.where(second, cell - 2 * entries, cell)
    level = lax.shift_right_logical(cell, (2 * part).bit_length() - 1)
    inside = cell - level * (2 * part)
    lower = inside >= part
    code = level * part + jnp.where(lower, inside - part + entries, inside)
    codes[...] = jnp.where(second, code + 2 * entries, code).astype(jnp.float32)

    left = lax.broadcasted_iota(jnp.int32, (slots // 2, rows), 1) < members
    lane = lax.broadcasted_iota(jnp.int32, (slots, entries), 1).astype(jnp.float32)

    def leave(step):
        here = pl.ds(step * together, together)
        place = out.at[here, pl.ds(share, slots // 2)]
        return pltpu.make_async_copy(staged.at[here], place, sems.at[step])

    @pl.loop(0, blocks // together)
    def _(step):
        made = []
        for i in range(together):
            block = step * together + i
            at = column_of(codes[pl.ds(block, 1), :])
            second = at >= 2.0 * entries
            at = jnp.where(second, at - 2.0 * entries, at)
            lower = at >= 1.0 * entries
            at = jnp.where(lower, at - 1.0 * entries, at)
            pick = jnp.where(lane == at, 1.0, 0.0).astype(jnp.bfloat16)
            found = dot(pick, region[block])
            total = jnp.where(lower, found[:, rows:], found[:, :rows])
            other = pltpu.roll(total, members, 1)
            to_left = jnp.where(second, other, total)[: slots // 2]
            to_right = jnp.where(second, total, other)[slots // 2 :]
            made.append(jnp.where(left, to_left, to_right).astype(jnp.bfloat16))
        for i, value in enumerate(made):
            staged[step * together + i] = value
        leave(step).start()

    for step in range(blocks // together):
        leave(step).wait()


def pick(variables, grid, packed, cells):
    levels, pairs, twice, columns = grid.shape
    blocks, slots = cells.shape
    together = next(n for n in (4, 2, 1) if blocks % n == 0)
    return pl.pallas_call(
        functools.partial(pick_kernel, variables, together),
        out_shape=jax.ShapeDtypeStruct(packed.shape, packed.dtype),
        in_specs=vmem(1) + hbm(1) + vmem(1),
        out_specs=pl.BlockSpec(memory_space=pltpu.HBM),
        scratch_shapes=[
            pltpu.VMEM((blocks, levels * pairs * (2 * EDGE + SPAN), twice), jnp.bfloat16),
            pltpu.VMEM((blocks, slots), jnp.float32),
            pltpu.VMEM((blocks, slots // 2, packed.shape[2]), jnp.bfloat16),
            pltpu.SemaphoreType.DMA((blocks // together,)),
        ],
        input_output_aliases={1: 0},
        compiler_params=params(20),
        cost_estimate=cost(4 * 10**9, 4 * 2**20),
    )(grid, packed, cells)


def join(a, b, left, members):
    return (
        jnp.where(left, a, pltpu.roll(b, members, 1)),
        jnp.where(left, pltpu.roll(a, members, 1), b),
    )


def batches(count, size):
    return [range(at, min(count, at + size)) for at in range(0, count, size)]


def left_lanes(shape):
    return lax.broadcasted_iota(jnp.int32, shape, 1) < shape[1] // 2


def deviations(states, raw, dev, at, size):
    groups, _, lanes = states.shape
    members = lanes // 2
    left = left_lanes((size, lanes))
    sums = [jnp.zeros((size, lanes), jnp.float32)] * 2
    for batch in batches(groups // 2, 4):
        made = [
            join(
                states[2 * j, :size, :].astype(jnp.float32),
                states[2 * j + 1, :size, :].astype(jnp.float32),
                left,
                members,
            )
            for j in batch
        ]
        for j, pair in zip(batch, made):
            here = slice(j * lanes, (j + 1) * lanes)
            for var in range(2):
                raw[var * size : (var + 1) * size, here] = pair[var]
            sums = [total + one for total, one in zip(sums, pair)]
    centre = jnp.concatenate([jnp.sum(x, axis=1, keepdims=True) for x in sums], axis=0)
    centre = centre * (1.0 / (groups * members))
    dev[at : at + 2 * size, :] = (raw[...] - centre).astype(jnp.bfloat16)
    return centre


def prepare_kernel(states, dev, centre, raw):
    mean = deviations(states, raw, dev, 0, states.shape[1])
    centre[...] = jnp.broadcast_to(mean, centre.shape)


def prepare(states):
    groups, near, lanes = states.shape
    total = groups * lanes // 2
    return pl.pallas_call(
        prepare_kernel,
        out_shape=[
            jax.ShapeDtypeStruct((2 * near, total), jnp.bfloat16),
            jax.ShapeDtypeStruct((2 * near, lanes), jnp.float32),
        ],
        in_specs=vmem(1),
        out_specs=vmem(2),
        scratch_shapes=[pltpu.VMEM((2 * near, total), jnp.float32)],
        compiler_params=params(6),
        cost_estimate=cost(10**8, 2 * 2**20),
    )(states)


def analyse_kernel(first, means, second, count, value, weight, out, raw, dev, obs, scaled_ref):
    groups, _, lanes = second.shape
    near = first.shape[0] // 2
    half = obs.shape[0] // 2
    far = second.shape[1] - half
    side = near + far
    slots = 2 * half
    members = lanes // 2
    total_members = groups * members
    left = left_lanes((half, lanes))

    for batch in batches(groups // 2, 4):
        made = [
            join(
                second[2 * j, far:, :].astype(jnp.float32),
                second[2 * j + 1, far:, :].astype(jnp.float32),
                left,
                members,
            )
            for j in batch
        ]
        for j, pair in zip(batch, made):
            here = slice(j * lanes, (j + 1) * lanes)
            obs[:half, here], obs[half:, here] = pair

    used = lax.broadcasted_iota(jnp.int32, (1, slots), 1) < count[0, 0]
    root = column_of(jnp.where(used, jnp.sqrt(weight[...]), 0.0))
    observed = obs[...]
    mean = jnp.sum(observed, axis=1, keepdims=True) * (1.0 / total_members)
    scaled = (observed - mean) * root
    energy = jnp.sum(jnp.sum(scaled * scaled, axis=1, keepdims=True), axis=0, keepdims=True)
    scaled_ref[...] = scaled.astype(jnp.bfloat16)
    misfit = row_of(root * (column_of(value[...]) - mean))

    c = total_members - 1.0
    s = energy * (1.0 / total_members) + c
    inverse = 1.0 / s
    a = c * inverse
    p = 1.5 - 0.5 * a
    p2 = p * p
    p3 = p2 * p
    base = 1.5 * p - 0.5 * a * p3
    q0 = -0.75 - 0.5 * (p3 - 1.5 * a * p2)
    q1 = -0.5 * (0.75 * a * p - 1.5 * p2)
    q2 = -0.5 * (0.75 * p - 0.125 * a)
    small = dot_rows(scaled_ref[...], scaled_ref[...]) * inverse
    diagonal = eye(slots)
    once = small.astype(jnp.bfloat16)
    square = dot(once, once).astype(jnp.bfloat16)
    tail = dot(square, (jnp.where(diagonal, q2, 0.0) + 0.0625 * small).astype(jnp.bfloat16))
    poly = jnp.where(diagonal, q0, 0.0) + q1 * small + tail

    def apply(vector):
        inner_part = jnp.sum(poly * vector, axis=1, keepdims=True)
        return jnp.sum(small * inner_part, axis=0, keepdims=True) + base * vector

    gain = apply(apply(misfit)) * inverse
    stretch = jnp.sqrt(a)
    alpha, factor = stretch * base, stretch * inverse
    centre = deviations(second, raw, dev, 0, far)
    cross = jnp.concatenate(
        [dot_rows(first[...], scaled_ref[...]), dot_rows(dev[...], scaled_ref[...])], axis=0
    )
    centre = jnp.concatenate([means[:, 0:1], centre], axis=0)
    shift = centre + jnp.sum(cross * gain, axis=1, keepdims=True)
    once = cross.astype(jnp.bfloat16)
    mix = sum(dot(once, part) for part in split(poly))
    mix = (mix * factor).astype(jnp.bfloat16)
    parts = ((first, 0, near, 0), (dev, 2 * near, far, near))
    for batch in batches(groups // 2, 2):
        made = []
        wide = slice(batch[0] * lanes, (batch[-1] + 1) * lanes)
        both = dot(mix, scaled_ref[:, wide]) + shift
        for j in batch:
            here = slice(j * lanes, (j + 1) * lanes)
            new = both[:, (j - batch[0]) * lanes :][:, :lanes]
            for ref, at, size, row in parts:
                one = new[at : at + 2 * size] + alpha * ref[:, here].astype(jnp.float32)
                pair = join(one[:size], one[size:], left_lanes((size, lanes)), members)
                made += [(2 * j + i, row, x.astype(jnp.bfloat16)) for i, x in enumerate(pair)]
        for group, row, value in made:
            out[group, row : row + value.shape[0], :] = value


def analyse(first, means, second, count, value, weight):
    groups, _, lanes = second.shape
    near = first.shape[0] // 2
    slots = value.shape[1]
    far = second.shape[1] - slots // 2
    total = groups * lanes // 2
    return pl.pallas_call(
        analyse_kernel,
        out_shape=jax.ShapeDtypeStruct((groups, near + far, lanes), jnp.bfloat16),
        in_specs=vmem(3) + smem(1) + vmem(2),
        out_specs=pl.BlockSpec(memory_space=pltpu.VMEM),
        scratch_shapes=[
            pltpu.VMEM((2 * far, total), jnp.float32),
            pltpu.VMEM((2 * far, total), jnp.bfloat16),
            pltpu.VMEM((slots, total), jnp.float32),
            pltpu.VMEM((slots, total), jnp.bfloat16),
        ],
        compiler_params=params(16),
        cost_estimate=cost(4 * 10**9, 4 * 2**20),
    )(first, means, second, count, value, weight)


def restore_kernel(blocks, out, turned, staged, sems):
    members, variables, levels, span, columns = out.shape
    lanes = members * variables
    identity = permutation(lanes, 0)
    near = span - 2 * STEPS
    for level in range(levels):
        made = []
        for r in range(0, span, 2):
            if STEPS <= r < span - STEPS:
                at = level * near + r - STEPS
            else:
                at = levels * near + level * 2 * STEPS + (r if r < STEPS else r - near)
            both = blocks[:, at * SPAN : (at + 2) * SPAN, :].astype(jnp.float32)
            for i in range(2):
                one = both[:, i * SPAN : (i + 1) * SPAN, :].reshape(columns, lanes)
                made.append((r + i, dot_rows(identity, one.astype(jnp.bfloat16))))
        for r, rows in made:
            turned[level, pl.ds(r, lanes, stride=span), :] = rows

    chunks = staged.shape[0]
    size = members // chunks
    copies = []
    for i in range(chunks):
        for level in range(levels):
            for var in range(variables):
                at = (var * members + i * size) * span
                part = turned[level, at : at + size * span, :].reshape(size, span, columns)
                staged[i, :, var, level] = part.astype(jnp.bfloat16)
        place = out.at[pl.ds(i * size, size)]
        copies.append(pltpu.make_async_copy(staged.at[i], place, sems.at[i]))
        copies[-1].start()
    for copy in copies:
        copy.wait()


def restore(dims, blocks):
    members, variables, levels, span, columns = dims
    chunks = next(n for n in (4, 2, 1) if members % n == 0)
    return pl.pallas_call(
        restore_kernel,
        out_shape=jax.ShapeDtypeStruct((members, variables, levels, span, columns), jnp.bfloat16),
        in_specs=vmem(1),
        out_specs=pl.BlockSpec(memory_space=pltpu.HBM),
        scratch_shapes=[
            pltpu.VMEM((levels, variables * members * span, columns), jnp.float32),
            pltpu.VMEM((chunks, members // chunks, variables, levels, span, columns), jnp.bfloat16),
            pltpu.SemaphoreType.DMA((chunks,)),
        ],
        compiler_params=params(10),
        cost_estimate=cost(2 * 10**9, 2 * 2**20),
    )(blocks)


def neighbours(field, axis):
    count = lax.axis_size(axis)
    low = lax.ppermute(field, axis, [(i, (i + 1) % count) for i in range(count)])
    if count == 2:
        return (low,)
    return low, lax.ppermute(field, axis, [((i + 1) % count, i) for i in range(count)])


def exchange(blocks):
    return lax.all_to_all(blocks, "grp", split_axis=0, concat_axis=0, tiled=True)


def on_device(start, diffusivity, eastward, northward, cells, count, value, weight):
    members, variables, levels, span, columns = dims = start.shape
    whole = start.reshape(members * variables, levels, span, columns)
    own, centre, near, model = inner(whole, (diffusivity, eastward, northward), variables)
    sides = neighbours(own, "tile")
    first, means = prepare(exchange(near))
    grid, packed = outer(dims, own, sides, model, centre, cells.shape[2])
    second = exchange(pick(variables, grid, packed, cells[0]))
    updated = analyse(first, means, second, count, value[0], weight[0])
    return restore(dims, exchange(updated))


def solution(mesh):
    return jax.shard_map(
        on_device,
        mesh=mesh,
        in_specs=(
            P("grp", None, None, "tile", None),
            P(),
            P(),
            P(),
            P("tile", None, None),
            P("tile", "grp"),
            P("tile", "grp", None),
            P("tile", "grp", None),
        ),
        out_specs=P("grp", None, None, "tile", None),
        check_vma=False,
    )
```

```python
import functools

import jax
import jax.numpy as jnp
from jax import lax
from jax.experimental import pallas as pl
from jax.experimental.pallas import tpu as pltpu
from jax.sharding import PartitionSpec as P

SPAN = 8
STEPS = 2
EDGE = SPAN // 2

ROWS = (((1,), (1,)), ((), ()))


def params(mebibytes, **kw):
    return pltpu.CompilerParams(vmem_limit_bytes=mebibytes * 2**20, **kw)


def cost(flops, size):
    return pl.CostEstimate(flops=flops, bytes_accessed=size, transcendentals=0)


def vmem(count):
    return [pl.BlockSpec(memory_space=pltpu.VMEM)] * count


def hbm(count):
    return [pl.BlockSpec(memory_space=pltpu.HBM)] * count


def smem(count):
    return [pl.BlockSpec(memory_space=pltpu.SMEM)] * count


def dot(a, b, **kw):
    return jnp.dot(a, b, preferred_element_type=jnp.float32, **kw)


def split(x):
    high = x.astype(jnp.bfloat16)
    return high, (x - high.astype(jnp.float32)).astype(jnp.bfloat16)


def dot_rows(a, b):
    return lax.dot_general(a, b, ROWS, preferred_element_type=jnp.float32)


def permutation(size, shift):
    row = lax.broadcasted_iota(jnp.int32, (size, size), 0)
    column = lax.broadcasted_iota(jnp.int32, (size, size), 1)
    return (lax.rem(row + shift + size, size) == column).astype(jnp.bfloat16)


def eye(size):
    row = lax.broadcasted_iota(jnp.int32, (size, size), 0)
    column = lax.broadcasted_iota(jnp.int32, (size, size), 1)
    return row == column


def column_of(row):
    return jnp.sum(jnp.where(eye(row.shape[1]), row, 0.0), axis=1, keepdims=True)


def row_of(column):
    return jnp.sum(jnp.where(eye(column.shape[0]), column, 0.0), axis=0, keepdims=True)


def both_ways(columns):
    pair = jnp.concatenate([permutation(columns, -1), permutation(columns, 1)], axis=1)
    return jnp.concatenate([pair, pair], axis=0)


def forecast_rows(read, first, last, coefficients, shifts):
    middle, east, west, north, south = coefficients

    def step(below, here, above, ahead, behind):
        return middle * here + east * above + west * below + north * ahead + south * behind

    rows = [read(r) for r in range(first - 2, last + 2)]
    tiles, _, columns = rows[0].shape
    flat = jnp.concatenate(rows[1:-1], axis=0).reshape(-1, columns)
    moved = dot(jnp.concatenate(split(flat), axis=1), shifts)
    ahead = moved[:, :columns].reshape(-1, 8, columns)
    behind = moved[:, columns:].reshape(-1, 8, columns)
    once, twice = [], []
    for i, r in enumerate(range(first - 1, last + 1)):
        here = slice(i * tiles, (i + 1) * tiles)
        once.append(step(*rows[i : i + 3], ahead[here], behind[here]))
        if i >= 2:
            one = once[-2]
            new = step(*once[-3:], pltpu.roll(one, columns - 1, 2), pltpu.roll(one, 1, 2))
            twice.append((r - 1, new.reshape(-1, columns).astype(jnp.bfloat16)))
    return twice


def coefficients_of(level, diff, east, north):
    spread = jnp.broadcast_to(diff[pl.ds(level, 1), :], (8, diff.shape[1]))
    u = 0.5 * east[level]
    w = 0.5 * north[level]
    return 1.0 - 4.0 * spread, spread - u, spread + u, spread - w, spread + w


def row_reader(level, var, own, low, high):
    span, columns = own.shape[2], own.shape[4]

    def read(r):
        ref, at = (low, r + span) if r < 0 else (own, r) if r < span else (high, r - span)
        return ref[var, level, at].reshape(-1, 8, columns)

    return read


def pack_rows(pairs, identity, store, first):
    lanes = pairs[0].shape[0] // 2
    packed = []
    for pair in pairs:
        turned = dot_rows(identity, pair)
        parts = [turned[:, i * lanes : (i + 1) * lanes].reshape(-1, SPAN, lanes) for i in range(2)]
        packed.append(jnp.concatenate(parts, axis=1).astype(jnp.bfloat16))
    for i, value in enumerate(packed):
        at = first + i * 2 * SPAN
        store[:, at : at + 2 * SPAN, :] = value


def inner_kernel(own, *refs):
    raw, (slabs, fields, packed, model) = refs[:3], refs[3:7]
    local, (whole, staged, in_sems, raw_sems, out_sems) = refs[7:10], refs[10:]
    members, variables, levels, span, columns = own.shape
    count = span - 2 * STEPS

    def arrive(level):
        return [
            pltpu.make_async_copy(own.at[:, var, level], whole.at[level, var], in_sems.at[level, var])
            for var in range(variables)
        ]

    def leave(level):
        size = count * SPAN
        here = pl.ds(pl.multiple_of(level * size, size), size)
        return pltpu.make_async_copy(staged.at[level], packed.at[:, here], out_sems.at[level])

    copies = [pltpu.make_async_copy(x, y, raw_sems.at[i]) for i, (x, y) in enumerate(zip(raw, local))]
    for copy in copies:
        copy.start()
    for level in range(min(2, levels)):
        for copy in arrive(level):
            copy.start()
    identity = permutation(columns, 0)
    shifts = both_ways(columns)
    for copy in copies:
        copy.wait()

    @pl.loop(0, levels)
    def _(level):
        coefficients = coefficients_of(level, *local)
        for i, one in enumerate(coefficients):
            model[level, i] = one
        for copy in arrive(level):
            copy.wait()

        @pl.when(level + 2 < levels)
        def _():
            for copy in arrive(level + 2):
                copy.start()

        reads, made = [], []
        for var in range(variables):
            view = whole.at[level, var].reshape(members * span, columns)

            def read(r):
                rows = view[pl.ds(r, members, stride=span), :]
                reads.append((var, r, rows))
                return rows.reshape(-1, 8, columns)

            for r, value in forecast_rows(read, STEPS, span - STEPS, coefficients, shifts):
                made.append((var, r, value))
        pairs = []
        for first in range(STEPS, span - STEPS, 2):
            rows = [one for r in (first, first + 1) for _, at, one in made if at == r]
            pairs.append(jnp.concatenate(rows, axis=0))
        pack_rows(pairs, identity, staged.at[level], 0)
        leave(level).start()
        for var, r, value in made:
            fields[level, r - STEPS, var * members : (var + 1) * members, :] = value
        for var, r, rows in reads:
            slabs[var, level, r] = rows

    for level in range(levels):
        leave(level).wait()


def inner(own, raw):
    members, variables, levels, span, columns = own.shape
    lanes = variables * members
    blocks = columns // SPAN
    count = span - 2 * STEPS
    fixed = [pltpu.with_memory_space_constraint(x, pltpu.HBM) for x in (own, *raw)]
    return pl.pallas_call(
        inner_kernel,
        out_shape=[
            jax.ShapeDtypeStruct((variables, levels, span, members, columns), jnp.float32),
            jax.ShapeDtypeStruct((levels, count, lanes, columns), jnp.bfloat16),
            jax.ShapeDtypeStruct((blocks, levels * count * SPAN, lanes), jnp.bfloat16),
            jax.ShapeDtypeStruct((levels, 5, 8, columns), jnp.float32),
        ],
        in_specs=hbm(4),
        out_specs=vmem(2) + hbm(1) + vmem(1),
        scratch_shapes=[
            pltpu.VMEM(raw[0].shape, jnp.float32),
            pltpu.SMEM(raw[1].shape, jnp.float32),
            pltpu.SMEM(raw[2].shape, jnp.float32),
            pltpu.VMEM((levels, variables, members, span, columns), jnp.float32),
            pltpu.VMEM((levels, blocks, count * SPAN, lanes), jnp.bfloat16),
            pltpu.SemaphoreType.DMA((levels, variables)),
            pltpu.SemaphoreType.DMA((3,)),
            pltpu.SemaphoreType.DMA((levels,)),
        ],
        compiler_params=params(10),
        cost_estimate=cost(2 * 10**9, 4 * 2**20),
    )(*fixed)


def outer_kernel(near, own, *rest):
    sides, rest = rest[:near], rest[near:]
    model, centre, grid, packed, staged, near_tiles, sems, out_sems, near_sems = rest
    variables, levels, span, members, columns = own.shape
    rows_each = variables * members
    pairs = (2 * EDGE + span) // 2
    size = STEPS * 2 * SPAN
    identity = permutation(columns, 0)
    shifts = both_ways(columns)

    def arrive(level):
        return [
            pltpu.make_async_copy(
                side.at[:, level], near_tiles.at[i, :, level], near_sems.at[i, level]
            )
            for i, side in enumerate(sides)
        ]

    for level in range(levels):
        for copy in arrive(level):
            copy.start()

    def leave(level):
        here = pl.ds(pl.multiple_of(level * size, size), size)
        return pltpu.make_async_copy(staged.at[level], packed.at[:, here], out_sems.at[level])

    copies = []
    for r in range(STEPS, span - STEPS):
        half, pair = divmod(r + EDGE, pairs)
        place = grid.at[:, pair, pl.ds(half * rows_each, rows_each)]
        copies.append(pltpu.make_async_copy(centre.at[:, r - STEPS], place, sems.at[r - STEPS]))
        copies[-1].start()

    @pl.loop(0, levels)
    def _(level):
        for copy in arrive(level):
            copy.wait()
        coefficients = [model[level, i] for i in range(5)]
        made = []
        for var in range(variables):
            read = row_reader(level, var, own, near_tiles.at[0], near_tiles.at[near - 1])
            for first, last in ((-EDGE, STEPS), (span - STEPS, span + EDGE)):
                for r, value in forecast_rows(read, first, last, coefficients, shifts):
                    made.append((var, r, value))
        sheets = []
        for first in (0, span - STEPS):
            rows = [one for r in range(first, first + STEPS) for _, at, one in made if at == r]
            sheets.append(jnp.concatenate(rows, axis=0))
        pack_rows(sheets, identity, staged.at[level], 0)
        leave(level).start()
        for var, r, value in made:
            half, pair = divmod(r + EDGE, pairs)
            at = half * rows_each + var * members
            grid[level, pair, at : at + members, :] = value

    for level in range(levels):
        leave(level).wait()
    for copy in copies:
        copy.wait()


def outer(dims, own, sides, model, centre, slots):
    members, variables, levels, span, columns = dims
    lanes = members * variables
    blocks = columns // SPAN
    near = len(sides)
    pairs = (2 * EDGE + span) // 2
    return pl.pallas_call(
        functools.partial(outer_kernel, near),
        out_shape=[
            jax.ShapeDtypeStruct((levels, pairs, 2 * lanes, columns), jnp.bfloat16),
            jax.ShapeDtypeStruct(
                (blocks, levels * 2 * STEPS * SPAN + slots // 2, lanes), jnp.bfloat16
            ),
        ],
        in_specs=vmem(1) + hbm(near) + vmem(1) + hbm(1),
        out_specs=vmem(1) + hbm(1),
        scratch_shapes=[
            pltpu.VMEM((levels, blocks, 2 * STEPS * SPAN, lanes), jnp.bfloat16),
            pltpu.VMEM((near, *own.shape), jnp.float32),
            pltpu.SemaphoreType.DMA((span - 2 * STEPS,)),
            pltpu.SemaphoreType.DMA((levels,)),
            pltpu.SemaphoreType.DMA((near, levels)),
        ],
        compiler_params=params(16),
        cost_estimate=cost(2 * 10**9, 8 * 2**20),
    )(own, *(pltpu.with_memory_space_constraint(x, pltpu.HBM) for x in sides), model, centre)


def pick_kernel(variables, together, grid, _, cells, out, region, codes, staged, sems):
    levels, pairs, twice, columns = grid.shape
    rows = twice // 2
    members = rows // variables
    blocks, slots = cells.shape
    width = 2 * EDGE + SPAN
    part = pairs * width
    entries = levels * part
    share = out.shape[1] - slots // 2

    order = permutation(columns, -EDGE)
    batch = next(n for n in (4, 2, 1) if pairs % n == 0)
    for level in range(levels):
        for start in range(0, pairs, batch):
            made = []
            for i in range(batch):
                even = dot_rows(order, grid[level, start + i])
                odd = jnp.concatenate([even[SPAN:], even[:SPAN]], axis=0)
                made.append((even.astype(jnp.bfloat16), odd.astype(jnp.bfloat16)))
            for i, both in enumerate(made):
                at = (level * pairs + start + i) * width
                for first, value in enumerate(both):
                    for j in range(columns // width):
                        piece = value[j * width : (j + 1) * width, :]
                        region[2 * j + first, at : at + width, :] = piece

    cell = cells[...]
    second = cell >= 2 * entries
    cell = jnp.where(second, cell - 2 * entries, cell)
    level = lax.shift_right_logical(cell, (2 * part).bit_length() - 1)
    inside = cell - level * (2 * part)
    lower = inside >= part
    code = level * part + jnp.where(lower, inside - part + entries, inside)
    codes[...] = jnp.where(second, code + 2 * entries, code).astype(jnp.float32)

    left = lax.broadcasted_iota(jnp.int32, (slots // 2, rows), 1) < members
    lane = lax.broadcasted_iota(jnp.int32, (slots, entries), 1).astype(jnp.float32)

    def leave(step):
        here = pl.ds(step * together, together)
        place = out.at[here, pl.ds(share, slots // 2)]
        return pltpu.make_async_copy(staged.at[here], place, sems.at[step])

    @pl.loop(0, blocks // together)
    def _(step):
        made = []
        for i in range(together):
            block = step * together + i
            at = column_of(codes[pl.ds(block, 1), :])
            second = at >= 2.0 * entries
            at = jnp.where(second, at - 2.0 * entries, at)
            lower = at >= 1.0 * entries
            at = jnp.where(lower, at - 1.0 * entries, at)
            pick = jnp.where(lane == at, 1.0, 0.0).astype(jnp.bfloat16)
            found = dot(pick, region[block])
            total = jnp.where(lower, found[:, rows:], found[:, :rows])
            other = pltpu.roll(total, members, 1)
            to_left = jnp.where(second, other, total)[: slots // 2]
            to_right = jnp.where(second, total, other)[slots // 2 :]
            made.append(jnp.where(left, to_left, to_right).astype(jnp.bfloat16))
        for i, value in enumerate(made):
            staged[step * together + i] = value
        leave(step).start()

    for step in range(blocks // together):
        leave(step).wait()


def pick(variables, grid, packed, cells):
    levels, pairs, twice, columns = grid.shape
    blocks, slots = cells.shape
    together = next(n for n in (4, 2, 1) if blocks % n == 0)
    return pl.pallas_call(
        functools.partial(pick_kernel, variables, together),
        out_shape=jax.ShapeDtypeStruct(packed.shape, packed.dtype),
        in_specs=vmem(1) + hbm(1) + vmem(1),
        out_specs=pl.BlockSpec(memory_space=pltpu.HBM),
        scratch_shapes=[
            pltpu.VMEM((blocks, levels * pairs * (2 * EDGE + SPAN), twice), jnp.bfloat16),
            pltpu.VMEM((blocks, slots), jnp.float32),
            pltpu.VMEM((blocks, slots // 2, packed.shape[2]), jnp.bfloat16),
            pltpu.SemaphoreType.DMA((blocks // together,)),
        ],
        input_output_aliases={1: 0},
        compiler_params=params(20),
        cost_estimate=cost(4 * 10**9, 4 * 2**20),
    )(grid, packed, cells)


def join(a, b, left, members):
    return (
        jnp.where(left, a, pltpu.roll(b, members, 1)),
        jnp.where(left, pltpu.roll(a, members, 1), b),
    )


def batches(count, size):
    return [range(at, min(count, at + size)) for at in range(0, count, size)]


def left_lanes(shape):
    return lax.broadcasted_iota(jnp.int32, shape, 1) < shape[1] // 2


def deviations(states, raw, dev, at, size):
    groups, _, lanes = states.shape
    members = lanes // 2
    left = left_lanes((size, lanes))
    sums = [jnp.zeros((size, lanes), jnp.float32)] * 2
    for batch in batches(groups // 2, 4):
        made = [
            join(
                states[2 * j, :size, :].astype(jnp.float32),
                states[2 * j + 1, :size, :].astype(jnp.float32),
                left,
                members,
            )
            for j in batch
        ]
        for j, pair in zip(batch, made):
            here = slice(j * lanes, (j + 1) * lanes)
            for var in range(2):
                raw[var * size : (var + 1) * size, here] = pair[var]
            sums = [total + one for total, one in zip(sums, pair)]
    centre = jnp.concatenate([jnp.sum(x, axis=1, keepdims=True) for x in sums], axis=0)
    centre = centre * (1.0 / (groups * members))
    dev[at : at + 2 * size, :] = (raw[...] - centre).astype(jnp.bfloat16)
    return centre


def prepare_kernel(states, dev, centre, raw):
    mean = deviations(states, raw, dev, 0, states.shape[1])
    centre[...] = jnp.broadcast_to(mean, centre.shape)


def prepare(states):
    groups, near, lanes = states.shape
    total = groups * lanes // 2
    return pl.pallas_call(
        prepare_kernel,
        out_shape=[
            jax.ShapeDtypeStruct((2 * near, total), jnp.bfloat16),
            jax.ShapeDtypeStruct((2 * near, lanes), jnp.float32),
        ],
        in_specs=vmem(1),
        out_specs=vmem(2),
        scratch_shapes=[pltpu.VMEM((2 * near, total), jnp.float32)],
        compiler_params=params(6),
        cost_estimate=cost(10**8, 2 * 2**20),
    )(states)


def analyse_kernel(first, means, second, count, value, weight, out, raw, dev, obs, scaled_ref):
    groups, _, lanes = second.shape
    near = first.shape[0] // 2
    half = obs.shape[0] // 2
    far = second.shape[1] - half
    side = near + far
    slots = 2 * half
    members = lanes // 2
    total_members = groups * members
    left = left_lanes((half, lanes))

    for batch in batches(groups // 2, 4):
        made = [
            join(
                second[2 * j, far:, :].astype(jnp.float32),
                second[2 * j + 1, far:, :].astype(jnp.float32),
                left,
                members,
            )
            for j in batch
        ]
        for j, pair in zip(batch, made):
            here = slice(j * lanes, (j + 1) * lanes)
            obs[:half, here], obs[half:, here] = pair

    used = lax.broadcasted_iota(jnp.int32, (1, slots), 1) < count[0, 0]
    root = column_of(jnp.where(used, jnp.sqrt(weight[...]), 0.0))
    observed = obs[...]
    mean = jnp.sum(observed, axis=1, keepdims=True) * (1.0 / total_members)
    scaled = (observed - mean) * root
    energy = jnp.sum(jnp.sum(scaled * scaled, axis=1, keepdims=True), axis=0, keepdims=True)
    scaled_ref[...] = scaled.astype(jnp.bfloat16)
    misfit = row_of(root * (column_of(value[...]) - mean))

    c = total_members - 1.0
    s = energy * (1.0 / total_members) + c
    inverse = 1.0 / s
    a = c * inverse
    p = 1.5 - 0.5 * a
    p2 = p * p
    p3 = p2 * p
    base = 1.5 * p - 0.5 * a * p3
    q0 = -0.75 - 0.5 * (p3 - 1.5 * a * p2)
    q1 = -0.5 * (0.75 * a * p - 1.5 * p2)
    q2 = -0.5 * (0.75 * p - 0.125 * a)
    small = dot_rows(scaled_ref[...], scaled_ref[...]) * inverse
    diagonal = eye(slots)
    once = small.astype(jnp.bfloat16)
    square = dot(once, once).astype(jnp.bfloat16)
    tail = dot(square, (jnp.where(diagonal, q2, 0.0) + 0.0625 * small).astype(jnp.bfloat16))
    poly = jnp.where(diagonal, q0, 0.0) + q1 * small + tail

    def apply(vector):
        inner_part = jnp.sum(poly * vector, axis=1, keepdims=True)
        return jnp.sum(small * inner_part, axis=0, keepdims=True) + base * vector

    gain = apply(apply(misfit)) * inverse
    stretch = jnp.sqrt(a)
    alpha, factor = stretch * base, stretch * inverse
    centre = deviations(second, raw, dev, 0, far)
    cross = jnp.concatenate(
        [dot_rows(first[...], scaled_ref[...]), dot_rows(dev[...], scaled_ref[...])], axis=0
    )
    centre = jnp.concatenate([means[:, 0:1], centre], axis=0)
    shift = centre + jnp.sum(cross * gain, axis=1, keepdims=True)
    once = cross.astype(jnp.bfloat16)
    mix = sum(dot(once, part) for part in split(poly))
    mix = (mix * factor).astype(jnp.bfloat16)
    parts = ((first, 0, near, 0), (dev, 2 * near, far, near))
    for batch in batches(groups // 2, 2):
        made = []
        wide = slice(batch[0] * lanes, (batch[-1] + 1) * lanes)
        both = dot(mix, scaled_ref[:, wide]) + shift
        for j in batch:
            here = slice(j * lanes, (j + 1) * lanes)
            new = both[:, (j - batch[0]) * lanes :][:, :lanes]
            for ref, at, size, row in parts:
                one = new[at : at + 2 * size] + alpha * ref[:, here].astype(jnp.float32)
                pair = join(one[:size], one[size:], left_lanes((size, lanes)), members)
                made += [(2 * j + i, row, x.astype(jnp.bfloat16)) for i, x in enumerate(pair)]
        for group, row, value in made:
            out[group, row : row + value.shape[0], :] = value


def analyse(first, means, second, count, value, weight):
    groups, _, lanes = second.shape
    near = first.shape[0] // 2
    slots = value.shape[1]
    far = second.shape[1] - slots // 2
    total = groups * lanes // 2
    return pl.pallas_call(
        analyse_kernel,
        out_shape=jax.ShapeDtypeStruct((groups, near + far, lanes), jnp.bfloat16),
        in_specs=vmem(3) + smem(1) + vmem(2),
        out_specs=pl.BlockSpec(memory_space=pltpu.VMEM),
        scratch_shapes=[
            pltpu.VMEM((2 * far, total), jnp.float32),
            pltpu.VMEM((2 * far, total), jnp.bfloat16),
            pltpu.VMEM((slots, total), jnp.float32),
            pltpu.VMEM((slots, total), jnp.bfloat16),
        ],
        compiler_params=params(16),
        cost_estimate=cost(4 * 10**9, 4 * 2**20),
    )(first, means, second, count, value, weight)


def restore_kernel(blocks, out, turned, staged, sems):
    members, variables, levels, span, columns = out.shape
    lanes = members * variables
    identity = permutation(lanes, 0)
    near = span - 2 * STEPS
    for level in range(levels):
        made = []
        for r in range(0, span, 2):
            if STEPS <= r < span - STEPS:
                at = level * near + r - STEPS
            else:
                at = levels * near + level * 2 * STEPS + (r if r < STEPS else r - near)
            both = blocks[:, at * SPAN : (at + 2) * SPAN, :].astype(jnp.float32)
            for i in range(2):
                one = both[:, i * SPAN : (i + 1) * SPAN, :].reshape(columns, lanes)
                made.append((r + i, dot_rows(identity, one.astype(jnp.bfloat16))))
        for r, rows in made:
            turned[level, pl.ds(r, lanes, stride=span), :] = rows

    chunks = staged.shape[0]
    size = members // chunks
    copies = []
    for i in range(chunks):
        for level in range(levels):
            for var in range(variables):
                at = (var * members + i * size) * span
                part = turned[level, at : at + size * span, :].reshape(size, span, columns)
                staged[i, :, var, level] = part.astype(jnp.bfloat16)
        place = out.at[pl.ds(i * size, size)]
        copies.append(pltpu.make_async_copy(staged.at[i], place, sems.at[i]))
        copies[-1].start()
    for copy in copies:
        copy.wait()


def restore(dims, blocks):
    members, variables, levels, span, columns = dims
    chunks = next(n for n in (4, 2, 1) if members % n == 0)
    return pl.pallas_call(
        restore_kernel,
        out_shape=jax.ShapeDtypeStruct((members, variables, levels, span, columns), jnp.bfloat16),
        in_specs=vmem(1),
        out_specs=pl.BlockSpec(memory_space=pltpu.HBM),
        scratch_shapes=[
            pltpu.VMEM((levels, variables * members * span, columns), jnp.float32),
            pltpu.VMEM((chunks, members // chunks, variables, levels, span, columns), jnp.bfloat16),
            pltpu.SemaphoreType.DMA((chunks,)),
        ],
        compiler_params=params(10),
        cost_estimate=cost(2 * 10**9, 2 * 2**20),
    )(blocks)


def neighbours(field, axis):
    count = lax.axis_size(axis)
    low = lax.ppermute(field, axis, [(i, (i + 1) % count) for i in range(count)])
    if count == 2:
        return (low,)
    return low, lax.ppermute(field, axis, [((i + 1) % count, i) for i in range(count)])


def exchange(blocks):
    return lax.all_to_all(blocks, "grp", split_axis=0, concat_axis=0, tiled=True)


def on_device(start, diffusivity, eastward, northward, cells, count, value, weight):
    members, variables, levels, span, columns = dims = start.shape
    own, centre, near, model = inner(start, (diffusivity, eastward, northward))
    sides = neighbours(own, "tile")
    first, means = prepare(exchange(near))
    grid, packed = outer(dims, own, sides, model, centre, cells.shape[2])
    second = exchange(pick(variables, grid, packed, cells[0]))
    updated = analyse(first, means, second, count, value[0], weight[0])
    return restore(dims, exchange(updated))


def solution(mesh):
    return jax.shard_map(
        on_device,
        mesh=mesh,
        in_specs=(
            P("grp", None, None, "tile", None),
            P(),
            P(),
            P(),
            P("tile", None, None),
            P("tile", "grp"),
            P("tile", "grp", None),
            P("tile", "grp", None),
        ),
        out_specs=P("grp", None, None, "tile", None),
        check_vma=False,
    )
```

```python
import functools

import jax
import jax.numpy as jnp
from jax import lax
from jax.experimental import pallas as pl
from jax.experimental.pallas import tpu as pltpu
from jax.sharding import PartitionSpec as P

SPAN = 8
STEPS = 2
EDGE = SPAN // 2

ROWS = (((1,), (1,)), ((), ()))


def params(mebibytes, **kw):
    return pltpu.CompilerParams(vmem_limit_bytes=mebibytes * 2**20, **kw)


def cost(flops, size):
    return pl.CostEstimate(flops=flops, bytes_accessed=size, transcendentals=0)


def vmem(count):
    return [pl.BlockSpec(memory_space=pltpu.VMEM)] * count


def hbm(count):
    return [pl.BlockSpec(memory_space=pltpu.HBM)] * count


def smem(count):
    return [pl.BlockSpec(memory_space=pltpu.SMEM)] * count


def dot(a, b, **kw):
    return jnp.dot(a, b, preferred_element_type=jnp.float32, **kw)


def split(x):
    high = x.astype(jnp.bfloat16)
    return high, (x - high.astype(jnp.float32)).astype(jnp.bfloat16)


def dot_rows(a, b):
    return lax.dot_general(a, b, ROWS, preferred_element_type=jnp.float32)


def permutation(size, shift):
    row = lax.broadcasted_iota(jnp.int32, (size, size), 0)
    column = lax.broadcasted_iota(jnp.int32, (size, size), 1)
    return (lax.rem(row + shift + size, size) == column).astype(jnp.bfloat16)


def eye(size):
    row = lax.broadcasted_iota(jnp.int32, (size, size), 0)
    column = lax.broadcasted_iota(jnp.int32, (size, size), 1)
    return row == column


def column_of(row):
    return jnp.sum(jnp.where(eye(row.shape[1]), row, 0.0), axis=1, keepdims=True)


def row_of(column):
    return jnp.sum(jnp.where(eye(column.shape[0]), column, 0.0), axis=0, keepdims=True)


def both_ways(columns):
    pair = jnp.concatenate([permutation(columns, -1), permutation(columns, 1)], axis=1)
    return jnp.concatenate([pair, pair], axis=0)


def forecast_rows(read, first, last, coefficients, shifts):
    middle, east, west, north, south = coefficients

    def step(below, here, above, ahead, behind):
        return middle * here + east * above + west * below + north * ahead + south * behind

    rows = [read(r) for r in range(first - 2, last + 2)]
    tiles, _, columns = rows[0].shape
    flat = jnp.concatenate(rows[1:-1], axis=0).reshape(-1, columns)
    moved = dot(jnp.concatenate(split(flat), axis=1), shifts)
    ahead = moved[:, :columns].reshape(-1, 8, columns)
    behind = moved[:, columns:].reshape(-1, 8, columns)
    once, twice = [], []
    for i, r in enumerate(range(first - 1, last + 1)):
        here = slice(i * tiles, (i + 1) * tiles)
        once.append(step(*rows[i : i + 3], ahead[here], behind[here]))
        if i >= 2:
            one = once[-2]
            new = step(*once[-3:], pltpu.roll(one, columns - 1, 2), pltpu.roll(one, 1, 2))
            twice.append((r - 1, new.reshape(-1, columns).astype(jnp.bfloat16)))
    return twice


def coefficients_of(level, diff, east, north):
    spread = jnp.broadcast_to(diff[pl.ds(level, 1), :], (8, diff.shape[1]))
    u = 0.5 * east[level]
    w = 0.5 * north[level]
    return 1.0 - 4.0 * spread, spread - u, spread + u, spread - w, spread + w


def row_reader(level, var, own, low, high):
    span, columns = own.shape[2], own.shape[4]

    def read(r):
        ref, at = (low, r + span) if r < 0 else (own, r) if r < span else (high, r - span)
        return ref[var, level, at].reshape(-1, 8, columns)

    return read


def pack_rows(pairs, identity, store, first):
    lanes = pairs[0].shape[0] // 2
    packed = []
    for pair in pairs:
        turned = dot_rows(identity, pair)
        parts = [turned[:, i * lanes : (i + 1) * lanes].reshape(-1, SPAN, lanes) for i in range(2)]
        packed.append(jnp.concatenate(parts, axis=1).astype(jnp.bfloat16))
    for i, value in enumerate(packed):
        at = first + i * 2 * SPAN
        store[:, at : at + 2 * SPAN, :] = value


def inner_kernel(own, *refs):
    raw, (slabs, fields, packed, model) = refs[:3], refs[3:7]
    local, (whole, staged, in_sems, raw_sems, out_sems) = refs[7:10], refs[10:]
    members, variables, levels, span, columns = own.shape
    count = span - 2 * STEPS

    arrivals = [
        pltpu.make_async_copy(own.at[:, var], whole.at[var], in_sems.at[var])
        for var in range(variables)
    ]

    def leave(level):
        size = count * SPAN
        here = pl.ds(pl.multiple_of(level * size, size), size)
        return pltpu.make_async_copy(staged.at[level], packed.at[:, here], out_sems.at[level])

    copies = [pltpu.make_async_copy(x, y, raw_sems.at[i]) for i, (x, y) in enumerate(zip(raw, local))]
    for copy in copies:
        copy.start()
    for copy in arrivals:
        copy.start()
    identity = permutation(columns, 0)
    shifts = both_ways(columns)
    for copy in copies:
        copy.wait()

    for var in range(variables):
        arrivals[var].wait()
        view = whole.at[var].reshape(members * levels * span, columns)

        @pl.loop(0, levels)
        def _(level):
            coefficients = coefficients_of(level, *local)
            reads = []

            def read(r):
                rows = view[pl.ds(level * span + r, members, stride=levels * span), :]
                reads.append((r, rows))
                return rows.reshape(-1, 8, columns)

            made = forecast_rows(read, STEPS, span - STEPS, coefficients, shifts)
            if var == variables - 1:
                pairs = []
                for first in range(STEPS, span - STEPS, 2):
                    rows = []
                    for r in (first, first + 1):
                        rows += [fields[level, r - STEPS, : var * members, :]] if var else []
                        rows += [one for at, one in made if at == r]
                    pairs.append(jnp.concatenate(rows, axis=0))
                pack_rows(pairs, identity, staged.at[level], 0)
                leave(level).start()
                for i, one in enumerate(coefficients):
                    model[level, i] = one
            for r, value in made:
                fields[level, r - STEPS, var * members : (var + 1) * members, :] = value
            for r, rows in reads:
                slabs[var, level, r] = rows

    for level in range(levels):
        leave(level).wait()


def inner(own, raw):
    members, variables, levels, span, columns = own.shape
    lanes = variables * members
    blocks = columns // SPAN
    count = span - 2 * STEPS
    fixed = [pltpu.with_memory_space_constraint(x, pltpu.HBM) for x in (own, *raw)]
    return pl.pallas_call(
        inner_kernel,
        out_shape=[
            jax.ShapeDtypeStruct((variables, levels, span, members, columns), jnp.float32),
            jax.ShapeDtypeStruct((levels, count, lanes, columns), jnp.bfloat16),
            jax.ShapeDtypeStruct((blocks, levels * count * SPAN, lanes), jnp.bfloat16),
            jax.ShapeDtypeStruct((levels, 5, 8, columns), jnp.float32),
        ],
        in_specs=hbm(4),
        out_specs=vmem(2) + hbm(1) + vmem(1),
        scratch_shapes=[
            pltpu.VMEM(raw[0].shape, jnp.float32),
            pltpu.SMEM(raw[1].shape, jnp.float32),
            pltpu.SMEM(raw[2].shape, jnp.float32),
            pltpu.VMEM((variables, members, levels, span, columns), jnp.float32),
            pltpu.VMEM((levels, blocks, count * SPAN, lanes), jnp.bfloat16),
            pltpu.SemaphoreType.DMA((variables,)),
            pltpu.SemaphoreType.DMA((3,)),
            pltpu.SemaphoreType.DMA((levels,)),
        ],
        compiler_params=params(10),
        cost_estimate=cost(2 * 10**9, 4 * 2**20),
    )(*fixed)


def outer_kernel(near, own, *rest):
    sides, rest = rest[:near], rest[near:]
    model, centre, grid, packed, staged, near_tiles, sems, out_sems, near_sems = rest
    variables, levels, span, members, columns = own.shape
    rows_each = variables * members
    pairs = (2 * EDGE + span) // 2
    size = STEPS * 2 * SPAN
    identity = permutation(columns, 0)
    shifts = both_ways(columns)

    def arrive(level):
        return [
            pltpu.make_async_copy(
                side.at[:, level], near_tiles.at[i, :, level], near_sems.at[i, level]
            )
            for i, side in enumerate(sides)
        ]

    for level in range(levels):
        for copy in arrive(level):
            copy.start()

    def leave(level):
        here = pl.ds(pl.multiple_of(level * size, size), size)
        return pltpu.make_async_copy(staged.at[level], packed.at[:, here], out_sems.at[level])

    copies = []
    for r in range(STEPS, span - STEPS):
        half, pair = divmod(r + EDGE, pairs)
        place = grid.at[:, pair, pl.ds(half * rows_each, rows_each)]
        copies.append(pltpu.make_async_copy(centre.at[:, r - STEPS], place, sems.at[r - STEPS]))
        copies[-1].start()

    @pl.loop(0, levels)
    def _(level):
        for copy in arrive(level):
            copy.wait()
        coefficients = [model[level, i] for i in range(5)]
        made = []
        for var in range(variables):
            read = row_reader(level, var, own, near_tiles.at[0], near_tiles.at[near - 1])
            for first, last in ((-EDGE, STEPS), (span - STEPS, span + EDGE)):
                for r, value in forecast_rows(read, first, last, coefficients, shifts):
                    made.append((var, r, value))
        sheets = []
        for first in (0, span - STEPS):
            rows = [one for r in range(first, first + STEPS) for _, at, one in made if at == r]
            sheets.append(jnp.concatenate(rows, axis=0))
        pack_rows(sheets, identity, staged.at[level], 0)
        leave(level).start()
        for var, r, value in made:
            half, pair = divmod(r + EDGE, pairs)
            at = half * rows_each + var * members
            grid[level, pair, at : at + members, :] = value

    for level in range(levels):
        leave(level).wait()
    for copy in copies:
        copy.wait()


def outer(dims, own, sides, model, centre, slots):
    members, variables, levels, span, columns = dims
    lanes = members * variables
    blocks = columns // SPAN
    near = len(sides)
    pairs = (2 * EDGE + span) // 2
    return pl.pallas_call(
        functools.partial(outer_kernel, near),
        out_shape=[
            jax.ShapeDtypeStruct((levels, pairs, 2 * lanes, columns), jnp.bfloat16),
            jax.ShapeDtypeStruct(
                (blocks, levels * 2 * STEPS * SPAN + slots // 2, lanes), jnp.bfloat16
            ),
        ],
        in_specs=vmem(1) + hbm(near) + vmem(1) + hbm(1),
        out_specs=vmem(1) + hbm(1),
        scratch_shapes=[
            pltpu.VMEM((levels, blocks, 2 * STEPS * SPAN, lanes), jnp.bfloat16),
            pltpu.VMEM((near, *own.shape), jnp.float32),
            pltpu.SemaphoreType.DMA((span - 2 * STEPS,)),
            pltpu.SemaphoreType.DMA((levels,)),
            pltpu.SemaphoreType.DMA((near, levels)),
        ],
        compiler_params=params(16),
        cost_estimate=cost(2 * 10**9, 8 * 2**20),
    )(own, *(pltpu.with_memory_space_constraint(x, pltpu.HBM) for x in sides), model, centre)


def pick_kernel(variables, together, grid, _, cells, out, region, codes, staged, sems):
    levels, pairs, twice, columns = grid.shape
    rows = twice // 2
    members = rows // variables
    blocks, slots = cells.shape
    width = 2 * EDGE + SPAN
    part = pairs * width
    entries = levels * part
    share = out.shape[1] - slots // 2

    order = permutation(columns, -EDGE)
    batch = next(n for n in (4, 2, 1) if pairs % n == 0)
    for level in range(levels):
        for start in range(0, pairs, batch):
            made = []
            for i in range(batch):
                even = dot_rows(order, grid[level, start + i])
                odd = jnp.concatenate([even[SPAN:], even[:SPAN]], axis=0)
                made.append((even.astype(jnp.bfloat16), odd.astype(jnp.bfloat16)))
            for i, both in enumerate(made):
                at = (level * pairs + start + i) * width
                for first, value in enumerate(both):
                    for j in range(columns // width):
                        piece = value[j * width : (j + 1) * width, :]
                        region[2 * j + first, at : at + width, :] = piece

    cell = cells[...]
    second = cell >= 2 * entries
    cell = jnp.where(second, cell - 2 * entries, cell)
    level = lax.shift_right_logical(cell, (2 * part).bit_length() - 1)
    inside = cell - level * (2 * part)
    lower = inside >= part
    code = level * part + jnp.where(lower, inside - part + entries, inside)
    codes[...] = jnp.where(second, code + 2 * entries, code).astype(jnp.float32)

    left = lax.broadcasted_iota(jnp.int32, (slots // 2, rows), 1) < members
    lane = lax.broadcasted_iota(jnp.int32, (slots, entries), 1).astype(jnp.float32)

    def leave(step):
        here = pl.ds(step * together, together)
        place = out.at[here, pl.ds(share, slots // 2)]
        return pltpu.make_async_copy(staged.at[here], place, sems.at[step])

    @pl.loop(0, blocks // together)
    def _(step):
        made = []
        for i in range(together):
            block = step * together + i
            at = column_of(codes[pl.ds(block, 1), :])
            second = at >= 2.0 * entries
            at = jnp.where(second, at - 2.0 * entries, at)
            lower = at >= 1.0 * entries
            at = jnp.where(lower, at - 1.0 * entries, at)
            pick = jnp.where(lane == at, 1.0, 0.0).astype(jnp.bfloat16)
            found = dot(pick, region[block])
            total = jnp.where(lower, found[:, rows:], found[:, :rows])
            other = pltpu.roll(total, members, 1)
            to_left = jnp.where(second, other, total)[: slots // 2]
            to_right = jnp.where(second, total, other)[slots // 2 :]
            made.append(jnp.where(left, to_left, to_right).astype(jnp.bfloat16))
        for i, value in enumerate(made):
            staged[step * together + i] = value
        leave(step).start()

    for step in range(blocks // together):
        leave(step).wait()


def pick(variables, grid, packed, cells):
    levels, pairs, twice, columns = grid.shape
    blocks, slots = cells.shape
    together = next(n for n in (4, 2, 1) if blocks % n == 0)
    return pl.pallas_call(
        functools.partial(pick_kernel, variables, together),
        out_shape=jax.ShapeDtypeStruct(packed.shape, packed.dtype),
        in_specs=vmem(1) + hbm(1) + vmem(1),
        out_specs=pl.BlockSpec(memory_space=pltpu.HBM),
        scratch_shapes=[
            pltpu.VMEM((blocks, levels * pairs * (2 * EDGE + SPAN), twice), jnp.bfloat16),
            pltpu.VMEM((blocks, slots), jnp.float32),
            pltpu.VMEM((blocks, slots // 2, packed.shape[2]), jnp.bfloat16),
            pltpu.SemaphoreType.DMA((blocks // together,)),
        ],
        input_output_aliases={1: 0},
        compiler_params=params(20),
        cost_estimate=cost(4 * 10**9, 4 * 2**20),
    )(grid, packed, cells)


def join(a, b, left, members):
    return (
        jnp.where(left, a, pltpu.roll(b, members, 1)),
        jnp.where(left, pltpu.roll(a, members, 1), b),
    )


def batches(count, size):
    return [range(at, min(count, at + size)) for at in range(0, count, size)]


def left_lanes(shape):
    return lax.broadcasted_iota(jnp.int32, shape, 1) < shape[1] // 2


def deviations(states, raw, dev, at, size):
    groups, _, lanes = states.shape
    members = lanes // 2
    left = left_lanes((size, lanes))
    sums = [jnp.zeros((size, lanes), jnp.float32)] * 2
    for batch in batches(groups // 2, 4):
        made = [
            join(
                states[2 * j, :size, :].astype(jnp.float32),
                states[2 * j + 1, :size, :].astype(jnp.float32),
                left,
                members,
            )
            for j in batch
        ]
        for j, pair in zip(batch, made):
            here = slice(j * lanes, (j + 1) * lanes)
            for var in range(2):
                raw[var * size : (var + 1) * size, here] = pair[var]
            sums = [total + one for total, one in zip(sums, pair)]
    centre = jnp.concatenate([jnp.sum(x, axis=1, keepdims=True) for x in sums], axis=0)
    centre = centre * (1.0 / (groups * members))
    dev[at : at + 2 * size, :] = (raw[...] - centre).astype(jnp.bfloat16)
    return centre


def prepare_kernel(states, dev, centre, raw):
    mean = deviations(states, raw, dev, 0, states.shape[1])
    centre[...] = jnp.broadcast_to(mean, centre.shape)


def prepare(states):
    groups, near, lanes = states.shape
    total = groups * lanes // 2
    return pl.pallas_call(
        prepare_kernel,
        out_shape=[
            jax.ShapeDtypeStruct((2 * near, total), jnp.bfloat16),
            jax.ShapeDtypeStruct((2 * near, lanes), jnp.float32),
        ],
        in_specs=vmem(1),
        out_specs=vmem(2),
        scratch_shapes=[pltpu.VMEM((2 * near, total), jnp.float32)],
        compiler_params=params(6),
        cost_estimate=cost(10**8, 2 * 2**20),
    )(states)


def analyse_kernel(first, means, second, count, value, weight, out, raw, dev, obs, scaled_ref):
    groups, _, lanes = second.shape
    near = first.shape[0] // 2
    half = obs.shape[0] // 2
    far = second.shape[1] - half
    side = near + far
    slots = 2 * half
    members = lanes // 2
    total_members = groups * members
    left = left_lanes((half, lanes))

    for batch in batches(groups // 2, 4):
        made = [
            join(
                second[2 * j, far:, :].astype(jnp.float32),
                second[2 * j + 1, far:, :].astype(jnp.float32),
                left,
                members,
            )
            for j in batch
        ]
        for j, pair in zip(batch, made):
            here = slice(j * lanes, (j + 1) * lanes)
            obs[:half, here], obs[half:, here] = pair

    used = lax.broadcasted_iota(jnp.int32, (1, slots), 1) < count[0, 0]
    root = column_of(jnp.where(used, jnp.sqrt(weight[...]), 0.0))
    observed = obs[...]
    mean = jnp.sum(observed, axis=1, keepdims=True) * (1.0 / total_members)
    scaled = (observed - mean) * root
    energy = jnp.sum(jnp.sum(scaled * scaled, axis=1, keepdims=True), axis=0, keepdims=True)
    scaled_ref[...] = scaled.astype(jnp.bfloat16)
    misfit = row_of(root * (column_of(value[...]) - mean))

    c = total_members - 1.0
    s = energy * (1.0 / total_members) + c
    inverse = 1.0 / s
    a = c * inverse
    p = 1.5 - 0.5 * a
    p2 = p * p
    p3 = p2 * p
    base = 1.5 * p - 0.5 * a * p3
    q0 = -0.75 - 0.5 * (p3 - 1.5 * a * p2)
    q1 = -0.5 * (0.75 * a * p - 1.5 * p2)
    q2 = -0.5 * (0.75 * p - 0.125 * a)
    small = dot_rows(scaled_ref[...], scaled_ref[...]) * inverse
    diagonal = eye(slots)
    once = small.astype(jnp.bfloat16)
    square = dot(once, once).astype(jnp.bfloat16)
    tail = dot(square, (jnp.where(diagonal, q2, 0.0) + 0.0625 * small).astype(jnp.bfloat16))
    poly = jnp.where(diagonal, q0, 0.0) + q1 * small + tail

    def apply(vector):
        inner_part = jnp.sum(poly * vector, axis=1, keepdims=True)
        return jnp.sum(small * inner_part, axis=0, keepdims=True) + base * vector

    gain = apply(apply(misfit)) * inverse
    stretch = jnp.sqrt(a)
    alpha, factor = stretch * base, stretch * inverse
    centre = deviations(second, raw, dev, 0, far)
    cross = jnp.concatenate(
        [dot_rows(first[...], scaled_ref[...]), dot_rows(dev[...], scaled_ref[...])], axis=0
    )
    centre = jnp.concatenate([means[:, 0:1], centre], axis=0)
    shift = centre + jnp.sum(cross * gain, axis=1, keepdims=True)
    once = cross.astype(jnp.bfloat16)
    mix = sum(dot(once, part) for part in split(poly))
    mix = (mix * factor).astype(jnp.bfloat16)
    parts = ((first, 0, near, 0), (dev, 2 * near, far, near))
    for batch in batches(groups // 2, 2):
        made = []
        wide = slice(batch[0] * lanes, (batch[-1] + 1) * lanes)
        both = dot(mix, scaled_ref[:, wide]) + shift
        for j in batch:
            here = slice(j * lanes, (j + 1) * lanes)
            new = both[:, (j - batch[0]) * lanes :][:, :lanes]
            for ref, at, size, row in parts:
                one = new[at : at + 2 * size] + alpha * ref[:, here].astype(jnp.float32)
                pair = join(one[:size], one[size:], left_lanes((size, lanes)), members)
                made += [(2 * j + i, row, x.astype(jnp.bfloat16)) for i, x in enumerate(pair)]
        for group, row, value in made:
            out[group, row : row + value.shape[0], :] = value


def analyse(first, means, second, count, value, weight):
    groups, _, lanes = second.shape
    near = first.shape[0] // 2
    slots = value.shape[1]
    far = second.shape[1] - slots // 2
    total = groups * lanes // 2
    return pl.pallas_call(
        analyse_kernel,
        out_shape=jax.ShapeDtypeStruct((groups, near + far, lanes), jnp.bfloat16),
        in_specs=vmem(3) + smem(1) + vmem(2),
        out_specs=pl.BlockSpec(memory_space=pltpu.VMEM),
        scratch_shapes=[
            pltpu.VMEM((2 * far, total), jnp.float32),
            pltpu.VMEM((2 * far, total), jnp.bfloat16),
            pltpu.VMEM((slots, total), jnp.float32),
            pltpu.VMEM((slots, total), jnp.bfloat16),
        ],
        compiler_params=params(16),
        cost_estimate=cost(4 * 10**9, 4 * 2**20),
    )(first, means, second, count, value, weight)


def restore_kernel(blocks, out, turned, staged, sems):
    members, variables, levels, span, columns = out.shape
    lanes = members * variables
    identity = permutation(lanes, 0)
    near = span - 2 * STEPS
    for level in range(levels):
        made = []
        for r in range(0, span, 2):
            if STEPS <= r < span - STEPS:
                at = level * near + r - STEPS
            else:
                at = levels * near + level * 2 * STEPS + (r if r < STEPS else r - near)
            both = blocks[:, at * SPAN : (at + 2) * SPAN, :].astype(jnp.float32)
            for i in range(2):
                one = both[:, i * SPAN : (i + 1) * SPAN, :].reshape(columns, lanes)
                made.append((r + i, dot_rows(identity, one.astype(jnp.bfloat16))))
        for r, rows in made:
            turned[level, pl.ds(r, lanes, stride=span), :] = rows

    chunks = staged.shape[0]
    size = members // chunks
    copies = []
    for i in range(chunks):
        for level in range(levels):
            for var in range(variables):
                at = (var * members + i * size) * span
                part = turned[level, at : at + size * span, :].reshape(size, span, columns)
                staged[i, :, var, level] = part.astype(jnp.bfloat16)
        place = out.at[pl.ds(i * size, size)]
        copies.append(pltpu.make_async_copy(staged.at[i], place, sems.at[i]))
        copies[-1].start()
    for copy in copies:
        copy.wait()


def restore(dims, blocks):
    members, variables, levels, span, columns = dims
    chunks = next(n for n in (4, 2, 1) if members % n == 0)
    return pl.pallas_call(
        restore_kernel,
        out_shape=jax.ShapeDtypeStruct((members, variables, levels, span, columns), jnp.bfloat16),
        in_specs=vmem(1),
        out_specs=pl.BlockSpec(memory_space=pltpu.HBM),
        scratch_shapes=[
            pltpu.VMEM((levels, variables * members * span, columns), jnp.float32),
            pltpu.VMEM((chunks, members // chunks, variables, levels, span, columns), jnp.bfloat16),
            pltpu.SemaphoreType.DMA((chunks,)),
        ],
        compiler_params=params(10),
        cost_estimate=cost(2 * 10**9, 2 * 2**20),
    )(blocks)


def neighbours(field, axis):
    count = lax.axis_size(axis)
    low = lax.ppermute(field, axis, [(i, (i + 1) % count) for i in range(count)])
    if count == 2:
        return (low,)
    return low, lax.ppermute(field, axis, [((i + 1) % count, i) for i in range(count)])


def exchange(blocks):
    return lax.all_to_all(blocks, "grp", split_axis=0, concat_axis=0, tiled=True)


def on_device(start, diffusivity, eastward, northward, cells, count, value, weight):
    members, variables, levels, span, columns = dims = start.shape
    own, centre, near, model = inner(start, (diffusivity, eastward, northward))
    sides = neighbours(own, "tile")
    first, means = prepare(exchange(near))
    grid, packed = outer(dims, own, sides, model, centre, cells.shape[2])
    second = exchange(pick(variables, grid, packed, cells[0]))
    updated = analyse(first, means, second, count, value[0], weight[0])
    return restore(dims, exchange(updated))


def solution(mesh):
    return jax.shard_map(
        on_device,
        mesh=mesh,
        in_specs=(
            P("grp", None, None, "tile", None),
            P(),
            P(),
            P(),
            P("tile", None, None),
            P("tile", "grp"),
            P("tile", "grp", None),
            P("tile", "grp", None),
        ),
        out_specs=P("grp", None, None, "tile", None),
        check_vma=False,
    )
```

```python
import functools

import jax
import jax.numpy as jnp
from jax import lax
from jax.experimental import pallas as pl
from jax.experimental.pallas import tpu as pltpu
from jax.sharding import PartitionSpec as P

SPAN = 8
STEPS = 2
EDGE = SPAN // 2

ROWS = (((1,), (1,)), ((), ()))


def params(mebibytes, **kw):
    return pltpu.CompilerParams(vmem_limit_bytes=mebibytes * 2**20, **kw)


def cost(flops, size):
    return pl.CostEstimate(flops=flops, bytes_accessed=size, transcendentals=0)


def vmem(count):
    return [pl.BlockSpec(memory_space=pltpu.VMEM)] * count


def hbm(count):
    return [pl.BlockSpec(memory_space=pltpu.HBM)] * count


def smem(count):
    return [pl.BlockSpec(memory_space=pltpu.SMEM)] * count


def dot(a, b, **kw):
    return jnp.dot(a, b, preferred_element_type=jnp.float32, **kw)


def split(x):
    high = x.astype(jnp.bfloat16)
    return high, (x - high.astype(jnp.float32)).astype(jnp.bfloat16)


def dot_rows(a, b):
    return lax.dot_general(a, b, ROWS, preferred_element_type=jnp.float32)


def permutation(size, shift):
    row = lax.broadcasted_iota(jnp.int32, (size, size), 0)
    column = lax.broadcasted_iota(jnp.int32, (size, size), 1)
    return (lax.rem(row + shift + size, size) == column).astype(jnp.bfloat16)


def eye(size):
    row = lax.broadcasted_iota(jnp.int32, (size, size), 0)
    column = lax.broadcasted_iota(jnp.int32, (size, size), 1)
    return row == column


def column_of(row):
    return jnp.sum(jnp.where(eye(row.shape[1]), row, 0.0), axis=1, keepdims=True)


def row_of(column):
    return jnp.sum(jnp.where(eye(column.shape[0]), column, 0.0), axis=0, keepdims=True)


def both_ways(columns):
    pair = jnp.concatenate([permutation(columns, -1), permutation(columns, 1)], axis=1)
    return jnp.concatenate([pair, pair], axis=0)


def forecast_rows(read, first, last, coefficients, shifts):
    middle, east, west, north, south = coefficients

    def step(below, here, above, ahead, behind):
        return middle * here + east * above + west * below + north * ahead + south * behind

    rows = [read(r) for r in range(first - 2, last + 2)]
    tiles, _, columns = rows[0].shape
    flat = jnp.concatenate(rows[1:-1], axis=0).reshape(-1, columns)
    moved = dot(jnp.concatenate(split(flat), axis=1), shifts)
    ahead = moved[:, :columns].reshape(-1, 8, columns)
    behind = moved[:, columns:].reshape(-1, 8, columns)
    once, twice = [], []
    for i, r in enumerate(range(first - 1, last + 1)):
        here = slice(i * tiles, (i + 1) * tiles)
        once.append(step(*rows[i : i + 3], ahead[here], behind[here]))
        if i >= 2:
            one = once[-2]
            new = step(*once[-3:], pltpu.roll(one, columns - 1, 2), pltpu.roll(one, 1, 2))
            twice.append((r - 1, new.reshape(-1, columns).astype(jnp.bfloat16)))
    return twice


def coefficients_of(level, diff, east, north):
    spread = jnp.broadcast_to(diff[pl.ds(level, 1), :], (8, diff.shape[1]))
    u = 0.5 * east[level]
    w = 0.5 * north[level]
    return 1.0 - 4.0 * spread, spread - u, spread + u, spread - w, spread + w


def row_reader(level, var, own, low, high):
    span, columns = own.shape[2], own.shape[4]

    def read(r):
        ref, at = (low, r + span) if r < 0 else (own, r) if r < span else (high, r - span)
        return ref[var, level, at].reshape(-1, 8, columns)

    return read


def pack_rows(pairs, identity, store, first):
    lanes = pairs[0].shape[0] // 2
    packed = []
    for pair in pairs:
        turned = dot_rows(identity, pair)
        parts = [turned[:, i * lanes : (i + 1) * lanes].reshape(-1, SPAN, lanes) for i in range(2)]
        packed.append(jnp.concatenate(parts, axis=1).astype(jnp.bfloat16))
    for i, value in enumerate(packed):
        at = first + i * 2 * SPAN
        store[:, at : at + 2 * SPAN, :] = value


def inner_kernel(own, *refs):
    raw, (slabs, fields, packed, model) = refs[:3], refs[3:7]
    local, (whole, staged, in_sems, raw_sems, out_sems) = refs[7:10], refs[10:]
    members, variables, levels, span, columns = own.shape
    count = span - 2 * STEPS

    def arrive(level):
        copies = []
        for var in range(variables):
            for half in range(2):
                here = pl.ds(half * (members // 2), members // 2)
                source, place = own.at[here, var, level], whole.at[level, var, here]
                copies.append(pltpu.make_async_copy(source, place, in_sems.at[level, var, half]))
        return copies

    def leave(level):
        size = count * SPAN
        here = pl.ds(pl.multiple_of(level * size, size), size)
        return pltpu.make_async_copy(staged.at[level], packed.at[:, here], out_sems.at[level])

    copies = [pltpu.make_async_copy(x, y, raw_sems.at[i]) for i, (x, y) in enumerate(zip(raw, local))]
    for copy in copies:
        copy.start()
    for level in range(levels):
        for copy in arrive(level):
            copy.start()
    identity = permutation(columns, 0)
    shifts = both_ways(columns)
    for copy in copies:
        copy.wait()

    @pl.loop(0, levels)
    def _(level):
        coefficients = coefficients_of(level, *local)
        for i, one in enumerate(coefficients):
            model[level, i] = one
        for copy in arrive(level):
            copy.wait()
        reads, made = [], []
        for var in range(variables):
            view = whole.at[level, var].reshape(members * span, columns)

            def read(r):
                rows = view[pl.ds(r, members, stride=span), :]
                reads.append((var, r, rows))
                return rows.reshape(-1, 8, columns)

            for r, value in forecast_rows(read, STEPS, span - STEPS, coefficients, shifts):
                made.append((var, r, value))
        pairs = []
        for first in range(STEPS, span - STEPS, 2):
            rows = [one for r in (first, first + 1) for _, at, one in made if at == r]
            pairs.append(jnp.concatenate(rows, axis=0))
        pack_rows(pairs, identity, staged.at[level], 0)
        leave(level).start()
        for var, r, value in made:
            fields[level, r - STEPS, var * members : (var + 1) * members, :] = value
        for var, r, rows in reads:
            slabs[var, level, r] = rows

    for level in range(levels):
        leave(level).wait()


def inner(own, raw):
    members, variables, levels, span, columns = own.shape
    lanes = variables * members
    blocks = columns // SPAN
    count = span - 2 * STEPS
    fixed = [pltpu.with_memory_space_constraint(x, pltpu.HBM) for x in (own, *raw)]
    return pl.pallas_call(
        inner_kernel,
        out_shape=[
            jax.ShapeDtypeStruct((variables, levels, span, members, columns), jnp.float32),
            jax.ShapeDtypeStruct((levels, count, lanes, columns), jnp.bfloat16),
            jax.ShapeDtypeStruct((blocks, levels * count * SPAN, lanes), jnp.bfloat16),
            jax.ShapeDtypeStruct((levels, 5, 8, columns), jnp.float32),
        ],
        in_specs=hbm(4),
        out_specs=vmem(2) + hbm(1) + vmem(1),
        scratch_shapes=[
            pltpu.VMEM(raw[0].shape, jnp.float32),
            pltpu.SMEM(raw[1].shape, jnp.float32),
            pltpu.SMEM(raw[2].shape, jnp.float32),
            pltpu.VMEM((levels, variables, members, span, columns), jnp.float32),
            pltpu.VMEM((levels, blocks, count * SPAN, lanes), jnp.bfloat16),
            pltpu.SemaphoreType.DMA((levels, variables, 2)),
            pltpu.SemaphoreType.DMA((3,)),
            pltpu.SemaphoreType.DMA((levels,)),
        ],
        compiler_params=params(10),
        cost_estimate=cost(2 * 10**9, 4 * 2**20),
    )(*fixed)


def outer_kernel(near, own, *rest):
    sides, rest = rest[:near], rest[near:]
    model, centre, grid, packed, staged, near_tiles, sems, out_sems, near_sems = rest
    variables, levels, span, members, columns = own.shape
    rows_each = variables * members
    pairs = (2 * EDGE + span) // 2
    size = STEPS * 2 * SPAN
    identity = permutation(columns, 0)
    shifts = both_ways(columns)

    def arrive(level):
        return [
            pltpu.make_async_copy(
                side.at[:, level], near_tiles.at[i, :, level], near_sems.at[i, level]
            )
            for i, side in enumerate(sides)
        ]

    for level in range(levels):
        for copy in arrive(level):
            copy.start()

    def leave(level):
        here = pl.ds(pl.multiple_of(level * size, size), size)
        return pltpu.make_async_copy(staged.at[level], packed.at[:, here], out_sems.at[level])

    copies = []
    for r in range(STEPS, span - STEPS):
        half, pair = divmod(r + EDGE, pairs)
        place = grid.at[:, pair, pl.ds(half * rows_each, rows_each)]
        copies.append(pltpu.make_async_copy(centre.at[:, r - STEPS], place, sems.at[r - STEPS]))
        copies[-1].start()

    @pl.loop(0, levels)
    def _(level):
        for copy in arrive(level):
            copy.wait()
        coefficients = [model[level, i] for i in range(5)]
        made = []
        for var in range(variables):
            read = row_reader(level, var, own, near_tiles.at[0], near_tiles.at[near - 1])
            for first, last in ((-EDGE, STEPS), (span - STEPS, span + EDGE)):
                for r, value in forecast_rows(read, first, last, coefficients, shifts):
                    made.append((var, r, value))
        sheets = []
        for first in (0, span - STEPS):
            rows = [one for r in range(first, first + STEPS) for _, at, one in made if at == r]
            sheets.append(jnp.concatenate(rows, axis=0))
        pack_rows(sheets, identity, staged.at[level], 0)
        leave(level).start()
        for var, r, value in made:
            half, pair = divmod(r + EDGE, pairs)
            at = half * rows_each + var * members
            grid[level, pair, at : at + members, :] = value

    for level in range(levels):
        leave(level).wait()
    for copy in copies:
        copy.wait()


def outer(dims, own, sides, model, centre, slots):
    members, variables, levels, span, columns = dims
    lanes = members * variables
    blocks = columns // SPAN
    near = len(sides)
    pairs = (2 * EDGE + span) // 2
    return pl.pallas_call(
        functools.partial(outer_kernel, near),
        out_shape=[
            jax.ShapeDtypeStruct((levels, pairs, 2 * lanes, columns), jnp.bfloat16),
            jax.ShapeDtypeStruct(
                (blocks, levels * 2 * STEPS * SPAN + slots // 2, lanes), jnp.bfloat16
            ),
        ],
        in_specs=vmem(1) + hbm(near) + vmem(1) + hbm(1),
        out_specs=vmem(1) + hbm(1),
        scratch_shapes=[
            pltpu.VMEM((levels, blocks, 2 * STEPS * SPAN, lanes), jnp.bfloat16),
            pltpu.VMEM((near, *own.shape), jnp.float32),
            pltpu.SemaphoreType.DMA((span - 2 * STEPS,)),
            pltpu.SemaphoreType.DMA((levels,)),
            pltpu.SemaphoreType.DMA((near, levels)),
        ],
        compiler_params=params(16),
        cost_estimate=cost(2 * 10**9, 8 * 2**20),
    )(own, *(pltpu.with_memory_space_constraint(x, pltpu.HBM) for x in sides), model, centre)


def pick_kernel(variables, together, grid, _, cells, out, region, codes, staged, sems):
    levels, pairs, twice, columns = grid.shape
    rows = twice // 2
    members = rows // variables
    blocks, slots = cells.shape
    width = 2 * EDGE + SPAN
    part = pairs * width
    entries = levels * part
    share = out.shape[1] - slots // 2

    order = permutation(columns, -EDGE)
    batch = next(n for n in (4, 2, 1) if pairs % n == 0)
    for level in range(levels):
        for start in range(0, pairs, batch):
            made = []
            for i in range(batch):
                even = dot_rows(order, grid[level, start + i])
                odd = jnp.concatenate([even[SPAN:], even[:SPAN]], axis=0)
                made.append((even.astype(jnp.bfloat16), odd.astype(jnp.bfloat16)))
            for i, both in enumerate(made):
                at = (level * pairs + start + i) * width
                for first, value in enumerate(both):
                    for j in range(columns // width):
                        piece = value[j * width : (j + 1) * width, :]
                        region[2 * j + first, at : at + width, :] = piece

    cell = cells[...]
    second = cell >= 2 * entries
    cell = jnp.where(second, cell - 2 * entries, cell)
    level = lax.shift_right_logical(cell, (2 * part).bit_length() - 1)
    inside = cell - level * (2 * part)
    lower = inside >= part
    code = level * part + jnp.where(lower, inside - part + entries, inside)
    codes[...] = jnp.where(second, code + 2 * entries, code).astype(jnp.float32)

    left = lax.broadcasted_iota(jnp.int32, (slots // 2, rows), 1) < members
    lane = lax.broadcasted_iota(jnp.int32, (slots, entries), 1).astype(jnp.float32)

    def leave(step):
        here = pl.ds(step * together, together)
        place = out.at[here, pl.ds(share, slots // 2)]
        return pltpu.make_async_copy(staged.at[here], place, sems.at[step])

    @pl.loop(0, blocks // together)
    def _(step):
        made = []
        for i in range(together):
            block = step * together + i
            at = column_of(codes[pl.ds(block, 1), :])
            second = at >= 2.0 * entries
            at = jnp.where(second, at - 2.0 * entries, at)
            lower = at >= 1.0 * entries
            at = jnp.where(lower, at - 1.0 * entries, at)
            pick = jnp.where(lane == at, 1.0, 0.0).astype(jnp.bfloat16)
            found = dot(pick, region[block])
            total = jnp.where(lower, found[:, rows:], found[:, :rows])
            other = pltpu.roll(total, members, 1)
            to_left = jnp.where(second, other, total)[: slots // 2]
            to_right = jnp.where(second, total, other)[slots // 2 :]
            made.append(jnp.where(left, to_left, to_right).astype(jnp.bfloat16))
        for i, value in enumerate(made):
            staged[step * together + i] = value
        leave(step).start()

    for step in range(blocks // together):
        leave(step).wait()


def pick(variables, grid, packed, cells):
    levels, pairs, twice, columns = grid.shape
    blocks, slots = cells.shape
    together = next(n for n in (4, 2, 1) if blocks % n == 0)
    return pl.pallas_call(
        functools.partial(pick_kernel, variables, together),
        out_shape=jax.ShapeDtypeStruct(packed.shape, packed.dtype),
        in_specs=vmem(1) + hbm(1) + vmem(1),
        out_specs=pl.BlockSpec(memory_space=pltpu.HBM),
        scratch_shapes=[
            pltpu.VMEM((blocks, levels * pairs * (2 * EDGE + SPAN), twice), jnp.bfloat16),
            pltpu.VMEM((blocks, slots), jnp.float32),
            pltpu.VMEM((blocks, slots // 2, packed.shape[2]), jnp.bfloat16),
            pltpu.SemaphoreType.DMA((blocks // together,)),
        ],
        input_output_aliases={1: 0},
        compiler_params=params(20),
        cost_estimate=cost(4 * 10**9, 4 * 2**20),
    )(grid, packed, cells)


def join(a, b, left, members):
    return (
        jnp.where(left, a, pltpu.roll(b, members, 1)),
        jnp.where(left, pltpu.roll(a, members, 1), b),
    )


def batches(count, size):
    return [range(at, min(count, at + size)) for at in range(0, count, size)]


def left_lanes(shape):
    return lax.broadcasted_iota(jnp.int32, shape, 1) < shape[1] // 2


def deviations(states, raw, dev, at, size):
    groups, _, lanes = states.shape
    members = lanes // 2
    left = left_lanes((size, lanes))
    sums = [jnp.zeros((size, lanes), jnp.float32)] * 2
    for batch in batches(groups // 2, 4):
        made = [
            join(
                states[2 * j, :size, :].astype(jnp.float32),
                states[2 * j + 1, :size, :].astype(jnp.float32),
                left,
                members,
            )
            for j in batch
        ]
        for j, pair in zip(batch, made):
            here = slice(j * lanes, (j + 1) * lanes)
            for var in range(2):
                raw[var * size : (var + 1) * size, here] = pair[var]
            sums = [total + one for total, one in zip(sums, pair)]
    centre = jnp.concatenate([jnp.sum(x, axis=1, keepdims=True) for x in sums], axis=0)
    centre = centre * (1.0 / (groups * members))
    dev[at : at + 2 * size, :] = (raw[...] - centre).astype(jnp.bfloat16)
    return centre


def prepare_kernel(states, dev, centre, raw):
    mean = deviations(states, raw, dev, 0, states.shape[1])
    centre[...] = jnp.broadcast_to(mean, centre.shape)


def prepare(states):
    groups, near, lanes = states.shape
    total = groups * lanes // 2
    return pl.pallas_call(
        prepare_kernel,
        out_shape=[
            jax.ShapeDtypeStruct((2 * near, total), jnp.bfloat16),
            jax.ShapeDtypeStruct((2 * near, lanes), jnp.float32),
        ],
        in_specs=vmem(1),
        out_specs=vmem(2),
        scratch_shapes=[pltpu.VMEM((2 * near, total), jnp.float32)],
        compiler_params=params(6),
        cost_estimate=cost(10**8, 2 * 2**20),
    )(states)


def analyse_kernel(first, means, second, count, value, weight, out, raw, dev, obs, scaled_ref):
    groups, _, lanes = second.shape
    near = first.shape[0] // 2
    half = obs.shape[0] // 2
    far = second.shape[1] - half
    side = near + far
    slots = 2 * half
    members = lanes // 2
    total_members = groups * members
    left = left_lanes((half, lanes))

    for batch in batches(groups // 2, 4):
        made = [
            join(
                second[2 * j, far:, :].astype(jnp.float32),
                second[2 * j + 1, far:, :].astype(jnp.float32),
                left,
                members,
            )
            for j in batch
        ]
        for j, pair in zip(batch, made):
            here = slice(j * lanes, (j + 1) * lanes)
            obs[:half, here], obs[half:, here] = pair

    used = lax.broadcasted_iota(jnp.int32, (1, slots), 1) < count[0, 0]
    root = column_of(jnp.where(used, jnp.sqrt(weight[...]), 0.0))
    observed = obs[...]
    mean = jnp.sum(observed, axis=1, keepdims=True) * (1.0 / total_members)
    scaled = (observed - mean) * root
    energy = jnp.sum(jnp.sum(scaled * scaled, axis=1, keepdims=True), axis=0, keepdims=True)
    scaled_ref[...] = scaled.astype(jnp.bfloat16)
    misfit = row_of(root * (column_of(value[...]) - mean))

    c = total_members - 1.0
    s = energy * (1.0 / total_members) + c
    inverse = 1.0 / s
    a = c * inverse
    p = 1.5 - 0.5 * a
    p2 = p * p
    p3 = p2 * p
    base = 1.5 * p - 0.5 * a * p3
    q0 = -0.75 - 0.5 * (p3 - 1.5 * a * p2)
    q1 = -0.5 * (0.75 * a * p - 1.5 * p2)
    q2 = -0.5 * (0.75 * p - 0.125 * a)
    small = dot_rows(scaled_ref[...], scaled_ref[...]) * inverse
    diagonal = eye(slots)
    once = small.astype(jnp.bfloat16)
    square = dot(once, once).astype(jnp.bfloat16)
    tail = dot(square, (jnp.where(diagonal, q2, 0.0) + 0.0625 * small).astype(jnp.bfloat16))
    poly = jnp.where(diagonal, q0, 0.0) + q1 * small + tail

    def apply(vector):
        inner_part = jnp.sum(poly * vector, axis=1, keepdims=True)
        return jnp.sum(small * inner_part, axis=0, keepdims=True) + base * vector

    gain = apply(apply(misfit)) * inverse
    stretch = jnp.sqrt(a)
    alpha, factor = stretch * base, stretch * inverse
    centre = deviations(second, raw, dev, 0, far)
    cross = jnp.concatenate(
        [dot_rows(first[...], scaled_ref[...]), dot_rows(dev[...], scaled_ref[...])], axis=0
    )
    centre = jnp.concatenate([means[:, 0:1], centre], axis=0)
    shift = centre + jnp.sum(cross * gain, axis=1, keepdims=True)
    once = cross.astype(jnp.bfloat16)
    mix = sum(dot(once, part) for part in split(poly))
    mix = (mix * factor).astype(jnp.bfloat16)
    parts = ((first, 0, near, 0), (dev, 2 * near, far, near))
    for batch in batches(groups // 2, 2):
        made = []
        wide = slice(batch[0] * lanes, (batch[-1] + 1) * lanes)
        both = dot(mix, scaled_ref[:, wide]) + shift
        for j in batch:
            here = slice(j * lanes, (j + 1) * lanes)
            new = both[:, (j - batch[0]) * lanes :][:, :lanes]
            for ref, at, size, row in parts:
                one = new[at : at + 2 * size] + alpha * ref[:, here].astype(jnp.float32)
                pair = join(one[:size], one[size:], left_lanes((size, lanes)), members)
                made += [(2 * j + i, row, x.astype(jnp.bfloat16)) for i, x in enumerate(pair)]
        for group, row, value in made:
            out[group, row : row + value.shape[0], :] = value


def analyse(first, means, second, count, value, weight):
    groups, _, lanes = second.shape
    near = first.shape[0] // 2
    slots = value.shape[1]
    far = second.shape[1] - slots // 2
    total = groups * lanes // 2
    return pl.pallas_call(
        analyse_kernel,
        out_shape=jax.ShapeDtypeStruct((groups, near + far, lanes), jnp.bfloat16),
        in_specs=vmem(3) + smem(1) + vmem(2),
        out_specs=pl.BlockSpec(memory_space=pltpu.VMEM),
        scratch_shapes=[
            pltpu.VMEM((2 * far, total), jnp.float32),
            pltpu.VMEM((2 * far, total), jnp.bfloat16),
            pltpu.VMEM((slots, total), jnp.float32),
            pltpu.VMEM((slots, total), jnp.bfloat16),
        ],
        compiler_params=params(16),
        cost_estimate=cost(4 * 10**9, 4 * 2**20),
    )(first, means, second, count, value, weight)


def restore_kernel(blocks, out, turned, staged, sems):
    members, variables, levels, span, columns = out.shape
    lanes = members * variables
    identity = permutation(lanes, 0)
    near = span - 2 * STEPS
    for level in range(levels):
        made = []
        for r in range(0, span, 2):
            if STEPS <= r < span - STEPS:
                at = level * near + r - STEPS
            else:
                at = levels * near + level * 2 * STEPS + (r if r < STEPS else r - near)
            both = blocks[:, at * SPAN : (at + 2) * SPAN, :].astype(jnp.float32)
            pair = [both[:, i * SPAN : (i + 1) * SPAN, :].reshape(columns, lanes) for i in range(2)]
            rows = dot_rows(identity, jnp.concatenate(pair, axis=0).astype(jnp.bfloat16))
            made += [(r + i, rows[:, i * columns : (i + 1) * columns]) for i in range(2)]
        for r, rows in made:
            turned[level, pl.ds(r, lanes, stride=span), :] = rows

    chunks = staged.shape[0]
    size = members // chunks
    copies = []
    for i in range(chunks):
        for level in range(levels):
            for var in range(variables):
                at = (var * members + i * size) * span
                part = turned[level, at : at + size * span, :].reshape(size, span, columns)
                staged[i, :, var, level] = part.astype(jnp.bfloat16)
        place = out.at[pl.ds(i * size, size)]
        copies.append(pltpu.make_async_copy(staged.at[i], place, sems.at[i]))
        copies[-1].start()
    for copy in copies:
        copy.wait()


def restore(dims, blocks):
    members, variables, levels, span, columns = dims
    chunks = next(n for n in (4, 2, 1) if members % n == 0)
    return pl.pallas_call(
        restore_kernel,
        out_shape=jax.ShapeDtypeStruct((members, variables, levels, span, columns), jnp.bfloat16),
        in_specs=vmem(1),
        out_specs=pl.BlockSpec(memory_space=pltpu.HBM),
        scratch_shapes=[
            pltpu.VMEM((levels, variables * members * span, columns), jnp.float32),
            pltpu.VMEM((chunks, members // chunks, variables, levels, span, columns), jnp.bfloat16),
            pltpu.SemaphoreType.DMA((chunks,)),
        ],
        compiler_params=params(10),
        cost_estimate=cost(2 * 10**9, 2 * 2**20),
    )(blocks)


def neighbours(field, axis):
    count = lax.axis_size(axis)
    low = lax.ppermute(field, axis, [(i, (i + 1) % count) for i in range(count)])
    if count == 2:
        return (low,)
    return low, lax.ppermute(field, axis, [((i + 1) % count, i) for i in range(count)])


def exchange(blocks):
    return lax.all_to_all(blocks, "grp", split_axis=0, concat_axis=0, tiled=True)


def on_device(start, diffusivity, eastward, northward, cells, count, value, weight):
    members, variables, levels, span, columns = dims = start.shape
    own, centre, near, model = inner(start, (diffusivity, eastward, northward))
    sides = neighbours(own, "tile")
    first, means = prepare(exchange(near))
    grid, packed = outer(dims, own, sides, model, centre, cells.shape[2])
    second = exchange(pick(variables, grid, packed, cells[0]))
    updated = analyse(first, means, second, count, value[0], weight[0])
    return restore(dims, exchange(updated))


def solution(mesh):
    return jax.shard_map(
        on_device,
        mesh=mesh,
        in_specs=(
            P("grp", None, None, "tile", None),
            P(),
            P(),
            P(),
            P("tile", None, None),
            P("tile", "grp"),
            P("tile", "grp", None),
            P("tile", "grp", None),
        ),
        out_specs=P("grp", None, None, "tile", None),
        check_vma=False,
    )
```

```python
import functools

import jax
import jax.numpy as jnp
from jax import lax
from jax.experimental import pallas as pl
from jax.experimental.pallas import tpu as pltpu
from jax.sharding import PartitionSpec as P

SPAN = 8
STEPS = 2
EDGE = SPAN // 2

ROWS = (((1,), (1,)), ((), ()))


def params(mebibytes, **kw):
    return pltpu.CompilerParams(vmem_limit_bytes=mebibytes * 2**20, **kw)


def cost(flops, size):
    return pl.CostEstimate(flops=flops, bytes_accessed=size, transcendentals=0)


def vmem(count):
    return [pl.BlockSpec(memory_space=pltpu.VMEM)] * count


def hbm(count):
    return [pl.BlockSpec(memory_space=pltpu.HBM)] * count


def smem(count):
    return [pl.BlockSpec(memory_space=pltpu.SMEM)] * count


def dot(a, b, **kw):
    return jnp.dot(a, b, preferred_element_type=jnp.float32, **kw)


def split(x):
    high = x.astype(jnp.bfloat16)
    return high, (x - high.astype(jnp.float32)).astype(jnp.bfloat16)


def dot_rows(a, b):
    return lax.dot_general(a, b, ROWS, preferred_element_type=jnp.float32)


def permutation(size, shift):
    row = lax.broadcasted_iota(jnp.int32, (size, size), 0)
    column = lax.broadcasted_iota(jnp.int32, (size, size), 1)
    return (lax.rem(row + shift + size, size) == column).astype(jnp.bfloat16)


def eye(size):
    row = lax.broadcasted_iota(jnp.int32, (size, size), 0)
    column = lax.broadcasted_iota(jnp.int32, (size, size), 1)
    return row == column


def column_of(row):
    return jnp.sum(jnp.where(eye(row.shape[1]), row, 0.0), axis=1, keepdims=True)


def row_of(column):
    return jnp.sum(jnp.where(eye(column.shape[0]), column, 0.0), axis=0, keepdims=True)


def both_ways(columns):
    pair = jnp.concatenate([permutation(columns, -1), permutation(columns, 1)], axis=1)
    return jnp.concatenate([pair, pair], axis=0)


def forecast_rows(read, first, last, coefficients, shifts):
    middle, east, west, north, south = coefficients

    def step(below, here, above, ahead, behind):
        return middle * here + east * above + west * below + north * ahead + south * behind

    rows = [read(r) for r in range(first - 2, last + 2)]
    tiles, _, columns = rows[0].shape
    flat = jnp.concatenate(rows[1:-1], axis=0).reshape(-1, columns)
    moved = dot(jnp.concatenate(split(flat), axis=1), shifts)
    ahead = moved[:, :columns].reshape(-1, 8, columns)
    behind = moved[:, columns:].reshape(-1, 8, columns)
    once, twice = [], []
    for i, r in enumerate(range(first - 1, last + 1)):
        here = slice(i * tiles, (i + 1) * tiles)
        once.append(step(*rows[i : i + 3], ahead[here], behind[here]))
        if i >= 2:
            one = once[-2]
            new = step(*once[-3:], pltpu.roll(one, columns - 1, 2), pltpu.roll(one, 1, 2))
            twice.append((r - 1, new.reshape(-1, columns).astype(jnp.bfloat16)))
    return twice


def coefficients_of(level, diff, east, north):
    spread = jnp.broadcast_to(diff[pl.ds(level, 1), :], (8, diff.shape[1]))
    u = 0.5 * east[level]
    w = 0.5 * north[level]
    return 1.0 - 4.0 * spread, spread - u, spread + u, spread - w, spread + w


def row_reader(level, var, own, low, high):
    span, columns = own.shape[2], own.shape[4]

    def read(r):
        ref, at = (low, r + span) if r < 0 else (own, r) if r < span else (high, r - span)
        return ref[var, level, at].reshape(-1, 8, columns)

    return read


def pack_rows(pairs, identity, store, first):
    lanes = pairs[0].shape[0] // 2
    packed = []
    for pair in pairs:
        turned = dot_rows(identity, pair)
        parts = [turned[:, i * lanes : (i + 1) * lanes].reshape(-1, SPAN, lanes) for i in range(2)]
        packed.append(jnp.concatenate(parts, axis=1).astype(jnp.bfloat16))
    for i, value in enumerate(packed):
        at = first + i * 2 * SPAN
        store[:, at : at + 2 * SPAN, :] = value


def inner_kernel(own, *refs):
    raw, (slabs, fields, packed, model) = refs[:3], refs[3:7]
    local, (whole, staged, in_sems, raw_sems, out_sems) = refs[7:10], refs[10:]
    members, variables, levels, span, columns = own.shape
    count = span - 2 * STEPS

    def arrive(level):
        return [
            pltpu.make_async_copy(own.at[:, var, level], whole.at[level, var], in_sems.at[level, var])
            for var in range(variables)
        ]

    def leave(level):
        size = count * SPAN
        here = pl.ds(pl.multiple_of(level * size, size), size)
        return pltpu.make_async_copy(staged.at[level], packed.at[:, here], out_sems.at[level])

    copies = [pltpu.make_async_copy(x, y, raw_sems.at[i]) for i, (x, y) in enumerate(zip(raw, local))]
    for copy in copies:
        copy.start()
    for level in range(min(2, levels)):
        for copy in arrive(level):
            copy.start()
    identity = permutation(columns, 0)
    shifts = both_ways(columns)
    for copy in copies:
        copy.wait()

    @pl.loop(0, levels)
    def _(level):
        coefficients = coefficients_of(level, *local)
        for i, one in enumerate(coefficients):
            model[level, i] = one
        for copy in arrive(level):
            copy.wait()

        @pl.when(level + 2 < levels)
        def _():
            for copy in arrive(level + 2):
                copy.start()

        reads, made = [], []
        for var in range(variables):
            view = whole.at[level, var].reshape(members * span, columns)

            def read(r):
                rows = view[pl.ds(r, members, stride=span), :]
                reads.append((var, r, rows))
                return rows.reshape(-1, 8, columns)

            for r, value in forecast_rows(read, STEPS, span - STEPS, coefficients, shifts):
                made.append((var, r, value))
        pairs = []
        for first in range(STEPS, span - STEPS, 2):
            rows = [one for r in (first, first + 1) for _, at, one in made if at == r]
            pairs.append(jnp.concatenate(rows, axis=0))
        pack_rows(pairs, identity, staged.at[level], 0)
        leave(level).start()
        for var, r, value in made:
            fields[level, r - STEPS, var * members : (var + 1) * members, :] = value
        for var, r, rows in reads:
            slabs[var, level, r] = rows

    for level in range(levels):
        leave(level).wait()


def inner(own, raw):
    members, variables, levels, span, columns = own.shape
    lanes = variables * members
    blocks = columns // SPAN
    count = span - 2 * STEPS
    fixed = [pltpu.with_memory_space_constraint(x, pltpu.HBM) for x in (own, *raw)]
    return pl.pallas_call(
        inner_kernel,
        out_shape=[
            jax.ShapeDtypeStruct((variables, levels, span, members, columns), jnp.float32),
            jax.ShapeDtypeStruct((levels, count, lanes, columns), jnp.bfloat16),
            jax.ShapeDtypeStruct((blocks, levels * count * SPAN, lanes), jnp.bfloat16),
            jax.ShapeDtypeStruct((levels, 5, 8, columns), jnp.float32),
        ],
        in_specs=hbm(4),
        out_specs=vmem(2) + hbm(1) + vmem(1),
        scratch_shapes=[
            pltpu.VMEM(raw[0].shape, jnp.float32),
            pltpu.SMEM(raw[1].shape, jnp.float32),
            pltpu.SMEM(raw[2].shape, jnp.float32),
            pltpu.VMEM((levels, variables, members, span, columns), jnp.float32),
            pltpu.VMEM((levels, blocks, count * SPAN, lanes), jnp.bfloat16),
            pltpu.SemaphoreType.DMA((levels, variables)),
            pltpu.SemaphoreType.DMA((3,)),
            pltpu.SemaphoreType.DMA((levels,)),
        ],
        compiler_params=params(10),
        cost_estimate=cost(2 * 10**9, 4 * 2**20),
    )(*fixed)


def outer_kernel(near, own, *rest):
    sides, rest = rest[:near], rest[near:]
    model, centre, grid, packed, staged, near_tiles, sems, out_sems, near_sems = rest
    variables, levels, span, members, columns = own.shape
    rows_each = variables * members
    pairs = (2 * EDGE + span) // 2
    size = STEPS * 2 * SPAN
    identity = permutation(columns, 0)
    shifts = both_ways(columns)

    def arrive(level):
        return [
            pltpu.make_async_copy(
                side.at[:, level], near_tiles.at[i, :, level], near_sems.at[i, level]
            )
            for i, side in enumerate(sides)
        ]

    for level in range(levels):
        for copy in arrive(level):
            copy.start()

    def leave(level):
        here = pl.ds(pl.multiple_of(level * size, size), size)
        return pltpu.make_async_copy(staged.at[level], packed.at[:, here], out_sems.at[level])

    copies = []
    for r in range(STEPS, span - STEPS):
        half, pair = divmod(r + EDGE, pairs)
        place = grid.at[:, pair, pl.ds(half * rows_each, rows_each)]
        copies.append(pltpu.make_async_copy(centre.at[:, r - STEPS], place, sems.at[r - STEPS]))
        copies[-1].start()

    @pl.loop(0, levels)
    def _(level):
        for copy in arrive(level):
            copy.wait()
        coefficients = [model[level, i] for i in range(5)]
        made = []
        for var in range(variables):
            read = row_reader(level, var, own, near_tiles.at[0], near_tiles.at[near - 1])
            for first, last in ((-EDGE, STEPS), (span - STEPS, span + EDGE)):
                for r, value in forecast_rows(read, first, last, coefficients, shifts):
                    made.append((var, r, value))
        sheets = []
        for first in (0, span - STEPS):
            rows = [one for r in range(first, first + STEPS) for _, at, one in made if at == r]
            sheets.append(jnp.concatenate(rows, axis=0))
        pack_rows(sheets, identity, staged.at[level], 0)
        leave(level).start()
        for var, r, value in made:
            half, pair = divmod(r + EDGE, pairs)
            at = half * rows_each + var * members
            grid[level, pair, at : at + members, :] = value

    for level in range(levels):
        leave(level).wait()
    for copy in copies:
        copy.wait()


def outer(dims, own, sides, model, centre, slots):
    members, variables, levels, span, columns = dims
    lanes = members * variables
    blocks = columns // SPAN
    near = len(sides)
    pairs = (2 * EDGE + span) // 2
    return pl.pallas_call(
        functools.partial(outer_kernel, near),
        out_shape=[
            jax.ShapeDtypeStruct((levels, pairs, 2 * lanes, columns), jnp.bfloat16),
            jax.ShapeDtypeStruct(
                (blocks, levels * 2 * STEPS * SPAN + slots // 2, lanes), jnp.bfloat16
            ),
        ],
        in_specs=vmem(1) + hbm(near) + vmem(1) + hbm(1),
        out_specs=vmem(1) + hbm(1),
        scratch_shapes=[
            pltpu.VMEM((levels, blocks, 2 * STEPS * SPAN, lanes), jnp.bfloat16),
            pltpu.VMEM((near, *own.shape), jnp.float32),
            pltpu.SemaphoreType.DMA((span - 2 * STEPS,)),
            pltpu.SemaphoreType.DMA((levels,)),
            pltpu.SemaphoreType.DMA((near, levels)),
        ],
        compiler_params=params(16),
        cost_estimate=cost(2 * 10**9, 8 * 2**20),
    )(own, *(pltpu.with_memory_space_constraint(x, pltpu.HBM) for x in sides), model, centre)


def pick_kernel(variables, together, grid, _, cells, out, region, codes, staged, sems):
    levels, pairs, twice, columns = grid.shape
    rows = twice // 2
    members = rows // variables
    blocks, slots = cells.shape
    width = 2 * EDGE + SPAN
    part = pairs * width
    entries = levels * part
    share = out.shape[1] - slots // 2

    order = permutation(columns, -EDGE)
    batch = next(n for n in (4, 2, 1) if pairs % n == 0)
    for level in range(levels):
        for start in range(0, pairs, batch):
            made = []
            for i in range(batch):
                even = dot_rows(order, grid[level, start + i])
                odd = jnp.concatenate([even[SPAN:], even[:SPAN]], axis=0)
                made.append((even.astype(jnp.bfloat16), odd.astype(jnp.bfloat16)))
            for i, both in enumerate(made):
                at = (level * pairs + start + i) * width
                for first, value in enumerate(both):
                    for j in range(columns // width):
                        piece = value[j * width : (j + 1) * width, :]
                        region[2 * j + first, at : at + width, :] = piece

    cell = cells[...]
    second = cell >= 2 * entries
    cell = jnp.where(second, cell - 2 * entries, cell)
    level = lax.shift_right_logical(cell, (2 * part).bit_length() - 1)
    inside = cell - level * (2 * part)
    lower = inside >= part
    code = level * part + jnp.where(lower, inside - part + entries, inside)
    codes[...] = jnp.where(second, code + 2 * entries, code).astype(jnp.float32)

    left = lax.broadcasted_iota(jnp.int32, (slots // 2, rows), 1) < members
    lane = lax.broadcasted_iota(jnp.int32, (slots, entries), 1).astype(jnp.float32)

    def leave(step):
        here = pl.ds(step * together, together)
        place = out.at[here, pl.ds(share, slots // 2)]
        return pltpu.make_async_copy(staged.at[here], place, sems.at[step])

    @pl.loop(0, blocks // together)
    def _(step):
        made = []
        for i in range(together):
            block = step * together + i
            at = column_of(codes[pl.ds(block, 1), :])
            second = at >= 2.0 * entries
            at = jnp.where(second, at - 2.0 * entries, at)
            lower = at >= 1.0 * entries
            at = jnp.where(lower, at - 1.0 * entries, at)
            pick = jnp.where(lane == at, 1.0, 0.0).astype(jnp.bfloat16)
            found = dot(pick, region[block])
            total = jnp.where(lower, found[:, rows:], found[:, :rows])
            other = pltpu.roll(total, members, 1)
            to_left = jnp.where(second, other, total)[: slots // 2]
            to_right = jnp.where(second, total, other)[slots // 2 :]
            made.append(jnp.where(left, to_left, to_right).astype(jnp.bfloat16))
        for i, value in enumerate(made):
            staged[step * together + i] = value
        leave(step).start()

    for step in range(blocks // together):
        leave(step).wait()


def pick(variables, grid, packed, cells):
    levels, pairs, twice, columns = grid.shape
    blocks, slots = cells.shape
    together = next(n for n in (4, 2, 1) if blocks % n == 0)
    return pl.pallas_call(
        functools.partial(pick_kernel, variables, together),
        out_shape=jax.ShapeDtypeStruct(packed.shape, packed.dtype),
        in_specs=vmem(1) + hbm(1) + vmem(1),
        out_specs=pl.BlockSpec(memory_space=pltpu.HBM),
        scratch_shapes=[
            pltpu.VMEM((blocks, levels * pairs * (2 * EDGE + SPAN), twice), jnp.bfloat16),
            pltpu.VMEM((blocks, slots), jnp.float32),
            pltpu.VMEM((blocks, slots // 2, packed.shape[2]), jnp.bfloat16),
            pltpu.SemaphoreType.DMA((blocks // together,)),
        ],
        input_output_aliases={1: 0},
        compiler_params=params(20),
        cost_estimate=cost(4 * 10**9, 4 * 2**20),
    )(grid, packed, cells)


def join(a, b, members):
    return (
        jnp.concatenate([a[:, :members], b[:, :members]], axis=1),
        jnp.concatenate([a[:, members:], b[:, members:]], axis=1),
    )


def batches(count, size):
    return [range(at, min(count, at + size)) for at in range(0, count, size)]


def deviations(states, raw, dev, at, size):
    groups, _, lanes = states.shape
    members = lanes // 2
    sums = [jnp.zeros((size, lanes), jnp.float32)] * 2
    for batch in batches(groups // 2, 4):
        made = [
            [
                x.astype(jnp.float32)
                for x in join(states[2 * j, :size, :], states[2 * j + 1, :size, :], members)
            ]
            for j in batch
        ]
        for j, pair in zip(batch, made):
            here = slice(j * lanes, (j + 1) * lanes)
            for var in range(2):
                raw[var * size : (var + 1) * size, here] = pair[var]
            sums = [total + one for total, one in zip(sums, pair)]
    centre = jnp.concatenate([jnp.sum(x, axis=1, keepdims=True) for x in sums], axis=0)
    centre = centre * (1.0 / (groups * members))
    dev[at : at + 2 * size, :] = (raw[...] - centre).astype(jnp.bfloat16)
    return centre


def prepare_kernel(states, dev, centre, raw):
    mean = deviations(states, raw, dev, 0, states.shape[1])
    centre[...] = jnp.broadcast_to(mean, centre.shape)


def prepare(states):
    groups, near, lanes = states.shape
    total = groups * lanes // 2
    return pl.pallas_call(
        prepare_kernel,
        out_shape=[
            jax.ShapeDtypeStruct((2 * near, total), jnp.bfloat16),
            jax.ShapeDtypeStruct((2 * near, lanes), jnp.float32),
        ],
        in_specs=vmem(1),
        out_specs=vmem(2),
        scratch_shapes=[pltpu.VMEM((2 * near, total), jnp.float32)],
        compiler_params=params(6),
        cost_estimate=cost(10**8, 2 * 2**20),
    )(states)


def analyse_kernel(first, means, second, count, value, weight, out, raw, dev, obs, scaled_ref):
    groups, _, lanes = second.shape
    near = first.shape[0] // 2
    half = obs.shape[0] // 2
    far = second.shape[1] - half
    side = near + far
    slots = 2 * half
    members = lanes // 2
    total_members = groups * members

    for batch in batches(groups // 2, 4):
        made = [
            [
                x.astype(jnp.float32)
                for x in join(second[2 * j, far:, :], second[2 * j + 1, far:, :], members)
            ]
            for j in batch
        ]
        for j, pair in zip(batch, made):
            here = slice(j * lanes, (j + 1) * lanes)
            obs[:half, here], obs[half:, here] = pair

    used = lax.broadcasted_iota(jnp.int32, (1, slots), 1) < count[0, 0]
    root = column_of(jnp.where(used, jnp.sqrt(weight[...]), 0.0))
    observed = obs[...]
    mean = jnp.sum(observed, axis=1, keepdims=True) * (1.0 / total_members)
    scaled = (observed - mean) * root
    energy = jnp.sum(jnp.sum(scaled * scaled, axis=1, keepdims=True), axis=0, keepdims=True)
    scaled_ref[...] = scaled.astype(jnp.bfloat16)
    misfit = row_of(root * (column_of(value[...]) - mean))

    c = total_members - 1.0
    s = energy * (1.0 / total_members) + c
    inverse = 1.0 / s
    a = c * inverse
    p = 1.5 - 0.5 * a
    p2 = p * p
    p3 = p2 * p
    base = 1.5 * p - 0.5 * a * p3
    q0 = -0.75 - 0.5 * (p3 - 1.5 * a * p2)
    q1 = -0.5 * (0.75 * a * p - 1.5 * p2)
    q2 = -0.5 * (0.75 * p - 0.125 * a)
    small = dot_rows(scaled_ref[...], scaled_ref[...]) * inverse
    diagonal = eye(slots)
    once = small.astype(jnp.bfloat16)
    square = dot(once, once).astype(jnp.bfloat16)
    tail = dot(square, (jnp.where(diagonal, q2, 0.0) + 0.0625 * small).astype(jnp.bfloat16))
    poly = jnp.where(diagonal, q0, 0.0) + q1 * small + tail

    def apply(vector):
        inner_part = jnp.sum(poly * vector, axis=1, keepdims=True)
        return jnp.sum(small * inner_part, axis=0, keepdims=True) + base * vector

    gain = apply(apply(misfit)) * inverse
    stretch = jnp.sqrt(a)
    alpha, factor = stretch * base, stretch * inverse
    centre = deviations(second, raw, dev, 0, far)
    cross = jnp.concatenate(
        [dot_rows(first[...], scaled_ref[...]), dot_rows(dev[...], scaled_ref[...])], axis=0
    )
    centre = jnp.concatenate([means[:, 0:1], centre], axis=0)
    shift = centre + jnp.sum(cross * gain, axis=1, keepdims=True)
    once = cross.astype(jnp.bfloat16)
    mix = sum(dot(once, part) for part in split(poly))
    mix = (mix * factor).astype(jnp.bfloat16)
    parts = ((first, 0, near, 0), (dev, 2 * near, far, near))
    for batch in batches(groups // 2, 2):
        made = []
        wide = slice(batch[0] * lanes, (batch[-1] + 1) * lanes)
        both = dot(mix, scaled_ref[:, wide]) + shift
        for j in batch:
            here = slice(j * lanes, (j + 1) * lanes)
            new = both[:, (j - batch[0]) * lanes :][:, :lanes]
            for ref, at, size, row in parts:
                one = new[at : at + 2 * size] + alpha * ref[:, here].astype(jnp.float32)
                one = one.astype(jnp.bfloat16)
                pair = join(one[:size], one[size:], members)
                made += [(2 * j + i, row, x) for i, x in enumerate(pair)]
        for group, row, value in made:
            out[group, row : row + value.shape[0], :] = value


def analyse(first, means, second, count, value, weight):
    groups, _, lanes = second.shape
    near = first.shape[0] // 2
    slots = value.shape[1]
    far = second.shape[1] - slots // 2
    total = groups * lanes // 2
    return pl.pallas_call(
        analyse_kernel,
        out_shape=jax.ShapeDtypeStruct((groups, near + far, lanes), jnp.bfloat16),
        in_specs=vmem(3) + smem(1) + vmem(2),
        out_specs=pl.BlockSpec(memory_space=pltpu.VMEM),
        scratch_shapes=[
            pltpu.VMEM((2 * far, total), jnp.float32),
            pltpu.VMEM((2 * far, total), jnp.bfloat16),
            pltpu.VMEM((slots, total), jnp.float32),
            pltpu.VMEM((slots, total), jnp.bfloat16),
        ],
        compiler_params=params(16),
        cost_estimate=cost(4 * 10**9, 4 * 2**20),
    )(first, means, second, count, value, weight)


def restore_kernel(blocks, out, turned, staged, sems):
    members, variables, levels, span, columns = out.shape
    lanes = members * variables
    identity = permutation(lanes, 0)
    near = span - 2 * STEPS
    for level in range(levels):
        made = []
        for r in range(0, span, 2):
            if STEPS <= r < span - STEPS:
                at = level * near + r - STEPS
            else:
                at = levels * near + level * 2 * STEPS + (r if r < STEPS else r - near)
            both = blocks[:, at * SPAN : (at + 2) * SPAN, :].astype(jnp.float32)
            pair = [both[:, i * SPAN : (i + 1) * SPAN, :].reshape(columns, lanes) for i in range(2)]
            rows = dot_rows(identity, jnp.concatenate(pair, axis=0).astype(jnp.bfloat16))
            made += [(r + i, rows[:, i * columns : (i + 1) * columns]) for i in range(2)]
        for r, rows in made:
            turned[level, pl.ds(r, lanes, stride=span), :] = rows

    chunks = staged.shape[0]
    size = members // chunks
    copies = []
    for i in range(chunks):
        for level in range(levels):
            for var in range(variables):
                at = (var * members + i * size) * span
                part = turned[level, at : at + size * span, :].reshape(size, span, columns)
                staged[i, :, var, level] = part.astype(jnp.bfloat16)
        place = out.at[pl.ds(i * size, size)]
        copies.append(pltpu.make_async_copy(staged.at[i], place, sems.at[i]))
        copies[-1].start()
    for copy in copies:
        copy.wait()


def restore(dims, blocks):
    members, variables, levels, span, columns = dims
    chunks = next(n for n in (4, 2, 1) if members % n == 0)
    return pl.pallas_call(
        restore_kernel,
        out_shape=jax.ShapeDtypeStruct((members, variables, levels, span, columns), jnp.bfloat16),
        in_specs=vmem(1),
        out_specs=pl.BlockSpec(memory_space=pltpu.HBM),
        scratch_shapes=[
            pltpu.VMEM((levels, variables * members * span, columns), jnp.float32),
            pltpu.VMEM((chunks, members // chunks, variables, levels, span, columns), jnp.bfloat16),
            pltpu.SemaphoreType.DMA((chunks,)),
        ],
        compiler_params=params(10),
        cost_estimate=cost(2 * 10**9, 2 * 2**20),
    )(blocks)


def neighbours(field, axis):
    count = lax.axis_size(axis)
    low = lax.ppermute(field, axis, [(i, (i + 1) % count) for i in range(count)])
    if count == 2:
        return (low,)
    return low, lax.ppermute(field, axis, [((i + 1) % count, i) for i in range(count)])


def exchange(blocks):
    return lax.all_to_all(blocks, "grp", split_axis=0, concat_axis=0, tiled=True)


def on_device(start, diffusivity, eastward, northward, cells, count, value, weight):
    members, variables, levels, span, columns = dims = start.shape
    own, centre, near, model = inner(start, (diffusivity, eastward, northward))
    sides = neighbours(own, "tile")
    first, means = prepare(exchange(near))
    grid, packed = outer(dims, own, sides, model, centre, cells.shape[2])
    second = exchange(pick(variables, grid, packed, cells[0]))
    updated = analyse(first, means, second, count, value[0], weight[0])
    return restore(dims, exchange(updated))


def solution(mesh):
    return jax.shard_map(
        on_device,
        mesh=mesh,
        in_specs=(
            P("grp", None, None, "tile", None),
            P(),
            P(),
            P(),
            P("tile", None, None),
            P("tile", "grp"),
            P("tile", "grp", None),
            P("tile", "grp", None),
        ),
        out_specs=P("grp", None, None, "tile", None),
        check_vma=False,
    )
```

```python
import functools

import jax
import jax.numpy as jnp
from jax import lax
from jax.experimental import pallas as pl
from jax.experimental.pallas import tpu as pltpu
from jax.sharding import PartitionSpec as P

SPAN = 8
STEPS = 2
EDGE = SPAN // 2

ROWS = (((1,), (1,)), ((), ()))


def params(mebibytes, **kw):
    return pltpu.CompilerParams(vmem_limit_bytes=mebibytes * 2**20, **kw)


def cost(flops, size):
    return pl.CostEstimate(flops=flops, bytes_accessed=size, transcendentals=0)


def vmem(count):
    return [pl.BlockSpec(memory_space=pltpu.VMEM)] * count


def hbm(count):
    return [pl.BlockSpec(memory_space=pltpu.HBM)] * count


def smem(count):
    return [pl.BlockSpec(memory_space=pltpu.SMEM)] * count


def dot(a, b, **kw):
    return jnp.dot(a, b, preferred_element_type=jnp.float32, **kw)


def split(x):
    high = x.astype(jnp.bfloat16)
    return high, (x - high.astype(jnp.float32)).astype(jnp.bfloat16)


def dot_rows(a, b):
    return lax.dot_general(a, b, ROWS, preferred_element_type=jnp.float32)


def permutation(size, shift):
    row = lax.broadcasted_iota(jnp.int32, (size, size), 0)
    column = lax.broadcasted_iota(jnp.int32, (size, size), 1)
    return (lax.rem(row + shift + size, size) == column).astype(jnp.bfloat16)


def eye(size):
    row = lax.broadcasted_iota(jnp.int32, (size, size), 0)
    column = lax.broadcasted_iota(jnp.int32, (size, size), 1)
    return row == column


def column_of(row):
    return jnp.sum(jnp.where(eye(row.shape[1]), row, 0.0), axis=1, keepdims=True)


def row_of(column):
    return jnp.sum(jnp.where(eye(column.shape[0]), column, 0.0), axis=0, keepdims=True)


def both_ways(columns):
    pair = jnp.concatenate([permutation(columns, -1), permutation(columns, 1)], axis=1)
    return jnp.concatenate([pair, pair], axis=0)


def forecast_rows(read, first, last, coefficients, shifts):
    middle, east, west, north, south = coefficients

    def step(below, here, above, ahead, behind):
        return middle * here + east * above + west * below + north * ahead + south * behind

    rows = [read(r) for r in range(first - 2, last + 2)]
    tiles, _, columns = rows[0].shape
    flat = jnp.concatenate(rows[1:-1], axis=0).reshape(-1, columns)
    moved = dot(jnp.concatenate(split(flat), axis=1), shifts)
    ahead = moved[:, :columns].reshape(-1, 8, columns)
    behind = moved[:, columns:].reshape(-1, 8, columns)
    once, twice = [], []
    for i, r in enumerate(range(first - 1, last + 1)):
        here = slice(i * tiles, (i + 1) * tiles)
        once.append(step(*rows[i : i + 3], ahead[here], behind[here]))
        if i >= 2:
            one = once[-2]
            new = step(*once[-3:], pltpu.roll(one, columns - 1, 2), pltpu.roll(one, 1, 2))
            twice.append((r - 1, new.reshape(-1, columns).astype(jnp.bfloat16)))
    return twice


def coefficients_of(level, diff, east, north):
    spread = jnp.broadcast_to(diff[pl.ds(level, 1), :], (8, diff.shape[1]))
    u = 0.5 * east[level]
    w = 0.5 * north[level]
    return 1.0 - 4.0 * spread, spread - u, spread + u, spread - w, spread + w


def row_reader(level, var, own, low, high):
    span, columns = own.shape[2], own.shape[4]

    def read(r):
        ref, at = (low, r + span) if r < 0 else (own, r) if r < span else (high, r - span)
        return ref[var, level, at].reshape(-1, 8, columns)

    return read


def pack_rows(pairs, identity, store, first):
    lanes = pairs[0].shape[0] // 2
    packed = []
    for pair in pairs:
        turned = dot_rows(identity, pair)
        parts = [turned[:, i * lanes : (i + 1) * lanes].reshape(-1, SPAN, lanes) for i in range(2)]
        packed.append(jnp.concatenate(parts, axis=1).astype(jnp.bfloat16))
    for i, value in enumerate(packed):
        at = first + i * 2 * SPAN
        store[:, at : at + 2 * SPAN, :] = value


def inner_kernel(own, *refs):
    raw, (slabs, fields, packed, model) = refs[:3], refs[3:7]
    local, (whole, staged, in_sems, raw_sems, out_sems) = refs[7:10], refs[10:]
    members, variables, levels, span, columns = own.shape
    count = span - 2 * STEPS

    def arrive(level):
        return [
            pltpu.make_async_copy(own.at[:, var, level], whole.at[level, var], in_sems.at[level, var])
            for var in range(variables)
        ]

    def leave(level):
        size = count * SPAN
        here = pl.ds(pl.multiple_of(level * size, size), size)
        return pltpu.make_async_copy(staged.at[level], packed.at[:, here], out_sems.at[level])

    copies = [pltpu.make_async_copy(x, y, raw_sems.at[i]) for i, (x, y) in enumerate(zip(raw, local))]
    for copy in copies:
        copy.start()
    for level in range(min(2, levels)):
        for copy in arrive(level):
            copy.start()
    identity = permutation(columns, 0)
    shifts = both_ways(columns)
    for copy in copies:
        copy.wait()

    def pack(level):
        pairs = [
            fields[level, r : r + 2].reshape(2 * variables * members, columns)
            for r in range(0, count, 2)
        ]
        pack_rows(pairs, identity, staged.at[level], 0)

    def advance(level):
        coefficients = coefficients_of(level, *local)
        reads, made = [], []
        for var in range(variables):
            view = whole.at[level, var].reshape(members * span, columns)

            def read(r):
                rows = view[pl.ds(r, members, stride=span), :]
                reads.append((var, r, rows))
                return rows.reshape(-1, 8, columns)

            for r, value in forecast_rows(read, STEPS, span - STEPS, coefficients, shifts):
                made.append((var, r, value))

        def store():
            for i, one in enumerate(coefficients):
                model[level, i] = one
            for var, r, value in made:
                fields[level, r - STEPS, var * members : (var + 1) * members, :] = value
            for var, r, rows in reads:
                slabs[var, level, r] = rows

        return store

    for copy in arrive(0):
        copy.wait()
    if levels > 2:
        for copy in arrive(2):
            copy.start()
    advance(0)()

    @pl.loop(1, levels)
    def _(level):
        for copy in arrive(level):
            copy.wait()

        @pl.when(level + 2 < levels)
        def _():
            for copy in arrive(level + 2):
                copy.start()

        store = advance(level)
        pack(level - 1)
        store()
        leave(level - 1).start()

    pack(levels - 1)
    leave(levels - 1).start()
    for level in range(levels):
        leave(level).wait()


def inner(own, raw):
    members, variables, levels, span, columns = own.shape
    lanes = variables * members
    blocks = columns // SPAN
    count = span - 2 * STEPS
    fixed = [pltpu.with_memory_space_constraint(x, pltpu.HBM) for x in (own, *raw)]
    return pl.pallas_call(
        inner_kernel,
        out_shape=[
            jax.ShapeDtypeStruct((variables, levels, span, members, columns), jnp.float32),
            jax.ShapeDtypeStruct((levels, count, lanes, columns), jnp.bfloat16),
            jax.ShapeDtypeStruct((blocks, levels * count * SPAN, lanes), jnp.bfloat16),
            jax.ShapeDtypeStruct((levels, 5, 8, columns), jnp.float32),
        ],
        in_specs=hbm(4),
        out_specs=vmem(2) + hbm(1) + vmem(1),
        scratch_shapes=[
            pltpu.VMEM(raw[0].shape, jnp.float32),
            pltpu.SMEM(raw[1].shape, jnp.float32),
            pltpu.SMEM(raw[2].shape, jnp.float32),
            pltpu.VMEM((levels, variables, members, span, columns), jnp.float32),
            pltpu.VMEM((levels, blocks, count * SPAN, lanes), jnp.bfloat16),
            pltpu.SemaphoreType.DMA((levels, variables)),
            pltpu.SemaphoreType.DMA((3,)),
            pltpu.SemaphoreType.DMA((levels,)),
        ],
        compiler_params=params(10),
        cost_estimate=cost(2 * 10**9, 4 * 2**20),
    )(*fixed)


def outer_kernel(near, own, *rest):
    sides, rest = rest[:near], rest[near:]
    model, centre, grid, packed, staged, near_tiles, sems, out_sems, near_sems = rest
    variables, levels, span, members, columns = own.shape
    rows_each = variables * members
    pairs = (2 * EDGE + span) // 2
    size = STEPS * 2 * SPAN
    identity = permutation(columns, 0)
    shifts = both_ways(columns)

    def arrive(level):
        return [
            pltpu.make_async_copy(
                side.at[:, level], near_tiles.at[i, :, level], near_sems.at[i, level]
            )
            for i, side in enumerate(sides)
        ]

    for level in range(levels):
        for copy in arrive(level):
            copy.start()

    def leave(level):
        here = pl.ds(pl.multiple_of(level * size, size), size)
        return pltpu.make_async_copy(staged.at[level], packed.at[:, here], out_sems.at[level])

    copies = []
    for r in range(STEPS, span - STEPS):
        half, pair = divmod(r + EDGE, pairs)
        place = grid.at[:, pair, pl.ds(half * rows_each, rows_each)]
        copies.append(pltpu.make_async_copy(centre.at[:, r - STEPS], place, sems.at[r - STEPS]))
        copies[-1].start()

    @pl.loop(0, levels)
    def _(level):
        for copy in arrive(level):
            copy.wait()
        coefficients = [model[level, i] for i in range(5)]
        made = []
        for var in range(variables):
            read = row_reader(level, var, own, near_tiles.at[0], near_tiles.at[near - 1])
            for first, last in ((-EDGE, STEPS), (span - STEPS, span + EDGE)):
                for r, value in forecast_rows(read, first, last, coefficients, shifts):
                    made.append((var, r, value))
        sheets = []
        for first in (0, span - STEPS):
            rows = [one for r in range(first, first + STEPS) for _, at, one in made if at == r]
            sheets.append(jnp.concatenate(rows, axis=0))
        pack_rows(sheets, identity, staged.at[level], 0)
        leave(level).start()
        for var, r, value in made:
            half, pair = divmod(r + EDGE, pairs)
            at = half * rows_each + var * members
            grid[level, pair, at : at + members, :] = value

    for level in range(levels):
        leave(level).wait()
    for copy in copies:
        copy.wait()


def outer(dims, own, sides, model, centre, slots):
    members, variables, levels, span, columns = dims
    lanes = members * variables
    blocks = columns // SPAN
    near = len(sides)
    pairs = (2 * EDGE + span) // 2
    return pl.pallas_call(
        functools.partial(outer_kernel, near),
        out_shape=[
            jax.ShapeDtypeStruct((levels, pairs, 2 * lanes, columns), jnp.bfloat16),
            jax.ShapeDtypeStruct(
                (blocks, levels * 2 * STEPS * SPAN + slots // 2, lanes), jnp.bfloat16
            ),
        ],
        in_specs=vmem(1) + hbm(near) + vmem(1) + hbm(1),
        out_specs=vmem(1) + hbm(1),
        scratch_shapes=[
            pltpu.VMEM((levels, blocks, 2 * STEPS * SPAN, lanes), jnp.bfloat16),
            pltpu.VMEM((near, *own.shape), jnp.float32),
            pltpu.SemaphoreType.DMA((span - 2 * STEPS,)),
            pltpu.SemaphoreType.DMA((levels,)),
            pltpu.SemaphoreType.DMA((near, levels)),
        ],
        compiler_params=params(16),
        cost_estimate=cost(2 * 10**9, 8 * 2**20),
    )(own, *(pltpu.with_memory_space_constraint(x, pltpu.HBM) for x in sides), model, centre)


def pick_kernel(variables, together, grid, _, cells, out, region, codes, staged, sems):
    levels, pairs, twice, columns = grid.shape
    rows = twice // 2
    members = rows // variables
    blocks, slots = cells.shape
    width = 2 * EDGE + SPAN
    part = pairs * width
    entries = levels * part
    share = out.shape[1] - slots // 2

    order = permutation(columns, -EDGE)
    batch = next(n for n in (4, 2, 1) if pairs % n == 0)
    for level in range(levels):
        for start in range(0, pairs, batch):
            made = []
            for i in range(batch):
                even = dot_rows(order, grid[level, start + i])
                odd = jnp.concatenate([even[SPAN:], even[:SPAN]], axis=0)
                made.append((even.astype(jnp.bfloat16), odd.astype(jnp.bfloat16)))
            for i, both in enumerate(made):
                at = (level * pairs + start + i) * width
                for first, value in enumerate(both):
                    for j in range(columns // width):
                        piece = value[j * width : (j + 1) * width, :]
                        region[2 * j + first, at : at + width, :] = piece

    cell = cells[...]
    second = cell >= 2 * entries
    cell = jnp.where(second, cell - 2 * entries, cell)
    level = lax.shift_right_logical(cell, (2 * part).bit_length() - 1)
    inside = cell - level * (2 * part)
    lower = inside >= part
    code = level * part + jnp.where(lower, inside - part + entries, inside)
    codes[...] = jnp.where(second, code + 2 * entries, code).astype(jnp.float32)

    left = lax.broadcasted_iota(jnp.int32, (slots // 2, rows), 1) < members
    lane = lax.broadcasted_iota(jnp.int32, (slots, entries), 1).astype(jnp.float32)

    def leave(step):
        here = pl.ds(step * together, together)
        place = out.at[here, pl.ds(share, slots // 2)]
        return pltpu.make_async_copy(staged.at[here], place, sems.at[step])

    @pl.loop(0, blocks // together)
    def _(step):
        made = []
        for i in range(together):
            block = step * together + i
            at = column_of(codes[pl.ds(block, 1), :])
            second = at >= 2.0 * entries
            at = jnp.where(second, at - 2.0 * entries, at)
            lower = at >= 1.0 * entries
            at = jnp.where(lower, at - 1.0 * entries, at)
            pick = jnp.where(lane == at, 1.0, 0.0).astype(jnp.bfloat16)
            found = dot(pick, region[block])
            total = jnp.where(lower, found[:, rows:], found[:, :rows])
            other = pltpu.roll(total, members, 1)
            to_left = jnp.where(second, other, total)[: slots // 2]
            to_right = jnp.where(second, total, other)[slots // 2 :]
            made.append(jnp.where(left, to_left, to_right).astype(jnp.bfloat16))
        for i, value in enumerate(made):
            staged[step * together + i] = value
        leave(step).start()

    for step in range(blocks // together):
        leave(step).wait()


def pick(variables, grid, packed, cells):
    levels, pairs, twice, columns = grid.shape
    blocks, slots = cells.shape
    together = next(n for n in (4, 2, 1) if blocks % n == 0)
    return pl.pallas_call(
        functools.partial(pick_kernel, variables, together),
        out_shape=jax.ShapeDtypeStruct(packed.shape, packed.dtype),
        in_specs=vmem(1) + hbm(1) + vmem(1),
        out_specs=pl.BlockSpec(memory_space=pltpu.HBM),
        scratch_shapes=[
            pltpu.VMEM((blocks, levels * pairs * (2 * EDGE + SPAN), twice), jnp.bfloat16),
            pltpu.VMEM((blocks, slots), jnp.float32),
            pltpu.VMEM((blocks, slots // 2, packed.shape[2]), jnp.bfloat16),
            pltpu.SemaphoreType.DMA((blocks // together,)),
        ],
        input_output_aliases={1: 0},
        compiler_params=params(20),
        cost_estimate=cost(4 * 10**9, 4 * 2**20),
    )(grid, packed, cells)


def join(a, b, members):
    return (
        jnp.concatenate([a[:, :members], b[:, :members]], axis=1),
        jnp.concatenate([a[:, members:], b[:, members:]], axis=1),
    )


def batches(count, size):
    return [range(at, min(count, at + size)) for at in range(0, count, size)]


def deviations(states, raw, dev, at, size):
    groups, _, lanes = states.shape
    members = lanes // 2
    sums = [jnp.zeros((size, lanes), jnp.float32)] * 2
    for batch in batches(groups // 2, 4):
        made = [
            [
                x.astype(jnp.float32)
                for x in join(states[2 * j, :size, :], states[2 * j + 1, :size, :], members)
            ]
            for j in batch
        ]
        for j, pair in zip(batch, made):
            here = slice(j * lanes, (j + 1) * lanes)
            for var in range(2):
                raw[var * size : (var + 1) * size, here] = pair[var]
            sums = [total + one for total, one in zip(sums, pair)]
    centre = jnp.concatenate([jnp.sum(x, axis=1, keepdims=True) for x in sums], axis=0)
    centre = centre * (1.0 / (groups * members))
    dev[at : at + 2 * size, :] = (raw[...] - centre).astype(jnp.bfloat16)
    return centre


def prepare_kernel(states, dev, centre, raw):
    mean = deviations(states, raw, dev, 0, states.shape[1])
    centre[...] = jnp.broadcast_to(mean, centre.shape)


def prepare(states):
    groups, near, lanes = states.shape
    total = groups * lanes // 2
    return pl.pallas_call(
        prepare_kernel,
        out_shape=[
            jax.ShapeDtypeStruct((2 * near, total), jnp.bfloat16),
            jax.ShapeDtypeStruct((2 * near, lanes), jnp.float32),
        ],
        in_specs=vmem(1),
        out_specs=vmem(2),
        scratch_shapes=[pltpu.VMEM((2 * near, total), jnp.float32)],
        compiler_params=params(6),
        cost_estimate=cost(10**8, 2 * 2**20),
    )(states)


def analyse_kernel(first, means, second, count, value, weight, out, raw, dev, obs, scaled_ref):
    groups, _, lanes = second.shape
    near = first.shape[0] // 2
    half = obs.shape[0] // 2
    far = second.shape[1] - half
    side = near + far
    slots = 2 * half
    members = lanes // 2
    total_members = groups * members

    for batch in batches(groups // 2, 4):
        made = [
            [
                x.astype(jnp.float32)
                for x in join(second[2 * j, far:, :], second[2 * j + 1, far:, :], members)
            ]
            for j in batch
        ]
        for j, pair in zip(batch, made):
            here = slice(j * lanes, (j + 1) * lanes)
            obs[:half, here], obs[half:, here] = pair

    used = lax.broadcasted_iota(jnp.int32, (1, slots), 1) < count[0, 0]
    root = column_of(jnp.where(used, jnp.sqrt(weight[...]), 0.0))
    observed = obs[...]
    mean = jnp.sum(observed, axis=1, keepdims=True) * (1.0 / total_members)
    scaled = (observed - mean) * root
    energy = jnp.sum(jnp.sum(scaled * scaled, axis=1, keepdims=True), axis=0, keepdims=True)
    scaled_ref[...] = scaled.astype(jnp.bfloat16)
    misfit = row_of(root * (column_of(value[...]) - mean))

    c = total_members - 1.0
    s = energy * (1.0 / total_members) + c
    inverse = 1.0 / s
    a = c * inverse
    p = 1.5 - 0.5 * a
    p2 = p * p
    p3 = p2 * p
    base = 1.5 * p - 0.5 * a * p3
    q0 = -0.75 - 0.5 * (p3 - 1.5 * a * p2)
    q1 = -0.5 * (0.75 * a * p - 1.5 * p2)
    q2 = -0.5 * (0.75 * p - 0.125 * a)
    small = dot_rows(scaled_ref[...], scaled_ref[...]) * inverse
    diagonal = eye(slots)
    once = small.astype(jnp.bfloat16)
    square = dot(once, once).astype(jnp.bfloat16)
    tail = dot(square, (jnp.where(diagonal, q2, 0.0) + 0.0625 * small).astype(jnp.bfloat16))
    poly = jnp.where(diagonal, q0, 0.0) + q1 * small + tail

    def apply(vector):
        inner_part = jnp.sum(poly * vector, axis=1, keepdims=True)
        return jnp.sum(small * inner_part, axis=0, keepdims=True) + base * vector

    gain = apply(apply(misfit)) * inverse
    stretch = jnp.sqrt(a)
    alpha, factor = stretch * base, stretch * inverse
    centre = deviations(second, raw, dev, 0, far)
    cross = jnp.concatenate(
        [dot_rows(first[...], scaled_ref[...]), dot_rows(dev[...], scaled_ref[...])], axis=0
    )
    centre = jnp.concatenate([means[:, 0:1], centre], axis=0)
    shift = centre + jnp.sum(cross * gain, axis=1, keepdims=True)
    once = cross.astype(jnp.bfloat16)
    mix = sum(dot(once, part) for part in split(poly))
    mix = (mix * factor).astype(jnp.bfloat16)
    parts = ((first, 0, near, 0), (dev, 2 * near, far, near))
    for batch in batches(groups // 2, 2):
        made = []
        wide = slice(batch[0] * lanes, (batch[-1] + 1) * lanes)
        both = dot(mix, scaled_ref[:, wide]) + shift
        for j in batch:
            here = slice(j * lanes, (j + 1) * lanes)
            new = both[:, (j - batch[0]) * lanes :][:, :lanes]
            for ref, at, size, row in parts:
                one = new[at : at + 2 * size] + alpha * ref[:, here].astype(jnp.float32)
                one = one.astype(jnp.bfloat16)
                pair = join(one[:size], one[size:], members)
                made += [(2 * j + i, row, x) for i, x in enumerate(pair)]
        for group, row, value in made:
            out[group, row : row + value.shape[0], :] = value


def analyse(first, means, second, count, value, weight):
    groups, _, lanes = second.shape
    near = first.shape[0] // 2
    slots = value.shape[1]
    far = second.shape[1] - slots // 2
    total = groups * lanes // 2
    return pl.pallas_call(
        analyse_kernel,
        out_shape=jax.ShapeDtypeStruct((groups, near + far, lanes), jnp.bfloat16),
        in_specs=vmem(3) + smem(1) + vmem(2),
        out_specs=pl.BlockSpec(memory_space=pltpu.VMEM),
        scratch_shapes=[
            pltpu.VMEM((2 * far, total), jnp.float32),
            pltpu.VMEM((2 * far, total), jnp.bfloat16),
            pltpu.VMEM((slots, total), jnp.float32),
            pltpu.VMEM((slots, total), jnp.bfloat16),
        ],
        compiler_params=params(16),
        cost_estimate=cost(4 * 10**9, 4 * 2**20),
    )(first, means, second, count, value, weight)


def restore_kernel(blocks, out, turned, staged, sems):
    members, variables, levels, span, columns = out.shape
    lanes = members * variables
    identity = permutation(lanes, 0)
    near = span - 2 * STEPS
    for level in range(levels):
        made = []
        for r in range(0, span, 2):
            if STEPS <= r < span - STEPS:
                at = level * near + r - STEPS
            else:
                at = levels * near + level * 2 * STEPS + (r if r < STEPS else r - near)
            both = blocks[:, at * SPAN : (at + 2) * SPAN, :].astype(jnp.float32)
            pair = [both[:, i * SPAN : (i + 1) * SPAN, :].reshape(columns, lanes) for i in range(2)]
            rows = dot_rows(identity, jnp.concatenate(pair, axis=0).astype(jnp.bfloat16))
            made += [(r + i, rows[:, i * columns : (i + 1) * columns]) for i in range(2)]
        for r, rows in made:
            turned[level, pl.ds(r, lanes, stride=span), :] = rows

    chunks = staged.shape[0]
    size = members // chunks
    copies = []
    for i in range(chunks):
        for level in range(levels):
            for var in range(variables):
                at = (var * members + i * size) * span
                part = turned[level, at : at + size * span, :].reshape(size, span, columns)
                staged[i, :, var, level] = part.astype(jnp.bfloat16)
        place = out.at[pl.ds(i * size, size)]
        copies.append(pltpu.make_async_copy(staged.at[i], place, sems.at[i]))
        copies[-1].start()
    for copy in copies:
        copy.wait()


def restore(dims, blocks):
    members, variables, levels, span, columns = dims
    chunks = next(n for n in (4, 2, 1) if members % n == 0)
    return pl.pallas_call(
        restore_kernel,
        out_shape=jax.ShapeDtypeStruct((members, variables, levels, span, columns), jnp.bfloat16),
        in_specs=vmem(1),
        out_specs=pl.BlockSpec(memory_space=pltpu.HBM),
        scratch_shapes=[
            pltpu.VMEM((levels, variables * members * span, columns), jnp.float32),
            pltpu.VMEM((chunks, members // chunks, variables, levels, span, columns), jnp.bfloat16),
            pltpu.SemaphoreType.DMA((chunks,)),
        ],
        compiler_params=params(10),
        cost_estimate=cost(2 * 10**9, 2 * 2**20),
    )(blocks)


def neighbours(field, axis):
    count = lax.axis_size(axis)
    low = lax.ppermute(field, axis, [(i, (i + 1) % count) for i in range(count)])
    if count == 2:
        return (low,)
    return low, lax.ppermute(field, axis, [((i + 1) % count, i) for i in range(count)])


def exchange(blocks):
    return lax.all_to_all(blocks, "grp", split_axis=0, concat_axis=0, tiled=True)


def on_device(start, diffusivity, eastward, northward, cells, count, value, weight):
    members, variables, levels, span, columns = dims = start.shape
    own, centre, near, model = inner(start, (diffusivity, eastward, northward))
    sides = neighbours(own, "tile")
    first, means = prepare(exchange(near))
    grid, packed = outer(dims, own, sides, model, centre, cells.shape[2])
    second = exchange(pick(variables, grid, packed, cells[0]))
    updated = analyse(first, means, second, count, value[0], weight[0])
    return restore(dims, exchange(updated))


def solution(mesh):
    return jax.shard_map(
        on_device,
        mesh=mesh,
        in_specs=(
            P("grp", None, None, "tile", None),
            P(),
            P(),
            P(),
            P("tile", None, None),
            P("tile", "grp"),
            P("tile", "grp", None),
            P("tile", "grp", None),
        ),
        out_specs=P("grp", None, None, "tile", None),
        check_vma=False,
    )
```

```python
import functools

import jax
import jax.numpy as jnp
from jax import lax
from jax.experimental import pallas as pl
from jax.experimental.pallas import tpu as pltpu
from jax.sharding import PartitionSpec as P

SPAN = 8
STEPS = 2
EDGE = SPAN // 2

ROWS = (((1,), (1,)), ((), ()))


def params(mebibytes, **kw):
    return pltpu.CompilerParams(vmem_limit_bytes=mebibytes * 2**20, **kw)


def cost(flops, size):
    return pl.CostEstimate(flops=flops, bytes_accessed=size, transcendentals=0)


def vmem(count):
    return [pl.BlockSpec(memory_space=pltpu.VMEM)] * count


def hbm(count):
    return [pl.BlockSpec(memory_space=pltpu.HBM)] * count


def smem(count):
    return [pl.BlockSpec(memory_space=pltpu.SMEM)] * count


def dot(a, b, **kw):
    return jnp.dot(a, b, preferred_element_type=jnp.float32, **kw)


def split(x):
    high = x.astype(jnp.bfloat16)
    return high, (x - high.astype(jnp.float32)).astype(jnp.bfloat16)


def dot_rows(a, b):
    return lax.dot_general(a, b, ROWS, preferred_element_type=jnp.float32)


def permutation(size, shift):
    row = lax.broadcasted_iota(jnp.int32, (size, size), 0)
    column = lax.broadcasted_iota(jnp.int32, (size, size), 1)
    return (lax.rem(row + shift + size, size) == column).astype(jnp.bfloat16)


def eye(size):
    row = lax.broadcasted_iota(jnp.int32, (size, size), 0)
    column = lax.broadcasted_iota(jnp.int32, (size, size), 1)
    return row == column


def column_of(row):
    return jnp.sum(jnp.where(eye(row.shape[1]), row, 0.0), axis=1, keepdims=True)


def row_of(column):
    return jnp.sum(jnp.where(eye(column.shape[0]), column, 0.0), axis=0, keepdims=True)


def both_ways(columns):
    pair = jnp.concatenate([permutation(columns, -1), permutation(columns, 1)], axis=1)
    return jnp.concatenate([pair, pair], axis=0)


def forecast_rows(read, first, last, coefficients, shifts):
    middle, east, west, north, south = coefficients

    def step(below, here, above, ahead, behind):
        return middle * here + east * above + west * below + north * ahead + south * behind

    rows = [read(r) for r in range(first - 2, last + 2)]
    tiles, _, columns = rows[0].shape
    flat = jnp.concatenate(rows[1:-1], axis=0).reshape(-1, columns)
    moved = dot(jnp.concatenate(split(flat), axis=1), shifts)
    ahead = moved[:, :columns].reshape(-1, 8, columns)
    behind = moved[:, columns:].reshape(-1, 8, columns)
    once, twice = [], []
    for i, r in enumerate(range(first - 1, last + 1)):
        here = slice(i * tiles, (i + 1) * tiles)
        once.append(step(*rows[i : i + 3], ahead[here], behind[here]))
        if i >= 2:
            one = once[-2]
            new = step(*once[-3:], pltpu.roll(one, columns - 1, 2), pltpu.roll(one, 1, 2))
            twice.append((r - 1, new.reshape(-1, columns).astype(jnp.bfloat16)))
    return twice


def coefficients_of(level, diff, east, north):
    spread = jnp.broadcast_to(diff[pl.ds(level, 1), :], (8, diff.shape[1]))
    u = 0.5 * east[level]
    w = 0.5 * north[level]
    return 1.0 - 4.0 * spread, spread - u, spread + u, spread - w, spread + w


def row_reader(level, var, own, low, high):
    span, columns = own.shape[2], own.shape[4]

    def read(r):
        ref, at = (low, r + span) if r < 0 else (own, r) if r < span else (high, r - span)
        return ref[var, level, at].reshape(-1, 8, columns)

    return read


def pack_rows(pairs, identity, store, first):
    lanes = pairs[0].shape[0] // 2
    packed = []
    for pair in pairs:
        turned = dot_rows(identity, pair)
        parts = [turned[:, i * lanes : (i + 1) * lanes].reshape(-1, SPAN, lanes) for i in range(2)]
        packed.append(jnp.concatenate(parts, axis=1).astype(jnp.bfloat16))
    for i, value in enumerate(packed):
        at = first + i * 2 * SPAN
        store[:, at : at + 2 * SPAN, :] = value


def inner_kernel(own, *refs):
    raw, (slabs, fields, packed, model) = refs[:3], refs[3:7]
    local, (whole, staged, in_sems, raw_sems, out_sems) = refs[7:10], refs[10:]
    members, variables, levels, span, columns = own.shape
    count = span - 2 * STEPS

    def arrive(level):
        return [
            pltpu.make_async_copy(own.at[:, var, level], whole.at[level, var], in_sems.at[level, var])
            for var in range(variables)
        ]

    def leave(level):
        size = count * SPAN
        here = pl.ds(pl.multiple_of(level * size, size), size)
        return pltpu.make_async_copy(staged.at[level], packed.at[:, here], out_sems.at[level])

    copies = [pltpu.make_async_copy(x, y, raw_sems.at[i]) for i, (x, y) in enumerate(zip(raw, local))]
    for copy in copies:
        copy.start()
    for level in range(min(2, levels)):
        for copy in arrive(level):
            copy.start()
    identity = permutation(columns, 0)
    shifts = both_ways(columns)
    for copy in copies:
        copy.wait()

    def pack(level):
        pairs = [
            fields[level, r : r + 2].reshape(2 * variables * members, columns)
            for r in range(0, count, 2)
        ]
        pack_rows(pairs, identity, staged.at[level], 0)

    def advance(level):
        coefficients = coefficients_of(level, *local)
        reads, made = [], []
        for var in range(variables):
            view = whole.at[level, var].reshape(members * span, columns)

            def read(r):
                rows = view[pl.ds(r, members, stride=span), :]
                reads.append((var, r, rows))
                return rows.reshape(-1, 8, columns)

            for r, value in forecast_rows(read, STEPS, span - STEPS, coefficients, shifts):
                made.append((var, r, value))

        def store():
            for i, one in enumerate(coefficients):
                model[level, i] = one
            for var, r, value in made:
                fields[level, r - STEPS, var * members : (var + 1) * members, :] = value
            for var, r, rows in reads:
                slabs[var, level, r] = rows

        return store

    for copy in arrive(0):
        copy.wait()
    if levels > 2:
        for copy in arrive(2):
            copy.start()
    advance(0)()

    @pl.loop(1, levels)
    def _(level):
        for copy in arrive(level):
            copy.wait()

        @pl.when(level + 2 < levels)
        def _():
            for copy in arrive(level + 2):
                copy.start()

        store = advance(level)
        pack(level - 1)
        store()
        leave(level - 1).start()

    pack(levels - 1)
    leave(levels - 1).start()
    for level in range(levels):
        leave(level).wait()


def inner(own, raw):
    members, variables, levels, span, columns = own.shape
    lanes = variables * members
    blocks = columns // SPAN
    count = span - 2 * STEPS
    fixed = [pltpu.with_memory_space_constraint(x, pltpu.HBM) for x in (own, *raw)]
    return pl.pallas_call(
        inner_kernel,
        out_shape=[
            jax.ShapeDtypeStruct((variables, levels, span, members, columns), jnp.float32),
            jax.ShapeDtypeStruct((levels, count, lanes, columns), jnp.bfloat16),
            jax.ShapeDtypeStruct((blocks, levels * count * SPAN, lanes), jnp.bfloat16),
            jax.ShapeDtypeStruct((levels, 5, 8, columns), jnp.float32),
        ],
        in_specs=hbm(4),
        out_specs=vmem(2) + hbm(1) + vmem(1),
        scratch_shapes=[
            pltpu.VMEM(raw[0].shape, jnp.float32),
            pltpu.SMEM(raw[1].shape, jnp.float32),
            pltpu.SMEM(raw[2].shape, jnp.float32),
            pltpu.VMEM((levels, variables, members, span, columns), jnp.float32),
            pltpu.VMEM((levels, blocks, count * SPAN, lanes), jnp.bfloat16),
            pltpu.SemaphoreType.DMA((levels, variables)),
            pltpu.SemaphoreType.DMA((3,)),
            pltpu.SemaphoreType.DMA((levels,)),
        ],
        compiler_params=params(10),
        cost_estimate=cost(2 * 10**9, 4 * 2**20),
    )(*fixed)


def outer_kernel(near, own, *rest):
    sides, rest = rest[:near], rest[near:]
    model, centre, grid, packed, staged, near_tiles, sems, out_sems, near_sems = rest
    variables, levels, span, members, columns = own.shape
    rows_each = variables * members
    pairs = (2 * EDGE + span) // 2
    size = STEPS * 2 * SPAN
    identity = permutation(columns, 0)
    shifts = both_ways(columns)

    def arrive(level):
        return [
            pltpu.make_async_copy(
                side.at[:, level], near_tiles.at[i, :, level], near_sems.at[i, level]
            )
            for i, side in enumerate(sides)
        ]

    for level in range(levels):
        for copy in arrive(level):
            copy.start()

    def leave(level):
        here = pl.ds(pl.multiple_of(level * size, size), size)
        return pltpu.make_async_copy(staged.at[level], packed.at[:, here], out_sems.at[level])

    copies = []
    for r in range(STEPS, span - STEPS):
        half, pair = divmod(r + EDGE, pairs)
        place = grid.at[:, pair, pl.ds(half * rows_each, rows_each)]
        copies.append(pltpu.make_async_copy(centre.at[:, r - STEPS], place, sems.at[r - STEPS]))
        copies[-1].start()

    @pl.loop(0, levels)
    def _(level):
        for copy in arrive(level):
            copy.wait()
        coefficients = [model[level, i] for i in range(5)]
        made = []
        for var in range(variables):
            read = row_reader(level, var, own, near_tiles.at[0], near_tiles.at[near - 1])
            for first, last in ((-EDGE, STEPS), (span - STEPS, span + EDGE)):
                for r, value in forecast_rows(read, first, last, coefficients, shifts):
                    made.append((var, r, value))
        sheets = []
        for first in (0, span - STEPS):
            rows = [one for r in range(first, first + STEPS) for _, at, one in made if at == r]
            sheets.append(jnp.concatenate(rows, axis=0))
        pack_rows(sheets, identity, staged.at[level], 0)
        leave(level).start()
        for var, r, value in made:
            half, pair = divmod(r + EDGE, pairs)
            at = half * rows_each + var * members
            grid[level, pair, at : at + members, :] = value

    for level in range(levels):
        leave(level).wait()
    for copy in copies:
        copy.wait()


def outer(dims, own, sides, model, centre, slots):
    members, variables, levels, span, columns = dims
    lanes = members * variables
    blocks = columns // SPAN
    near = len(sides)
    pairs = (2 * EDGE + span) // 2
    return pl.pallas_call(
        functools.partial(outer_kernel, near),
        out_shape=[
            jax.ShapeDtypeStruct((levels, pairs, 2 * lanes, columns), jnp.bfloat16),
            jax.ShapeDtypeStruct(
                (blocks, levels * 2 * STEPS * SPAN + slots // 2, lanes), jnp.bfloat16
            ),
        ],
        in_specs=vmem(1) + hbm(near) + vmem(1) + hbm(1),
        out_specs=vmem(1) + hbm(1),
        scratch_shapes=[
            pltpu.VMEM((levels, blocks, 2 * STEPS * SPAN, lanes), jnp.bfloat16),
            pltpu.VMEM((near, *own.shape), jnp.float32),
            pltpu.SemaphoreType.DMA((span - 2 * STEPS,)),
            pltpu.SemaphoreType.DMA((levels,)),
            pltpu.SemaphoreType.DMA((near, levels)),
        ],
        compiler_params=params(16),
        cost_estimate=cost(2 * 10**9, 8 * 2**20),
    )(own, *(pltpu.with_memory_space_constraint(x, pltpu.HBM) for x in sides), model, centre)


def pick_kernel(variables, together, grid, _, cells, out, region, codes, staged, sems):
    levels, pairs, twice, columns = grid.shape
    rows = twice // 2
    members = rows // variables
    blocks, slots = cells.shape
    width = 2 * EDGE + SPAN
    part = pairs * width
    entries = levels * part
    share = out.shape[1] - slots // 2

    order = permutation(columns, -EDGE)
    batch = next(n for n in (4, 2, 1) if pairs % n == 0)
    for level in range(levels):
        for start in range(0, pairs, batch):
            made = []
            for i in range(batch):
                even = dot_rows(order, grid[level, start + i])
                odd = jnp.concatenate([even[SPAN:], even[:SPAN]], axis=0)
                made.append((even.astype(jnp.bfloat16), odd.astype(jnp.bfloat16)))
            for i, both in enumerate(made):
                at = (level * pairs + start + i) * width
                for first, value in enumerate(both):
                    for j in range(columns // width):
                        piece = value[j * width : (j + 1) * width, :]
                        region[2 * j + first, at : at + width, :] = piece

    cell = cells[...]
    second = cell >= 2 * entries
    cell = jnp.where(second, cell - 2 * entries, cell)
    level = lax.shift_right_logical(cell, (2 * part).bit_length() - 1)
    inside = cell - level * (2 * part)
    lower = inside >= part
    code = level * part + jnp.where(lower, inside - part + entries, inside)
    codes[...] = jnp.where(second, code + 2 * entries, code).astype(jnp.float32)

    left = lax.broadcasted_iota(jnp.int32, (slots // 2, rows), 1) < members
    lane = lax.broadcasted_iota(jnp.int32, (slots, entries), 1).astype(jnp.float32)

    def leave(step):
        here = pl.ds(step * together, together)
        place = out.at[here, pl.ds(share, slots // 2)]
        return pltpu.make_async_copy(staged.at[here], place, sems.at[step])

    @pl.loop(0, blocks // together)
    def _(step):
        made = []
        for i in range(together):
            block = step * together + i
            at = column_of(codes[pl.ds(block, 1), :])
            second = at >= 2.0 * entries
            at = jnp.where(second, at - 2.0 * entries, at)
            lower = at >= 1.0 * entries
            at = jnp.where(lower, at - 1.0 * entries, at)
            pick = jnp.where(lane == at, 1.0, 0.0).astype(jnp.bfloat16)
            found = dot(pick, region[block])
            total = jnp.where(lower, found[:, rows:], found[:, :rows])
            other = pltpu.roll(total, members, 1)
            to_left = jnp.where(second, other, total)[: slots // 2]
            to_right = jnp.where(second, total, other)[slots // 2 :]
            made.append(jnp.where(left, to_left, to_right).astype(jnp.bfloat16))
        for i, value in enumerate(made):
            staged[step * together + i] = value
        leave(step).start()

    for step in range(blocks // together):
        leave(step).wait()


def pick(variables, grid, packed, cells):
    levels, pairs, twice, columns = grid.shape
    blocks, slots = cells.shape
    together = next(n for n in (4, 2, 1) if blocks % n == 0)
    return pl.pallas_call(
        functools.partial(pick_kernel, variables, together),
        out_shape=jax.ShapeDtypeStruct(packed.shape, packed.dtype),
        in_specs=vmem(1) + hbm(1) + vmem(1),
        out_specs=pl.BlockSpec(memory_space=pltpu.HBM),
        scratch_shapes=[
            pltpu.VMEM((blocks, levels * pairs * (2 * EDGE + SPAN), twice), jnp.bfloat16),
            pltpu.VMEM((blocks, slots), jnp.float32),
            pltpu.VMEM((blocks, slots // 2, packed.shape[2]), jnp.bfloat16),
            pltpu.SemaphoreType.DMA((blocks // together,)),
        ],
        input_output_aliases={1: 0},
        compiler_params=params(20),
        cost_estimate=cost(4 * 10**9, 4 * 2**20),
    )(grid, packed, cells)


def join(a, b, members):
    return (
        jnp.concatenate([a[:, :members], b[:, :members]], axis=1),
        jnp.concatenate([a[:, members:], b[:, members:]], axis=1),
    )


def batches(count, size):
    return [range(at, min(count, at + size)) for at in range(0, count, size)]


def deviations(states, raw, dev, at, size):
    groups, _, lanes = states.shape
    members = lanes // 2
    sums = [jnp.zeros((size, lanes), jnp.float32)] * 2
    for batch in batches(groups // 2, 4):
        made = [
            [
                x.astype(jnp.float32)
                for x in join(states[2 * j, :size, :], states[2 * j + 1, :size, :], members)
            ]
            for j in batch
        ]
        for j, pair in zip(batch, made):
            here = slice(j * lanes, (j + 1) * lanes)
            for var in range(2):
                raw[var * size : (var + 1) * size, here] = pair[var]
            sums = [total + one for total, one in zip(sums, pair)]
    centre = jnp.concatenate([jnp.sum(x, axis=1, keepdims=True) for x in sums], axis=0)
    centre = centre * (1.0 / (groups * members))
    dev[at : at + 2 * size, :] = (raw[...] - centre).astype(jnp.bfloat16)
    return centre


def prepare_kernel(states, count, value, weight, dev, centre, roots, values, raw):
    mean = deviations(states, raw, dev, 0, states.shape[1])
    centre[...] = jnp.broadcast_to(mean, centre.shape)
    used = lax.broadcasted_iota(jnp.int32, weight.shape, 1) < count[0, 0]
    root = column_of(jnp.where(used, jnp.sqrt(weight[...]), 0.0))
    roots[...] = jnp.broadcast_to(root, roots.shape)
    values[...] = jnp.broadcast_to(column_of(value[...]), values.shape)


def prepare(states, count, value, weight):
    groups, near, lanes = states.shape
    total = groups * lanes // 2
    column = jax.ShapeDtypeStruct((value.shape[1], lanes), jnp.float32)
    return pl.pallas_call(
        prepare_kernel,
        out_shape=[
            jax.ShapeDtypeStruct((2 * near, total), jnp.bfloat16),
            jax.ShapeDtypeStruct((2 * near, lanes), jnp.float32),
            column,
            column,
        ],
        in_specs=vmem(1) + smem(1) + vmem(2),
        out_specs=vmem(4),
        scratch_shapes=[pltpu.VMEM((2 * near, total), jnp.float32)],
        compiler_params=params(6),
        cost_estimate=cost(10**8, 2 * 2**20),
    )(states, count, value, weight)


def analyse_kernel(first, means, roots, values, second, out, raw, dev, obs, scaled_ref):
    groups, _, lanes = second.shape
    near = first.shape[0] // 2
    half = obs.shape[0] // 2
    far = second.shape[1] - half
    side = near + far
    slots = 2 * half
    members = lanes // 2
    total_members = groups * members

    for batch in batches(groups // 2, 4):
        made = [
            [
                x.astype(jnp.float32)
                for x in join(second[2 * j, far:, :], second[2 * j + 1, far:, :], members)
            ]
            for j in batch
        ]
        for j, pair in zip(batch, made):
            here = slice(j * lanes, (j + 1) * lanes)
            obs[:half, here], obs[half:, here] = pair

    root = roots[:, 0:1]
    observed = obs[...]
    mean = jnp.sum(observed, axis=1, keepdims=True) * (1.0 / total_members)
    scaled = (observed - mean) * root
    energy = jnp.sum(jnp.sum(scaled * scaled, axis=1, keepdims=True), axis=0, keepdims=True)
    scaled_ref[...] = scaled.astype(jnp.bfloat16)
    misfit = row_of(root * (values[:, 0:1] - mean))

    c = total_members - 1.0
    s = energy * (1.0 / total_members) + c
    inverse = 1.0 / s
    a = c * inverse
    p = 1.5 - 0.5 * a
    p2 = p * p
    p3 = p2 * p
    base = 1.5 * p - 0.5 * a * p3
    q0 = -0.75 - 0.5 * (p3 - 1.5 * a * p2)
    q1 = -0.5 * (0.75 * a * p - 1.5 * p2)
    q2 = -0.5 * (0.75 * p - 0.125 * a)
    small = dot_rows(scaled_ref[...], scaled_ref[...]) * inverse
    diagonal = eye(slots)
    once = small.astype(jnp.bfloat16)
    square = dot(once, once).astype(jnp.bfloat16)
    tail = dot(square, (jnp.where(diagonal, q2, 0.0) + 0.0625 * small).astype(jnp.bfloat16))
    poly = jnp.where(diagonal, q0, 0.0) + q1 * small + tail

    def apply(vector):
        inner_part = jnp.sum(poly * vector, axis=1, keepdims=True)
        return jnp.sum(small * inner_part, axis=0, keepdims=True) + base * vector

    gain = apply(apply(misfit)) * inverse
    stretch = jnp.sqrt(a)
    alpha, factor = stretch * base, stretch * inverse
    centre = deviations(second, raw, dev, 0, far)
    cross = jnp.concatenate(
        [dot_rows(first[...], scaled_ref[...]), dot_rows(dev[...], scaled_ref[...])], axis=0
    )
    centre = jnp.concatenate([means[:, 0:1], centre], axis=0)
    shift = centre + jnp.sum(cross * gain, axis=1, keepdims=True)
    once = cross.astype(jnp.bfloat16)
    mix = sum(dot(once, part) for part in split(poly))
    mix = (mix * factor).astype(jnp.bfloat16)
    parts = ((first, 0, near, 0), (dev, 2 * near, far, near))
    for batch in batches(groups // 2, 2):
        made = []
        wide = slice(batch[0] * lanes, (batch[-1] + 1) * lanes)
        both = dot(mix, scaled_ref[:, wide]) + shift
        for j in batch:
            here = slice(j * lanes, (j + 1) * lanes)
            new = both[:, (j - batch[0]) * lanes :][:, :lanes]
            for ref, at, size, row in parts:
                one = new[at : at + 2 * size] + alpha * ref[:, here].astype(jnp.float32)
                one = one.astype(jnp.bfloat16)
                pair = join(one[:size], one[size:], members)
                made += [(2 * j + i, row, x) for i, x in enumerate(pair)]
        for group, row, value in made:
            out[group, row : row + value.shape[0], :] = value


def analyse(first, means, roots, values, second):
    groups, _, lanes = second.shape
    near = first.shape[0] // 2
    slots = values.shape[0]
    far = second.shape[1] - slots // 2
    total = groups * lanes // 2
    return pl.pallas_call(
        analyse_kernel,
        out_shape=jax.ShapeDtypeStruct((groups, near + far, lanes), jnp.bfloat16),
        in_specs=vmem(5),
        out_specs=pl.BlockSpec(memory_space=pltpu.VMEM),
        scratch_shapes=[
            pltpu.VMEM((2 * far, total), jnp.float32),
            pltpu.VMEM((2 * far, total), jnp.bfloat16),
            pltpu.VMEM((slots, total), jnp.float32),
            pltpu.VMEM((slots, total), jnp.bfloat16),
        ],
        compiler_params=params(16),
        cost_estimate=cost(4 * 10**9, 4 * 2**20),
    )(first, means, roots, values, second)


def restore_kernel(blocks, out, turned, staged, sems):
    members, variables, levels, span, columns = out.shape
    lanes = members * variables
    identity = permutation(lanes, 0)
    near = span - 2 * STEPS
    for level in range(levels):
        made = []
        for r in range(0, span, 2):
            if STEPS <= r < span - STEPS:
                at = level * near + r - STEPS
            else:
                at = levels * near + level * 2 * STEPS + (r if r < STEPS else r - near)
            both = blocks[:, at * SPAN : (at + 2) * SPAN, :].astype(jnp.float32)
            pair = [both[:, i * SPAN : (i + 1) * SPAN, :].reshape(columns, lanes) for i in range(2)]
            rows = dot_rows(identity, jnp.concatenate(pair, axis=0).astype(jnp.bfloat16))
            made += [(r + i, rows[:, i * columns : (i + 1) * columns]) for i in range(2)]
        for r, rows in made:
            turned[level, pl.ds(r, lanes, stride=span), :] = rows

    chunks = staged.shape[0]
    size = members // chunks
    copies = []
    for i in range(chunks):
        for level in range(levels):
            for var in range(variables):
                at = (var * members + i * size) * span
                part = turned[level, at : at + size * span, :].reshape(size, span, columns)
                staged[i, :, var, level] = part.astype(jnp.bfloat16)
        place = out.at[pl.ds(i * size, size)]
        copies.append(pltpu.make_async_copy(staged.at[i], place, sems.at[i]))
        copies[-1].start()
    for copy in copies:
        copy.wait()


def restore(dims, blocks):
    members, variables, levels, span, columns = dims
    chunks = next(n for n in (4, 2, 1) if members % n == 0)
    return pl.pallas_call(
        restore_kernel,
        out_shape=jax.ShapeDtypeStruct((members, variables, levels, span, columns), jnp.bfloat16),
        in_specs=vmem(1),
        out_specs=pl.BlockSpec(memory_space=pltpu.HBM),
        scratch_shapes=[
            pltpu.VMEM((levels, variables * members * span, columns), jnp.float32),
            pltpu.VMEM((chunks, members // chunks, variables, levels, span, columns), jnp.bfloat16),
            pltpu.SemaphoreType.DMA((chunks,)),
        ],
        compiler_params=params(10),
        cost_estimate=cost(2 * 10**9, 2 * 2**20),
    )(blocks)


def neighbours(field, axis):
    count = lax.axis_size(axis)
    low = lax.ppermute(field, axis, [(i, (i + 1) % count) for i in range(count)])
    if count == 2:
        return (low,)
    return low, lax.ppermute(field, axis, [((i + 1) % count, i) for i in range(count)])


def exchange(blocks):
    return lax.all_to_all(blocks, "grp", split_axis=0, concat_axis=0, tiled=True)


def on_device(start, diffusivity, eastward, northward, cells, count, value, weight):
    members, variables, levels, span, columns = dims = start.shape
    own, centre, near, model = inner(start, (diffusivity, eastward, northward))
    sides = neighbours(own, "tile")
    prepared = prepare(exchange(near), count, value[0], weight[0])
    grid, packed = outer(dims, own, sides, model, centre, cells.shape[2])
    second = exchange(pick(variables, grid, packed, cells[0]))
    updated = analyse(*prepared, second)
    return restore(dims, exchange(updated))


def solution(mesh):
    return jax.shard_map(
        on_device,
        mesh=mesh,
        in_specs=(
            P("grp", None, None, "tile", None),
            P(),
            P(),
            P(),
            P("tile", None, None),
            P("tile", "grp"),
            P("tile", "grp", None),
            P("tile", "grp", None),
        ),
        out_specs=P("grp", None, None, "tile", None),
        check_vma=False,
    )
```

```python
import functools

import jax
import jax.numpy as jnp
from jax import lax
from jax.experimental import pallas as pl
from jax.experimental.pallas import tpu as pltpu
from jax.sharding import PartitionSpec as P

SPAN = 8
STEPS = 2
EDGE = SPAN // 2

ROWS = (((1,), (1,)), ((), ()))


def params(mebibytes, **kw):
    return pltpu.CompilerParams(vmem_limit_bytes=mebibytes * 2**20, **kw)


def cost(flops, size):
    return pl.CostEstimate(flops=flops, bytes_accessed=size, transcendentals=0)


def vmem(count):
    return [pl.BlockSpec(memory_space=pltpu.VMEM)] * count


def hbm(count):
    return [pl.BlockSpec(memory_space=pltpu.HBM)] * count


def smem(count):
    return [pl.BlockSpec(memory_space=pltpu.SMEM)] * count


def dot(a, b, **kw):
    return jnp.dot(a, b, preferred_element_type=jnp.float32, **kw)


def split(x):
    high = x.astype(jnp.bfloat16)
    return high, (x - high.astype(jnp.float32)).astype(jnp.bfloat16)


def dot_rows(a, b):
    return lax.dot_general(a, b, ROWS, preferred_element_type=jnp.float32)


def permutation(size, shift):
    row = lax.broadcasted_iota(jnp.int32, (size, size), 0)
    column = lax.broadcasted_iota(jnp.int32, (size, size), 1)
    return (lax.rem(row + shift + size, size) == column).astype(jnp.bfloat16)


def eye(size):
    row = lax.broadcasted_iota(jnp.int32, (size, size), 0)
    column = lax.broadcasted_iota(jnp.int32, (size, size), 1)
    return row == column


def column_of(row):
    return jnp.sum(jnp.where(eye(row.shape[1]), row, 0.0), axis=1, keepdims=True)


def row_of(column):
    return jnp.sum(jnp.where(eye(column.shape[0]), column, 0.0), axis=0, keepdims=True)


def both_ways(columns):
    pair = jnp.concatenate([permutation(columns, -1), permutation(columns, 1)], axis=1)
    return jnp.concatenate([pair, pair], axis=0)


def forecast_rows(read, first, last, coefficients, shifts):
    middle, east, west, north, south = coefficients

    def step(below, here, above, ahead, behind):
        return middle * here + east * above + west * below + north * ahead + south * behind

    rows = [read(r) for r in range(first - 2, last + 2)]
    tiles, _, columns = rows[0].shape
    flat = jnp.concatenate(rows[1:-1], axis=0).reshape(-1, columns)
    moved = dot(jnp.concatenate(split(flat), axis=1), shifts)
    ahead = moved[:, :columns].reshape(-1, 8, columns)
    behind = moved[:, columns:].reshape(-1, 8, columns)
    once, twice = [], []
    for i, r in enumerate(range(first - 1, last + 1)):
        here = slice(i * tiles, (i + 1) * tiles)
        once.append(step(*rows[i : i + 3], ahead[here], behind[here]))
        if i >= 2:
            one = once[-2]
            new = step(*once[-3:], pltpu.roll(one, columns - 1, 2), pltpu.roll(one, 1, 2))
            twice.append((r - 1, new.reshape(-1, columns).astype(jnp.bfloat16)))
    return twice


def coefficients_of(level, diff, east, north):
    spread = jnp.broadcast_to(diff[pl.ds(level, 1), :], (8, diff.shape[1]))
    u = 0.5 * east[level]
    w = 0.5 * north[level]
    return 1.0 - 4.0 * spread, spread - u, spread + u, spread - w, spread + w


def row_reader(level, var, own, low, high):
    span, columns = own.shape[2], own.shape[4]

    def read(r):
        ref, at = (low, r + span) if r < 0 else (own, r) if r < span else (high, r - span)
        return ref[var, level, at].reshape(-1, 8, columns)

    return read


def pack_rows(pairs, identity, store, first):
    lanes = pairs[0].shape[0] // 2
    packed = []
    for pair in pairs:
        turned = dot_rows(identity, pair)
        parts = [turned[:, i * lanes : (i + 1) * lanes].reshape(-1, SPAN, lanes) for i in range(2)]
        packed.append(jnp.concatenate(parts, axis=1).astype(jnp.bfloat16))
    for i, value in enumerate(packed):
        at = first + i * 2 * SPAN
        store[:, at : at + 2 * SPAN, :] = value


def inner_kernel(own, *refs):
    raw, (slabs, fields, packed, model) = refs[:3], refs[3:7]
    local, (whole, staged, in_sems, raw_sems, out_sems) = refs[7:10], refs[10:]
    members, variables, levels, span, columns = own.shape
    count = span - 2 * STEPS

    def arrive(level):
        return [
            pltpu.make_async_copy(own.at[:, var, level], whole.at[level, var], in_sems.at[level, var])
            for var in range(variables)
        ]

    def leave(level):
        size = count * SPAN
        here = pl.ds(pl.multiple_of(level * size, size), size)
        return pltpu.make_async_copy(staged.at[level], packed.at[:, here], out_sems.at[level])

    copies = [pltpu.make_async_copy(x, y, raw_sems.at[i]) for i, (x, y) in enumerate(zip(raw, local))]
    for copy in copies:
        copy.start()
    for level in range(min(2, levels)):
        for copy in arrive(level):
            copy.start()
    identity = permutation(columns, 0)
    shifts = both_ways(columns)
    for copy in copies:
        copy.wait()

    def pack(level):
        pairs = [
            fields[level, r : r + 2].reshape(2 * variables * members, columns)
            for r in range(0, count, 2)
        ]
        pack_rows(pairs, identity, staged.at[level], 0)

    def advance(level):
        coefficients = coefficients_of(level, *local)
        reads, made = [], []
        for var in range(variables):
            view = whole.at[level, var].reshape(members * span, columns)

            def read(r):
                rows = view[pl.ds(r, members, stride=span), :]
                reads.append((var, r, rows))
                return rows.reshape(-1, 8, columns)

            for r, value in forecast_rows(read, STEPS, span - STEPS, coefficients, shifts):
                made.append((var, r, value))

        def store():
            for i, one in enumerate(coefficients):
                model[level, i] = one
            for var, r, value in made:
                fields[level, r - STEPS, var * members : (var + 1) * members, :] = value
            for var, r, rows in reads:
                slabs[var, level, r] = rows

        return store

    for copy in arrive(0):
        copy.wait()
    if levels > 2:
        for copy in arrive(2):
            copy.start()
    advance(0)()

    @pl.loop(1, levels)
    def _(level):
        for copy in arrive(level):
            copy.wait()

        @pl.when(level + 2 < levels)
        def _():
            for copy in arrive(level + 2):
                copy.start()

        store = advance(level)
        pack(level - 1)
        store()
        leave(level - 1).start()

    pack(levels - 1)
    leave(levels - 1).start()
    for level in range(levels):
        leave(level).wait()


def inner(own, raw):
    members, variables, levels, span, columns = own.shape
    lanes = variables * members
    blocks = columns // SPAN
    count = span - 2 * STEPS
    fixed = [pltpu.with_memory_space_constraint(x, pltpu.HBM) for x in (own, *raw)]
    return pl.pallas_call(
        inner_kernel,
        out_shape=[
            jax.ShapeDtypeStruct((variables, levels, span, members, columns), jnp.float32),
            jax.ShapeDtypeStruct((levels, count, lanes, columns), jnp.bfloat16),
            jax.ShapeDtypeStruct((blocks, levels * count * SPAN, lanes), jnp.bfloat16),
            jax.ShapeDtypeStruct((levels, 5, 8, columns), jnp.float32),
        ],
        in_specs=hbm(4),
        out_specs=vmem(2) + hbm(1) + vmem(1),
        scratch_shapes=[
            pltpu.VMEM(raw[0].shape, jnp.float32),
            pltpu.SMEM(raw[1].shape, jnp.float32),
            pltpu.SMEM(raw[2].shape, jnp.float32),
            pltpu.VMEM((levels, variables, members, span, columns), jnp.float32),
            pltpu.VMEM((levels, blocks, count * SPAN, lanes), jnp.bfloat16),
            pltpu.SemaphoreType.DMA((levels, variables)),
            pltpu.SemaphoreType.DMA((3,)),
            pltpu.SemaphoreType.DMA((levels,)),
        ],
        compiler_params=params(10),
        cost_estimate=cost(2 * 10**9, 4 * 2**20),
    )(*fixed)


def outer_kernel(near, own, *rest):
    sides, rest = rest[:near], rest[near:]
    model, centre, grid, packed, staged, near_tiles, sems, out_sems, near_sems = rest
    variables, levels, span, members, columns = own.shape
    rows_each = variables * members
    pairs = (2 * EDGE + span) // 2
    size = STEPS * 2 * SPAN
    identity = permutation(columns, 0)
    shifts = both_ways(columns)

    def arrive(level):
        return [
            pltpu.make_async_copy(
                side.at[:, level], near_tiles.at[i, :, level], near_sems.at[i, level]
            )
            for i, side in enumerate(sides)
        ]

    for level in range(levels):
        for copy in arrive(level):
            copy.start()

    def leave(level):
        here = pl.ds(pl.multiple_of(level * size, size), size)
        return pltpu.make_async_copy(staged.at[level], packed.at[:, here], out_sems.at[level])

    copies = []
    for r in range(STEPS, span - STEPS):
        half, pair = divmod(r + EDGE, pairs)
        place = grid.at[:, pair, pl.ds(half * rows_each, rows_each)]
        copies.append(pltpu.make_async_copy(centre.at[:, r - STEPS], place, sems.at[r - STEPS]))
        copies[-1].start()

    @pl.loop(0, levels)
    def _(level):
        for copy in arrive(level):
            copy.wait()
        coefficients = [model[level, i] for i in range(5)]
        made = []
        for var in range(variables):
            read = row_reader(level, var, own, near_tiles.at[0], near_tiles.at[near - 1])
            for first, last in ((-EDGE, STEPS), (span - STEPS, span + EDGE)):
                for r, value in forecast_rows(read, first, last, coefficients, shifts):
                    made.append((var, r, value))
        sheets = []
        for first in (0, span - STEPS):
            rows = [one for r in range(first, first + STEPS) for _, at, one in made if at == r]
            sheets.append(jnp.concatenate(rows, axis=0))
        pack_rows(sheets, identity, staged.at[level], 0)
        leave(level).start()
        for var, r, value in made:
            half, pair = divmod(r + EDGE, pairs)
            at = half * rows_each + var * members
            grid[level, pair, at : at + members, :] = value

    for level in range(levels):
        leave(level).wait()
    for copy in copies:
        copy.wait()


def outer(dims, own, sides, model, centre, slots):
    members, variables, levels, span, columns = dims
    lanes = members * variables
    blocks = columns // SPAN
    near = len(sides)
    pairs = (2 * EDGE + span) // 2
    return pl.pallas_call(
        functools.partial(outer_kernel, near),
        out_shape=[
            jax.ShapeDtypeStruct((levels, pairs, 2 * lanes, columns), jnp.bfloat16),
            jax.ShapeDtypeStruct(
                (blocks, levels * 2 * STEPS * SPAN + slots // 2, lanes), jnp.bfloat16
            ),
        ],
        in_specs=vmem(1) + hbm(near) + vmem(1) + hbm(1),
        out_specs=vmem(1) + hbm(1),
        scratch_shapes=[
            pltpu.VMEM((levels, blocks, 2 * STEPS * SPAN, lanes), jnp.bfloat16),
            pltpu.VMEM((near, *own.shape), jnp.float32),
            pltpu.SemaphoreType.DMA((span - 2 * STEPS,)),
            pltpu.SemaphoreType.DMA((levels,)),
            pltpu.SemaphoreType.DMA((near, levels)),
        ],
        compiler_params=params(16),
        cost_estimate=cost(2 * 10**9, 8 * 2**20),
    )(own, *(pltpu.with_memory_space_constraint(x, pltpu.HBM) for x in sides), model, centre)


def pick_kernel(variables, together, grid, _, cells, out, region, codes, staged, sems):
    levels, pairs, twice, columns = grid.shape
    rows = twice // 2
    members = rows // variables
    blocks, slots = cells.shape
    width = 2 * EDGE + SPAN
    part = pairs * width
    entries = levels * part
    share = out.shape[1] - slots // 2

    order = permutation(columns, -EDGE)
    batch = next(n for n in (4, 2, 1) if pairs % n == 0)
    for level in range(levels):
        for start in range(0, pairs, batch):
            made = []
            for i in range(batch):
                even = dot_rows(order, grid[level, start + i])
                odd = jnp.concatenate([even[SPAN:], even[:SPAN]], axis=0)
                made.append((even.astype(jnp.bfloat16), odd.astype(jnp.bfloat16)))
            for i, both in enumerate(made):
                at = (level * pairs + start + i) * width
                for first, value in enumerate(both):
                    for j in range(columns // width):
                        piece = value[j * width : (j + 1) * width, :]
                        region[2 * j + first, at : at + width, :] = piece

    cell = cells[...]
    second = cell >= 2 * entries
    cell = jnp.where(second, cell - 2 * entries, cell)
    level = lax.shift_right_logical(cell, (2 * part).bit_length() - 1)
    inside = cell - level * (2 * part)
    lower = inside >= part
    code = level * part + jnp.where(lower, inside - part + entries, inside)
    codes[...] = jnp.where(second, code + 2 * entries, code).astype(jnp.float32)

    left = lax.broadcasted_iota(jnp.int32, (slots // 2, rows), 1) < members
    lane = lax.broadcasted_iota(jnp.int32, (slots, entries), 1).astype(jnp.float32)

    def leave(step):
        here = pl.ds(step * together, together)
        place = out.at[here, pl.ds(share, slots // 2)]
        return pltpu.make_async_copy(staged.at[here], place, sems.at[step])

    @pl.loop(0, blocks // together)
    def _(step):
        made = []
        for i in range(together):
            block = step * together + i
            at = column_of(codes[pl.ds(block, 1), :])
            second = at >= 2.0 * entries
            at = jnp.where(second, at - 2.0 * entries, at)
            lower = at >= 1.0 * entries
            at = jnp.where(lower, at - 1.0 * entries, at)
            pick = jnp.where(lane == at, 1.0, 0.0).astype(jnp.bfloat16)
            found = dot(pick, region[block])
            total = jnp.where(lower, found[:, rows:], found[:, :rows])
            other = pltpu.roll(total, members, 1)
            to_left = jnp.where(second, other, total)[: slots // 2]
            to_right = jnp.where(second, total, other)[slots // 2 :]
            made.append(jnp.where(left, to_left, to_right).astype(jnp.bfloat16))
        for i, value in enumerate(made):
            staged[step * together + i] = value
        leave(step).start()

    for step in range(blocks // together):
        leave(step).wait()


def pick(variables, grid, packed, cells):
    levels, pairs, twice, columns = grid.shape
    blocks, slots = cells.shape
    together = next(n for n in (4, 2, 1) if blocks % n == 0)
    return pl.pallas_call(
        functools.partial(pick_kernel, variables, together),
        out_shape=jax.ShapeDtypeStruct(packed.shape, packed.dtype),
        in_specs=vmem(1) + hbm(1) + vmem(1),
        out_specs=pl.BlockSpec(memory_space=pltpu.HBM),
        scratch_shapes=[
            pltpu.VMEM((blocks, levels * pairs * (2 * EDGE + SPAN), twice), jnp.bfloat16),
            pltpu.VMEM((blocks, slots), jnp.float32),
            pltpu.VMEM((blocks, slots // 2, packed.shape[2]), jnp.bfloat16),
            pltpu.SemaphoreType.DMA((blocks // together,)),
        ],
        input_output_aliases={1: 0},
        compiler_params=params(20),
        cost_estimate=cost(4 * 10**9, 4 * 2**20),
    )(grid, packed, cells)


def join(a, b, members):
    return (
        jnp.concatenate([a[:, :members], b[:, :members]], axis=1),
        jnp.concatenate([a[:, members:], b[:, members:]], axis=1),
    )


def batches(count, size):
    return [range(at, min(count, at + size)) for at in range(0, count, size)]


def deviations(states, raw, dev, at, size):
    groups, _, lanes = states.shape
    members = lanes // 2
    sums = [jnp.zeros((size, lanes), jnp.float32)] * 2
    for batch in batches(groups // 2, 4):
        made = [
            [
                x.astype(jnp.float32)
                for x in join(states[2 * j, :size, :], states[2 * j + 1, :size, :], members)
            ]
            for j in batch
        ]
        for j, pair in zip(batch, made):
            here = slice(j * lanes, (j + 1) * lanes)
            for var in range(2):
                raw[var * size : (var + 1) * size, here] = pair[var]
            sums = [total + one for total, one in zip(sums, pair)]
    centre = jnp.concatenate([jnp.sum(x, axis=1, keepdims=True) for x in sums], axis=0)
    centre = centre * (1.0 / (groups * members))
    dev[at : at + 2 * size, :] = (raw[...] - centre).astype(jnp.bfloat16)
    return centre


def prepare_kernel(states, count, value, weight, dev, centre, roots, values, raw):
    mean = deviations(states, raw, dev, 0, states.shape[1])
    centre[...] = jnp.broadcast_to(mean, centre.shape)
    used = lax.broadcasted_iota(jnp.int32, weight.shape, 1) < count[0, 0]
    root = column_of(jnp.where(used, jnp.sqrt(weight[...]), 0.0))
    roots[...] = jnp.broadcast_to(root, roots.shape)
    values[...] = jnp.broadcast_to(column_of(value[...]), values.shape)


def prepare(states, count, value, weight):
    groups, near, lanes = states.shape
    total = groups * lanes // 2
    column = jax.ShapeDtypeStruct((value.shape[1], lanes), jnp.float32)
    return pl.pallas_call(
        prepare_kernel,
        out_shape=[
            jax.ShapeDtypeStruct((2 * near, total), jnp.bfloat16),
            jax.ShapeDtypeStruct((2 * near, lanes), jnp.float32),
            column,
            column,
        ],
        in_specs=vmem(1) + smem(1) + vmem(2),
        out_specs=vmem(4),
        scratch_shapes=[pltpu.VMEM((2 * near, total), jnp.float32)],
        compiler_params=params(6),
        cost_estimate=cost(10**8, 2 * 2**20),
    )(states, count, value, weight)


def analyse_kernel(first, means, roots, values, second, out, raw, dev, obs, scaled_ref):
    groups, _, lanes = second.shape
    near = first.shape[0] // 2
    half = obs.shape[0] // 2
    far = second.shape[1] - half
    side = near + far
    slots = 2 * half
    members = lanes // 2
    total_members = groups * members

    for batch in batches(groups // 2, 4):
        made = [
            [
                x.astype(jnp.float32)
                for x in join(second[2 * j, far:, :], second[2 * j + 1, far:, :], members)
            ]
            for j in batch
        ]
        for j, pair in zip(batch, made):
            here = slice(j * lanes, (j + 1) * lanes)
            obs[:half, here], obs[half:, here] = pair

    root = roots[:, 0:1]
    observed = obs[...]
    mean = jnp.sum(observed, axis=1, keepdims=True) * (1.0 / total_members)
    scaled = (observed - mean) * root
    energy = jnp.sum(jnp.sum(scaled * scaled, axis=1, keepdims=True), axis=0, keepdims=True)
    scaled_ref[...] = scaled.astype(jnp.bfloat16)
    misfit = row_of(root * (values[:, 0:1] - mean))

    c = total_members - 1.0
    s = energy * (1.0 / total_members) + c
    inverse = 1.0 / s
    a = c * inverse
    p = 1.5 - 0.5 * a
    p2 = p * p
    p3 = p2 * p
    base = 1.5 * p - 0.5 * a * p3
    q0 = -0.75 - 0.5 * (p3 - 1.5 * a * p2)
    q1 = -0.5 * (0.75 * a * p - 1.5 * p2)
    q2 = -0.5 * (0.75 * p - 0.125 * a)
    small = dot_rows(scaled_ref[...], scaled_ref[...]) * inverse
    diagonal = eye(slots)
    once = small.astype(jnp.bfloat16)
    square = dot(once, once).astype(jnp.bfloat16)
    tail = dot(square, (jnp.where(diagonal, q2, 0.0) + 0.0625 * small).astype(jnp.bfloat16))
    poly = jnp.where(diagonal, q0, 0.0) + q1 * small + tail

    def apply(vector):
        inner_part = jnp.sum(poly * vector, axis=1, keepdims=True)
        return jnp.sum(small * inner_part, axis=0, keepdims=True) + base * vector

    gain = apply(apply(misfit)) * inverse
    stretch = jnp.sqrt(a)
    alpha, factor = stretch * base, stretch * inverse
    centre = deviations(second, raw, dev, 0, far)
    cross = jnp.concatenate(
        [dot_rows(first[...], scaled_ref[...]), dot_rows(dev[...], scaled_ref[...])], axis=0
    )
    centre = jnp.concatenate([means[:, 0:1], centre], axis=0)
    shift = centre + jnp.sum(cross * gain, axis=1, keepdims=True)
    once = cross.astype(jnp.bfloat16)
    mix = sum(dot(once, part) for part in split(poly))
    mix = (mix * factor).astype(jnp.bfloat16)
    parts = ((first, 0, near, 0), (dev, 2 * near, far, near))
    for batch in batches(groups // 2, 4):
        made = []
        wide = slice(batch[0] * lanes, (batch[-1] + 1) * lanes)
        both = dot(mix, scaled_ref[:, wide]) + shift
        for j in batch:
            here = slice(j * lanes, (j + 1) * lanes)
            new = both[:, (j - batch[0]) * lanes :][:, :lanes]
            for ref, at, size, row in parts:
                one = new[at : at + 2 * size] + alpha * ref[:, here].astype(jnp.float32)
                one = one.astype(jnp.bfloat16)
                pair = join(one[:size], one[size:], members)
                made += [(2 * j + i, row, x) for i, x in enumerate(pair)]
        for group, row, value in made:
            out[group, row : row + value.shape[0], :] = value


def analyse(first, means, roots, values, second):
    groups, _, lanes = second.shape
    near = first.shape[0] // 2
    slots = values.shape[0]
    far = second.shape[1] - slots // 2
    total = groups * lanes // 2
    return pl.pallas_call(
        analyse_kernel,
        out_shape=jax.ShapeDtypeStruct((groups, near + far, lanes), jnp.bfloat16),
        in_specs=vmem(5),
        out_specs=pl.BlockSpec(memory_space=pltpu.VMEM),
        scratch_shapes=[
            pltpu.VMEM((2 * far, total), jnp.float32),
            pltpu.VMEM((2 * far, total), jnp.bfloat16),
            pltpu.VMEM((slots, total), jnp.float32),
            pltpu.VMEM((slots, total), jnp.bfloat16),
        ],
        compiler_params=params(16),
        cost_estimate=cost(4 * 10**9, 4 * 2**20),
    )(first, means, roots, values, second)


def restore_kernel(blocks, out, turned, staged, sems):
    members, variables, levels, span, columns = out.shape
    lanes = members * variables
    identity = permutation(lanes, 0)
    near = span - 2 * STEPS
    for level in range(levels):
        made = []
        for r in range(0, span, 2):
            if STEPS <= r < span - STEPS:
                at = level * near + r - STEPS
            else:
                at = levels * near + level * 2 * STEPS + (r if r < STEPS else r - near)
            both = blocks[:, at * SPAN : (at + 2) * SPAN, :].astype(jnp.float32)
            pair = [both[:, i * SPAN : (i + 1) * SPAN, :].reshape(columns, lanes) for i in range(2)]
            rows = dot_rows(identity, jnp.concatenate(pair, axis=0).astype(jnp.bfloat16))
            made += [(r + i, rows[:, i * columns : (i + 1) * columns]) for i in range(2)]
        for r, rows in made:
            turned[level, pl.ds(r, lanes, stride=span), :] = rows

    chunks = staged.shape[0]
    size = members // chunks
    copies = []
    for i in range(chunks):
        for level in range(levels):
            for var in range(variables):
                at = (var * members + i * size) * span
                part = turned[level, at : at + size * span, :].reshape(size, span, columns)
                staged[i, :, var, level] = part.astype(jnp.bfloat16)
        place = out.at[pl.ds(i * size, size)]
        copies.append(pltpu.make_async_copy(staged.at[i], place, sems.at[i]))
        copies[-1].start()
    for copy in copies:
        copy.wait()


def restore(dims, blocks):
    members, variables, levels, span, columns = dims
    chunks = next(n for n in (4, 2, 1) if members % n == 0)
    return pl.pallas_call(
        restore_kernel,
        out_shape=jax.ShapeDtypeStruct((members, variables, levels, span, columns), jnp.bfloat16),
        in_specs=vmem(1),
        out_specs=pl.BlockSpec(memory_space=pltpu.HBM),
        scratch_shapes=[
            pltpu.VMEM((levels, variables * members * span, columns), jnp.float32),
            pltpu.VMEM((chunks, members // chunks, variables, levels, span, columns), jnp.bfloat16),
            pltpu.SemaphoreType.DMA((chunks,)),
        ],
        compiler_params=params(10),
        cost_estimate=cost(2 * 10**9, 2 * 2**20),
    )(blocks)


def neighbours(field, axis):
    count = lax.axis_size(axis)
    low = lax.ppermute(field, axis, [(i, (i + 1) % count) for i in range(count)])
    if count == 2:
        return (low,)
    return low, lax.ppermute(field, axis, [((i + 1) % count, i) for i in range(count)])


def exchange(blocks):
    return lax.all_to_all(blocks, "grp", split_axis=0, concat_axis=0, tiled=True)


def on_device(start, diffusivity, eastward, northward, cells, count, value, weight):
    members, variables, levels, span, columns = dims = start.shape
    own, centre, near, model = inner(start, (diffusivity, eastward, northward))
    sides = neighbours(own, "tile")
    prepared = prepare(exchange(near), count, value[0], weight[0])
    grid, packed = outer(dims, own, sides, model, centre, cells.shape[2])
    second = exchange(pick(variables, grid, packed, cells[0]))
    updated = analyse(*prepared, second)
    return restore(dims, exchange(updated))


def solution(mesh):
    return jax.shard_map(
        on_device,
        mesh=mesh,
        in_specs=(
            P("grp", None, None, "tile", None),
            P(),
            P(),
            P(),
            P("tile", None, None),
            P("tile", "grp"),
            P("tile", "grp", None),
            P("tile", "grp", None),
        ),
        out_specs=P("grp", None, None, "tile", None),
        check_vma=False,
    )
```
